32 devices in a mesh: blk: 16 (over z, y, x), tp: 2 (over core).
Axes of the slice: x: 2, y: 2, z: 4, core: 2. Of those that a mesh axis runs over, the one named last changes fastest.
Arguments:
- tokens: bfloat16 [2, 2048, 1024], P(None, 'blk'), may hold values from -6 to 6
- memory: bfloat16 [9408, 1024], P('blk'), may hold values from -6 to 6
- segment_ids: int32 [2, 2048], P(None, 'blk'), may hold values from 0 to 2, as said below
- token_valid: int32 [2, 2048], P(None, 'blk'), may hold values from 0 to 1, as said below
- segment_page: int32 [2, 3], replicated, may hold values from 0 to 15
- gain_one: float32 [1024], replicated, may hold values from 0.5 to 1.5
- weight_query: bfloat16 [1024, 1024], P(None, 'tp'), may hold values from -0.1875 to 0.1875
- weight_key: bfloat16 [1024, 1024], P(None, 'tp'), may hold values from -0.1875 to 0.1875
- weight_value: bfloat16 [1024, 1024], P(None, 'tp'), may hold values from -0.1875 to 0.1875
- weight_out: bfloat16 [1024, 1024], P('tp'), may hold values from -1.5 to 1.5
- gain_two: float32 [1024], replicated, may hold values from 0.5 to 1.5
- cross_query: bfloat16 [1024, 1024], P(None, 'tp'), may hold values from -0.1875 to 0.1875
- cross_key: bfloat16 [1024, 1024], P(None, 'tp'), may hold values from -0.1875 to 0.1875
- cross_value: bfloat16 [1024, 1024], P(None, 'tp'), may hold values from -0.1875 to 0.1875
- cross_out: bfloat16 [1024, 1024], P('tp'), may hold values from -0.75 to 0.75
- gain_three: float32 [1024], replicated, may hold values from 0.5 to 1.5
- weight_up: bfloat16 [1024, 4096], P(None, 'tp'), may hold values from -0.1875 to 0.1875
- weight_down: bfloat16 [4096, 1024], P('tp'), may hold values from -0.09375 to 0.09375
- cotangent: bfloat16 [2, 2048, 1024], P(None, 'blk'), may hold values from -6 to 6
Outputs:
- out: bfloat16 [2, 2048, 1024], P(None, 'blk')
- grad_input: float32 [2, 2048, 1024], P(None, 'blk')
- grad_memory: float32 [9408, 1024], P('blk')
- grad_weight_query: float32 [1024, 1024], P('blk', 'tp')
- grad_weight_key: float32 [1024, 1024], P('blk', 'tp')
- grad_weight_value: float32 [1024, 1024], P('blk', 'tp')
- grad_weight_out: float32 [1024, 1024], P('tp', 'blk')
- grad_cross_query: float32 [1024, 1024], P('blk', 'tp')
- grad_cross_key: float32 [1024, 1024], P('blk', 'tp')
- grad_cross_value: float32 [1024, 1024], P('blk', 'tp')
- grad_cross_out: float32 [1024, 1024], P('tp', 'blk')
- grad_weight_up: float32 [1024, 4096], P('blk', 'tp')
- grad_weight_down: float32 [4096, 1024], P('tp', 'blk')
- grad_gain_one: float32 [1024], P('blk')
- grad_gain_two: float32 [1024], P('blk')
- grad_gain_three: float32 [1024], P('blk')
The draws below stay inside these ranges and needn't reach their ends.
Inputs may be any that keep to these rules, and one draw needn't show every extreme that they name: `segment_ids`: never falls along a packed row; each of the 3 segments of a row holds 1 to 1984 tokens, and one segment of every row holds exactly 1984. `token_valid`: 1 at the first token of every segment.
All inputs are finite; a program needn't handle non-finite values.
Results may differ from the reference program's by a relative error of at most 0.028.
Values may be sent and summed in bfloat16 or wider, within the bound.
A program may use at most 320 MiB of HBM per device.

```python
import math
import jax
import jax.numpy as jnp
from jax import lax

D = 1024
HEADS = 16
FF = 4096
MEM_LEN = 588
HEAD_DIM = 64
PACKS = 2
NSEG = 3
PAGES = 16
TOKENS = 2048
SEG_MOST = 1984
MEM_ROWS = 9408


def pack_layout(key):
    big_key, cut_key = jax.random.split(key)
    biggest = jax.random.randint(big_key, (), 0, NSEG)
    remaining = TOKENS - SEG_MOST
    cuts = jnp.sort(jax.random.permutation(cut_key, remaining - 1)[:NSEG - 2] + 1)
    edges = jnp.concatenate([jnp.zeros((1,), jnp.int32), cuts.astype(jnp.int32), jnp.full((1,), remaining, jnp.int32)])
    pieces = edges[1:] - edges[:-1]
    order = jnp.arange(NSEG, dtype=jnp.int32)
    before = pieces[jnp.clip(order, 0, NSEG - 2)]
    after = pieces[jnp.clip(order - 1, 0, NSEG - 2)]
    lengths = jnp.where(order < biggest, before, jnp.where(order == biggest, SEG_MOST, after)).astype(jnp.int32)
    starts = jnp.cumsum(lengths) - lengths
    positions = jnp.arange(TOKENS, dtype=jnp.int32)
    segments = jnp.sum((positions[:, None] >= starts[None, :]).astype(jnp.int32), axis=1) - 1
    begins = jnp.any(positions[:, None] == starts[None, :], axis=1)
    return (segments.astype(jnp.int32), begins)


def segment_layout(key):
    key = jax.random.fold_in(key, 11)
    pack_keys = jax.random.split(key, PACKS)
    return jax.vmap(pack_layout)(pack_keys)


def draw_segment_ids(key, part):
    segments, begins = segment_layout(key)
    return segments


def draw_token_valid(key, part):
    segments, begins = segment_layout(key)
    key = jax.random.fold_in(key, 5)
    keeping = jax.random.randint(key, (PACKS, TOKENS), 0, 8) > 0
    return jnp.where(keeping | begins, 1, 0).astype(jnp.int32)


def with_ends(array, key, low, high):
    extent = array.shape
    spot = [jax.random.randint(jax.random.fold_in(key, axis), (), 0, extent[axis]) for axis in range(len(extent))]
    array = array.at[tuple(spot)].set(low)
    longest = extent.index(max(extent))
    spot[longest] = (spot[longest] + 1) % extent[longest]
    return array.at[tuple(spot)].set(high)


def block_scale(key, extent, shards, low, top_value):
    level, own = 1.0, jax.random.fold_in(key, 6)
    for position, blocks in shards:
        heights = jnp.exp(jax.random.uniform(jax.random.fold_in(own, position), (blocks,), jnp.float32, low / len(shards), top_value / len(shards)))
        level = level * jnp.repeat(heights, extent[position] // blocks).reshape([-1 if axis == position else 1 for axis in range(len(extent))])
    return level


def bell_draw(rng, dims, deviation, most, shards=(), kind=jnp.bfloat16):
    array = deviation * jax.random.normal(rng, dims, jnp.float32)
    if shards:
        array = array * block_scale(rng, dims, shards, -0.22, 0.18)
    return jnp.clip(array, -most, most).astype(kind)


def setup_inputs(seed: int = 0) -> dict:
    key_of = jax.random.split(jax.random.key(seed), 20)
    tokens = bell_draw(key_of[0], (PACKS, TOKENS, D), 1.0, 6.0, ((1, 16),))
    memory = bell_draw(key_of[1], (MEM_ROWS, D), 1.0, 6.0, ((0, 16),))
    segment_ids = draw_segment_ids(jax.random.fold_in(key_of[19], 71), 0)
    token_valid = draw_token_valid(jax.random.fold_in(key_of[19], 71), 0)
    segment_page = with_ends(jax.random.randint(key_of[4], (PACKS, NSEG), 0, PAGES), jax.random.fold_in(key_of[4], 1), 0, PAGES - 1).astype(jnp.int32)
    gain_one = jnp.clip(1.0 + 0.1 * jax.random.normal(key_of[5], (D,), jnp.float32), 0.5, 1.5)
    weight_query = bell_draw(key_of[6], (D, D), D ** -0.5, 0.1875, ((1, 2),))
    weight_key = bell_draw(key_of[7], (D, D), D ** -0.5, 0.1875, ((1, 2),))
    weight_value = bell_draw(key_of[8], (D, D), D ** -0.5, 0.1875, ((1, 2),))
    weight_out = bell_draw(key_of[9], (D, D), (D // 64) ** -0.5, 1.5, ((0, 2),))
    gain_two = jnp.clip(1.0 + 0.1 * jax.random.normal(key_of[10], (D,), jnp.float32), 0.5, 1.5)
    cross_query = bell_draw(key_of[11], (D, D), D ** -0.5, 0.1875, ((1, 2),))
    cross_key = bell_draw(key_of[12], (D, D), D ** -0.5, 0.1875, ((1, 2),))
    cross_value = bell_draw(key_of[13], (D, D), D ** -0.5, 0.1875, ((1, 2),))
    cross_out = bell_draw(key_of[14], (D, D), (D // 16) ** -0.5, 0.75, ((0, 2),))
    gain_three = jnp.clip(1.0 + 0.1 * jax.random.normal(key_of[15], (D,), jnp.float32), 0.5, 1.5)
    weight_up = bell_draw(key_of[16], (D, FF), D ** -0.5, 0.1875, ((1, 2),))
    weight_down = bell_draw(key_of[17], (FF, D), FF ** -0.5, 0.09375, ((0, 2),))
    cotangent = bell_draw(key_of[18], (PACKS, TOKENS, D), 1.0, 6.0, ((1, 16),))
    return {"tokens": tokens, "memory": memory, "segment_ids": segment_ids, "token_valid": token_valid, "segment_page": segment_page, "gain_one": gain_one, "weight_query": weight_query, "weight_key": weight_key, "weight_value": weight_value, "weight_out": weight_out, "gain_two": gain_two, "cross_query": cross_query, "cross_key": cross_key, "cross_value": cross_value, "cross_out": cross_out, "gain_three": gain_three, "weight_up": weight_up, "weight_down": weight_down, "cotangent": cotangent}


EPS = 1e-05
HIGHEST = lax.Precision.HIGHEST

@jax.custom_vjp
def low(v):
    return lax.optimization_barrier(v.astype(jnp.bfloat16)).astype(jnp.float32)

@jax.custom_vjp
def low_back(v):
    return v

def low_keep(v):
    return (low(v), None)

def low_pass(kept, grad):
    return (grad,)

def back_keep(v):
    return (v, None)

def back_low(kept, grad):
    return (low(grad),)
low.defvjp(low_keep, low_pass)
low_back.defvjp(back_keep, back_low)

def layer_norm(value, gain):
    mean = lax.optimization_barrier(jnp.mean(value, axis=-1, keepdims=True))
    centred = value - mean
    return centred * lax.rsqrt(lax.optimization_barrier(jnp.mean(centred * centred, axis=-1, keepdims=True)) + EPS) * gain

def matmul(left, right):
    return jnp.dot(left, right, precision=HIGHEST)

def attend(query, keys, values, allowed):
    scores = low_back(jnp.dot(query, keys.T, precision=HIGHEST) * HEAD_DIM ** (-0.5))
    scores = jnp.where(allowed, scores, -jnp.inf)
    largest = lax.optimization_barrier(jnp.max(scores, axis=1, keepdims=True))
    exp_scores = jnp.exp(scores - largest)
    weights = exp_scores / lax.optimization_barrier(jnp.sum(exp_scores, axis=1, keepdims=True))
    return matmul(low(weights), values)

def split_heads(value):
    return value.reshape(value.shape[0], HEADS, HEAD_DIM).transpose(1, 0, 2)

def join_heads(value):
    return value.transpose(1, 0, 2).reshape(value.shape[1], HEADS * HEAD_DIM)

def attention(query, keys, values, query_rule):
    total_rows = query.shape[1]
    block = math.gcd(total_rows, 512)
    starts = jnp.arange(total_rows // block, dtype=jnp.int32) * block

    def per_head(parts):
        query_head, key_head, value_head = parts

        def per_block(start):
            rows = lax.dynamic_slice_in_dim(query_head, start, block, 0)
            return attend(rows, key_head, value_head, query_rule(start, block))
        return lax.map(jax.checkpoint(per_block), starts).reshape(total_rows, HEAD_DIM)
    return lax.map(per_head, (query, keys, values))

def forward(tokens, memory, gain_one, weight_query, weight_key, weight_value, weight_out, gain_two, cross_query, cross_key, cross_value, cross_out, gain_three, weight_up, weight_down, segment_ids, token_valid, segment_page):
    packs, length, width = tokens.shape
    total_rows = packs * length
    flat_tokens = tokens.reshape(total_rows, width)
    slot_ids = (jnp.arange(packs, dtype=jnp.int32)[:, None] * NSEG + segment_ids).reshape(total_rows).astype(jnp.int32)
    valid_flat = token_valid.reshape(total_rows)
    key_positions = jnp.arange(total_rows, dtype=jnp.int32)
    row_page = segment_page.reshape(packs * NSEG)[slot_ids]
    key_page = jnp.arange(memory.shape[0], dtype=jnp.int32) // MEM_LEN

    def self_rule(start, block):
        segment_rows = lax.dynamic_slice_in_dim(slot_ids, start, block)
        position_rows = start + jnp.arange(block, dtype=jnp.int32)
        same = segment_rows[:, None] == slot_ids[None, :]
        causal = key_positions[None, :] <= position_rows[:, None]
        return same & causal & (valid_flat[None, :] == 1)

    def cross_rule(start, block):
        return lax.dynamic_slice_in_dim(row_page, start, block)[:, None] == key_page[None, :]
    hidden_one = low(layer_norm(flat_tokens, gain_one))
    queries = split_heads(low(low_back(matmul(hidden_one, weight_query))))
    keys = split_heads(low(low_back(matmul(hidden_one, weight_key))))
    values = split_heads(low(low_back(matmul(hidden_one, weight_value))))
    mixed = low(low_back(join_heads(attention(queries, keys, values, self_rule))))
    residual_one = flat_tokens + low_back(matmul(mixed, weight_out))
    hidden_two = low(layer_norm(residual_one, gain_two))
    cross_queries = split_heads(low(low_back(matmul(hidden_two, cross_query))))
    page_keys = split_heads(low(low_back(matmul(memory, cross_key))))
    page_values = split_heads(low(low_back(matmul(memory, cross_value))))
    cross_mixed = low(low_back(join_heads(attention(cross_queries, page_keys, page_values, cross_rule))))
    residual_two = residual_one + low_back(matmul(cross_mixed, cross_out))
    hidden_three = low(layer_norm(residual_two, gain_three))
    up_value = low_back(matmul(hidden_three, weight_up))
    gelu_low = low(jax.nn.gelu(up_value, approximate=False))
    result = residual_two + low_back(matmul(gelu_low, weight_down))
    return result.reshape(packs, length, width)

def reference(tokens, memory, segment_ids, token_valid, segment_page, gain_one, weight_query, weight_key, weight_value, weight_out, gain_two, cross_query, cross_key, cross_value, cross_out, gain_three, weight_up, weight_down, cotangent):
    floats = [tokens, memory, gain_one, weight_query, weight_key, weight_value, weight_out, gain_two, cross_query, cross_key, cross_value, cross_out, gain_three, weight_up, weight_down]
    floats = [value.astype(jnp.float32) for value in floats]

    def wrapped(*values):
        return forward(*values, segment_ids, token_valid, segment_page)
    result, pull = jax.vjp(wrapped, *floats)
    grads = pull(cotangent.astype(jnp.float32))
    return (result.astype(jnp.bfloat16), grads[0], grads[1], grads[3], grads[4], grads[5], grads[6], grads[8], grads[9], grads[10], grads[11], grads[13], grads[14], grads[2], grads[7], grads[12])
```

```python
import functools

import jax
import jax.numpy as jnp
from jax import lax
from jax.experimental import pallas as pl
from jax.experimental.pallas import tpu as pltpu
from jax.sharding import PartitionSpec as P

MEM_LEN = 588
HEAD_DIM = 64
NSEG = 3
EPS = 1e-05
NEG = -1e30
EXP2_SCALE = HEAD_DIM**-0.5 * 1.4426950408889634
SCALE = HEAD_DIM**-0.5
LANES = 128
BF16 = jnp.bfloat16
F32 = jnp.float32
MESH = pl.DeviceIdType.MESH
VMEM_LIMIT = 56 * 1024 * 1024


def dot(left, right, contract_left, contract_right):
    return lax.dot_general(
        left, right, (((contract_left,), (contract_right,)), ((), ())), preferred_element_type=F32
    )


def exchange(collective_id, items):
    count = len(items)
    most = max(item[2] for item in items)

    def body(*refs):
        sources, targets = refs[:count], refs[count : 2 * count]
        send_sem, recv_sem, own_sem = refs[2 * count :]
        me = lax.axis_index("blk")
        barrier = pltpu.get_barrier_semaphore()
        for offset in range(1, most):
            pl.semaphore_signal(
                barrier, inc=1, device_id={"blk": me ^ offset}, device_id_type=MESH
            )
        pl.semaphore_wait(barrier, most - 1)
        copies = []
        for offset in range(1, most):
            for index, (_, _, group, source, target) in enumerate(items):
                if offset >= group:
                    continue
                peer = me ^ offset
                copy = pltpu.make_async_remote_copy(
                    src_ref=source(sources[index], peer),
                    dst_ref=target(targets[index], me),
                    send_sem=send_sem.at[index, offset],
                    recv_sem=recv_sem.at[index, offset],
                    device_id={"blk": peer},
                    device_id_type=MESH,
                )
                copy.start()
                copies.append(copy)
        for index, (_, _, group, source, target) in enumerate(items):
            copy = pltpu.make_async_copy(
                source(sources[index], me), target(targets[index], me), own_sem.at[index]
            )
            copy.start()
            copies.append(copy)
        for copy in copies:
            copy.wait()

    outs = pl.pallas_call(
        body,
        out_shape=[jax.ShapeDtypeStruct(item[1], item[0].dtype) for item in items],
        in_specs=[pl.BlockSpec(memory_space=pl.ANY)] * count,
        out_specs=[pl.BlockSpec(memory_space=pl.ANY)] * count,
        scratch_shapes=[
            pltpu.SemaphoreType.DMA((count, most)),
            pltpu.SemaphoreType.DMA((count, most)),
            pltpu.SemaphoreType.DMA((count,)),
        ],
        compiler_params=pltpu.CompilerParams(collective_id=collective_id, has_side_effects=True),
    )(*[item[0] for item in items])
    return outs


class Layout:
    def __init__(self, count, packs, heads, rows, mem_rows):
        self.count, self.packs, self.heads, self.rows = count, packs, heads, rows
        self.half = count // packs
        self.parts = self.half // heads
        self.mem_rows = mem_rows
        self.mem_pad = -(-mem_rows // LANES) * LANES
        self.pieces = MEM_LEN // mem_rows
        self.pages_half = self.half // self.pieces

    def head(self, device):
        return lax.rem(device, self.half) // self.parts

    def to_units(self, value):
        def source(ref, peer):
            return ref.at[
                :,
                pl.ds(self.head(peer) * HEAD_DIM, HEAD_DIM),
                pl.ds((peer // self.half) * self.rows, self.rows),
            ]

        def target(ref, me):
            return ref.at[:, :, pl.ds(me * self.rows, self.rows)]

        shape = (value.shape[0], HEAD_DIM, self.count * self.rows)
        return (value, shape, self.count, source, target)

    def codes_to_units(self, value):
        def source(ref, peer):
            return ref.at[peer // self.half]

        def target(ref, me):
            return ref.at[:, pl.ds(me * self.rows, self.rows)]

        return (value, (value.shape[1], self.count * self.rows), self.count, source, target)

    def from_units(self, value):
        def source(ref, peer):
            return ref.at[:, :, pl.ds(peer * self.rows, self.rows)]

        def target(ref, me):
            return ref.at[
                lax.rem(me, self.parts),
                :,
                pl.ds(self.head(me) * HEAD_DIM, HEAD_DIM),
                pl.ds((me // self.half) * self.rows, self.rows),
            ]

        shape = (self.parts, value.shape[0], self.heads * HEAD_DIM, self.packs * self.rows)
        return (value, shape, self.count, source, target)

    def memory_to_units(self, value):
        def source(ref, peer):
            return ref.at[:, pl.ds(self.head(peer) * HEAD_DIM, HEAD_DIM), :]

        def target(ref, me):
            return ref.at[lax.rem(me, self.half)]

        return (value, (self.half, 2, HEAD_DIM, self.mem_pad), self.half, source, target)

    def memory_from_units(self, value):
        def source(ref, peer):
            return ref.at[lax.rem(peer, self.half)]

        def target(ref, me):
            return ref.at[
                lax.rem(me, self.parts), :, pl.ds(self.head(me) * HEAD_DIM, HEAD_DIM), :
            ]

        shape = (self.parts, 2, self.heads * HEAD_DIM, self.mem_pad)
        return (value, shape, self.half, source, target)


def self_forward_body(block, parts, q_ref, k_ref, v_ref, code_ref, qseg_ref, qpos_ref, *rest):
    out_ref, low_ref, log_ref, key_ref = rest
    step = pl.program_id(0)

    @pl.when(step == 0)
    def _():
        key_ref[...] = k_ref[0].T

    query = q_ref[0]
    width = query.shape[1]
    segments, positions = qseg_ref[...], qpos_ref[...]

    def fold(index, state, causal):
        largest, total, weighted = state
        start = pl.multiple_of(index * block, block)
        scores = jnp.dot(key_ref[pl.ds(start, block), :], query, preferred_element_type=F32)
        allowed = code_ref[pl.ds(start, block), :] == segments
        if causal:
            places = start + lax.broadcasted_iota(jnp.int32, (block, width), 0)
            allowed = allowed & (places <= positions)
        scores = jnp.where(allowed, scores, NEG)
        new = jnp.maximum(largest, jnp.max(scores, axis=0, keepdims=True))
        weights = jnp.exp2((scores - new) * EXP2_SCALE)
        keep = jnp.exp2((largest - new) * EXP2_SCALE)
        total = total * keep + jnp.sum(weights, axis=0, keepdims=True)
        update = jnp.dot(
            v_ref[0, :, pl.ds(start, block)], weights.astype(BF16), preferred_element_type=F32
        )
        return (new, total, weighted * keep + update)

    state = (
        jnp.full((1, width), NEG, F32),
        jnp.zeros((1, width), F32),
        jnp.zeros((HEAD_DIM, width), F32),
    )
    state = lax.fori_loop(0, step * parts, lambda i, s: fold(i, s, False), state)
    for part in range(parts):
        state = fold(step * parts + part, state, True)
    largest, total, weighted = state
    result = weighted / total
    out_ref[...] = result
    low_ref[0] = result.astype(BF16)
    log_ref[...] = largest * EXP2_SCALE + jnp.log2(total)


def self_forward(query, qkv, code, qseg, qpos, parts):
    total, width = qkv.shape[2], query.shape[2]
    block = min(512, width)
    row = pl.BlockSpec((1, block), lambda i: (0, i))
    return pl.pallas_call(
        functools.partial(self_forward_body, block, parts),
        grid=(width // block,),
        in_specs=[
            pl.BlockSpec((1, HEAD_DIM, block), lambda i: (0, 0, i)),
            pl.BlockSpec((1, HEAD_DIM, total), lambda i: (1, 0, 0)),
            pl.BlockSpec((1, HEAD_DIM, total), lambda i: (2, 0, 0)),
            pl.BlockSpec((total, 1), lambda i: (0, 0)),
            row,
            row,
        ],
        out_specs=[
            pl.BlockSpec((HEAD_DIM, block), lambda i: (0, i)),
            pl.BlockSpec((1, HEAD_DIM, block), lambda i: (0, 0, i)),
            row,
        ],
        out_shape=[
            jax.ShapeDtypeStruct((HEAD_DIM, width), F32),
            jax.ShapeDtypeStruct((1, HEAD_DIM, width), BF16),
            jax.ShapeDtypeStruct((1, width), F32),
        ],
        scratch_shapes=[pltpu.VMEM((total, HEAD_DIM), BF16)],
        compiler_params=pltpu.CompilerParams(vmem_limit_bytes=VMEM_LIMIT),
    )(query, qkv, qkv, code, qseg, qpos)


def self_backward_body(block, parts, q_ref, k_ref, v_ref, code_ref, qseg_ref, qpos_ref, *rest):
    grad_ref, out_ref, log_ref, dq_ref, dkv_ref, key_ref, value_ref, dk_ref, dv_ref = rest
    step = pl.program_id(0)

    @pl.when(step == 0)
    def _():
        key_ref[...] = k_ref[0].T
        value_ref[...] = v_ref[0].T
        dk_ref[...] = jnp.zeros_like(dk_ref)
        dv_ref[...] = jnp.zeros_like(dv_ref)

    query, grad = q_ref[0], grad_ref[0]
    width = query.shape[1]
    segments, positions, logs = qseg_ref[...], qpos_ref[...], log_ref[...]
    row_dot = jnp.sum(grad.astype(F32) * out_ref[...], axis=0, keepdims=True)

    def fold(index, dq, causal):
        start = pl.multiple_of(index * block, block)
        here = pl.ds(start, block)
        scores = jnp.dot(key_ref[here, :], query, preferred_element_type=F32)
        allowed = code_ref[here, :] == segments
        if causal:
            places = start + lax.broadcasted_iota(jnp.int32, (block, width), 0)
            allowed = allowed & (places <= positions)
        weights = jnp.where(allowed, jnp.exp2(scores * EXP2_SCALE - logs), 0.0)
        weight_grad = jnp.dot(value_ref[here, :], grad, preferred_element_type=F32)
        score_grad = (weights * (weight_grad - row_dot)).astype(BF16)
        dv_ref[:, here] += dot(grad, weights.astype(BF16), 1, 1)
        dk_ref[:, here] += dot(query, score_grad, 1, 1)
        return dq + jnp.dot(k_ref[0, :, here], score_grad, preferred_element_type=F32)

    dq = jnp.zeros((HEAD_DIM, width), F32)
    dq = lax.fori_loop(0, step * parts, lambda i, s: fold(i, s, False), dq)
    for part in range(parts):
        dq = fold(step * parts + part, dq, True)
    dq_ref[0] = (dq * SCALE).astype(BF16)

    @pl.when(step == pl.num_programs(0) - 1)
    def _():
        dkv_ref[0] = (dk_ref[...] * SCALE).astype(BF16)
        dkv_ref[1] = dv_ref[...].astype(BF16)


def self_backward(query, qkv, code, qseg, qpos, grad, out, log, parts):
    total, width = qkv.shape[2], query.shape[2]
    block = min(512, width)
    row = pl.BlockSpec((1, block), lambda i: (0, i))
    column = pl.BlockSpec((1, HEAD_DIM, block), lambda i: (0, 0, i))
    return pl.pallas_call(
        functools.partial(self_backward_body, block, parts),
        grid=(width // block,),
        in_specs=[
            column,
            pl.BlockSpec((1, HEAD_DIM, total), lambda i: (1, 0, 0)),
            pl.BlockSpec((1, HEAD_DIM, total), lambda i: (2, 0, 0)),
            pl.BlockSpec((total, 1), lambda i: (0, 0)),
            row,
            row,
            column,
            pl.BlockSpec((HEAD_DIM, block), lambda i: (0, i)),
            row,
        ],
        out_specs=[column, pl.BlockSpec((2, HEAD_DIM, total), lambda i: (0, 0, 0))],
        out_shape=[
            jax.ShapeDtypeStruct((1, HEAD_DIM, width), BF16),
            jax.ShapeDtypeStruct((2, HEAD_DIM, total), BF16),
        ],
        scratch_shapes=[
            pltpu.VMEM((total, HEAD_DIM), BF16),
            pltpu.VMEM((total, HEAD_DIM), BF16),
            pltpu.VMEM((HEAD_DIM, total), F32),
            pltpu.VMEM((HEAD_DIM, total), F32),
        ],
        compiler_params=pltpu.CompilerParams(vmem_limit_bytes=VMEM_LIMIT),
    )(query, qkv, qkv, code, qseg, qpos, grad, out, log)


def page_rows(span, piece, real):
    places = lax.broadcasted_iota(jnp.int32, (span, 1), 0)
    return lax.rem(places, piece) < real


def cross_forward_body(piece, real, low_ref, high_ref, q_ref, kv_ref, qseg_ref, *rest):
    out_ref, outlow_ref, log_ref, key_ref = rest
    step = pl.program_id(0)

    @pl.when(step == 0)
    def _():
        for slot in range(NSEG):
            key_ref[slot] = kv_ref[slot, 0].T

    query, segments = q_ref[0], qseg_ref[...]
    width, span = query.shape[1], kv_ref.shape[3]
    present = page_rows(span, piece, real)

    def fold(slot, state):
        logs, result = state
        scores = jnp.dot(key_ref[slot], query, preferred_element_type=F32)
        scores = jnp.where(present, scores, NEG)
        largest = jnp.max(scores, axis=0, keepdims=True)
        weights = jnp.exp2((scores - largest) * EXP2_SCALE)
        total = jnp.sum(weights, axis=0, keepdims=True)
        part = jnp.dot(kv_ref[slot, 1], weights.astype(BF16), preferred_element_type=F32) / total
        mine = segments == slot
        return (
            jnp.where(mine, largest * EXP2_SCALE + jnp.log2(total), logs),
            jnp.where(mine, part, result),
        )

    state = (jnp.zeros((1, width), F32), jnp.zeros((HEAD_DIM, width), F32))
    logs, result = lax.fori_loop(low_ref[step], high_ref[step] + 1, fold, state)
    out_ref[...] = result
    outlow_ref[0] = result.astype(BF16)
    log_ref[...] = logs


def cross_forward(query, kv, qseg, low, high, piece, real):
    width, span = query.shape[2], kv.shape[3]
    block = min(512, width)
    row = pl.BlockSpec((1, block), lambda i, *_: (0, i))
    column = pl.BlockSpec((1, HEAD_DIM, block), lambda i, *_: (0, 0, i))
    return pl.pallas_call(
        functools.partial(cross_forward_body, piece, real),
        grid_spec=pltpu.PrefetchScalarGridSpec(
            num_scalar_prefetch=2,
            grid=(width // block,),
            in_specs=[
                column,
                pl.BlockSpec((NSEG, 2, HEAD_DIM, span), lambda i, *_: (0, 0, 0, 0)),
                row,
            ],
            out_specs=[pl.BlockSpec((HEAD_DIM, block), lambda i, *_: (0, i)), column, row],
            scratch_shapes=[pltpu.VMEM((NSEG, span, HEAD_DIM), BF16)],
        ),
        out_shape=[
            jax.ShapeDtypeStruct((HEAD_DIM, width), F32),
            jax.ShapeDtypeStruct((1, HEAD_DIM, width), BF16),
            jax.ShapeDtypeStruct((1, width), F32),
        ],
        compiler_params=pltpu.CompilerParams(vmem_limit_bytes=VMEM_LIMIT),
    )(low, high, query, kv, qseg)


def cross_backward_body(piece, real, low_ref, high_ref, q_ref, kv_ref, qseg_ref, *rest):
    grad_ref, out_ref, log_ref, dq_ref, dkv_ref, key_ref, value_ref, acc_ref = rest
    step = pl.program_id(0)

    @pl.when(step == 0)
    def _():
        for slot in range(NSEG):
            key_ref[slot] = kv_ref[slot, 0].T
            value_ref[slot] = kv_ref[slot, 1].T
        acc_ref[...] = jnp.zeros_like(acc_ref)

    query, grad, segments, logs = q_ref[0], grad_ref[0], qseg_ref[...], log_ref[...]
    width, span = query.shape[1], kv_ref.shape[3]
    row_dot = jnp.sum(grad.astype(F32) * out_ref[...], axis=0, keepdims=True)
    present = page_rows(span, piece, real)

    def fold(slot, dq):
        scores = jnp.dot(key_ref[slot], query, preferred_element_type=F32)
        allowed = present & (segments == slot)
        weights = jnp.where(allowed, jnp.exp2(scores * EXP2_SCALE - logs), 0.0)
        weight_grad = jnp.dot(value_ref[slot], grad, preferred_element_type=F32)
        score_grad = (weights * (weight_grad - row_dot)).astype(BF16)
        acc_ref[slot, 1] += dot(grad, weights.astype(BF16), 1, 1)
        acc_ref[slot, 0] += dot(query, score_grad, 1, 1)
        return dq + jnp.dot(kv_ref[slot, 0], score_grad, preferred_element_type=F32)

    dq = jnp.zeros((HEAD_DIM, width), F32)
    dq = lax.fori_loop(low_ref[step], high_ref[step] + 1, fold, dq)
    dq_ref[0] = (dq * SCALE).astype(BF16)

    @pl.when(step == pl.num_programs(0) - 1)
    def _():
        for slot in range(NSEG):
            dkv_ref[slot, 0] = (acc_ref[slot, 0] * SCALE).astype(BF16)
            dkv_ref[slot, 1] = acc_ref[slot, 1].astype(BF16)


def cross_backward(query, kv, qseg, low, high, grad, out, log, piece, real):
    width, span = query.shape[2], kv.shape[3]
    block = min(512, width)
    row = pl.BlockSpec((1, block), lambda i, *_: (0, i))
    column = pl.BlockSpec((1, HEAD_DIM, block), lambda i, *_: (0, 0, i))
    pages = pl.BlockSpec((NSEG, 2, HEAD_DIM, span), lambda i, *_: (0, 0, 0, 0))
    return pl.pallas_call(
        functools.partial(cross_backward_body, piece, real),
        grid_spec=pltpu.PrefetchScalarGridSpec(
            num_scalar_prefetch=2,
            grid=(width // block,),
            in_specs=[
                column,
                pages,
                row,
                column,
                pl.BlockSpec((HEAD_DIM, block), lambda i, *_: (0, i)),
                row,
            ],
            out_specs=[column, pages],
            scratch_shapes=[
                pltpu.VMEM((NSEG, span, HEAD_DIM), BF16),
                pltpu.VMEM((NSEG, span, HEAD_DIM), BF16),
                pltpu.VMEM((NSEG, 2, HEAD_DIM, span), F32),
            ],
        ),
        out_shape=[
            jax.ShapeDtypeStruct((1, HEAD_DIM, width), BF16),
            jax.ShapeDtypeStruct((NSEG, 2, HEAD_DIM, span), BF16),
        ],
        compiler_params=pltpu.CompilerParams(vmem_limit_bytes=VMEM_LIMIT),
    )(low, high, query, kv, qseg, grad, out, log)


def layer_norm(value, gain):
    mean = jnp.mean(value, axis=-1, keepdims=True)
    centred = value - mean
    inv_std = lax.rsqrt(jnp.mean(centred * centred, axis=-1, keepdims=True) + EPS)
    unit = centred * inv_std
    return ((unit * gain).astype(BF16), unit, inv_std)


def norm_back(grad, unit, inv_std, gain):
    scaled = grad * gain
    inner = (
        scaled
        - jnp.mean(scaled, axis=-1, keepdims=True)
        - unit * jnp.mean(scaled * unit, axis=-1, keepdims=True)
    )
    return inner * inv_std


def other_core(value):
    return lax.ppermute(value, "tp", [(0, 1), (1, 0)])


def tp_total(partial_sum):
    low = partial_sum.astype(BF16)
    return low.astype(F32) + other_core(low).astype(F32)


def reduce_scatter(grad, count, place):
    bits = count.bit_length() - 1
    rows, columns = grad.shape[0] // count, grad.shape[1]
    grad = grad.reshape((2,) * bits + (rows, columns))

    def run(piece, order):
        left = list(range(bits - 1, -1, -1))
        for bit in order:
            axis = left.index(bit)
            left.remove(bit)
            mine = (place >> bit) & 1
            keep = lax.dynamic_index_in_dim(piece, mine, axis, keepdims=False)
            send = lax.dynamic_index_in_dim(piece, 1 - mine, axis, keepdims=False).astype(BF16)
            pairs = [(i, i ^ (1 << bit)) for i in range(count)]
            piece = keep.astype(F32) + lax.ppermute(send, "blk", pairs).astype(F32)
        return piece

    first = list(range(bits))
    second = [1, 0] + first[2:]
    half = columns // 2
    return jnp.concatenate([run(grad[..., :half], first), run(grad[..., half:], second)], axis=-1)


def local(
    tokens,
    memory,
    segment_ids,
    token_valid,
    segment_page,
    gain_one,
    weight_query,
    weight_key,
    weight_value,
    weight_out,
    gain_two,
    cross_query,
    cross_key,
    cross_value,
    cross_out,
    gain_three,
    weight_up,
    weight_down,
    cotangent,
):
    packs, rows, width = tokens.shape
    heads = weight_query.shape[1] // HEAD_DIM
    count, place = lax.axis_size("blk"), lax.axis_index("blk")
    lay = Layout(count, packs, heads, rows, memory.shape[0])
    parts, half = lay.parts, lay.half
    flat_rows, total = packs * rows, count * rows
    share = width // count
    pack, part = place // half, lax.rem(place, parts)

    residual_in = tokens.reshape(flat_rows, width).astype(F32)
    hidden_one, unit_one, inv_one = layer_norm(residual_in, gain_one)
    qkv_tokens = jnp.stack(
        [dot(w, hidden_one, 0, 1).astype(BF16) for w in (weight_query, weight_key, weight_value)]
    )
    memory_padded = jnp.pad(memory, ((0, lay.mem_pad - lay.mem_rows), (0, 0)))
    kv_memory = jnp.stack(
        [dot(w, memory_padded, 0, 1).astype(BF16) for w in (cross_key, cross_value)]
    )
    codes = jnp.broadcast_to((segment_ids * 2 + token_valid)[:, None, :], (packs, 8, rows))
    qkv, codes, kv_half = exchange(
        0, [lay.to_units(qkv_tokens), lay.codes_to_units(codes), lay.memory_to_units(kv_memory)]
    )
    codes = codes[:1]
    segments = codes >> 1
    key_codes = jnp.where((codes & 1) == 1, segments, -1).reshape(total, 1)

    def own_part(value):
        if parts == 1:
            return value
        split = value.reshape(value.shape[:-1] + (count // parts, parts, rows))
        split = lax.dynamic_index_in_dim(split, part, split.ndim - 2, keepdims=False)
        return split.reshape(value.shape[:-1] + (total // parts,))

    def all_parts(value):
        if parts == 1:
            return value
        split = value.reshape(value.shape[:-1] + (count // parts, 1, rows))
        split = jnp.broadcast_to(split, value.shape[:-1] + (count // parts, parts, rows))
        return split.reshape(value.shape[:-1] + (total,))

    def pick_part(value):
        return lax.dynamic_index_in_dim(value, part, 0, keepdims=False)

    query = own_part(qkv[:1]) if parts > 1 else qkv
    query_segments = own_part(segments)
    query_positions = own_part(jnp.arange(total, dtype=jnp.int32)[None])

    slot_pages = segment_page.reshape(packs, NSEG)
    pages_here = lay.pages_half
    kv_pages = (
        kv_half.reshape(pages_here, lay.pieces, 2, HEAD_DIM, lay.mem_pad)
        .transpose(0, 2, 3, 1, 4)
        .reshape(pages_here, 2, HEAD_DIM, lay.pieces * lay.mem_pad)
    )
    first_page = pack * pages_here
    own_pages = lax.dynamic_index_in_dim(slot_pages, pack, 0, keepdims=False)
    twin_pages = lax.dynamic_index_in_dim(slot_pages, 1 - pack, 0, keepdims=False)

    def pages_of(wanted):
        found = [
            lax.dynamic_index_in_dim(
                kv_pages, jnp.clip(wanted[s] - first_page, 0, pages_here - 1), 0, keepdims=False
            )
            for s in range(NSEG)
        ]
        return jnp.stack(found)

    def is_here(wanted):
        return (wanted >= first_page) & (wanted < first_page + pages_here)

    twin_pairs = [(i, (i + half) % count) for i in range(count)]
    kv_twin = lax.ppermute(pages_of(twin_pages), "blk", twin_pairs)
    kv_slots = jnp.where(is_here(own_pages)[:, None, None, None], pages_of(own_pages), kv_twin)

    attention, attention_low, attention_log = self_forward(
        query, qkv, key_codes, query_segments, query_positions, parts
    )
    (mixed,) = exchange(1, [lay.from_units(all_parts(attention_low))])
    mixed = pick_part(mixed)[0]
    residual_one = residual_in + tp_total(dot(mixed, weight_out, 0, 0))
    hidden_two, unit_two, inv_two = layer_norm(residual_one, gain_two)

    cross_tokens = dot(cross_query, hidden_two, 0, 1).astype(BF16)[None]
    (cross_unit,) = exchange(2, [lay.to_units(cross_tokens)])
    cross_unit = own_part(cross_unit)
    block = min(512, total // parts)
    blocks = query_segments.reshape(-1, block)
    low, high = blocks[:, 0], blocks[:, -1]
    cross_attention, cross_low, cross_log = cross_forward(
        cross_unit, kv_slots, query_segments, low, high, lay.mem_pad, lay.mem_rows
    )
    (cross_mixed,) = exchange(3, [lay.from_units(all_parts(cross_low))])
    cross_mixed = pick_part(cross_mixed)[0]
    residual_two = residual_one + tp_total(dot(cross_mixed, cross_out, 0, 0))
    hidden_three, unit_three, inv_three = layer_norm(residual_two, gain_three)

    up_value = dot(hidden_three, weight_up, 1, 0)
    gelu_value, gelu_back = jax.vjp(functools.partial(jax.nn.gelu, approximate=False), up_value)
    gelu_low = gelu_value.astype(BF16)
    result = residual_two + tp_total(dot(gelu_low, weight_down, 1, 0))
    out = result.astype(BF16).reshape(packs, rows, width)
    down_in = cotangent.reshape(flat_rows, width)
    up_grad = gelu_back(dot(down_in, weight_down, 1, 1))[0].astype(BF16)
    grad_hidden = tp_total(dot(up_grad, weight_up, 1, 1))
    grad_two = down_in.astype(F32) + norm_back(grad_hidden, unit_three, inv_three, gain_three)
    feed_share = reduce_scatter(
        jnp.concatenate([dot(down_in, gelu_low, 0, 0), dot(hidden_three, up_grad, 0, 0)], axis=1),
        count,
        place,
    )

    cross_in = grad_two.astype(BF16)
    cross_grad = dot(cross_out, cross_in, 1, 1).astype(BF16)[None]
    (cross_grad,) = exchange(4, [lay.to_units(cross_grad)])
    cross_dq, cross_dkv = cross_backward(
        cross_unit,
        kv_slots,
        query_segments,
        low,
        high,
        own_part(cross_grad),
        cross_attention,
        cross_log,
        lay.mem_pad,
        lay.mem_rows,
    )
    twin_dkv = lax.ppermute(cross_dkv, "blk", twin_pairs)
    page_ids = first_page + jnp.arange(pages_here, dtype=jnp.int32)
    page_grad = sum(
        jnp.where(
            (pages[s] == page_ids)[:, None, None, None], grads[s].astype(F32)[None], 0.0
        )
        for pages, grads in ((own_pages, cross_dkv), (twin_pages, twin_dkv))
        for s in range(NSEG)
    ).astype(BF16)
    page_grad = (
        page_grad.reshape(pages_here, 2, HEAD_DIM, lay.pieces, lay.mem_pad)
        .transpose(0, 3, 1, 2, 4)
        .reshape(half, 2, HEAD_DIM, lay.mem_pad)
    )
    cross_dq_tokens, memory_grad = exchange(
        5, [lay.from_units(all_parts(cross_dq)), lay.memory_from_units(page_grad)]
    )
    cross_dq = pick_part(cross_dq_tokens)[0]
    if parts > 1:
        memory_grad = jnp.sum(memory_grad.astype(F32), axis=0).astype(BF16)
    else:
        memory_grad = memory_grad[0]
    dkc, dvc = memory_grad[0], memory_grad[1]
    grad_memory = tp_total(dot(dkc, cross_key, 0, 1) + dot(dvc, cross_value, 0, 1))
    grad_memory = grad_memory[: lay.mem_rows]

    grad_hidden = tp_total(dot(cross_dq, cross_query, 0, 1))
    grad_one = grad_two + norm_back(grad_hidden, unit_two, inv_two, gain_two)

    self_in = grad_one.astype(BF16)
    mixed_grad = dot(weight_out, self_in, 1, 1).astype(BF16)[None]
    (mixed_grad,) = exchange(6, [lay.to_units(mixed_grad)])
    middle_share = reduce_scatter(
        jnp.concatenate(
            [
                dot(cross_in, cross_mixed, 0, 1),
                dot(hidden_two, cross_dq, 0, 1),
                dot(memory_padded, dkc, 0, 1),
                dot(memory_padded, dvc, 0, 1),
                dot(self_in, mixed, 0, 1),
            ],
            axis=1,
        ),
        count,
        place,
    )
    dq, dkv = self_backward(
        query,
        qkv,
        key_codes,
        query_segments,
        query_positions,
        own_part(mixed_grad),
        attention,
        attention_log,
        parts,
    )
    (dqkv,) = exchange(7, [lay.from_units(jnp.concatenate([all_parts(dq), dkv], axis=0))])
    if parts > 1:
        dkv = jnp.sum(dqkv[:, 1:].astype(F32), axis=0).astype(BF16)
        dq, dk, dv = pick_part(dqkv)[0], dkv[0], dkv[1]
    else:
        dq, dk, dv = dqkv[0, 0], dqkv[0, 1], dqkv[0, 2]
    grad_hidden = tp_total(
        dot(dq, weight_query, 0, 1) + dot(dk, weight_key, 0, 1) + dot(dv, weight_value, 0, 1)
    )
    grad_input = grad_one + norm_back(grad_hidden, unit_one, inv_one, gain_one)
    grad_input = grad_input.reshape(packs, rows, width)
    first_share = reduce_scatter(
        jnp.concatenate([dot(hidden_one, d, 0, 1) for d in (dq, dk, dv)], axis=1), count, place
    )

    ff, wide = weight_up.shape[1], weight_query.shape[1]
    grad_down, grad_up = feed_share[:, :ff].T, feed_share[:, ff:]
    middle = [middle_share[:, i * wide : (i + 1) * wide] for i in range(5)]
    first = [first_share[:, i * wide : (i + 1) * wide] for i in range(3)]

    def own_rows(weight):
        return lax.dynamic_slice_in_dim(weight, place * share, share, 0).astype(F32)

    sums = jnp.stack(
        [
            sum(
                jnp.sum(own_rows(w) * g, axis=1)
                for w, g in zip((weight_query, weight_key, weight_value), first, strict=True)
            ),
            jnp.sum(own_rows(cross_query) * middle[1], axis=1),
            jnp.sum(own_rows(weight_up) * grad_up, axis=1),
        ]
    )
    gains = jnp.stack(
        [lax.dynamic_slice_in_dim(g, place * share, share) for g in (gain_one, gain_two, gain_three)]
    )
    gain_grads = (sums + other_core(sums)) / gains
    return (
        out,
        grad_input,
        grad_memory,
        first[0],
        first[1],
        first[2],
        middle[4].T,
        middle[1],
        middle[2],
        middle[3],
        middle[0].T,
        grad_up,
        grad_down,
        gain_grads[0],
        gain_grads[1],
        gain_grads[2],
    )


def solution(mesh):
    in_specs = (
        P(None, "blk", None),
        P("blk", None),
        P(None, "blk"),
        P(None, "blk"),
        P(),
        P(),
        P(None, "tp"),
        P(None, "tp"),
        P(None, "tp"),
        P("tp", None),
        P(),
        P(None, "tp"),
        P(None, "tp"),
        P(None, "tp"),
        P("tp", None),
        P(),
        P(None, "tp"),
        P("tp", None),
        P(None, "blk", None),
    )
    out_specs = (
        P(None, "blk", None),
        P(None, "blk", None),
        P("blk", None),
        P("blk", "tp"),
        P("blk", "tp"),
        P("blk", "tp"),
        P("tp", "blk"),
        P("blk", "tp"),
        P("blk", "tp"),
        P("blk", "tp"),
        P("tp", "blk"),
        P("blk", "tp"),
        P("tp", "blk"),
        P("blk"),
        P("blk"),
        P("blk"),
    )
    return jax.shard_map(local, mesh=mesh, in_specs=in_specs, out_specs=out_specs, check_vma=False)
```

```python
import functools

import jax
import jax.numpy as jnp
from jax import lax
from jax.experimental import pallas as pl
from jax.experimental.pallas import tpu as pltpu
from jax.sharding import PartitionSpec as P

MEM_LEN = 588
HEAD_DIM = 64
NSEG = 3
EPS = 1e-05
NEG = -1e30
EXP2_SCALE = HEAD_DIM**-0.5 * 1.4426950408889634
SCALE = HEAD_DIM**-0.5
LANES = 128
BF16 = jnp.bfloat16
F32 = jnp.float32
MESH = pl.DeviceIdType.MESH
VMEM_LIMIT = 56 * 1024 * 1024


def dot(left, right, contract_left, contract_right):
    return lax.dot_general(
        left, right, (((contract_left,), (contract_right,)), ((), ())), preferred_element_type=F32
    )


def exchange(collective_id, items):
    count = len(items)
    most = max(item[2] for item in items)

    def body(*refs):
        sources, targets = refs[:count], refs[count : 2 * count]
        send_sem, recv_sem, own_sem = refs[2 * count :]
        me = lax.axis_index("blk")
        barrier = pltpu.get_barrier_semaphore()
        for offset in range(1, most):
            pl.semaphore_signal(
                barrier, inc=1, device_id={"blk": me ^ offset}, device_id_type=MESH
            )
        pl.semaphore_wait(barrier, most - 1)
        copies = []
        for offset in range(1, most):
            for index, (_, _, group, source, target) in enumerate(items):
                if offset >= group:
                    continue
                peer = me ^ offset
                copy = pltpu.make_async_remote_copy(
                    src_ref=source(sources[index], peer),
                    dst_ref=target(targets[index], me),
                    send_sem=send_sem.at[index, offset],
                    recv_sem=recv_sem.at[index, offset],
                    device_id={"blk": peer},
                    device_id_type=MESH,
                )
                copy.start()
                copies.append(copy)
        for index, (_, _, group, source, target) in enumerate(items):
            copy = pltpu.make_async_copy(
                source(sources[index], me), target(targets[index], me), own_sem.at[index]
            )
            copy.start()
            copies.append(copy)
        for copy in copies:
            copy.wait()

    outs = pl.pallas_call(
        body,
        out_shape=[jax.ShapeDtypeStruct(item[1], item[0].dtype) for item in items],
        in_specs=[pl.BlockSpec(memory_space=pl.ANY)] * count,
        out_specs=[pl.BlockSpec(memory_space=pl.ANY)] * count,
        scratch_shapes=[
            pltpu.SemaphoreType.DMA((count, most)),
            pltpu.SemaphoreType.DMA((count, most)),
            pltpu.SemaphoreType.DMA((count,)),
        ],
        compiler_params=pltpu.CompilerParams(collective_id=collective_id, has_side_effects=True),
    )(*[item[0] for item in items])
    return outs


class Layout:
    def __init__(self, count, packs, heads, rows, mem_rows):
        self.count, self.packs, self.heads, self.rows = count, packs, heads, rows
        self.half = count // packs
        self.parts = self.half // heads
        self.mem_rows = mem_rows
        self.mem_pad = -(-mem_rows // LANES) * LANES
        self.pieces = MEM_LEN // mem_rows
        self.pages_half = self.half // self.pieces

    def head(self, device):
        return lax.rem(device, self.half) // self.parts

    def to_units(self, value):
        def source(ref, peer):
            return ref.at[
                :,
                pl.ds(self.head(peer) * HEAD_DIM, HEAD_DIM),
                pl.ds((peer // self.half) * self.rows, self.rows),
            ]

        def target(ref, me):
            return ref.at[:, :, pl.ds(me * self.rows, self.rows)]

        shape = (value.shape[0], HEAD_DIM, self.count * self.rows)
        return (value, shape, self.count, source, target)

    def codes_to_units(self, value):
        def source(ref, peer):
            return ref.at[peer // self.half]

        def target(ref, me):
            return ref.at[:, pl.ds(me * self.rows, self.rows)]

        return (value, (value.shape[1], self.count * self.rows), self.count, source, target)

    def from_units(self, value):
        def source(ref, peer):
            return ref.at[:, :, pl.ds(peer * self.rows, self.rows)]

        def target(ref, me):
            return ref.at[
                lax.rem(me, self.parts),
                :,
                pl.ds(self.head(me) * HEAD_DIM, HEAD_DIM),
                pl.ds((me // self.half) * self.rows, self.rows),
            ]

        shape = (self.parts, value.shape[0], self.heads * HEAD_DIM, self.packs * self.rows)
        return (value, shape, self.count, source, target)

    def memory_to_units(self, value):
        def source(ref, peer):
            return ref.at[:, pl.ds(self.head(peer) * HEAD_DIM, HEAD_DIM), :]

        def target(ref, me):
            return ref.at[lax.rem(me, self.half)]

        return (value, (self.half, 2, HEAD_DIM, self.mem_pad), self.half, source, target)

    def memory_from_units(self, value):
        def source(ref, peer):
            return ref.at[lax.rem(peer, self.half)]

        def target(ref, me):
            return ref.at[
                lax.rem(me, self.parts), :, pl.ds(self.head(me) * HEAD_DIM, HEAD_DIM), :
            ]

        shape = (self.parts, 2, self.heads * HEAD_DIM, self.mem_pad)
        return (value, shape, self.half, source, target)


def self_forward_body(block, parts, q_ref, k_ref, v_ref, code_ref, qseg_ref, qpos_ref, *rest):
    out_ref, low_ref, log_ref, key_ref = rest
    step = pl.program_id(0)

    @pl.when(step == 0)
    def _():
        key_ref[...] = k_ref[0].T

    query = q_ref[0]
    width = query.shape[1]
    segments, positions = qseg_ref[...], qpos_ref[...]

    def fold(index, state, causal):
        largest, total, weighted = state
        start = pl.multiple_of(index * block, block)
        scores = jnp.dot(key_ref[pl.ds(start, block), :], query, preferred_element_type=F32)
        allowed = code_ref[pl.ds(start, block), :] == segments
        if causal:
            places = start + lax.broadcasted_iota(jnp.int32, (block, width), 0)
            allowed = allowed & (places <= positions)
        scores = jnp.where(allowed, scores, NEG)
        new = jnp.maximum(largest, jnp.max(scores, axis=0, keepdims=True))
        weights = jnp.exp2((scores - new) * EXP2_SCALE)
        keep = jnp.exp2((largest - new) * EXP2_SCALE)
        total = total * keep + jnp.sum(weights, axis=0, keepdims=True)
        update = jnp.dot(
            v_ref[0, :, pl.ds(start, block)], weights.astype(BF16), preferred_element_type=F32
        )
        return (new, total, weighted * keep + update)

    state = (
        jnp.full((1, width), NEG, F32),
        jnp.zeros((1, width), F32),
        jnp.zeros((HEAD_DIM, width), F32),
    )
    state = lax.fori_loop(0, step * parts, lambda i, s: fold(i, s, False), state)
    for part in range(parts):
        state = fold(step * parts + part, state, True)
    largest, total, weighted = state
    result = weighted / total
    out_ref[...] = result
    low_ref[0] = result.astype(BF16)
    log_ref[...] = largest * EXP2_SCALE + jnp.log2(total)


def self_forward(query, qkv, code, qseg, qpos, parts):
    total, width = qkv.shape[2], query.shape[2]
    block = min(512, width)
    row = pl.BlockSpec((1, block), lambda i: (0, i))
    return pl.pallas_call(
        functools.partial(self_forward_body, block, parts),
        grid=(width // block,),
        in_specs=[
            pl.BlockSpec((1, HEAD_DIM, block), lambda i: (0, 0, i)),
            pl.BlockSpec((1, HEAD_DIM, total), lambda i: (1, 0, 0)),
            pl.BlockSpec((1, HEAD_DIM, total), lambda i: (2, 0, 0)),
            pl.BlockSpec((total, 1), lambda i: (0, 0)),
            row,
            row,
        ],
        out_specs=[
            pl.BlockSpec((HEAD_DIM, block), lambda i: (0, i)),
            pl.BlockSpec((1, HEAD_DIM, block), lambda i: (0, 0, i)),
            row,
        ],
        out_shape=[
            jax.ShapeDtypeStruct((HEAD_DIM, width), F32),
            jax.ShapeDtypeStruct((1, HEAD_DIM, width), BF16),
            jax.ShapeDtypeStruct((1, width), F32),
        ],
        scratch_shapes=[pltpu.VMEM((total, HEAD_DIM), BF16)],
        compiler_params=pltpu.CompilerParams(vmem_limit_bytes=VMEM_LIMIT),
    )(query, qkv, qkv, code, qseg, qpos)


def page_rows(span, piece, real):
    places = lax.broadcasted_iota(jnp.int32, (span, 1), 0)
    return lax.rem(places, piece) < real


def cross_forward_body(piece, real, low_ref, high_ref, q_ref, kv_ref, qseg_ref, *rest):
    out_ref, outlow_ref, log_ref, key_ref = rest
    step = pl.program_id(0)

    @pl.when(step == 0)
    def _():
        for slot in range(NSEG):
            key_ref[slot] = kv_ref[slot, 0].T

    query, segments = q_ref[0], qseg_ref[...]
    width, span = query.shape[1], kv_ref.shape[3]
    present = page_rows(span, piece, real)

    def fold(slot, state):
        logs, result = state
        scores = jnp.dot(key_ref[slot], query, preferred_element_type=F32)
        scores = jnp.where(present, scores, NEG)
        largest = jnp.max(scores, axis=0, keepdims=True)
        weights = jnp.exp2((scores - largest) * EXP2_SCALE)
        total = jnp.sum(weights, axis=0, keepdims=True)
        part = jnp.dot(kv_ref[slot, 1], weights.astype(BF16), preferred_element_type=F32) / total
        mine = segments == slot
        return (
            jnp.where(mine, largest * EXP2_SCALE + jnp.log2(total), logs),
            jnp.where(mine, part, result),
        )

    state = (jnp.zeros((1, width), F32), jnp.zeros((HEAD_DIM, width), F32))
    logs, result = lax.fori_loop(low_ref[step], high_ref[step] + 1, fold, state)
    out_ref[...] = result
    outlow_ref[0] = result.astype(BF16)
    log_ref[...] = logs


def cross_forward(query, kv, qseg, low, high, piece, real):
    width, span = query.shape[2], kv.shape[3]
    block = min(512, width)
    row = pl.BlockSpec((1, block), lambda i, *_: (0, i))
    column = pl.BlockSpec((1, HEAD_DIM, block), lambda i, *_: (0, 0, i))
    return pl.pallas_call(
        functools.partial(cross_forward_body, piece, real),
        grid_spec=pltpu.PrefetchScalarGridSpec(
            num_scalar_prefetch=2,
            grid=(width // block,),
            in_specs=[
                column,
                pl.BlockSpec((NSEG, 2, HEAD_DIM, span), lambda i, *_: (0, 0, 0, 0)),
                row,
            ],
            out_specs=[pl.BlockSpec((HEAD_DIM, block), lambda i, *_: (0, i)), column, row],
            scratch_shapes=[pltpu.VMEM((NSEG, span, HEAD_DIM), BF16)],
        ),
        out_shape=[
            jax.ShapeDtypeStruct((HEAD_DIM, width), F32),
            jax.ShapeDtypeStruct((1, HEAD_DIM, width), BF16),
            jax.ShapeDtypeStruct((1, width), F32),
        ],
        compiler_params=pltpu.CompilerParams(vmem_limit_bytes=VMEM_LIMIT),
    )(low, high, query, kv, qseg)


class Copies:
    def __init__(self, send_sem, recv_sem):
        self.send_sem, self.recv_sem, self.used = send_sem, recv_sem, 0

    def remote(self, source, target, device):
        index, self.used = self.used, self.used + 1
        copy = pltpu.make_async_remote_copy(
            src_ref=source,
            dst_ref=target,
            send_sem=self.send_sem.at[index],
            recv_sem=self.recv_sem.at[index],
            device_id=device,
            device_id_type=MESH,
        )
        copy.start()
        return copy

    def local(self, source, target):
        index, self.used = self.used, self.used + 1
        copy = pltpu.make_async_copy(source, target, self.send_sem.at[index])
        copy.start()
        return copy


def wait_all(copies):
    for copy in copies:
        copy.wait()


def reversed_bits(value, bits):
    return sum(((value >> b) & 1) << (bits - 1 - b) for b in range(bits))


class Halving:
    def __init__(self, copies, me, count, sums, arrivals):
        self.copies, self.me = copies, me
        self.bits = count.bit_length() - 1
        self.sums, self.arrivals = sums, arrivals
        self.quarter = sums.shape[1] // 2
        self.jobs, self.pending = [], []

    def neighbour(self, kind, step):
        bit = 1 - step if kind == 1 and step < 2 else step
        return {"blk": self.me ^ (1 << bit)}

    def add_job(self, column, width, make):
        here, started = pl.ds(column, width), []
        for kind in range(2):
            for half, quarter in enumerate((2, 3) if kind == 0 else (1, 3)):
                rows = pl.ds(half * self.quarter, self.quarter)
                self.sums[kind, rows, here] = make(kind, quarter).astype(BF16)
            started.append(
                self.copies.remote(
                    self.sums.at[kind, :, here],
                    self.arrivals[0].at[kind, :, here],
                    self.neighbour(kind, 0),
                )
            )
        self.jobs.append((here, make, started))

    def keep_jobs(self):
        for here, make, started in self.jobs:
            wait_all(started)
            for kind in range(2):
                for half, quarter in enumerate((0, 1) if kind == 0 else (0, 2)):
                    rows = pl.ds(half * self.quarter, self.quarter)
                    arrived = self.arrivals[0][kind, rows, here].astype(F32)
                    self.sums[kind, rows, here] = (make(kind, quarter) + arrived).astype(BF16)

    def send(self, step):
        rows = self.sums.shape[1] >> step
        self.pending = [
            self.copies.remote(
                self.sums.at[kind, pl.ds(rows, rows), :],
                self.arrivals[step].at[kind],
                self.neighbour(kind, step),
            )
            for kind in range(2)
        ]

    def receive(self, step, result=None):
        rows = self.sums.shape[1] >> step
        wait_all(self.pending)
        size = min(rows, 32)

        def add(index, _):
            here = pl.ds(pl.multiple_of(index * size, size), size)
            for kind in range(2):
                mine = self.sums[kind, here, :].astype(F32)
                total = mine + self.arrivals[step][kind, here, :].astype(F32)
                if result is None:
                    self.sums[kind, here, :] = total.astype(BF16)
                else:
                    result[kind, here, :] = total
            return 0

        lax.fori_loop(0, rows // size, add, 0)


def arrivals_shapes(count, width, columns):
    bits = count.bit_length() - 1
    return [pltpu.VMEM((2, width >> (step + 1), columns), BF16) for step in range(bits)]


def norm_back_rows(target, grad, unit, inv_std, gain, residual, low=None):
    step = 32

    def body(index, _):
        rows = pl.ds(pl.multiple_of(index * step, step), step)
        z = unit[rows, :]
        w = grad(rows) * gain[...]
        inner = w - jnp.mean(w, axis=1, keepdims=True) - z * jnp.mean(w * z, axis=1, keepdims=True)
        value = residual[rows, :] + inner * inv_std[rows, :]
        target[rows, :] = value
        if low is not None:
            low[rows, :] = value.astype(BF16)
        return 0

    lax.fori_loop(0, target.shape[0] // step, body, 0)


def backward_body(lay, names, late, scratch_names, *refs):
    r = dict(zip(names, refs, strict=False))
    outs = refs[len(names) : len(names) + 6]
    grad_input, memory_own, memory_other, feed_out, middle_out, first_out = outs
    s = dict(zip(scratch_names, refs[len(names) + 6 :], strict=True))
    count, parts, half, rows = lay.count, lay.parts, lay.half, lay.rows
    me, core = lax.axis_index("blk"), lax.axis_index("tp")
    bits = count.bit_length() - 1
    width, wide = r["dc"].shape[1], r["w_cross_out"].shape[0]
    flat_rows = r["dc"].shape[0]
    total, mine_total = r["qkv"].shape[2], r["qkv"].shape[2] // parts
    block = min(512 if parts == 1 else 256, mine_total)

    barrier = pltpu.get_barrier_semaphore()
    for offset in range(1, count):
        pl.semaphore_signal(barrier, inc=1, device_id={"blk": me ^ offset}, device_id_type=MESH)
    pl.semaphore_signal(barrier, inc=1, device_id={"tp": 1 - core}, device_id_type=MESH)
    copies = Copies(s["send_sem"], s["recv_sem"])
    loading = {}

    def load(name):
        loading[name] = copies.local(r[name], s["in_" + late[name]])

    for name, home in late.items():
        if name == home:
            load(name)

    def ready(*wanted):
        for name in wanted:
            loading[name].wait()
            r[name] = s["in_" + late[name]]

    def to_other_core(sent, arrived):
        return copies.remote(sent, arrived, {"tp": 1 - core})

    head, pack, part = lay.head(me), me // half, lax.rem(me, parts)

    def spread(source, target):
        started = []
        for offset in range(0, count, parts):
            peer = me ^ offset
            piece = source.at[
                pl.ds(lay.head(peer) * HEAD_DIM, HEAD_DIM), pl.ds((peer // half) * rows, rows)
            ]
            place = target.at[:, pl.ds((me // parts) * rows, rows)]
            if offset == 0:
                started.append(copies.local(piece, place))
            else:
                started.append(copies.remote(piece, place, {"blk": peer}))
        return started

    def collect(source, target):
        started = []
        place = target.at[pl.ds(head * HEAD_DIM, HEAD_DIM), pl.ds(pack * rows, rows)]
        for offset in range(0, count, parts):
            peer = me ^ offset
            piece = source.at[:, pl.ds((peer // parts) * rows, rows)]
            if offset == 0:
                started.append(copies.local(piece, place))
            else:
                started.append(copies.remote(piece, place, {"blk": peer}))
        return started

    def relative(target, value):
        share, most = width // count, s["turn"].shape[1]
        for start in range(0, value.shape[0], most):
            size = min(most, value.shape[0] - start)
            s["turn"][:, :size] = value[start : start + size, :].T
            for place in range(count):
                chunk = me ^ reversed_bits(place, bits)
                target[pl.ds(place * share, share), start : start + size] = s["turn"][
                    pl.ds(pl.multiple_of(chunk * share, share), share), :size
                ]

    quarter = width // 4

    def quarter_of(ref, index):
        return ref[pl.ds(index * quarter, quarter), :]

    ready("w_cross_out")
    s["out_small"][0] = dot(r["w_cross_out"][...], r["dc"][...], 1, 1).astype(BF16)
    pl.semaphore_wait(barrier, count)
    doc_copies = spread(s["out_small"].at[0], s["doc_unit"])
    load("w_out")

    feed = Halving(
        copies, me, count, s["feed_sums"], [s[f"feed_{i}"] for i in range(bits)]
    )
    ready("dm", "gelu", "h3", "du")
    relative(s["rel_dm"], r["dm"])
    relative(s["rel_h3"], r["h3"])
    load("h2")
    load("h1")
    step = 512
    for column in range(0, r["gelu"].shape[1], step):

        def make(kind, index, column=column):
            left, right = (("rel_dm", "gelu"), ("rel_h3", "du"))[kind]
            return dot(quarter_of(s[left], index), r[right][:, column : column + step], 1, 0)

        feed.add_job(column, step, make)

    ready("kv_slots", "cross_unit", "cross_att")
    slots, span = r["kv_slots"].shape[0], r["kv_slots"].shape[3]
    s["cross_key"][...] = r["kv_slots"][0, 0].T
    s["cross_value"][...] = r["kv_slots"][0, 1].T
    s["cross_acc"][...] = jnp.zeros_like(s["cross_acc"])
    present = page_rows(span, lay.mem_pad, lay.mem_rows)
    wait_all(doc_copies)

    def cross_block(here, slot, key_rows, value_rows):
        query, grad = r["cross_unit"][0, :, here], s["doc_unit"][:, here]
        row_dot = jnp.sum(grad.astype(F32) * r["cross_att"][:, here], axis=0, keepdims=True)
        scores = jnp.dot(key_rows, query, preferred_element_type=F32)
        allowed = present & (r["qslot"][:, here] == slot)
        weights = jnp.where(
            allowed, jnp.exp2(scores * EXP2_SCALE - r["cross_log"][:, here]), 0.0
        )
        weight_grad = jnp.dot(value_rows, grad, preferred_element_type=F32)
        score_grad = (weights * (weight_grad - row_dot)).astype(BF16)
        dq = jnp.dot(r["kv_slots"][slot, 0], score_grad, preferred_element_type=F32)
        return dq, dot(query, score_grad, 1, 1), dot(grad, weights.astype(BF16), 1, 1)

    narrow = min(256, mine_total)

    def main_slot(index, _):
        here = pl.ds(pl.multiple_of(index * narrow, narrow), narrow)
        dq, dk, dv = cross_block(here, 0, s["cross_key"][...], s["cross_value"][...])
        s["dq_acc"][:, here] = dq
        s["cross_acc"][0] += dk
        s["cross_acc"][1] += dv
        return 0

    lax.fori_loop(0, mine_total // narrow, main_slot, 0)
    s["dkv_low"][0, 0, 0] = (s["cross_acc"][0] * SCALE).astype(BF16)
    s["dkv_low"][0, 0, 1] = s["cross_acc"][1].astype(BF16)
    for slot in range(1, slots):
        key_rows, value_rows = r["kv_slots"][slot, 0].T, r["kv_slots"][slot, 1].T
        ends = []
        for start in (0, mine_total - LANES):
            here = pl.ds(start, LANES)
            ends.append(cross_block(here, slot, key_rows, value_rows))
            s["dq_acc"][:, here] += ends[-1][0]
        s["dkv_low"][0, slot, 0] = ((ends[0][1] + ends[1][1]) * SCALE).astype(BF16)
        s["dkv_low"][0, slot, 1] = (ends[0][2] + ends[1][2]).astype(BF16)
    load("att")
    s["dq_low"][0] = (s["dq_acc"][...] * SCALE).astype(BF16)
    dqc_copies = collect(s["dq_low"].at[0], s["in_small"].at[0])
    twin = copies.remote(
        s["dkv_low"].at[0], s["dkv_low"].at[1], {"blk": lax.rem(me + half, count)}
    )

    middle = Halving(
        copies, me, count, s["middle_sums"], [s[f"middle_{i}"] for i in range(bits)]
    )
    piece = wide // 2

    def weight_job(batch, place, left, right):
        def make(kind, index):
            return dot(quarter_of(left, index), right[kind * piece : (kind + 1) * piece, :], 1, 1)

        batch.add_job(place * piece, piece, make)

    ready("cross_mixed")
    relative(s["rel_dc"], r["dc"])
    weight_job(middle, 0, s["rel_dc"], r["cross_mixed"])

    ready("w_cross_query", "unit_two", "grad_two")
    wait_all(dqc_copies)
    for start in range(0, flat_rows, LANES):
        here = slice(start, start + LANES)
        s["tp_send"][here, :] = dot(s["in_small"][0, :, here].T, r["w_cross_query"][...], 1, 1).astype(
            BF16
        )
    tp_copy = to_other_core(s["tp_send"], s["tp_recv"].at[0])
    ready("h2")
    relative(s["rel_h2"], r["h2"])
    weight_job(middle, 1, s["rel_h2"], s["in_small"].at[0])
    tp_copy.wait()

    def both_cores(index):
        def grad(here):
            return s["tp_send"][here, :].astype(F32) + s["tp_recv"][index, here, :].astype(F32)

        return grad

    norm_back_rows(
        s["grad_one"], both_cores(0), r["unit_two"], r["inv_two"], r["gain_two"], r["grad_two"], s["da"]
    )
    ready("w_out")
    s["out_small"][1] = dot(r["w_out"][...], s["da"][...], 1, 1).astype(BF16)
    for name in ("w_q", "unit_one"):
        load(name)
    do_copies = spread(s["out_small"].at[1], s["do_unit"])
    ready("mixed")
    relative(s["rel_da"], s["da"])
    weight_job(middle, 2, s["rel_da"], r["mixed"])

    twin.wait()
    pages_here = lay.pages_half
    for page in range(pages_here):
        for piece_index in range(lay.pieces):
            here = slice(piece_index * lay.mem_pad, (piece_index + 1) * lay.mem_pad)
            value = None
            for side in range(2):
                for slot in range(slots):
                    term = r["hot"][side, slot, page] * s["dkv_low"][side, slot, :, :, here].astype(F32)
                    value = term if value is None else value + term
            s["page_grad"][page * lay.pieces + piece_index] = value.astype(BF16)
    memory_copies = []
    for offset in range(half):
        peer = me ^ offset
        source = s["page_grad"].at[lax.rem(peer, half)]
        place = s["mem_recv"].at[part, :, pl.ds(head * HEAD_DIM, HEAD_DIM), :]
        if offset == 0:
            memory_copies.append(copies.local(source, place))
        else:
            memory_copies.append(copies.remote(source, place, {"blk": peer}))

    ready("qkv", "att")
    if parts > 1:
        ready("query")
    query_ref = r["query"] if parts > 1 else r["qkv"]
    feed.keep_jobs()
    feed.send(1)
    s["dq_acc"][...] = jnp.zeros_like(s["dq_acc"])
    wait_all(do_copies)

    def key_block(key_index, _):
        here = pl.ds(pl.multiple_of(key_index * block, block), block)
        keys, values = r["qkv"][1, :, here], r["qkv"][2, :, here]
        key_rows, value_rows = keys.T, values.T
        codes = jnp.broadcast_to(r["code"][:, here], (8, block)).T[:, :1]

        def fold(index, grads, causal):
            dk, dv = grads
            columns = pl.ds(pl.multiple_of(index * block, block), block)
            query, grad = query_ref[0, :, columns], s["do_unit"][:, columns]
            row_dot = jnp.sum(grad.astype(F32) * r["att"][:, columns], axis=0, keepdims=True)
            scores = jnp.dot(key_rows, query, preferred_element_type=F32)
            allowed = codes == r["qseg"][:, columns]
            if causal:
                places = index * block + lax.broadcasted_iota(jnp.int32, (1, block), 1)
                positions = ((places // rows) * parts + part) * rows + places % rows
                key_places = key_index * block + lax.broadcasted_iota(
                    jnp.int32, (block, block), 0
                )
                allowed = allowed & (key_places <= positions)
            weights = jnp.where(allowed, jnp.exp2(scores * EXP2_SCALE - r["log"][:, columns]), 0.0)
            weight_grad = jnp.dot(value_rows, grad, preferred_element_type=F32)
            score_grad = (weights * (weight_grad - row_dot)).astype(BF16)
            s["dq_acc"][:, columns] += jnp.dot(keys, score_grad, preferred_element_type=F32)
            return (dk + dot(query, score_grad, 1, 1), dv + dot(grad, weights.astype(BF16), 1, 1))

        zeros = jnp.zeros((HEAD_DIM, block), F32)
        first_index = key_index // parts
        grads = fold(first_index, (zeros, zeros), True)
        dk, dv = lax.fori_loop(
            first_index + 1, mine_total // block, lambda i, g: fold(i, g, False), grads
        )
        r["qkv"][1, :, here] = (dk * SCALE).astype(BF16)
        r["qkv"][2, :, here] = dv.astype(BF16)
        return 0

    lax.fori_loop(0, total // block, key_block, 0)
    s["dq_low"][1] = (s["dq_acc"][...] * SCALE).astype(BF16)
    dq_copies = collect(s["dq_low"].at[1], s["in_small"].at[1])
    dkv_copies = []
    for offset in range(count):
        peer = me ^ offset
        source = r["qkv"].at[pl.ds(1, 2), :, pl.ds(peer * rows, rows)]
        place = s["dkv_recv"].at[
            part, :, pl.ds(head * HEAD_DIM, HEAD_DIM), pl.ds(pack * rows, rows)
        ]
        if offset == 0:
            dkv_copies.append(copies.local(source, place))
        else:
            dkv_copies.append(copies.remote(source, place, {"blk": peer}))

    ready("mem", "w_ck", "w_cv")
    wait_all(memory_copies)
    if parts > 1:
        for kind in range(2):
            value = s["mem_recv"][0, kind].astype(F32)
            for index in range(1, parts):
                value = value + s["mem_recv"][index, kind].astype(F32)
            s["mem_recv"][0, kind] = value.astype(BF16)
    for start in range(0, lay.mem_pad, LANES):
        here = slice(start, start + LANES)
        s["mem_send"][here, :] = (
            dot(s["mem_recv"][0, 0, :, here].T, r["w_ck"][...], 1, 1)
            + dot(s["mem_recv"][0, 1, :, here].T, r["w_cv"][...], 1, 1)
        ).astype(BF16)
    load("w_k")
    load("w_v")
    mem_copies = [
        to_other_core(s["mem_send"], memory_other),
        copies.local(s["mem_send"], memory_own),
    ]
    relative(s["rel_mem"], r["mem"])
    weight_job(middle, 3, s["rel_mem"], s["mem_recv"].at[0, 0])
    weight_job(middle, 4, s["rel_mem"], s["mem_recv"].at[0, 1])

    feed.receive(1)
    if bits > 2:
        feed.send(2)
    ready("w_q", "w_k", "w_v", "unit_one", "h1")
    relative(s["rel_h3"], r["h1"])
    wait_all(dq_copies)
    wait_all(dkv_copies)
    if parts > 1:
        for kind in range(2):
            value = s["dkv_recv"][0, kind].astype(F32)
            for index in range(1, parts):
                value = value + s["dkv_recv"][index, kind].astype(F32)
            s["dkv_recv"][0, kind] = value.astype(BF16)
    first = Halving(
        copies,
        me,
        count,
        s["feed_0"].at[:, :, pl.ds(0, 3 * wide // 2)],
        [s[f"first_{i}"] for i in range(bits)],
    )
    pieces = (s["in_small"].at[1], s["dkv_recv"].at[0, 0], s["dkv_recv"].at[0, 1])
    for place, value in enumerate(pieces):
        weight_job(first, place, s["rel_h3"], value)
    for start in range(0, flat_rows, LANES):
        here = slice(start, start + LANES)
        s["tp_send"][here, :] = sum(
            dot(value[:, here].T, r[weight][...], 1, 1)
            for value, weight in zip(pieces, ("w_q", "w_k", "w_v"), strict=True)
        ).astype(BF16)
    tp_copy = to_other_core(s["tp_send"], s["tp_recv"].at[1])
    middle.keep_jobs()
    middle.send(1)
    tp_copy.wait()

    def both_cores_two(here):
        return s["tp_send"][here, :].astype(F32) + s["tp_recv"][1, here, :].astype(F32)

    norm_back_rows(
        grad_input, both_cores_two, r["unit_one"], r["inv_one"], r["gain_one"], s["grad_one"]
    )

    batches = [(feed, feed_out, 2), (middle, middle_out, 1), (first, first_out, 0)]
    first.keep_jobs()
    first.send(1)
    middle.receive(1)
    middle.send(2)
    for step in range(2, bits):
        last = step == bits - 1
        feed.receive(step, feed_out if last else None)
        if not last:
            feed.send(step + 1)
        first.receive(step - 1)
        first.send(step)
        middle.receive(step, middle_out if last else None)
        if not last:
            middle.send(step + 1)
    first.receive(bits - 1, first_out)
    wait_all(mem_copies)


def backward(lay, values, hot, ff):
    parts, count, half = lay.parts, lay.count, lay.half
    width = values["dc"].shape[1]
    flat_rows, wide = values["dc"].shape[0], lay.heads * HEAD_DIM
    total = values["qkv"].shape[2]
    mine_total = total // parts
    span = lay.pieces * lay.mem_pad
    bits = count.bit_length() - 1
    if parts == 1:
        values.pop("query")
    late = [
        "w_cross_out", "dm", "gelu", "h3", "du", "kv_slots", "cross_unit", "cross_att", "cross_mixed",
        "w_cross_query", "unit_two", "grad_two", "mixed", "qkv", "mem",
        "w_ck", "w_cv",
    ]
    if parts > 1:
        late.append("query")
    late = {name: name for name in late}
    late.update(w_out="w_cross_out", w_q="w_cross_query", w_k="w_ck", w_v="w_cv")
    late.update(unit_one="unit_two", h2="dm", h1="h3", att="cross_att")
    early = [name for name in values if name not in late]
    names = ["hot"] + early + list(late)
    vmem, anywhere = pl.BlockSpec(memory_space=pltpu.VMEM), pl.BlockSpec(memory_space=pl.ANY)

    def buffer(*shape, dtype=BF16):
        return pltpu.VMEM(shape, dtype)

    scratch = {
        "send_sem": pltpu.SemaphoreType.DMA((7 * count + 96,)),
        "recv_sem": pltpu.SemaphoreType.DMA((7 * count + 96,)),
        "out_small": buffer(2, wide, flat_rows),
        "in_small": buffer(2, wide, flat_rows),
        "doc_unit": buffer(HEAD_DIM, mine_total),
        "do_unit": buffer(HEAD_DIM, mine_total),
        "dq_acc": buffer(HEAD_DIM, mine_total, dtype=F32),
        "dq_low": buffer(2, HEAD_DIM, mine_total),
        "turn": buffer(width, flat_rows),
        "rel_dm": buffer(width, flat_rows),
        "rel_h3": buffer(width, flat_rows),
        "rel_dc": buffer(width, flat_rows),
        "rel_h2": buffer(width, flat_rows),
        "rel_da": buffer(width, flat_rows),
        "rel_mem": buffer(width, lay.mem_pad),
        "cross_key": buffer(span, HEAD_DIM),
        "cross_value": buffer(span, HEAD_DIM),
        "cross_acc": buffer(2, HEAD_DIM, span, dtype=F32),
        "dkv_low": buffer(2, NSEG, 2, HEAD_DIM, span),
        "page_grad": buffer(half, 2, HEAD_DIM, lay.mem_pad),
        "mem_recv": buffer(parts, 2, wide, lay.mem_pad),
        "mem_send": buffer(lay.mem_pad, width),
        "tp_send": buffer(flat_rows, width),
        "tp_recv": buffer(2, flat_rows, width),
        "grad_one": buffer(flat_rows, width, dtype=F32),
        "da": buffer(flat_rows, width),
        "dkv_recv": buffer(parts, 2, wide, flat_rows),
    }
    columns = {"feed": ff, "middle": 5 * wide // 2, "first": 3 * wide // 2}
    for name, number in columns.items():
        if name != "first":
            scratch[name + "_sums"] = buffer(2, width // 2, number)
        for index, shape in enumerate(arrivals_shapes(count, width, number)):
            scratch[f"{name}_{index}"] = shape
    for name in dict.fromkeys(late.values()):
        scratch["in_" + name] = pltpu.VMEM(values[name].shape, values[name].dtype)
    share = width // count
    return pl.pallas_call(
        functools.partial(backward_body, lay, names, late, list(scratch)),
        out_shape=[
            jax.ShapeDtypeStruct((flat_rows, width), F32),
            jax.ShapeDtypeStruct((lay.mem_pad, width), BF16),
            jax.ShapeDtypeStruct((lay.mem_pad, width), BF16),
        ]
        + [jax.ShapeDtypeStruct((2, share, columns[name]), F32) for name in columns],
        in_specs=[pl.BlockSpec(memory_space=pltpu.SMEM)] + [vmem] * len(early) + [anywhere] * len(late),
        out_specs=[vmem, anywhere, anywhere, vmem, vmem, vmem],
        scratch_shapes=list(scratch.values()),
        compiler_params=pltpu.CompilerParams(
            collective_id=4, has_side_effects=True, vmem_limit_bytes=62 * 1024 * 1024
        ),
    )(hot, *[values[name] for name in early + list(late)])


def layer_norm(value, gain):
    mean = jnp.mean(value, axis=-1, keepdims=True)
    centred = value - mean
    inv_std = lax.rsqrt(jnp.mean(centred * centred, axis=-1, keepdims=True) + EPS)
    unit = centred * inv_std
    return ((unit * gain).astype(BF16), unit, inv_std)


def norm_back(grad, unit, inv_std, gain):
    scaled = grad * gain
    inner = (
        scaled
        - jnp.mean(scaled, axis=-1, keepdims=True)
        - unit * jnp.mean(scaled * unit, axis=-1, keepdims=True)
    )
    return inner * inv_std


def other_core(value):
    return lax.ppermute(value, "tp", [(0, 1), (1, 0)])


def tp_total(partial_sum):
    low = partial_sum.astype(BF16)
    return low.astype(F32) + other_core(low).astype(F32)


def local(
    tokens,
    memory,
    segment_ids,
    token_valid,
    segment_page,
    gain_one,
    weight_query,
    weight_key,
    weight_value,
    weight_out,
    gain_two,
    cross_query,
    cross_key,
    cross_value,
    cross_out,
    gain_three,
    weight_up,
    weight_down,
    cotangent,
):
    packs, rows, width = tokens.shape
    heads = weight_query.shape[1] // HEAD_DIM
    count, place = lax.axis_size("blk"), lax.axis_index("blk")
    lay = Layout(count, packs, heads, rows, memory.shape[0])
    parts, half = lay.parts, lay.half
    flat_rows, total = packs * rows, count * rows
    share = width // count
    pack, part = place // half, lax.rem(place, parts)

    residual_in = tokens.reshape(flat_rows, width).astype(F32)
    hidden_one, unit_one, inv_one = layer_norm(residual_in, gain_one)
    qkv_tokens = jnp.stack(
        [dot(w, hidden_one, 0, 1).astype(BF16) for w in (weight_query, weight_key, weight_value)]
    )
    memory_padded = jnp.pad(memory, ((0, lay.mem_pad - lay.mem_rows), (0, 0)))
    kv_memory = jnp.stack(
        [dot(w, memory_padded, 0, 1).astype(BF16) for w in (cross_key, cross_value)]
    )
    codes = jnp.broadcast_to((segment_ids * 2 + token_valid)[:, None, :], (packs, 8, rows))
    qkv, codes, kv_half = exchange(
        0, [lay.to_units(qkv_tokens), lay.codes_to_units(codes), lay.memory_to_units(kv_memory)]
    )
    codes = codes[:1]
    segments = codes >> 1
    key_codes = jnp.where((codes & 1) == 1, segments, -1).reshape(total, 1)

    def own_part(value):
        if parts == 1:
            return value
        split = value.reshape(value.shape[:-1] + (count // parts, parts, rows))
        split = lax.dynamic_index_in_dim(split, part, split.ndim - 2, keepdims=False)
        return split.reshape(value.shape[:-1] + (total // parts,))

    def all_parts(value):
        if parts == 1:
            return value
        split = value.reshape(value.shape[:-1] + (count // parts, 1, rows))
        split = jnp.broadcast_to(split, value.shape[:-1] + (count // parts, parts, rows))
        return split.reshape(value.shape[:-1] + (total,))

    def pick_part(value):
        return lax.dynamic_index_in_dim(value, part, 0, keepdims=False)

    query = own_part(qkv[:1]) if parts > 1 else qkv
    query_segments = own_part(segments)
    query_positions = own_part(jnp.arange(total, dtype=jnp.int32)[None])

    slot_pages = segment_page.reshape(packs, NSEG)
    pages_here = lay.pages_half
    kv_pages = (
        kv_half.reshape(pages_here, lay.pieces, 2, HEAD_DIM, lay.mem_pad)
        .transpose(0, 2, 3, 1, 4)
        .reshape(pages_here, 2, HEAD_DIM, lay.pieces * lay.mem_pad)
    )
    first_page = pack * pages_here
    longest = jnp.argmax(
        jnp.sum((segments == jnp.arange(NSEG, dtype=jnp.int32)[:, None]).astype(jnp.int32), axis=1)
    ).astype(jnp.int32)
    own_pages = jnp.roll(lax.dynamic_index_in_dim(slot_pages, pack, 0, keepdims=False), -longest)
    twin_pages = lax.ppermute(own_pages, "blk", [(i, (i + count // packs) % count) for i in range(count)])
    query_slots = lax.rem(query_segments - longest + NSEG, NSEG)

    def pages_of(wanted):
        found = [
            lax.dynamic_index_in_dim(
                kv_pages, jnp.clip(wanted[s] - first_page, 0, pages_here - 1), 0, keepdims=False
            )
            for s in range(NSEG)
        ]
        return jnp.stack(found)

    def is_here(wanted):
        return (wanted >= first_page) & (wanted < first_page + pages_here)

    twin_pairs = [(i, (i + half) % count) for i in range(count)]
    kv_twin = lax.ppermute(pages_of(twin_pages), "blk", twin_pairs)
    kv_slots = jnp.where(is_here(own_pages)[:, None, None, None], pages_of(own_pages), kv_twin)

    attention, attention_low, attention_log = self_forward(
        query, qkv, key_codes, query_segments, query_positions, parts
    )
    (mixed,) = exchange(1, [lay.from_units(all_parts(attention_low))])
    mixed = pick_part(mixed)[0]
    residual_one = residual_in + tp_total(dot(mixed, weight_out, 0, 0))
    hidden_two, unit_two, inv_two = layer_norm(residual_one, gain_two)

    cross_tokens = dot(cross_query, hidden_two, 0, 1).astype(BF16)[None]
    (cross_unit,) = exchange(2, [lay.to_units(cross_tokens)])
    cross_unit = own_part(cross_unit)
    block = min(512, total // parts)
    blocks = query_slots.reshape(-1, block)
    low, high = jnp.min(blocks, axis=1), jnp.max(blocks, axis=1)
    cross_attention, cross_low, cross_log = cross_forward(
        cross_unit, kv_slots, query_slots, low, high, lay.mem_pad, lay.mem_rows
    )
    (cross_mixed,) = exchange(3, [lay.from_units(all_parts(cross_low))])
    cross_mixed = pick_part(cross_mixed)[0]
    residual_two = residual_one + tp_total(dot(cross_mixed, cross_out, 0, 0))
    hidden_three, unit_three, inv_three = layer_norm(residual_two, gain_three)

    up_value = dot(hidden_three, weight_up, 1, 0)
    gelu_value, gelu_back = jax.vjp(functools.partial(jax.nn.gelu, approximate=False), up_value)
    gelu_low = gelu_value.astype(BF16)
    result = residual_two + tp_total(dot(gelu_low, weight_down, 1, 0))
    out = result.astype(BF16).reshape(packs, rows, width)
    down_in = cotangent.reshape(flat_rows, width)
    up_grad = gelu_back(dot(down_in, weight_down, 1, 1))[0].astype(BF16)
    grad_hidden = tp_total(dot(up_grad, weight_up, 1, 1))
    grad_two = down_in.astype(F32) + norm_back(grad_hidden, unit_three, inv_three, gain_three)

    page_ids = first_page + jnp.arange(pages_here, dtype=jnp.int32)
    hot = (jnp.stack([own_pages, twin_pages])[:, :, None] == page_ids).astype(F32)
    values = {
        "dc": grad_two.astype(BF16),
        "dm": down_in,
        "gelu": gelu_low,
        "h3": hidden_three,
        "du": up_grad,
        "grad_two": grad_two,
        "unit_two": unit_two,
        "inv_two": inv_two,
        "gain_two": gain_two[None],
        "unit_one": unit_one,
        "inv_one": inv_one,
        "gain_one": gain_one[None],
        "h2": hidden_two,
        "h1": hidden_one,
        "mixed": mixed,
        "cross_mixed": cross_mixed,
        "mem": memory_padded,
        "qkv": qkv,
        "query": query,
        "code": key_codes.reshape(1, total).astype(F32),
        "qseg": query_segments.astype(F32),
        "att": attention,
        "log": attention_log,
        "cross_unit": cross_unit,
        "kv_slots": kv_slots,
        "qslot": query_slots,
        "cross_att": cross_attention,
        "cross_log": cross_log,
        "w_cross_out": cross_out,
        "w_cross_query": cross_query,
        "w_out": weight_out,
        "w_ck": cross_key,
        "w_cv": cross_value,
        "w_q": weight_query,
        "w_k": weight_key,
        "w_v": weight_value,
    }
    grad_input, memory_own, memory_other, feed_share, middle_share, first_share = backward(
        lay, values, hot, weight_up.shape[1]
    )
    grad_memory = (memory_own.astype(F32) + memory_other.astype(F32))[: lay.mem_rows]
    grad_input = grad_input.reshape(packs, rows, width)

    wide = weight_query.shape[1]
    grad_down, grad_up = feed_share[0].T, feed_share[1]

    def columns_of(value, index):
        return jnp.concatenate(
            [value[kind, :, index * wide // 2 : (index + 1) * wide // 2] for kind in range(2)], axis=1
        )

    middle = [columns_of(middle_share, i) for i in range(5)]
    first = [columns_of(first_share, i) for i in range(3)]

    def own_rows(weight):
        return lax.dynamic_slice_in_dim(weight, place * share, share, 0).astype(F32)

    sums = jnp.stack(
        [
            sum(
                jnp.sum(own_rows(w) * g, axis=1)
                for w, g in zip((weight_query, weight_key, weight_value), first, strict=True)
            ),
            jnp.sum(own_rows(cross_query) * middle[1], axis=1),
            jnp.sum(own_rows(weight_up) * grad_up, axis=1),
        ]
    )
    gains = jnp.stack(
        [lax.dynamic_slice_in_dim(g, place * share, share) for g in (gain_one, gain_two, gain_three)]
    )
    gain_grads = (sums + other_core(sums)) / gains
    return (
        out,
        grad_input,
        grad_memory,
        first[0],
        first[1],
        first[2],
        middle[2].T,
        middle[1],
        middle[3],
        middle[4],
        middle[0].T,
        grad_up,
        grad_down,
        gain_grads[0],
        gain_grads[1],
        gain_grads[2],
    )


def solution(mesh):
    in_specs = (
        P(None, "blk", None),
        P("blk", None),
        P(None, "blk"),
        P(None, "blk"),
        P(),
        P(),
        P(None, "tp"),
        P(None, "tp"),
        P(None, "tp"),
        P("tp", None),
        P(),
        P(None, "tp"),
        P(None, "tp"),
        P(None, "tp"),
        P("tp", None),
        P(),
        P(None, "tp"),
        P("tp", None),
        P(None, "blk", None),
    )
    out_specs = (
        P(None, "blk", None),
        P(None, "blk", None),
        P("blk", None),
        P("blk", "tp"),
        P("blk", "tp"),
        P("blk", "tp"),
        P("tp", "blk"),
        P("blk", "tp"),
        P("blk", "tp"),
        P("blk", "tp"),
        P("tp", "blk"),
        P("blk", "tp"),
        P("tp", "blk"),
        P("blk"),
        P("blk"),
        P("blk"),
    )
    return jax.shard_map(local, mesh=mesh, in_specs=in_specs, out_specs=out_specs, check_vma=False)
```

```python
import functools

import jax
import jax.numpy as jnp
from jax import lax
from jax.experimental import pallas as pl
from jax.experimental.pallas import tpu as pltpu
from jax.sharding import PartitionSpec as P

MEM_LEN = 588
HEAD_DIM = 64
NSEG = 3
EPS = 1e-05
NEG = -1e30
EXP2_SCALE = HEAD_DIM**-0.5 * 1.4426950408889634
SCALE = HEAD_DIM**-0.5
LANES = 128
BF16 = jnp.bfloat16
F32 = jnp.float32
MESH = pl.DeviceIdType.MESH


def dot(left, right, contract_left, contract_right):
    return lax.dot_general(
        left, right, (((contract_left,), (contract_right,)), ((), ())), preferred_element_type=F32
    )


def wait_all(copies):
    for copy in copies:
        copy.wait()


class Layout:
    def __init__(self, count, packs, heads, rows, mem_rows):
        self.count, self.packs, self.heads, self.rows = count, packs, heads, rows
        self.half = count // packs
        self.parts = self.half // heads
        self.mem_rows = mem_rows
        self.mem_pad = -(-mem_rows // LANES) * LANES
        self.pieces = MEM_LEN // mem_rows
        self.pages_half = self.half // self.pieces

    def head(self, device):
        return lax.rem(device, self.half) // self.parts


def page_rows(span, piece, real):
    places = lax.broadcasted_iota(jnp.int32, (span, 1), 0)
    return lax.rem(places, piece) < real


def erf(value):
    x = jnp.clip(value, -3.832506856900711, 3.832506856900711)
    square = x * x
    top = jnp.float32(0.00022905065861350646)
    for coefficient in (0.0034082910107109506, 0.050955695062380861, 0.18520832239976145, 1.128379143519084):
        top = top * square + coefficient
    low = jnp.float32(-1.1791602954361697e-7)
    for coefficient in (
        0.000023547966471313185,
        0.0010179625278914885,
        0.014070470171167667,
        0.11098505178285362,
        0.49746925110067538,
        1.0,
    ):
        low = low * square + coefficient
    return x * top / low


def normed_rows(source, gain, low):
    step = 32

    def body(index, _):
        rows = pl.ds(pl.multiple_of(index * step, step), step)
        value = source(rows)
        centred = value - jnp.mean(value, axis=1, keepdims=True)
        inv_std = lax.rsqrt(jnp.mean(centred * centred, axis=1, keepdims=True) + EPS)
        low[rows, :] = (centred * inv_std * gain[...]).astype(BF16)
        return 0

    lax.fori_loop(0, low.shape[0] // step, body, 0)


def norm_back_rows(target, grad, source, gain, residual, low=None):
    step = 32

    def body(index, _):
        rows = pl.ds(pl.multiple_of(index * step, step), step)
        value = source(rows)
        centred = value - jnp.mean(value, axis=1, keepdims=True)
        inv_std = lax.rsqrt(jnp.mean(centred * centred, axis=1, keepdims=True) + EPS)
        z = centred * inv_std
        w = grad(rows) * gain[...]
        inner = w - jnp.mean(w, axis=1, keepdims=True) - z * jnp.mean(w * z, axis=1, keepdims=True)
        value = residual(rows) + inner * inv_std
        target[rows, :] = value
        if low is not None:
            low[rows, :] = value.astype(BF16)
        return 0

    lax.fori_loop(0, target.shape[0] // step, body, 0)


class Links:
    def __init__(self, lay, scratch):
        self.lay = lay
        self.me, self.core = lax.axis_index("blk"), lax.axis_index("tp")
        self.head, self.pack = lay.head(self.me), self.me // lay.half
        self.part = lax.rem(self.me, lay.parts)
        self.send_sem, self.recv_sem, self.used = scratch["send_sem"], scratch["recv_sem"], 0
        self.barrier = pltpu.get_barrier_semaphore()

    def announce(self, everyone=False):
        for offset in range(self.lay.count):
            if offset > 0:
                self.signal(offset, self.core)
            if offset == 0 or everyone:
                self.signal(offset, 1 - self.core)

    def signal(self, offset, core):
        device = {"blk": self.me ^ offset, "tp": core}
        pl.semaphore_signal(self.barrier, inc=1, device_id=device, device_id_type=MESH)

    def all_here(self, everyone=False):
        pl.semaphore_wait(self.barrier, (2 if everyone else 1) * self.lay.count - (1 if everyone else 0))

    def take(self, number=1):
        index, self.used = self.used, self.used + number
        return index

    def described(self, index, source, target, device):
        return pltpu.make_async_remote_copy(
            src_ref=source,
            dst_ref=target,
            send_sem=self.send_sem.at[index],
            recv_sem=self.recv_sem.at[index],
            device_id=device,
            device_id_type=MESH,
        )

    def remote(self, source, target, device):
        copy = self.described(self.take(), source, target, device)
        copy.start()
        return copy

    def local(self, source, target):
        copy = pltpu.make_async_copy(source, target, self.send_sem.at[self.take()])
        copy.start()
        return copy

    def to(self, offset, source, target):
        if offset == 0:
            return self.local(source, target)
        return self.remote(source, target, {"blk": self.me ^ offset})

    def to_other_core(self, source, target):
        return self.remote(source, target, {"tp": 1 - self.core})

    def spread(self, source, target, every=False):
        lay, step = self.lay, 1 if every else self.lay.parts
        started = []
        for offset in range(0, lay.count, step):
            peer = self.me ^ offset
            piece = source.at[
                pl.ds(lay.head(peer) * HEAD_DIM, HEAD_DIM), pl.ds((peer // lay.half) * lay.rows, lay.rows)
            ]
            started.append(self.to(offset, piece, target.at[:, pl.ds((self.me // step) * lay.rows, lay.rows)]))
        return started

    def unit_place(self, target):
        lay = self.lay
        return target.at[pl.ds(self.head * HEAD_DIM, HEAD_DIM), pl.ds(self.pack * lay.rows, lay.rows)]

    def collect(self, source, target):
        lay, started = self.lay, []
        for offset in range(0, lay.count, lay.parts):
            peer = self.me ^ offset
            piece = source.at[:, pl.ds((peer // lay.parts) * lay.rows, lay.rows)]
            started.append(self.to(offset, piece, self.unit_place(target)))
        return started

    def collect_later(self, source, target):
        lay = self.lay
        first = self.take(lay.count // lay.parts)

        def send(number):
            peer = number * lay.parts + self.part
            piece, place = source.at[:, pl.ds(number * lay.rows, lay.rows)], self.unit_place(target)

            @pl.when(peer != self.me)
            def _():
                index = first + (peer ^ self.me) // lay.parts
                self.described(index, piece, place, {"blk": peer}).start()

            @pl.when(peer == self.me)
            def _():
                pltpu.make_async_copy(piece, place, self.send_sem.at[first]).start()

        def wait():
            piece = source.at[:, pl.ds(0, lay.rows)]
            for offset in range(0, lay.count, lay.parts):
                peer = self.me ^ offset
                index = first + offset // lay.parts
                if offset == 0:
                    pltpu.make_async_copy(piece, self.unit_place(target), self.send_sem.at[index]).wait()
                else:
                    self.described(index, piece, self.unit_place(target), {"blk": peer}).wait()

        return send, wait


def forward_body(lay, names, late, out_names, scratch_names, *refs):
    r = dict(zip(names, refs, strict=False))
    o = dict(zip(out_names, refs[len(names) :], strict=False))
    s = dict(zip(scratch_names, refs[len(names) + len(out_names) :], strict=True))
    count, parts, half, rows = lay.count, lay.parts, lay.half, lay.rows
    links = Links(lay, s)
    me, core = links.me, links.core
    links.announce()
    flat_rows, width = r["x"].shape
    wide, ff = s["w_out"].shape[0], r["w_up"].shape[1]
    total = count * rows
    mine_total = total // parts
    loading = {name: links.local(r[name], s[name]) for name in late}
    leaving = []

    def ready(*wanted):
        for name in wanted:
            loading[name].wait()

    def emit(*wanted):
        for name in wanted:
            leaving.append(links.local(s[name], o[name]))

    half_rows = pl.ds(pl.multiple_of(core * wide, wide), wide)
    normed_rows(lambda here: r["x"][here, :].astype(F32), r["gain_one"], s["h1"])
    s["h1_turned"][...] = s["h1"][:, half_rows].T
    other, group = me ^ half, 4
    ready("mem", "w_ck", "w_cv")
    for index, name in enumerate(("w_ck", "w_cv")):
        s["kv_tok"][index] = dot(s["mem"][...], s[name][...], 1, 0).astype(BF16).T
    links.all_here()

    def pack_chunk(owner, first=0, size=wide):
        here = pl.ds(pl.multiple_of(core * wide, wide) + first, size)
        return s["h1_all"].at[here, pl.ds(pl.multiple_of(owner * rows, rows), rows)]

    hand_over = links.remote(
        s["h1_turned"].at[:, pl.ds((1 - links.pack) * rows, rows)], pack_chunk(me), {"blk": other}
    )
    links.local(s["h1_turned"].at[:, pl.ds(links.pack * rows, rows)], pack_chunk(me)).wait()
    ways = half.bit_length() - 1
    shares = [16 * (wide // 16 // ways + (way < wide // 16 % ways)) for way in range(ways)]

    def double(step, owners):
        started = []
        for way in range(ways):
            first, order = sum(shares[:way]), [(way + turn) % ways for turn in range(step + 1)]
            held = [0]
            for bit in order[:-1]:
                held += [offset ^ (1 << bit) for offset in held]
            for owner in owners:
                for offset in held:
                    piece = pack_chunk(owner ^ offset, first, shares[way])
                    started.append(links.to(1 << order[-1], piece, piece))
        return started

    near_copies = double(0, [me])
    code_copies = []
    for offset in range(count):
        peer = me ^ offset
        code_copies.append(
            links.to(offset, r["codes"].at[peer // half], s["codes"].at[:, pl.ds(me * rows, rows)])
        )
    hand_over.wait()
    near_copies += double(0, [other])

    for index, name in enumerate(("w_q", "w_k", "w_v")):
        ready(name)
        s["turn"][...] = s[name][...].T
        s["w_unit"][index * HEAD_DIM : (index + 1) * HEAD_DIM, :] = s["turn"][
            pl.ds(pl.multiple_of(links.head * HEAD_DIM, HEAD_DIM), HEAD_DIM), :
        ]

    wait_all(near_copies)
    for step in range(1, ways):
        wait_all(double(step, [me, other]))
    core_copy = links.to_other_core(s["h1_all"].at[half_rows, :], s["h1_all"].at[half_rows, :])
    memory_copies = []
    for offset in range(half):
        peer = me ^ offset
        piece = s["kv_tok"].at[:, pl.ds(lay.head(peer) * HEAD_DIM, HEAD_DIM), :]
        memory_copies.append(links.to(offset, piece, s["kv_half"].at[lax.rem(me, half)]))
    core_copy.wait()
    pack_copy = links.local(s["h1_all"].at[half_rows, :], o["h1_pack"])
    for start in range(0, total, 512):
        columns = slice(start, start + 512)
        value = dot(s["w_unit"][...], s["h1_all"][:, columns], 1, 0).astype(BF16)
        for index in range(3):
            s["qkv"][index, :, columns] = value[index * HEAD_DIM : (index + 1) * HEAD_DIM, :]

    wait_all(code_copies)
    codes = s["codes"][:1, :]
    segments = jnp.floor(codes * 0.5)
    s["code"][...] = jnp.where(codes - 2.0 * segments > 0.5, segments, -1.0)
    lengths = [
        jnp.sum((segments == float(slot)).astype(F32), axis=1, keepdims=True) for slot in range(NSEG)
    ]
    first_longest = ((lengths[0] >= lengths[1]) & (lengths[0] >= lengths[2])).astype(F32)
    second_longest = (lengths[1] >= lengths[2]).astype(F32) * (1.0 - first_longest)
    longest = 2.0 - 2.0 * first_longest - second_longest
    order = segments - longest
    order = jnp.where(order < 0.0, order + float(NSEG), order)
    if parts == 1:
        s["qseg"][...], s["qslot"][...] = segments, order
    else:
        s["rows"][0:1, :], s["rows"][1:2, :] = segments, order
        for piece in range(count // parts):
            there = pl.ds((piece * parts + links.part) * rows, rows)
            s["qseg"][:, piece * rows : (piece + 1) * rows] = s["rows"][0:1, there]
            s["qslot"][:, piece * rows : (piece + 1) * rows] = s["rows"][1:2, there]
            s["query"][:, piece * rows : (piece + 1) * rows] = s["qkv"][0, :, there]
    s["longest"][...] = jnp.broadcast_to(longest, s["longest"].shape)
    emit("qkv", "code", "qseg", "qslot", "longest")
    if parts > 1:
        emit("query")

    block = min(512 if parts == 1 else 256, mine_total)
    s["key"][...] = s["qkv"][1].T
    send_mixed, wait_mixed = links.collect_later(s["low"].at[0], s["mixed"])
    for index in reversed(range(mine_total // block)):
        columns = slice(index * block, (index + 1) * block)
        query = s["query"][:, columns] if parts > 1 else s["qkv"][0, :, columns]
        mine = s["qseg"][:, columns]
        places = index * block + lax.broadcasted_iota(jnp.int32, (1, block), 1)
        positions = ((places // rows) * parts + links.part) * rows + places % rows

        def fold(key_index, state, causal, query=query, mine=mine, positions=positions):
            largest, weight_sum, weighted = state
            start = pl.multiple_of(key_index * block, block)
            here = pl.ds(start, block)
            scores = jnp.dot(s["key"][here, :], query, preferred_element_type=F32)
            allowed = jnp.broadcast_to(s["code"][:, here], (8, block)).T[:, :1] == mine
            if causal:
                key_places = start + lax.broadcasted_iota(jnp.int32, (block, block), 0)
                allowed = allowed & (key_places <= positions)
            scores = jnp.where(allowed, scores, NEG)
            new = jnp.maximum(largest, jnp.max(scores, axis=0, keepdims=True))
            weights = jnp.exp2((scores - new) * EXP2_SCALE)
            keep = jnp.exp2((largest - new) * EXP2_SCALE)
            weight_sum = weight_sum * keep + jnp.sum(weights, axis=0, keepdims=True)
            update = jnp.dot(s["qkv"][2, :, here], weights.astype(BF16), preferred_element_type=F32)
            return (new, weight_sum, weighted * keep + update)

        state = (
            jnp.full((1, block), NEG, F32),
            jnp.zeros((1, block), F32),
            jnp.zeros((HEAD_DIM, block), F32),
        )
        state = lax.fori_loop(0, index * parts, lambda j, c, fold=fold: fold(j, c, False), state)
        for extra in range(parts):
            state = fold(index * parts + extra, state, True)
        largest, weight_sum, weighted = state
        result = weighted / weight_sum
        s["att"][:, columns] = result
        s["low"][0, :, columns] = result.astype(BF16)
        s["log"][:, columns] = largest * EXP2_SCALE + jnp.log2(weight_sum)
        for piece in range(index * block // rows, (index + 1) * block // rows):
            send_mixed(piece)
    emit("att", "log")
    pack_copy.wait()
    w_up = s["h1_all"].at[:, pl.ds(0, ff)]
    up_load = links.local(r["w_up"], w_up)

    def product_rows(left, right, sent, arrived):
        started = []
        for start in range(0, flat_rows, rows):
            here = slice(start, start + rows)
            sent[here, :] = dot(left[:, here].T, right[...], 1, 0).astype(BF16)
            started.append(links.to_other_core(sent.at[pl.ds(start, rows)], arrived.at[pl.ds(start, rows)]))
        return started

    def to_group(source, target):
        started = [links.local(source, target.at[0])]
        for offset in range(1, group):
            started.append(links.to(offset, source.at[:, half_rows], target.at[offset, :, half_rows]))
        return started

    def group_to_other_core(target):
        others = target.at[pl.ds(1, group - 1), :, half_rows]
        return links.to_other_core(others, others)

    def both(sent, arrived):
        return lambda here: sent[here, :].astype(F32) + arrived[here, :].astype(F32)

    def add_rows(target, *terms):
        step = 32

        def body(index, _):
            here = pl.ds(pl.multiple_of(index * step, step), step)
            target[here, :] = sum(term(here) for term in terms).astype(target.dtype)
            return 0

        lax.fori_loop(0, flat_rows // step, body, 0)

    wait_all(memory_copies)
    for side in range(2):
        for slot in range(NSEG):
            for piece in range(lay.pieces):
                value = s["kv_half"][r["pages"][side, slot] * lay.pieces + piece]
                value = value.astype(F32) * r["here"][side, slot]
                s["kv_found"][side, slot, :, :, piece * lay.mem_pad : (piece + 1) * lay.mem_pad] = (
                    value.astype(BF16)
                )

    def to_twin(slot):
        return links.remote(s["kv_found"].at[1, slot], s["kv_twin"].at[slot], {"blk": other})

    twin_copies = [to_twin(slot) for slot in range(NSEG)]

    ready("w_out")
    wait_mixed()
    emit("mixed")
    started = product_rows(s["mixed"], s["w_out"], s["sent"].at[0], s["arrived"].at[0])
    wait_all(started)
    add_rows(
        s["r1"], lambda here: r["x"][here, :].astype(F32), both(s["sent"].at[0], s["arrived"].at[0])
    )
    normed_rows(lambda here: s["r1"][here, :], r["gain_two"], s["h2"])
    ready("w_cross_query")
    s["tok"][0] = dot(s["h2"][...], s["w_cross_query"][...], 1, 0).astype(BF16).T
    query_copies = links.spread(s["tok"].at[0], s["cross_unit"])
    ready("cot")
    cot_copies = to_group(s["cot"], o["dm_group"])
    emit("r1", "h2")

    wait_all(twin_copies)
    is_first = (s["longest"][:1, :1] < 0.5).astype(F32)
    is_second = (s["longest"][:1, :1] < 1.5).astype(F32) - is_first
    is_third = 1.0 - is_first - is_second
    for kind in range(2):
        found = [
            s["kv_found"][0, slot, kind].astype(F32)
            + s["kv_twin"][slot, kind].astype(F32) * (1.0 - r["here"][0, slot])
            for slot in range(NSEG)
        ]
        for slot in range(NSEG):
            value = (
                found[slot] * is_first
                + found[(slot + 1) % NSEG] * is_second
                + found[(slot + 2) % NSEG] * is_third
            )
            s["kv_slots"][slot, kind] = value.astype(BF16)
    emit("kv_slots")

    narrow = min(256, mine_total)
    present = page_rows(lay.pieces * lay.mem_pad, lay.mem_pad, lay.mem_rows)
    key_rows = [s["kv_slots"][slot, 0].T for slot in range(NSEG)]
    send_cross, wait_cross = links.collect_later(s["low"].at[1], s["cross_mixed"])
    wait_all(query_copies)
    emit("cross_unit")

    def attend(columns, slot):
        scores = jnp.dot(key_rows[slot], s["cross_unit"][:, columns], preferred_element_type=F32)
        scores = jnp.where(present, scores, NEG)
        largest = jnp.max(scores, axis=0, keepdims=True)
        weights = jnp.exp2((scores - largest) * EXP2_SCALE)
        weight_sum = jnp.sum(weights, axis=0, keepdims=True)
        result = jnp.dot(s["kv_slots"][slot, 1], weights.astype(BF16), preferred_element_type=F32)
        return result / weight_sum, largest * EXP2_SCALE + jnp.log2(weight_sum)

    for index in range(mine_total // narrow):
        columns = slice(index * narrow, (index + 1) * narrow)
        s["cross_att"][:, columns], s["cross_log"][:, columns] = attend(columns, 0)
        ends = [0] if index == 0 else []
        ends += [mine_total - LANES] if index == mine_total // narrow - 1 else []
        for start in ends:
            columns = slice(start, start + LANES)
            for slot in range(1, NSEG):
                result, logs = attend(columns, slot)
                here = s["qslot"][:, columns] == float(slot)
                s["cross_att"][:, columns] = jnp.where(here, result, s["cross_att"][:, columns])
                s["cross_log"][:, columns] = jnp.where(here, logs, s["cross_log"][:, columns])
        columns = slice(index * narrow, (index + 1) * narrow)
        s["low"][1, :, columns] = s["cross_att"][:, columns].astype(BF16)
        for piece in range(index * narrow // rows, (index + 1) * narrow // rows):
            send_cross(piece)
    emit("cross_att", "cross_log")
    ready("w_cross_out")
    wait_cross()
    emit("cross_mixed")
    started = product_rows(s["cross_mixed"], s["w_cross_out"], s["sent"].at[1], s["arrived"].at[1])
    wait_all(started)
    add_rows(s["r2"], lambda here: s["r1"][here, :], both(s["sent"].at[1], s["arrived"].at[1]))
    normed_rows(lambda here: s["r2"][here, :], r["gain_three"], s["h3"])
    h3_copies = to_group(s["h3"], o["h3_group"])

    ready("w_down")
    up_load.wait()
    slice_width = ff // group
    first_gelu, place = links.take(group), lax.rem(me, group)

    def gelu_copy(number, offset):
        columns = pl.ds(number * slice_width, slice_width)
        device = {"blk": me ^ offset}
        return links.described(
            first_gelu + offset, s["gelu"].at[:, columns], o["gelu_group"].at[offset], device
        )

    def gelu_local(number):
        columns = pl.ds(number * slice_width, slice_width)
        return pltpu.make_async_copy(
            s["gelu"].at[:, columns], o["gelu_group"].at[0], links.send_sem.at[first_gelu]
        )

    s["down_sum"][...] = jnp.zeros_like(s["down_sum"])
    s["up_sum"][...] = jnp.zeros_like(s["up_sum"])
    piece_rows = LANES
    for number in range(group):
        columns = slice(number * slice_width, (number + 1) * slice_width)
        for start in range(0, flat_rows, piece_rows):
            here = slice(start, start + piece_rows)
            u = dot(s["h3"][here, :], w_up[:, columns], 1, 0)
            grad = dot(s["cot"][here, :], s["w_down"][columns, :], 1, 1)
            normal = 0.5 + 0.5 * erf(u * 0.7071067811865476)
            s["gelu"][here, columns] = (u * normal).astype(BF16)
            slope = normal + u * jnp.exp2(u * u * -0.7213475204444817) * 0.3989422804014327
            s["du"][here, columns] = (slope * grad).astype(BF16)

        @pl.when(number != place)
        def _(number=number):
            gelu_copy(number, number ^ place).start()

        @pl.when(number == place)
        def _(number=number):
            gelu_local(number).start()

        s["down_sum"][...] += dot(s["gelu"][:, columns], s["w_down"][columns, :], 1, 0)
        s["up_sum"][...] += dot(s["du"][:, columns], w_up[:, columns], 1, 1)
    emit("du")
    s["sent"][2] = s["up_sum"][...].astype(BF16)
    up_copy = links.to_other_core(s["sent"].at[2], s["arrived"].at[2])
    s["sent"][3] = s["down_sum"][...].astype(BF16)
    down_copy = links.to_other_core(s["sent"].at[3], s["arrived"].at[3])
    wait_all(cot_copies)
    wait_all(h3_copies)
    group_copies = [group_to_other_core(o["dm_group"]), group_to_other_core(o["h3_group"])]
    up_copy.wait()
    norm_back_rows(
        s["grad_two"],
        both(s["sent"].at[2], s["arrived"].at[2]),
        lambda here: s["r2"][here, :],
        r["gain_three"],
        lambda here: s["cot"][here, :].astype(F32),
        s["dc"],
    )
    emit("grad_two", "dc")
    down_copy.wait()
    add_rows(s["out"], lambda here: s["r2"][here, :], both(s["sent"].at[3], s["arrived"].at[3]))
    emit("out")
    gelu_local(0).wait()
    for offset in range(1, group):
        gelu_copy(0, offset).wait()
    wait_all(group_copies)
    wait_all(leaving)


def forward(lay, values, ff):
    parts, count, half, rows = lay.parts, lay.count, lay.half, lay.rows
    flat_rows, width = values["x"].shape
    wide, total = lay.heads * HEAD_DIM, lay.count * lay.rows
    mine_total = total // parts
    span = lay.pieces * lay.mem_pad
    early = ["x", "codes", "gain_one", "gain_two", "gain_three"]
    late = [name for name in values if name not in early + ["pages", "here", "w_up"]]
    names = ["pages", "here"] + early + late + ["w_up"]

    def shape(*dims, dtype=BF16):
        return jax.ShapeDtypeStruct(dims, dtype)

    kept = {
        "qkv": shape(3, HEAD_DIM, total),
        "code": shape(1, total, dtype=F32),
        "qseg": shape(1, mine_total, dtype=F32),
        "qslot": shape(1, mine_total, dtype=F32),
        "longest": shape(8, LANES, dtype=F32),
        "att": shape(HEAD_DIM, mine_total, dtype=F32),
        "log": shape(1, mine_total, dtype=F32),
        "mixed": shape(wide, flat_rows),
        "r1": shape(flat_rows, width, dtype=F32),
        "h2": shape(flat_rows, width),
        "cross_unit": shape(HEAD_DIM, mine_total),
        "kv_slots": shape(NSEG, 2, HEAD_DIM, span),
        "cross_att": shape(HEAD_DIM, mine_total, dtype=F32),
        "cross_log": shape(1, mine_total, dtype=F32),
        "cross_mixed": shape(wide, flat_rows),
        "grad_two": shape(flat_rows, width, dtype=F32),
        "dc": shape(flat_rows, width),
        "out": shape(flat_rows, width),
        "du": shape(flat_rows, ff),
    }
    if parts > 1:
        kept["query"] = shape(HEAD_DIM, mine_total)
    gathered = {
        "dm_group": shape(4, flat_rows, width),
        "h3_group": shape(4, flat_rows, width),
        "gelu_group": shape(4, flat_rows, ff // 4),
        "h1_pack": shape(wide, total),
    }
    scratch = {
        "h1": shape(flat_rows, width),
        "h1_all": shape(width, total),
        "turn": shape(wide, width),
        "w_unit": shape(3 * HEAD_DIM, width),
        "tok": shape(1, wide, flat_rows),
        "h3": shape(flat_rows, width),
        "gelu": shape(flat_rows, ff),
        "codes": shape(8, total, dtype=F32),
        "kv_tok": shape(2, wide, lay.mem_pad),
        "kv_half": shape(half, 2, HEAD_DIM, lay.mem_pad),
        "kv_found": shape(2, NSEG, 2, HEAD_DIM, span),
        "kv_twin": shape(NSEG, 2, HEAD_DIM, span),
        "key": shape(total, HEAD_DIM),
        "low": shape(2, HEAD_DIM, mine_total),
        "h1_turned": shape(wide, flat_rows),
        "sent": shape(4, flat_rows, width),
        "arrived": shape(4, flat_rows, width),
        "r2": shape(flat_rows, width, dtype=F32),
        "down_sum": shape(flat_rows, width, dtype=F32),
        "up_sum": shape(flat_rows, width, dtype=F32),
    }
    if parts > 1:
        scratch["rows"] = shape(8, total, dtype=F32)
    scratch = {name: pltpu.VMEM(value.shape, value.dtype) for name, value in {**scratch, **kept}.items()}
    for name in late:
        scratch[name] = pltpu.VMEM(values[name].shape, values[name].dtype)
    semaphores = pltpu.SemaphoreType.DMA((10 * count + 128,))
    scratch = {"send_sem": semaphores, "recv_sem": semaphores, **scratch}
    outs = {**kept, **gathered}
    anywhere = pl.BlockSpec(memory_space=pl.ANY)
    results = pl.pallas_call(
        functools.partial(forward_body, lay, names, late, list(outs), list(scratch)),
        out_shape=list(outs.values()),
        in_specs=[pl.BlockSpec(memory_space=pltpu.SMEM)] * 2
        + [pl.BlockSpec(memory_space=pltpu.VMEM)] * len(early)
        + [anywhere] * (len(late) + 1),
        out_specs=[anywhere] * len(outs),
        scratch_shapes=list(scratch.values()),
        compiler_params=pltpu.CompilerParams(
            collective_id=0, has_side_effects=True, vmem_limit_bytes=63 * 1024 * 1024
        ),
    )(*[values[name] for name in names])
    return dict(zip(outs, results, strict=True))


def reversed_bits(value, bits):
    return sum(((value >> b) & 1) << (bits - 1 - b) for b in range(bits))


class Halving:
    def __init__(self, links, bits, sums, arrivals, crossed=True):
        self.links, self.bits, self.crossed = links, bits, crossed
        self.sums, self.arrivals = sums, arrivals
        self.quarter = sums.shape[1] // 2
        self.jobs, self.pending = [], []

    def neighbour(self, kind, step):
        bit = self.bits[1 - step if self.crosses(kind) and step < 2 else step]
        return {"blk": self.links.me ^ (1 << bit)}

    def crosses(self, kind):
        return kind == 1 and self.crossed

    def add_job(self, column, width, make):
        here, started = pl.ds(column, width), []
        for kind in range(2):
            for half, quarter in enumerate((1, 3) if self.crosses(kind) else (2, 3)):
                rows = pl.ds(half * self.quarter, self.quarter)
                self.sums[kind, rows, here] = make(kind, quarter).astype(BF16)
            started.append(
                self.links.remote(
                    self.sums.at[kind, :, here],
                    self.arrivals[0].at[kind, :, here],
                    self.neighbour(kind, 0),
                )
            )
        self.jobs.append((here, make, started))

    def keep_jobs(self):
        for here, make, started in self.jobs:
            wait_all(started)
            for kind in range(2):
                for half, quarter in enumerate((0, 2) if self.crosses(kind) else (0, 1)):
                    rows = pl.ds(half * self.quarter, self.quarter)
                    arrived = self.arrivals[0][kind, rows, here].astype(F32)
                    self.sums[kind, rows, here] = (make(kind, quarter) + arrived).astype(BF16)
        self.send(1)

    def send(self, step):
        rows = self.sums.shape[1] >> step
        self.pending = [
            self.links.remote(
                self.sums.at[kind, pl.ds(rows, rows), :],
                self.arrivals[step].at[kind],
                self.neighbour(kind, step),
            )
            for kind in range(2)
        ]

    def receive(self, step, result=None):
        rows = self.sums.shape[1] >> step
        wait_all(self.pending)
        size = min(rows, 32)

        def add(index, _):
            here = pl.ds(pl.multiple_of(index * size, size), size)
            for kind in range(2):
                mine = self.sums[kind, here, :].astype(F32)
                total = mine + self.arrivals[step][kind, here, :].astype(F32)
                if result is None:
                    self.sums[kind, here, :] = total.astype(BF16)
                else:
                    result[kind, here, :] = total
            return 0

        lax.fori_loop(0, rows // size, add, 0)
        if step + 1 < len(self.bits):
            self.send(step + 1)


def arrivals_shapes(bits, width, columns):
    return [pltpu.VMEM((2, width >> (step + 1), columns), BF16) for step in range(bits)]


def backward_body(lay, names, late, scratch_names, *refs):
    r = dict(zip(names, refs, strict=False))
    outs = refs[len(names) : len(names) + 7]
    grad_input, memory_own, memory_other, feed_out, middle_out, pages_out, first_out = outs
    s = dict(zip(scratch_names, refs[len(names) + 7 :], strict=True))
    count, parts, half, rows = lay.count, lay.parts, lay.half, lay.rows
    links = Links(lay, s)
    me, core, head, pack, part = links.me, links.core, links.head, links.pack, links.part
    bits = count.bit_length() - 1
    flat_rows, width = r["dc"].shape
    wide = r["w_cross_out"].shape[0]
    total = r["qkv"].shape[2]
    mine_total = total // parts
    share = width // count
    block = min(512 if parts == 1 else 256, mine_total)
    links.announce(everyone=True)
    loading = {}

    def load(name):
        loading[name] = links.local(r[name], s["in_" + late[name]])

    for name, home in late.items():
        if name == home:
            load(name)
    h1_copy = links.local(r["h1_pack"].at[:, pl.ds(0, s["h1"].shape[1])], s["h1"])

    def ready(*wanted):
        for name in wanted:
            loading[name].wait()
            r[name] = s["in_" + late[name]]

    def relative(target, value, shift=0, column=0):
        number, most = count >> shift, s["turn"].shape[1]
        size_rows = width // number
        for start in range(0, value.shape[0], most):
            size = min(most, value.shape[0] - start)
            s["turn"][:, :size] = value[start : start + size, :].T
            for place in range(number):
                chunk = (me >> shift) ^ reversed_bits(place, bits - shift)
                target[pl.ds(place * size_rows, size_rows), column + start : column + start + size] = s[
                    "turn"
                ][pl.ds(pl.multiple_of(chunk * size_rows, size_rows), size_rows), :size]

    quarter = width // 4

    def quarter_of(ref, index):
        return ref[pl.ds(index * quarter, quarter), :]

    def batch(name, chosen, crossed=True):
        arrivals = [s[f"{name}_{i}"] for i in range(len(chosen))]
        return Halving(links, chosen, s[name + "_sums"], arrivals, crossed)

    piece = wide // 2

    def weight_job(target, place, left, right):
        def make(kind, index):
            return dot(quarter_of(left, index), right[kind * piece : (kind + 1) * piece, :], 1, 1)

        target.add_job(place * piece, piece, make)

    ready("w_cross_out")
    s["out_small"][0] = dot(r["w_cross_out"][...], r["dc"][...], 1, 1).astype(BF16)
    links.all_here(everyone=True)
    doc_copies = links.spread(s["out_small"].at[0], s["doc_unit"])
    load("w_out")

    group = 4
    ready("gelu_group")
    slice_width = r["gelu_group"].shape[2]
    du_copies = []
    for offset in range(group):
        number = lax.rem(me ^ offset, group)
        columns = pl.ds(pl.multiple_of(number * slice_width, slice_width), slice_width)
        du_copies.append(links.to(offset, r["du"].at[:, columns], s["du_group"].at[offset]))

    ready("dm_group")
    for offset in range(group):
        relative(s["rel_dm"], r["dm_group"].at[offset], 2, offset * flat_rows)

    def feed_job(left, right):
        def make(kind, index):
            here = slice(kind * slice_width // 2, (kind + 1) * slice_width // 2)
            return dot(
                quarter_of(left, index), right[:, :, here].reshape(group * flat_rows, slice_width // 2), 1, 0
            )

        return make

    down, up = batch("down", range(2, bits)), batch("up", range(2, bits))
    down.add_job(0, slice_width // 2, feed_job(s["rel_dm"], r["gelu_group"]))
    middle, pages = batch("middle", range(bits)), batch("pages", range(bits))
    ready("cross_mixed")
    relative(s["rel_dc"], r["dc"])
    weight_job(middle, 0, s["rel_dc"], r["cross_mixed"])
    ready("h3_group")
    for offset in range(group):
        relative(s["rel_h3"], r["h3_group"].at[offset], 2, offset * flat_rows)

    ready("kv_slots", "cross_unit", "cross_att")
    slots, span = r["kv_slots"].shape[0], r["kv_slots"].shape[3]
    s["cross_key"][...] = r["kv_slots"][0, 0].T
    s["cross_value"][...] = r["kv_slots"][0, 1].T
    s["cross_acc"][...] = jnp.zeros_like(s["cross_acc"])
    present = page_rows(span, lay.mem_pad, lay.mem_rows)
    wait_all(doc_copies)

    def cross_block(here, slot, key_rows, value_rows):
        query, grad = r["cross_unit"][:, here], s["doc_unit"][:, here]
        row_dot = jnp.sum(grad.astype(F32) * r["cross_att"][:, here], axis=0, keepdims=True)
        scores = jnp.dot(key_rows, query, preferred_element_type=F32)
        allowed = present & (r["qslot"][:, here] == float(slot))
        weights = jnp.where(allowed, jnp.exp2(scores * EXP2_SCALE - r["cross_log"][:, here]), 0.0)
        weight_grad = jnp.dot(value_rows, grad, preferred_element_type=F32)
        score_grad = (weights * (weight_grad - row_dot)).astype(BF16)
        dq = jnp.dot(r["kv_slots"][slot, 0], score_grad, preferred_element_type=F32)
        return dq, dot(query, score_grad, 1, 1), dot(grad, weights.astype(BF16), 1, 1)

    narrow = min(256, mine_total)

    def main_slot(index, _):
        here = pl.ds(pl.multiple_of(index * narrow, narrow), narrow)
        dq, dk, dv = cross_block(here, 0, s["cross_key"][...], s["cross_value"][...])
        s["dq_acc"][:, here] = dq
        s["cross_acc"][0] += dk
        s["cross_acc"][1] += dv
        return 0

    lax.fori_loop(0, mine_total // narrow, main_slot, 0)
    s["dkv_low"][1, 0, 0] = (s["cross_acc"][0] * SCALE).astype(BF16)
    s["dkv_low"][1, 0, 1] = s["cross_acc"][1].astype(BF16)
    for slot in range(1, slots):
        key_rows, value_rows = r["kv_slots"][slot, 0].T, r["kv_slots"][slot, 1].T
        ends = []
        for start in (0, mine_total - LANES):
            here = pl.ds(start, LANES)
            ends.append(cross_block(here, slot, key_rows, value_rows))
            s["dq_acc"][:, here] += ends[-1][0]
        s["dkv_low"][1, slot, 0] = ((ends[0][1] + ends[1][1]) * SCALE).astype(BF16)
        s["dkv_low"][1, slot, 1] = (ends[0][2] + ends[1][2]).astype(BF16)
    load("att")
    s["dq_low"][...] = (s["dq_acc"][...] * SCALE).astype(BF16)
    dqc_copies = links.collect(s["dq_low"], s["in_small"].at[0])
    is_first = (r["longest"][:1, :1] < 0.5).astype(F32)
    is_second = (r["longest"][:1, :1] < 1.5).astype(F32) - is_first
    is_third = 1.0 - is_first - is_second
    for kind in range(2):
        found = [s["dkv_low"][1, slot, kind].astype(F32) for slot in range(slots)]
        for slot in range(slots):
            value = (
                found[slot] * is_first
                + found[(slot + 2) % slots] * is_second
                + found[(slot + 1) % slots] * is_third
            )
            s["dkv_low"][0, slot, kind] = value.astype(BF16)
    def to_twin(slot):
        return links.remote(s["dkv_low"].at[0, slot], s["dkv_twin"].at[slot], {"blk": me ^ half})

    twin_copies = [to_twin(slot) for slot in range(slots)]
    down.keep_jobs()

    ready("w_cross_query")
    wait_all(dqc_copies)
    tp_copies = []
    for start in range(0, flat_rows, rows):
        here = slice(start, start + rows)
        s["tp_send"][here, :] = dot(s["in_small"][0, :, here].T, r["w_cross_query"][...], 1, 1).astype(BF16)
        tp_copies.append(
            links.to_other_core(s["tp_send"].at[pl.ds(start, rows)], s["tp_recv"].at[0, pl.ds(start, rows)])
        )
    ready("h2", "r1", "grad_two")
    relative(s["rel_h2"], r["h2"])
    load("x")
    weight_job(middle, 1, s["rel_h2"], s["in_small"].at[0])
    wait_all(tp_copies)

    def both_cores(index):
        def grad(here):
            return s["tp_send"][here, :].astype(F32) + s["tp_recv"][index, here, :].astype(F32)

        return grad

    norm_back_rows(
        s["grad_one"],
        both_cores(0),
        lambda here: r["r1"][here, :],
        r["gain_two"],
        lambda here: r["grad_two"][here, :],
        s["da"],
    )
    ready("w_out")
    s["out_small"][1] = dot(r["w_out"][...], s["da"][...], 1, 1).astype(BF16)
    do_copies = links.spread(s["out_small"].at[1], s["do_unit"])
    load("w_q")
    ready("mixed")
    relative(s["rel_da"], s["da"])
    weight_job(middle, 2, s["rel_da"], r["mixed"])
    wait_all(du_copies)
    up.add_job(0, slice_width // 2, feed_job(s["rel_h3"], s["du_group"]))

    wait_all(twin_copies)
    for page in range(lay.pages_half):
        for piece_index in range(lay.pieces):
            here = slice(piece_index * lay.mem_pad, (piece_index + 1) * lay.mem_pad)
            value = None
            for side, source in enumerate((s["dkv_low"].at[0], s["dkv_twin"])):
                for slot in range(slots):
                    term = r["hot"][side, slot, page] * source[slot, :, :, here].astype(F32)
                    value = term if value is None else value + term
            s["page_grad"][page * lay.pieces + piece_index] = value.astype(BF16)
    memory_copies = []
    for offset in range(half):
        source = s["page_grad"].at[lax.rem(me ^ offset, half)]
        place = s["mem_recv"].at[part, :, pl.ds(head * HEAD_DIM, HEAD_DIM), :]
        memory_copies.append(links.to(offset, source, place))

    ready("qkv", "att")
    if parts > 1:
        ready("query")
    s["dq_acc"][...] = jnp.zeros_like(s["dq_acc"])
    wait_all(do_copies)

    def key_block(key_index, _):
        here = pl.ds(pl.multiple_of(key_index * block, block), block)
        keys, values = r["qkv"][1, :, here], r["qkv"][2, :, here]
        key_rows, value_rows = keys.T, values.T
        codes = jnp.broadcast_to(r["code"][:, here], (8, block)).T[:, :1]

        def fold(index, grads, causal):
            dk, dv = grads
            columns = pl.ds(pl.multiple_of(index * block, block), block)
            query = r["query"][:, columns] if parts > 1 else r["qkv"][0, :, columns]
            grad = s["do_unit"][:, columns]
            row_dot = jnp.sum(grad.astype(F32) * r["att"][:, columns], axis=0, keepdims=True)
            scores = jnp.dot(key_rows, query, preferred_element_type=F32)
            allowed = codes == r["qseg"][:, columns]
            if causal:
                places = index * block + lax.broadcasted_iota(jnp.int32, (1, block), 1)
                positions = ((places // rows) * parts + part) * rows + places % rows
                key_places = key_index * block + lax.broadcasted_iota(jnp.int32, (block, block), 0)
                allowed = allowed & (key_places <= positions)
            weights = jnp.where(allowed, jnp.exp2(scores * EXP2_SCALE - r["log"][:, columns]), 0.0)
            weight_grad = jnp.dot(value_rows, grad, preferred_element_type=F32)
            score_grad = (weights * (weight_grad - row_dot)).astype(BF16)
            s["dq_acc"][:, columns] += jnp.dot(keys, score_grad, preferred_element_type=F32)
            return (dk + dot(query, score_grad, 1, 1), dv + dot(grad, weights.astype(BF16), 1, 1))

        zeros = jnp.zeros((HEAD_DIM, block), F32)
        first_index = key_index // parts
        grads = fold(first_index, (zeros, zeros), True)
        dk, dv = lax.fori_loop(
            first_index + 1, mine_total // block, lambda i, g: fold(i, g, False), grads
        )
        r["qkv"][1, :, here] = (dk * SCALE).astype(BF16)
        r["qkv"][2, :, here] = dv.astype(BF16)
        return 0

    lax.fori_loop(0, total // block, key_block, 0)
    if parts == 1:
        r["qkv"][0] = (s["dq_acc"][...] * SCALE).astype(BF16)
        dq_copies = links.collect(r["qkv"].at[0], s["in_small"].at[1])
    else:
        r["qkv"][0] = jnp.zeros((HEAD_DIM, total), BF16)
        for number in range(count // parts):
            value = (s["dq_acc"][:, number * rows : (number + 1) * rows] * SCALE).astype(BF16)
            s["dq_low"][:, number * rows : (number + 1) * rows] = value
            r["qkv"][0, :, pl.ds((number * parts + part) * rows, rows)] = value
        dq_copies = links.collect(s["dq_low"], s["in_small"].at[1])
    unit_copy = links.to_other_core(r["qkv"], s["unit_other"])
    dkv_copies = []
    for offset in range(count):
        peer = me ^ offset
        source = r["qkv"].at[pl.ds(1, 2), :, pl.ds(peer * rows, rows)]
        place = s["dkv_recv"].at[part, :, pl.ds(head * HEAD_DIM, HEAD_DIM), pl.ds(pack * rows, rows)]
        dkv_copies.append(links.to(offset, source, place))
    up.keep_jobs()

    unit_copy.wait()
    first_send, first_recv = links.take(count), links.take(count)
    number_to = count // 2

    def first_copy(index, number, source_device=None):
        target_core = core if index == 0 else 1 - core
        slot = me if source_device is None else source_device
        return pltpu.make_async_remote_copy(
            src_ref=s["first_low"].at[index, pl.ds(number * share, share), :],
            dst_ref=s["first_recv"].at[slot],
            send_sem=links.send_sem.at[first_send + index * number_to + number],
            recv_sem=links.recv_sem.at[first_recv + slot],
            device_id={"blk": core * number_to + number, "tp": target_core},
            device_id_type=MESH,
        )

    for index, ref in enumerate((r["qkv"], s["unit_other"])):
        value, most = None, s["h1"].shape[1]
        for start in range(0, total, most):
            if start + index > 0 and total > most:
                h1_copy = links.local(r["h1_pack"].at[:, pl.ds(start, most)], s["h1"])
            if start + index == 0 or total > most:
                h1_copy.wait()
            term = dot(s["h1"][...], ref[:, :, start : start + most].reshape(3 * HEAD_DIM, most), 1, 1)
            value = term if value is None else value + term
        s["first_low"][index] = value.astype(BF16)
        for number in range(number_to):
            if index == 1:
                first_copy(index, number).start()
                continue
            own = me == core * number_to + number

            @pl.when(jnp.logical_not(own))
            def _(number=number):
                first_copy(0, number).start()

            @pl.when(own)
            def _(number=number):
                pltpu.make_async_copy(
                    s["first_low"].at[0, pl.ds(number * share, share), :],
                    s["first_recv"].at[me],
                    links.recv_sem.at[first_recv + me],
                ).start()

    middle.keep_jobs()

    ready("mem", "w_ck", "w_cv")
    wait_all(memory_copies)
    if parts > 1:
        for kind in range(2):
            value = s["mem_recv"][0, kind].astype(F32)
            for index in range(1, parts):
                value = value + s["mem_recv"][index, kind].astype(F32)
            s["mem_recv"][0, kind] = value.astype(BF16)
    relative(s["rel_mem"], r["mem"])
    weight_job(pages, 0, s["rel_mem"], s["mem_recv"].at[0, 0])
    weight_job(pages, 1, s["rel_mem"], s["mem_recv"].at[0, 1])
    for start in range(0, lay.mem_pad, LANES):
        here = slice(start, start + LANES)
        s["mem_send"][here, :] = (
            dot(s["mem_recv"][0, 0, :, here].T, r["w_ck"][...], 1, 1)
            + dot(s["mem_recv"][0, 1, :, here].T, r["w_cv"][...], 1, 1)
        ).astype(BF16)
    load("w_k")
    load("w_v")
    mem_copies = [
        links.to_other_core(s["mem_send"], memory_other),
        links.local(s["mem_send"], memory_own),
    ]
    down.receive(1)

    ready("w_q", "w_k", "w_v", "x")
    wait_all(dq_copies)
    wait_all(dkv_copies)
    if parts > 1:
        for kind in range(2):
            value = s["dkv_recv"][0, kind].astype(F32)
            for index in range(1, parts):
                value = value + s["dkv_recv"][index, kind].astype(F32)
            s["dkv_recv"][0, kind] = value.astype(BF16)
    pieces = (s["in_small"].at[1], s["dkv_recv"].at[0, 0], s["dkv_recv"].at[0, 1])
    tp_copies = []
    for start in range(0, flat_rows, rows):
        here = slice(start, start + rows)
        s["tp_send"][here, :] = sum(
            dot(value[:, here].T, r[weight][...], 1, 1)
            for value, weight in zip(pieces, ("w_q", "w_k", "w_v"), strict=True)
        ).astype(BF16)
        tp_copies.append(
            links.to_other_core(s["tp_send"].at[pl.ds(start, rows)], s["tp_recv"].at[1, pl.ds(start, rows)])
        )
    middle.receive(1)
    wait_all(tp_copies)
    norm_back_rows(
        grad_input,
        both_cores(1),
        lambda here: r["x"][here, :].astype(F32),
        r["gain_one"],
        lambda here: s["grad_one"][here, :],
    )
    pages.keep_jobs()
    up.receive(1)
    for step in range(2, bits - 2):
        down.receive(step)
        up.receive(step)
    final_copies = []
    for offset in range(group):
        rows_to = pl.ds(lax.rem(me ^ offset, group) * share, share)
        for index, sums in enumerate((s["down_sums"], s["up_sums"])):
            place = s["feed_last"].at[index, lax.rem(me, group)]
            final_copies.append(links.to(offset, sums.at[:, rows_to, :], place))

    for step in range(2, bits + 1):
        pages.receive(step - 1, pages_out if step == bits else None)
        if step < bits:
            middle.receive(step, middle_out if step == bits - 1 else None)
    wait_all(final_copies)
    for index in range(2):
        for number in range(group):
            for kind in range(2):
                start = number * slice_width + kind * slice_width // 2
                feed_out[index, :, start : start + slice_width // 2] = s["feed_last"][
                    index, number, kind
                ].astype(F32)
    for index in range(2):
        for number in range(number_to):
            if index == 1:
                first_copy(index, number).wait_send()
            else:

                @pl.when(me != core * number_to + number)
                def _(number=number):
                    first_copy(0, number).wait_send()

    for device in range(count):
        first_copy(0, 0, device).wait_recv()
    for index in range(lay.heads):
        value = None
        for side in range(2):
            for number in range(parts):
                term = s["first_recv"][side * half + index * parts + number].astype(F32)
                value = term if value is None else value + term
        first_out[index] = value
    wait_all(mem_copies)


def backward(lay, values, hot, ff):
    parts, count, half, rows = lay.parts, lay.count, lay.half, lay.rows
    flat_rows, width = values["dc"].shape
    wide = lay.heads * HEAD_DIM
    total = count * rows
    mine_total = total // parts
    span = lay.pieces * lay.mem_pad
    bits = count.bit_length() - 1
    late = [
        "w_cross_out", "dm_group", "h3_group", "gelu_group", "kv_slots", "cross_unit", "cross_att",
        "cross_mixed", "w_cross_query", "r1", "grad_two", "mixed", "qkv", "mem", "h2", "w_ck", "w_cv",
    ]
    if parts > 1:
        late.append("query")
    late = {name: name for name in late}
    late.update(w_out="w_cross_out", w_q="w_cross_query", w_k="w_ck", w_v="w_cv", att="cross_att", x="h2")
    far = ["h1_pack", "du"]
    early = [name for name in values if name not in late and name not in far]
    names = ["hot"] + early + list(late) + far
    vmem, anywhere = pl.BlockSpec(memory_space=pltpu.VMEM), pl.BlockSpec(memory_space=pl.ANY)

    def buffer(*shape, dtype=BF16):
        return pltpu.VMEM(shape, dtype)

    share = width // count
    scratch = {
        "send_sem": pltpu.SemaphoreType.DMA((9 * count + 128,)),
        "recv_sem": pltpu.SemaphoreType.DMA((9 * count + 128,)),
        "out_small": buffer(2, wide, flat_rows),
        "in_small": buffer(2, wide, flat_rows),
        "doc_unit": buffer(HEAD_DIM, mine_total),
        "do_unit": buffer(HEAD_DIM, mine_total),
        "dq_acc": buffer(HEAD_DIM, mine_total, dtype=F32),
        "dq_low": buffer(HEAD_DIM, mine_total),
        "turn": buffer(width, flat_rows),
        "rel_dm": buffer(width, 4 * flat_rows),
        "rel_h3": buffer(width, 4 * flat_rows),
        "rel_dc": buffer(width, flat_rows),
        "rel_h2": buffer(width, flat_rows),
        "rel_da": buffer(width, flat_rows),
        "rel_mem": buffer(width, lay.mem_pad),
        "feed_last": buffer(2, 4, 2, share, ff // 8),
        "du_group": buffer(4, flat_rows, ff // 4),
        "h1": buffer(wide, min(total, 2048)),
        "cross_key": buffer(span, HEAD_DIM),
        "cross_value": buffer(span, HEAD_DIM),
        "cross_acc": buffer(2, HEAD_DIM, span, dtype=F32),
        "dkv_low": buffer(2, NSEG, 2, HEAD_DIM, span),
        "dkv_twin": buffer(NSEG, 2, HEAD_DIM, span),
        "page_grad": buffer(half, 2, HEAD_DIM, lay.mem_pad),
        "mem_recv": buffer(parts, 2, wide, lay.mem_pad),
        "mem_send": buffer(lay.mem_pad, width),
        "tp_send": buffer(flat_rows, width),
        "tp_recv": buffer(2, flat_rows, width),
        "grad_one": buffer(flat_rows, width, dtype=F32),
        "da": buffer(flat_rows, width),
        "dkv_recv": buffer(parts, 2, wide, flat_rows),
        "unit_other": buffer(3, HEAD_DIM, total),
        "first_low": buffer(2, wide, 3 * HEAD_DIM),
        "first_recv": buffer(count, share, 3 * HEAD_DIM),
    }
    columns = {"down": ff // 8, "up": ff // 8, "middle": 3 * wide // 2, "pages": wide}
    for name, number in columns.items():
        scratch[name + "_sums"] = buffer(2, width // 2, number)
        steps = bits - 2 if name in ("down", "up") else bits
        for index, shape in enumerate(arrivals_shapes(steps, width, number)):
            scratch[f"{name}_{index}"] = shape
    homes = {}
    for name, home in late.items():
        homes.setdefault(home, values[name])
    for home, value in homes.items():
        scratch["in_" + home] = pltpu.VMEM(value.shape, value.dtype)

    return pl.pallas_call(
        functools.partial(backward_body, lay, names, late, list(scratch)),
        out_shape=[
            jax.ShapeDtypeStruct((flat_rows, width), F32),
            jax.ShapeDtypeStruct((lay.mem_pad, width), BF16),
            jax.ShapeDtypeStruct((lay.mem_pad, width), BF16),
            jax.ShapeDtypeStruct((2, share, ff), F32),
            jax.ShapeDtypeStruct((2, share, columns["middle"]), F32),
            jax.ShapeDtypeStruct((2, share, columns["pages"]), F32),
            jax.ShapeDtypeStruct((lay.heads, share, 3 * HEAD_DIM), F32),
        ],
        in_specs=[pl.BlockSpec(memory_space=pltpu.SMEM)] + [vmem] * len(early) + [anywhere] * (len(late) + len(far)),
        out_specs=[vmem, anywhere, anywhere, vmem, vmem, vmem, vmem],
        scratch_shapes=list(scratch.values()),
        compiler_params=pltpu.CompilerParams(
            collective_id=1, has_side_effects=True, vmem_limit_bytes=63 * 1024 * 1024
        ),
    )(hot, *[values[name] for name in early + list(late) + far])


def local(
    tokens,
    memory,
    segment_ids,
    token_valid,
    segment_page,
    gain_one,
    weight_query,
    weight_key,
    weight_value,
    weight_out,
    gain_two,
    cross_query,
    cross_key,
    cross_value,
    cross_out,
    gain_three,
    weight_up,
    weight_down,
    cotangent,
):
    packs, rows, width = tokens.shape
    wide, ff = weight_query.shape[1], weight_up.shape[1]
    count, place = lax.axis_size("blk"), lax.axis_index("blk")
    lay = Layout(count, packs, wide // HEAD_DIM, rows, memory.shape[0])
    flat_rows, share = packs * rows, width // count
    pack = place // lay.half

    first_page = pack * lay.pages_half
    wanted = jnp.stack(
        [lax.dynamic_index_in_dim(segment_page, p, 0, keepdims=False) for p in (pack, 1 - pack)]
    )
    here = ((wanted >= first_page) & (wanted < first_page + lay.pages_half)).astype(F32)
    pages = jnp.clip(wanted - first_page, 0, lay.pages_half - 1)
    hot = (wanted[:, :, None] == first_page + jnp.arange(lay.pages_half, dtype=jnp.int32)).astype(F32)

    x = tokens.reshape(flat_rows, width)
    mem = jnp.pad(memory, ((0, lay.mem_pad - lay.mem_rows), (0, 0)))
    codes = (segment_ids * 2 + token_valid).astype(F32)
    kept = forward(
        lay,
        {
            "pages": pages,
            "here": here,
            "x": x,
            "codes": jnp.broadcast_to(codes[:, None, :], (packs, 8, rows)),
            "gain_one": gain_one[None],
            "gain_two": gain_two[None],
            "gain_three": gain_three[None],
            "w_q": weight_query,
            "w_k": weight_key,
            "w_v": weight_value,
            "mem": mem,
            "w_ck": cross_key,
            "w_cv": cross_value,
            "cot": cotangent.reshape(flat_rows, width),
            "w_out": weight_out,
            "w_cross_query": cross_query,
            "w_cross_out": cross_out,
            "w_up": weight_up,
            "w_down": weight_down,
        },
        ff,
    )
    out = kept.pop("out").reshape(packs, rows, width)
    grad_input, memory_own, memory_other, feed, middle, pages_grad, first = backward(
        lay,
        {
            **kept,
            "x": x,
            "gain_one": gain_one[None],
            "gain_two": gain_two[None],
            "mem": mem,
            "w_cross_out": cross_out,
            "w_cross_query": cross_query,
            "w_out": weight_out,
            "w_ck": cross_key,
            "w_cv": cross_value,
            "w_q": weight_query,
            "w_k": weight_key,
            "w_v": weight_value,
        },
        hot,
        ff,
    )
    grad_memory = (memory_own.astype(F32) + memory_other.astype(F32))[: lay.mem_rows]
    grad_down, grad_up = feed[0].T, feed[1]

    def columns_of(value, index):
        return jnp.concatenate(
            [value[kind, :, index * wide // 2 : (index + 1) * wide // 2] for kind in range(2)], axis=1
        )

    grad_cross_out, grad_cross_query, grad_out = [columns_of(middle, i) for i in range(3)]
    grad_cross_key, grad_cross_value = [columns_of(pages_grad, i) for i in range(2)]
    first = first.reshape(lay.heads, share, 3, HEAD_DIM).transpose(2, 1, 0, 3).reshape(3, share, wide)

    def own_rows(weight):
        return lax.dynamic_slice_in_dim(weight, place * share, share, 0).astype(F32)

    sums = jnp.stack(
        [
            sum(
                jnp.sum(own_rows(weight) * first[i], axis=1)
                for i, weight in enumerate((weight_query, weight_key, weight_value))
            ),
            jnp.sum(own_rows(cross_query) * grad_cross_query, axis=1),
            jnp.sum(own_rows(weight_up) * grad_up, axis=1),
        ]
    )
    gains = jnp.stack(
        [lax.dynamic_slice_in_dim(gain, place * share, share) for gain in (gain_one, gain_two, gain_three)]
    )
    gain_grads = (sums + lax.ppermute(sums, "tp", [(0, 1), (1, 0)])) / gains
    return (
        out,
        grad_input.reshape(packs, rows, width),
        grad_memory,
        first[0],
        first[1],
        first[2],
        grad_out.T,
        grad_cross_query,
        grad_cross_key,
        grad_cross_value,
        grad_cross_out.T,
        grad_up,
        grad_down,
        gain_grads[0],
        gain_grads[1],
        gain_grads[2],
    )


def solution(mesh):
    in_specs = (
        P(None, "blk", None),
        P("blk", None),
        P(None, "blk"),
        P(None, "blk"),
        P(),
        P(),
        P(None, "tp"),
        P(None, "tp"),
        P(None, "tp"),
        P("tp", None),
        P(),
        P(None, "tp"),
        P(None, "tp"),
        P(None, "tp"),
        P("tp", None),
        P(),
        P(None, "tp"),
        P("tp", None),
        P(None, "blk", None),
    )
    out_specs = (
        P(None, "blk", None),
        P(None, "blk", None),
        P("blk", None),
        P("blk", "tp"),
        P("blk", "tp"),
        P("blk", "tp"),
        P("tp", "blk"),
        P("blk", "tp"),
        P("blk", "tp"),
        P("blk", "tp"),
        P("tp", "blk"),
        P("blk", "tp"),
        P("tp", "blk"),
        P("blk"),
        P("blk"),
        P("blk"),
    )
    return jax.shard_map(local, mesh=mesh, in_specs=in_specs, out_specs=out_specs, check_vma=False)
```

```python
import functools

import jax
import jax.numpy as jnp
from jax import lax
from jax.experimental import pallas as pl
from jax.experimental.pallas import tpu as pltpu
from jax.sharding import PartitionSpec as P

MEM_LEN = 588
HEAD_DIM = 64
NSEG = 3
EPS = 1e-05
NEG = -1e30
EXP2_SCALE = HEAD_DIM**-0.5 * 1.4426950408889634
SCALE = HEAD_DIM**-0.5
LANES = 128
BF16 = jnp.bfloat16
F32 = jnp.float32
MESH = pl.DeviceIdType.MESH


def dot(left, right, contract_left, contract_right):
    return lax.dot_general(
        left, right, (((contract_left,), (contract_right,)), ((), ())), preferred_element_type=F32
    )


def wait_all(copies):
    for copy in copies:
        copy.wait()


class Layout:
    def __init__(self, count, packs, heads, rows, mem_rows):
        self.count, self.packs, self.heads, self.rows = count, packs, heads, rows
        self.half = count // packs
        self.parts = self.half // heads
        self.mem_rows = mem_rows
        self.mem_pad = -(-mem_rows // LANES) * LANES
        self.pieces = MEM_LEN // mem_rows
        self.pages_half = self.half // self.pieces

    def head(self, device):
        return lax.rem(device, self.half) // self.parts


def page_rows(span, piece, real):
    places = lax.broadcasted_iota(jnp.int32, (span, 1), 0)
    return lax.rem(places, piece) < real


def erf(value):
    x = jnp.clip(value, -3.832506856900711, 3.832506856900711)
    square = x * x
    top = jnp.float32(0.00022905065861350646)
    for coefficient in (0.0034082910107109506, 0.050955695062380861, 0.18520832239976145, 1.128379143519084):
        top = top * square + coefficient
    low = jnp.float32(-1.1791602954361697e-7)
    for coefficient in (
        0.000023547966471313185,
        0.0010179625278914885,
        0.014070470171167667,
        0.11098505178285362,
        0.49746925110067538,
        1.0,
    ):
        low = low * square + coefficient
    return x * top / low


def normed_rows(source, gain, low):
    step = 32

    def body(index, _):
        rows = pl.ds(pl.multiple_of(index * step, step), step)
        value = source(rows)
        centred = value - jnp.mean(value, axis=1, keepdims=True)
        inv_std = lax.rsqrt(jnp.mean(centred * centred, axis=1, keepdims=True) + EPS)
        low[rows, :] = (centred * inv_std * gain[...]).astype(BF16)
        return 0

    lax.fori_loop(0, low.shape[0] // step, body, 0)


def norm_back_rows(target, grad, source, gain, residual, low=None):
    step = 32

    def body(index, _):
        rows = pl.ds(pl.multiple_of(index * step, step), step)
        value = source(rows)
        centred = value - jnp.mean(value, axis=1, keepdims=True)
        inv_std = lax.rsqrt(jnp.mean(centred * centred, axis=1, keepdims=True) + EPS)
        z = centred * inv_std
        w = grad(rows) * gain[...]
        inner = w - jnp.mean(w, axis=1, keepdims=True) - z * jnp.mean(w * z, axis=1, keepdims=True)
        value = residual(rows) + inner * inv_std
        target[rows, :] = value
        if low is not None:
            low[rows, :] = value.astype(BF16)
        return 0

    lax.fori_loop(0, target.shape[0] // step, body, 0)


class Links:
    def __init__(self, lay, scratch):
        self.lay = lay
        self.me, self.core = lax.axis_index("blk"), lax.axis_index("tp")
        self.head, self.pack = lay.head(self.me), self.me // lay.half
        self.part = lax.rem(self.me, lay.parts)
        self.send_sem, self.recv_sem, self.used = scratch["send_sem"], scratch["recv_sem"], 0
        self.barrier = pltpu.get_barrier_semaphore()

    def announce(self, everyone=False):
        for offset in range(self.lay.count):
            if offset > 0:
                self.signal(offset, self.core)
            if offset == 0 or everyone:
                self.signal(offset, 1 - self.core)

    def signal(self, offset, core):
        device = {"blk": self.me ^ offset, "tp": core}
        pl.semaphore_signal(self.barrier, inc=1, device_id=device, device_id_type=MESH)

    def all_here(self, everyone=False):
        pl.semaphore_wait(self.barrier, (2 if everyone else 1) * self.lay.count - (1 if everyone else 0))

    def take(self, number=1):
        index, self.used = self.used, self.used + number
        return index

    def described(self, index, source, target, device):
        return pltpu.make_async_remote_copy(
            src_ref=source,
            dst_ref=target,
            send_sem=self.send_sem.at[index],
            recv_sem=self.recv_sem.at[index],
            device_id=device,
            device_id_type=MESH,
        )

    def remote(self, source, target, device):
        copy = self.described(self.take(), source, target, device)
        copy.start()
        return copy

    def local(self, source, target):
        copy = pltpu.make_async_copy(source, target, self.send_sem.at[self.take()])
        copy.start()
        return copy

    def to(self, offset, source, target):
        if offset == 0:
            return self.local(source, target)
        return self.remote(source, target, {"blk": self.me ^ offset})

    def to_other_core(self, source, target):
        return self.remote(source, target, {"tp": 1 - self.core})

    def spread(self, source, target, every=False):
        lay, step = self.lay, 1 if every else self.lay.parts
        started = []
        for offset in range(0, lay.count, step):
            peer = self.me ^ offset
            piece = source.at[
                pl.ds(lay.head(peer) * HEAD_DIM, HEAD_DIM), pl.ds((peer // lay.half) * lay.rows, lay.rows)
            ]
            started.append(self.to(offset, piece, target.at[:, pl.ds((self.me // step) * lay.rows, lay.rows)]))
        return started

    def unit_place(self, target):
        lay = self.lay
        return target.at[pl.ds(self.head * HEAD_DIM, HEAD_DIM), pl.ds(self.pack * lay.rows, lay.rows)]

    def collect(self, source, target):
        lay, started = self.lay, []
        for offset in range(0, lay.count, lay.parts):
            peer = self.me ^ offset
            piece = source.at[:, pl.ds((peer // lay.parts) * lay.rows, lay.rows)]
            started.append(self.to(offset, piece, self.unit_place(target)))
        return started

    def collect_later(self, source, target):
        lay = self.lay
        first = self.take(lay.count // lay.parts)

        def send(number):
            peer = number * lay.parts + self.part
            piece, place = source.at[:, pl.ds(number * lay.rows, lay.rows)], self.unit_place(target)

            @pl.when(peer != self.me)
            def _():
                index = first + (peer ^ self.me) // lay.parts
                self.described(index, piece, place, {"blk": peer}).start()

            @pl.when(peer == self.me)
            def _():
                pltpu.make_async_copy(piece, place, self.send_sem.at[first]).start()

        def wait():
            piece = source.at[:, pl.ds(0, lay.rows)]
            for offset in range(0, lay.count, lay.parts):
                peer = self.me ^ offset
                index = first + offset // lay.parts
                if offset == 0:
                    pltpu.make_async_copy(piece, self.unit_place(target), self.send_sem.at[index]).wait()
                else:
                    self.described(index, piece, self.unit_place(target), {"blk": peer}).wait()

        return send, wait


HALVES = ("keys_half", "values_half")


def forward_body(lay, names, late, out_names, scratch_names, *refs):
    r = dict(zip(names, refs, strict=False))
    o = dict(zip(out_names, refs[len(names) :], strict=False))
    s = dict(zip(scratch_names, refs[len(names) + len(out_names) :], strict=True))
    count, parts, half, rows = lay.count, lay.parts, lay.half, lay.rows
    links = Links(lay, s)
    me, core = links.me, links.core
    links.announce()
    flat_rows, width = r["x"].shape
    wide, ff = s["w_out"].shape[0], r["w_up"].shape[1]
    total = count * rows
    mine_total = total // parts
    loading = {name: links.local(r[name], s[name]) for name in late}
    leaving = []

    def page_of(side, slot):
        place = r["segment_page"][links.pack if side == 0 else 1 - links.pack, slot] - (
            links.pack * lay.pages_half
        )
        inside = (place >= 0) & (place < lay.pages_half)
        return jnp.clip(place, 0, lay.pages_half - 1), jnp.where(inside, 1.0, 0.0)

    codes = (r["segment_ids"][...] * 2 + r["token_valid"][...]).astype(F32)
    for pack in range(lay.packs):
        s["code_tok"][pack] = jnp.broadcast_to(codes[pack : pack + 1, :], (8, rows))

    def ready(*wanted):
        for name in wanted:
            loading[name].wait()

    def emit(*wanted):
        for name in wanted:
            leaving.append(links.local(s[name], o[name]))

    half_rows = pl.ds(pl.multiple_of(core * wide, wide), wide)
    normed_rows(lambda here: r["x"][here, :].astype(F32), r["gain_one"], s["h1"])
    s["h1_turned"][...] = s["h1"][:, half_rows].T
    other, group = me ^ half, 4
    s["mem"][lay.mem_rows // 16 * 16 :, :] = jnp.zeros_like(s["mem"][lay.mem_rows // 16 * 16 :, :])
    s["mem"][: lay.mem_rows, :] = r["memory"][...]
    emit("mem")
    ready("w_ck", "w_cv")
    for index, name in enumerate(("w_ck", "w_cv")):
        s["kv_tok"][index] = dot(s["mem"][...], s[name][...], 1, 0).astype(BF16).T
    links.all_here()

    def pack_chunk(owner, first=0, size=wide):
        here = pl.ds(pl.multiple_of(core * wide, wide) + first, size)
        return s["h1_all"].at[here, pl.ds(pl.multiple_of(owner * rows, rows), rows)]

    hand_over = links.remote(
        s["h1_turned"].at[:, pl.ds((1 - links.pack) * rows, rows)], pack_chunk(me), {"blk": other}
    )
    links.local(s["h1_turned"].at[:, pl.ds(links.pack * rows, rows)], pack_chunk(me)).wait()
    ways = half.bit_length() - 1
    shares = [16 * (wide // 16 // ways + (way < wide // 16 % ways)) for way in range(ways)]

    def double(step, owners):
        started = []
        for way in range(ways):
            first, order = sum(shares[:way]), [(way + turn) % ways for turn in range(step + 1)]
            held = [0]
            for bit in order[:-1]:
                held += [offset ^ (1 << bit) for offset in held]
            for owner in owners:
                for offset in held:
                    piece = pack_chunk(owner ^ offset, first, shares[way])
                    started.append(links.to(1 << order[-1], piece, piece))
        return started

    near_copies = double(0, [me])

    def memory_part(kind):
        started = []
        for offset in range(half):
            piece = s["kv_tok"].at[kind, pl.ds(lay.head(me ^ offset) * HEAD_DIM, HEAD_DIM), :]
            started.append(links.to(offset, piece, s[HALVES[kind]].at[lax.rem(me, half)]))
        return started

    memory_copies = [memory_part(0)]

    def find_pages(kind):
        wait_all(memory_copies[kind])
        for side in range(2):
            for slot in range(NSEG):
                page, here = page_of(side, slot)
                for piece in range(lay.pieces):
                    value = s[HALVES[kind]][page * lay.pieces + piece].astype(F32) * here
                    columns = slice(piece * lay.mem_pad, (piece + 1) * lay.mem_pad)
                    s["kv_found"][kind, side, slot, :, columns] = value.astype(BF16)
        twin_copies.append(
            links.remote(s["kv_found"].at[kind, 1], s["kv_twin"].at[kind], {"blk": other})
        )

    twin_copies = []
    code_copies = []
    for offset in range(count):
        peer = me ^ offset
        code_copies.append(
            links.to(offset, s["code_tok"].at[peer // half], s["codes"].at[:, pl.ds(me * rows, rows)])
        )
    hand_over.wait()
    near_copies += double(0, [other])

    for index, name in enumerate(("w_q", "w_k", "w_v")):
        ready(name)
        s["turn"][...] = s[name][...].T
        s["w_unit"][index * HEAD_DIM : (index + 1) * HEAD_DIM, :] = s["turn"][
            pl.ds(pl.multiple_of(links.head * HEAD_DIM, HEAD_DIM), HEAD_DIM), :
        ]

    wait_all(near_copies)
    find_pages(0)
    for step in range(1, ways):
        wait_all(double(step, [me, other]))
    core_copy = links.to_other_core(s["h1_all"].at[half_rows, :], s["h1_all"].at[half_rows, :])
    memory_copies.append(memory_part(1))
    core_copy.wait()
    pack_copy = links.local(s["h1_all"].at[half_rows, :], o["h1_pack"])
    for start in range(0, total, 512):
        columns = slice(start, start + 512)
        value = dot(s["w_unit"][...], s["h1_all"][:, columns], 1, 0).astype(BF16)
        for index in range(3):
            s["qkv"][index, :, columns] = value[index * HEAD_DIM : (index + 1) * HEAD_DIM, :]

    wait_all(code_copies)
    codes = s["codes"][:1, :]
    segments = jnp.floor(codes * 0.5)
    s["code"][...] = jnp.where(codes - 2.0 * segments > 0.5, segments, -1.0)
    lengths = [
        jnp.sum((segments == float(slot)).astype(F32), axis=1, keepdims=True) for slot in range(NSEG)
    ]
    first_longest = ((lengths[0] >= lengths[1]) & (lengths[0] >= lengths[2])).astype(F32)
    second_longest = (lengths[1] >= lengths[2]).astype(F32) * (1.0 - first_longest)
    longest = 2.0 - 2.0 * first_longest - second_longest
    order = segments - longest
    order = jnp.where(order < 0.0, order + float(NSEG), order)
    if parts == 1:
        s["qseg"][...], s["qslot"][...] = segments, order
    else:
        s["rows"][0:1, :], s["rows"][1:2, :] = segments, order
        for piece in range(count // parts):
            there = pl.ds((piece * parts + links.part) * rows, rows)
            s["qseg"][:, piece * rows : (piece + 1) * rows] = s["rows"][0:1, there]
            s["qslot"][:, piece * rows : (piece + 1) * rows] = s["rows"][1:2, there]
            s["query"][:, piece * rows : (piece + 1) * rows] = s["qkv"][0, :, there]
    s["longest"][...] = jnp.broadcast_to(longest, s["longest"].shape)
    emit("qkv", "code", "qseg", "qslot", "longest")
    if parts > 1:
        emit("query")

    block = min(512 if parts == 1 else 256, mine_total)
    s["key"][...] = s["qkv"][1].T
    send_mixed, wait_mixed = links.collect_later(s["low"].at[0], s["mixed"])
    for index in reversed(range(mine_total // block)):
        columns = slice(index * block, (index + 1) * block)
        query = s["query"][:, columns] if parts > 1 else s["qkv"][0, :, columns]
        mine = s["qseg"][:, columns]
        places = index * block + lax.broadcasted_iota(jnp.int32, (1, block), 1)
        positions = ((places // rows) * parts + links.part) * rows + places % rows

        def fold(key_index, state, causal, query=query, mine=mine, positions=positions):
            largest, weight_sum, weighted = state
            start = pl.multiple_of(key_index * block, block)
            here = pl.ds(start, block)
            scores = jnp.dot(s["key"][here, :], query, preferred_element_type=F32)
            allowed = jnp.broadcast_to(s["code"][:, here], (8, block)).T[:, :1] == mine
            if causal:
                key_places = start + lax.broadcasted_iota(jnp.int32, (block, block), 0)
                allowed = allowed & (key_places <= positions)
            scores = jnp.where(allowed, scores, NEG)
            new = jnp.maximum(largest, jnp.max(scores, axis=0, keepdims=True))
            weights = jnp.exp2((scores - new) * EXP2_SCALE)
            keep = jnp.exp2((largest - new) * EXP2_SCALE)
            weight_sum = weight_sum * keep + jnp.sum(weights, axis=0, keepdims=True)
            update = jnp.dot(s["qkv"][2, :, here], weights.astype(BF16), preferred_element_type=F32)
            return (new, weight_sum, weighted * keep + update)

        state = (
            jnp.full((1, block), NEG, F32),
            jnp.zeros((1, block), F32),
            jnp.zeros((HEAD_DIM, block), F32),
        )
        state = lax.fori_loop(0, index * parts, lambda j, c, fold=fold: fold(j, c, False), state)
        for extra in range(parts):
            state = fold(index * parts + extra, state, True)
        largest, weight_sum, weighted = state
        result = weighted / weight_sum
        s["att"][:, columns] = result
        s["low"][0, :, columns] = result.astype(BF16)
        s["log"][:, columns] = largest * EXP2_SCALE + jnp.log2(weight_sum)
        for piece in range(index * block // rows, (index + 1) * block // rows):
            send_mixed(piece)
    emit("att", "log")
    pack_copy.wait()
    w_up = s["h1_all"].at[:, pl.ds(0, ff)]
    up_load = links.local(r["w_up"], w_up)

    def product_rows(left, right, sent, arrived):
        started = []
        for start in range(0, flat_rows, rows):
            here = slice(start, start + rows)
            sent[here, :] = dot(left[:, here].T, right[...], 1, 0).astype(BF16)
            started.append(links.to_other_core(sent.at[pl.ds(start, rows)], arrived.at[pl.ds(start, rows)]))
        return started

    def to_group(source, target):
        started = [links.local(source, target.at[0])]
        for offset in range(1, group):
            started.append(links.to(offset, source.at[:, half_rows], target.at[offset, :, half_rows]))
        return started

    def group_to_other_core(target):
        others = target.at[pl.ds(1, group - 1), :, half_rows]
        return links.to_other_core(others, others)

    def both(sent, arrived):
        return lambda here: sent[here, :].astype(F32) + arrived[here, :].astype(F32)

    def add_rows(target, *terms):
        step = 32

        def body(index, _):
            here = pl.ds(pl.multiple_of(index * step, step), step)
            target[here, :] = sum(term(here) for term in terms).astype(target.dtype)
            return 0

        lax.fori_loop(0, flat_rows // step, body, 0)

    find_pages(1)
    ready("w_out")
    wait_mixed()
    emit("mixed")
    started = product_rows(s["mixed"], s["w_out"], s["sent"].at[0], s["arrived"].at[0])
    wait_all(started)
    add_rows(
        s["r1"], lambda here: r["x"][here, :].astype(F32), both(s["sent"].at[0], s["arrived"].at[0])
    )
    normed_rows(lambda here: s["r1"][here, :], r["gain_two"], s["h2"])
    ready("w_cross_query")
    s["tok"][0] = dot(s["h2"][...], s["w_cross_query"][...], 1, 0).astype(BF16).T
    query_copies = links.spread(s["tok"].at[0], s["cross_unit"])
    ready("cot")
    cot_copies = to_group(s["cot"], o["dm_group"])
    emit("r1", "h2")

    wait_all(twin_copies)
    is_first = (s["longest"][:1, :1] < 0.5).astype(F32)
    is_second = (s["longest"][:1, :1] < 1.5).astype(F32) - is_first
    is_third = 1.0 - is_first - is_second
    for kind in range(2):
        found = [
            s["kv_found"][kind, 0, slot].astype(F32)
            + s["kv_twin"][kind, slot].astype(F32) * (1.0 - page_of(0, slot)[1])
            for slot in range(NSEG)
        ]
        for slot in range(NSEG):
            value = (
                found[slot] * is_first
                + found[(slot + 1) % NSEG] * is_second
                + found[(slot + 2) % NSEG] * is_third
            )
            s["kv_slots"][slot, kind] = value.astype(BF16)
    emit("kv_slots")

    narrow = min(256, mine_total)
    present = page_rows(lay.pieces * lay.mem_pad, lay.mem_pad, lay.mem_rows)
    key_rows = [s["kv_slots"][slot, 0].T for slot in range(NSEG)]
    send_cross, wait_cross = links.collect_later(s["low"].at[1], s["cross_mixed"])
    wait_all(query_copies)
    emit("cross_unit")

    def attend(columns, slot):
        scores = jnp.dot(key_rows[slot], s["cross_unit"][:, columns], preferred_element_type=F32)
        scores = jnp.where(present, scores, NEG)
        largest = jnp.max(scores, axis=0, keepdims=True)
        weights = jnp.exp2((scores - largest) * EXP2_SCALE)
        weight_sum = jnp.sum(weights, axis=0, keepdims=True)
        result = jnp.dot(s["kv_slots"][slot, 1], weights.astype(BF16), preferred_element_type=F32)
        return result / weight_sum, largest * EXP2_SCALE + jnp.log2(weight_sum)

    for index in range(mine_total // narrow):
        columns = slice(index * narrow, (index + 1) * narrow)
        s["cross_att"][:, columns], s["cross_log"][:, columns] = attend(columns, 0)
        ends = [0] if index == 0 else []
        ends += [mine_total - LANES] if index == mine_total // narrow - 1 else []
        for start in ends:
            columns = slice(start, start + LANES)
            for slot in range(1, NSEG):
                result, logs = attend(columns, slot)
                here = s["qslot"][:, columns] == float(slot)
                s["cross_att"][:, columns] = jnp.where(here, result, s["cross_att"][:, columns])
                s["cross_log"][:, columns] = jnp.where(here, logs, s["cross_log"][:, columns])
        columns = slice(index * narrow, (index + 1) * narrow)
        s["low"][1, :, columns] = s["cross_att"][:, columns].astype(BF16)
        for piece in range(index * narrow // rows, (index + 1) * narrow // rows):
            send_cross(piece)
    emit("cross_att", "cross_log")
    ready("w_cross_out")
    wait_cross()
    emit("cross_mixed")
    started = product_rows(s["cross_mixed"], s["w_cross_out"], s["sent"].at[1], s["arrived"].at[1])
    wait_all(started)
    add_rows(s["r2"], lambda here: s["r1"][here, :], both(s["sent"].at[1], s["arrived"].at[1]))
    normed_rows(lambda here: s["r2"][here, :], r["gain_three"], s["h1"])
    h3_copies = to_group(s["h1"], o["h3_group"])

    ready("w_down")
    up_load.wait()
    slice_width = ff // group
    s["down_sum"][...] = jnp.zeros_like(s["down_sum"])
    s["up_sum"][...] = jnp.zeros_like(s["up_sum"])
    piece_rows = LANES
    for number in range(group):
        columns = slice(number * slice_width, (number + 1) * slice_width)
        for start in range(0, flat_rows, piece_rows):
            here = slice(start, start + piece_rows)
            u = dot(s["h1"][here, :], w_up[:, columns], 1, 0)
            grad = dot(s["cot"][here, :], s["w_down"][columns, :], 1, 1)
            normal = 0.5 + 0.5 * erf(u * 0.7071067811865476)
            s["gelu"][here, columns] = (u * normal).astype(BF16)
            slope = normal + u * jnp.exp2(u * u * -0.7213475204444817) * 0.3989422804014327
            s["du"][here, columns] = (slope * grad).astype(BF16)
        s["down_sum"][...] += dot(s["gelu"][:, columns], s["w_down"][columns, :], 1, 0)
        s["up_sum"][...] += dot(s["du"][:, columns], w_up[:, columns], 1, 1)
    emit("gelu", "du")
    s["sent"][2] = s["up_sum"][...].astype(BF16)
    up_copy = links.to_other_core(s["sent"].at[2], s["arrived"].at[2])
    s["sent"][3] = s["down_sum"][...].astype(BF16)
    down_copy = links.to_other_core(s["sent"].at[3], s["arrived"].at[3])
    up_copy.wait()
    norm_back_rows(
        s["grad_two"],
        both(s["sent"].at[2], s["arrived"].at[2]),
        lambda here: s["r2"][here, :],
        r["gain_three"],
        lambda here: s["cot"][here, :].astype(F32),
        s["dc"],
    )
    s["tok"][0] = dot(s["w_cross_out"][...], s["dc"][...], 1, 1).astype(BF16)
    doc_copies = links.spread(s["tok"].at[0], s["doc_unit"])
    emit("grad_two", "dc")
    wait_all(cot_copies)
    wait_all(h3_copies)
    group_copies = [group_to_other_core(o["dm_group"]), group_to_other_core(o["h3_group"])]
    down_copy.wait()
    add_rows(s["sent"].at[3], lambda here: s["r2"][here, :], both(s["sent"].at[3], s["arrived"].at[3]))
    leaving.append(links.local(s["sent"].at[3], o["out"]))
    wait_all(doc_copies)
    emit("doc_unit")
    wait_all(group_copies)
    wait_all(leaving)


def forward(lay, values, ff):
    parts, count, half, rows = lay.parts, lay.count, lay.half, lay.rows
    flat_rows, width = values["x"].shape
    wide, total = lay.heads * HEAD_DIM, lay.count * lay.rows
    mine_total = total // parts
    span = lay.pieces * lay.mem_pad
    early = ["x", "segment_ids", "token_valid", "memory", "gain_one", "gain_two", "gain_three"]
    late = [name for name in values if name not in early + ["segment_page", "w_up"]]
    names = ["segment_page"] + early + late + ["w_up"]

    def shape(*dims, dtype=BF16):
        return jax.ShapeDtypeStruct(dims, dtype)

    kept = {
        "qkv": shape(3, HEAD_DIM, total),
        "code": shape(1, total, dtype=F32),
        "qseg": shape(1, mine_total, dtype=F32),
        "qslot": shape(1, mine_total, dtype=F32),
        "longest": shape(8, LANES, dtype=F32),
        "att": shape(HEAD_DIM, mine_total, dtype=F32),
        "log": shape(1, mine_total, dtype=F32),
        "mixed": shape(wide, flat_rows),
        "r1": shape(flat_rows, width, dtype=F32),
        "h2": shape(flat_rows, width),
        "cross_unit": shape(HEAD_DIM, mine_total),
        "kv_slots": shape(NSEG, 2, HEAD_DIM, span),
        "cross_att": shape(HEAD_DIM, mine_total, dtype=F32),
        "cross_log": shape(1, mine_total, dtype=F32),
        "cross_mixed": shape(wide, flat_rows),
        "grad_two": shape(flat_rows, width, dtype=F32),
        "dc": shape(flat_rows, width),
        "doc_unit": shape(HEAD_DIM, mine_total),
        "mem": shape(lay.mem_pad, width),
        "gelu": shape(flat_rows, ff),
        "du": shape(flat_rows, ff),
    }
    if parts > 1:
        kept["query"] = shape(HEAD_DIM, mine_total)
    gathered = {
        "dm_group": shape(4, flat_rows, width),
        "h3_group": shape(4, flat_rows, width),
        "out": shape(flat_rows, width),
        "h1_pack": shape(wide, total),
    }
    scratch = {
        "h1": shape(flat_rows, width),
        "h1_all": shape(width, total),
        "turn": shape(wide, width),
        "w_unit": shape(3 * HEAD_DIM, width),
        "tok": shape(1, wide, flat_rows),
        "codes": shape(8, total, dtype=F32),
        "code_tok": shape(lay.packs, 8, rows, dtype=F32),
        "kv_tok": shape(2, wide, lay.mem_pad),
        "keys_half": shape(half, HEAD_DIM, lay.mem_pad),
        "values_half": shape(half, HEAD_DIM, lay.mem_pad),
        "kv_found": shape(2, 2, NSEG, HEAD_DIM, span),
        "kv_twin": shape(2, NSEG, HEAD_DIM, span),
        "key": shape(total, HEAD_DIM),
        "low": shape(2, HEAD_DIM, mine_total),
        "h1_turned": shape(wide, flat_rows),
        "sent": shape(4, flat_rows, width),
        "arrived": shape(4, flat_rows, width),
        "r2": shape(flat_rows, width, dtype=F32),
        "down_sum": shape(flat_rows, width, dtype=F32),
        "up_sum": shape(flat_rows, width, dtype=F32),
    }
    if parts > 1:
        scratch["rows"] = shape(8, total, dtype=F32)
    scratch = {name: pltpu.VMEM(value.shape, value.dtype) for name, value in {**scratch, **kept}.items()}
    for name in late:
        scratch[name] = pltpu.VMEM(values[name].shape, values[name].dtype)
    semaphores = pltpu.SemaphoreType.DMA((10 * count + 128,))
    scratch = {"send_sem": semaphores, "recv_sem": semaphores, **scratch}
    outs = {**kept, **gathered}
    anywhere = pl.BlockSpec(memory_space=pl.ANY)
    results = pl.pallas_call(
        functools.partial(forward_body, lay, names, late, list(outs), list(scratch)),
        out_shape=list(outs.values()),
        in_specs=[pl.BlockSpec(memory_space=pltpu.SMEM)]
        + [pl.BlockSpec(memory_space=pltpu.VMEM)] * len(early)
        + [anywhere] * (len(late) + 1),
        out_specs=[anywhere] * len(outs),
        scratch_shapes=list(scratch.values()),
        compiler_params=pltpu.CompilerParams(
            collective_id=0, has_side_effects=True, vmem_limit_bytes=63 * 1024 * 1024
        ),
    )(*[values[name] for name in names])
    return dict(zip(outs, results, strict=True))


def reversed_bits(value, bits):
    return sum(((value >> b) & 1) << (bits - 1 - b) for b in range(bits))


class Halving:
    def __init__(self, links, bits, sums, arrivals, crossed=True):
        self.links, self.bits, self.crossed = links, bits, crossed
        self.sums, self.arrivals = sums, arrivals
        self.quarter = sums.shape[1] // 2
        self.jobs, self.pending = [], []

    def neighbour(self, kind, step):
        bit = self.bits[1 - step if self.crosses(kind) and step < 2 else step]
        return {"blk": self.links.me ^ (1 << bit)}

    def crosses(self, kind):
        return kind == 1 and self.crossed

    def add_job(self, column, width, make):
        here, started = pl.ds(column, width), []
        for kind in range(2):
            for half, quarter in enumerate((1, 3) if self.crosses(kind) else (2, 3)):
                rows = pl.ds(half * self.quarter, self.quarter)
                self.sums[kind, rows, here] = make(kind, quarter).astype(BF16)
            started.append(
                self.links.remote(
                    self.sums.at[kind, :, here],
                    self.arrivals[0].at[kind, :, here],
                    self.neighbour(kind, 0),
                )
            )
        self.jobs.append((here, make, started))

    def keep_jobs(self):
        for here, make, started in self.jobs:
            wait_all(started)
            for kind in range(2):
                for half, quarter in enumerate((0, 2) if self.crosses(kind) else (0, 1)):
                    rows = pl.ds(half * self.quarter, self.quarter)
                    arrived = self.arrivals[0][kind, rows, here].astype(F32)
                    self.sums[kind, rows, here] = (make(kind, quarter) + arrived).astype(BF16)
        self.send(1)

    def send(self, step):
        rows = self.sums.shape[1] >> step
        self.pending = [
            self.links.remote(
                self.sums.at[kind, pl.ds(rows, rows), :],
                self.arrivals[step].at[kind],
                self.neighbour(kind, step),
            )
            for kind in range(2)
        ]

    def receive(self, step, result=None):
        rows = self.sums.shape[1] >> step
        wait_all(self.pending)
        size = min(rows, 32)

        def add(index, _):
            here = pl.ds(pl.multiple_of(index * size, size), size)
            for kind in range(2):
                mine = self.sums[kind, here, :].astype(F32)
                total = mine + self.arrivals[step][kind, here, :].astype(F32)
                if result is None:
                    self.sums[kind, here, :] = total.astype(BF16)
                else:
                    result[kind, here, :] = total
            return 0

        lax.fori_loop(0, rows // size, add, 0)
        if step + 1 < len(self.bits):
            self.send(step + 1)


def arrivals_shapes(bits, width, columns):
    return [pltpu.VMEM((2, width >> (step + 1), columns), BF16) for step in range(bits)]


OUTS = (
    "input", "memory_own", "memory_other", "query", "key", "value", "out", "cross_query", "cross_key",
    "cross_value", "cross_out", "up", "down", "gains",
)


def backward_body(lay, names, late, scratch_names, *refs):
    r = dict(zip(names, refs, strict=False))
    o = dict(zip(OUTS, refs[len(names) :], strict=False))
    s = dict(zip(scratch_names, refs[len(names) + len(OUTS) :], strict=True))
    far = dict(r)
    count, parts, half, rows = lay.count, lay.parts, lay.half, lay.rows
    links = Links(lay, s)
    me, core, head, pack, part = links.me, links.core, links.head, links.pack, links.part
    bits = count.bit_length() - 1
    flat_rows, width = r["dc"].shape
    wide = r["w_out"].shape[0]
    total = r["qkv"].shape[2]
    mine_total = total // parts
    share = width // count
    block = min(512 if parts == 1 else 256, mine_total)
    links.announce(everyone=True)
    loading = {}

    def load(name):
        loading[name] = links.local(r[name], s["in_" + late[name]])

    for name, home in late.items():
        if name == home:
            load(name)
    own_rows = pl.ds(pl.multiple_of(me * share, share), share)
    row_copies = [
        links.local(far[name].at[own_rows, :], s["rows_" + name])
        for name in ("w_q", "w_k", "w_v", "w_cross_query", "w_up")
    ]
    h1_copy = links.local(r["h1_pack"].at[:, pl.ds(0, s["h1"].shape[1])], s["h1"])

    def ready(*wanted):
        for name in wanted:
            loading[name].wait()
            r[name] = s["in_" + late[name]]

    def relative(target, value, shift=0, column=0):
        number, most = count >> shift, s["turn"].shape[1]
        size_rows = width // number
        for start in range(0, value.shape[0], most):
            size = min(most, value.shape[0] - start)
            s["turn"][:, :size] = value[start : start + size, :].T
            for place in range(number):
                chunk = (me >> shift) ^ reversed_bits(place, bits - shift)
                target[pl.ds(place * size_rows, size_rows), column + start : column + start + size] = s[
                    "turn"
                ][pl.ds(pl.multiple_of(chunk * size_rows, size_rows), size_rows), :size]

    quarter = width // 4

    def quarter_of(ref, index):
        return ref[pl.ds(index * quarter, quarter), :]

    def batch(name, chosen, crossed=True):
        arrivals = [s[f"{name}_{i}"] for i in range(len(chosen))]
        return Halving(links, chosen, s[name + "_sums"], arrivals, crossed)

    piece = wide // 2

    def weight_job(target, place, left, right):
        def make(kind, index):
            return dot(quarter_of(left, index), right[kind * piece : (kind + 1) * piece, :], 1, 1)

        target.add_job(place * piece, piece, make)

    group = 4
    slice_width = s["gelu_group"].shape[2]
    links.all_here(everyone=True)

    def to_group(name):
        started = []
        for offset in range(group):
            number = lax.rem(me ^ offset, group)
            columns = pl.ds(pl.multiple_of(number * slice_width, slice_width), slice_width)
            started.append(links.to(offset, r[name].at[:, columns], s[name + "_group"].at[offset]))
        return started

    gelu_copies = to_group("gelu")

    ready("kv_slots", "cross_unit", "cross_att", "doc_unit")
    slots, span = r["kv_slots"].shape[0], r["kv_slots"].shape[3]
    s["cross_key"][...] = r["kv_slots"][0, 0].T
    s["cross_value"][...] = r["kv_slots"][0, 1].T
    s["cross_acc"][...] = jnp.zeros_like(s["cross_acc"])
    present = page_rows(span, lay.mem_pad, lay.mem_rows)

    def cross_block(here, slot, key_rows, value_rows):
        query, grad = r["cross_unit"][:, here], r["doc_unit"][:, here]
        row_dot = jnp.sum(grad.astype(F32) * r["cross_att"][:, here], axis=0, keepdims=True)
        scores = jnp.dot(key_rows, query, preferred_element_type=F32)
        allowed = present & (r["qslot"][:, here] == float(slot))
        weights = jnp.where(allowed, jnp.exp2(scores * EXP2_SCALE - r["cross_log"][:, here]), 0.0)
        weight_grad = jnp.dot(value_rows, grad, preferred_element_type=F32)
        score_grad = (weights * (weight_grad - row_dot)).astype(BF16)
        dq = jnp.dot(r["kv_slots"][slot, 0], score_grad, preferred_element_type=F32)
        return dq, dot(query, score_grad, 1, 1), dot(grad, weights.astype(BF16), 1, 1)

    narrow = min(256, mine_total)

    def main_slot(index, _):
        here = pl.ds(pl.multiple_of(index * narrow, narrow), narrow)
        dq, dk, dv = cross_block(here, 0, s["cross_key"][...], s["cross_value"][...])
        s["dq_acc"][:, here] = dq
        s["cross_acc"][0] += dk
        s["cross_acc"][1] += dv
        return 0

    lax.fori_loop(0, mine_total // narrow, main_slot, 0)
    s["dkv_low"][1, 0, 0] = (s["cross_acc"][0] * SCALE).astype(BF16)
    s["dkv_low"][1, 0, 1] = s["cross_acc"][1].astype(BF16)
    for slot in range(1, slots):
        key_rows, value_rows = r["kv_slots"][slot, 0].T, r["kv_slots"][slot, 1].T
        ends = []
        for start in (0, mine_total - LANES):
            here = pl.ds(start, LANES)
            ends.append(cross_block(here, slot, key_rows, value_rows))
            s["dq_acc"][:, here] += ends[-1][0]
        s["dkv_low"][1, slot, 0] = ((ends[0][1] + ends[1][1]) * SCALE).astype(BF16)
        s["dkv_low"][1, slot, 1] = (ends[0][2] + ends[1][2]).astype(BF16)
    load("att")
    s["dq_low"][...] = (s["dq_acc"][...] * SCALE).astype(BF16)
    dqc_copies = links.collect(s["dq_low"], s["in_small"].at[0])
    is_first = (r["longest"][:1, :1] < 0.5).astype(F32)
    is_second = (r["longest"][:1, :1] < 1.5).astype(F32) - is_first
    is_third = 1.0 - is_first - is_second
    for kind in range(2):
        found = [s["dkv_low"][1, slot, kind].astype(F32) for slot in range(slots)]
        for slot in range(slots):
            value = (
                found[slot] * is_first
                + found[(slot + 2) % slots] * is_second
                + found[(slot + 1) % slots] * is_third
            )
            s["dkv_low"][0, slot, kind] = value.astype(BF16)
    def to_twin(slot):
        return links.remote(s["dkv_low"].at[0, slot], s["dkv_twin"].at[slot], {"blk": me ^ half})

    twin_copies = [to_twin(slot) for slot in range(slots)]

    ready("dm_group")
    for offset in range(group):
        relative(s["rel_dm"], r["dm_group"].at[offset], 2, offset * flat_rows)

    def feed_job(left, right):
        def make(kind, index):
            here = slice(kind * slice_width // 2, (kind + 1) * slice_width // 2)
            return dot(
                quarter_of(left, index), right[:, :, here].reshape(group * flat_rows, slice_width // 2), 1, 0
            )

        return make

    down, up = [batch(name, range(2, bits), crossed=False) for name in ("down", "up")]
    wait_all(gelu_copies)
    down.add_job(0, slice_width // 2, feed_job(s["rel_dm"], s["gelu_group"]))
    du_copies = to_group("du")
    middle, pages = batch("middle", range(bits)), batch("pages", range(bits))
    ready("cross_mixed")
    relative(s["rel_dc"], r["dc"])
    weight_job(middle, 0, s["rel_dc"], r["cross_mixed"])
    ready("h3_group")
    for offset in range(group):
        relative(s["rel_h3"], r["h3_group"].at[offset], 2, offset * flat_rows)

    ready("w_cross_query")
    wait_all(dqc_copies)
    tp_copies = []
    for start in range(0, flat_rows, rows):
        here = slice(start, start + rows)
        s["tp_send"][here, :] = dot(s["in_small"][0, :, here].T, r["w_cross_query"][...], 1, 1).astype(BF16)
        tp_copies.append(
            links.to_other_core(s["tp_send"].at[pl.ds(start, rows)], s["tp_recv"].at[0, pl.ds(start, rows)])
        )
    ready("h2", "r1", "grad_two")
    relative(s["rel_h2"], r["h2"])
    load("x")
    weight_job(middle, 1, s["rel_h2"], s["in_small"].at[0])
    wait_all(tp_copies)

    def both_cores(index):
        def grad(here):
            return s["tp_send"][here, :].astype(F32) + s["tp_recv"][index, here, :].astype(F32)

        return grad

    norm_back_rows(
        s["grad_one"],
        both_cores(0),
        lambda here: r["r1"][here, :],
        r["gain_two"],
        lambda here: r["grad_two"][here, :],
        s["da"],
    )
    ready("w_out")
    s["out_small"][0] = dot(r["w_out"][...], s["da"][...], 1, 1).astype(BF16)
    do_copies = links.spread(s["out_small"].at[0], s["do_unit"])
    load("w_q")
    ready("mixed")
    relative(s["rel_da"], s["da"])
    weight_job(middle, 2, s["rel_da"], r["mixed"])
    def hot(side, slot, page):
        wanted = r["segment_page"][pack if side == 0 else 1 - pack, slot]
        return jnp.where(wanted == pack * lay.pages_half + page, 1.0, 0.0)

    wait_all(twin_copies)
    for page in range(lay.pages_half):
        for piece_index in range(lay.pieces):
            here = slice(piece_index * lay.mem_pad, (piece_index + 1) * lay.mem_pad)
            value = None
            for side, source in enumerate((s["dkv_low"].at[0], s["dkv_twin"])):
                for slot in range(slots):
                    term = hot(side, slot, page) * source[slot, :, :, here].astype(F32)
                    value = term if value is None else value + term
            s["page_grad"][page * lay.pieces + piece_index] = value.astype(BF16)
    memory_copies = []
    for offset in range(half):
        source = s["page_grad"].at[lax.rem(me ^ offset, half)]
        place = s["mem_recv"].at[part, :, pl.ds(head * HEAD_DIM, HEAD_DIM), :]
        memory_copies.append(links.to(offset, source, place))

    ready("qkv", "att")
    if parts > 1:
        ready("query")
    s["dq_acc"][...] = jnp.zeros_like(s["dq_acc"])
    wait_all(do_copies)

    def key_block(key_index, _):
        here = pl.ds(pl.multiple_of(key_index * block, block), block)
        keys, values = r["qkv"][1, :, here], r["qkv"][2, :, here]
        key_rows, value_rows = keys.T, values.T
        codes = jnp.broadcast_to(r["code"][:, here], (8, block)).T[:, :1]

        def fold(index, grads, causal):
            dk, dv = grads
            columns = pl.ds(pl.multiple_of(index * block, block), block)
            query = r["query"][:, columns] if parts > 1 else r["qkv"][0, :, columns]
            grad = s["do_unit"][:, columns]
            row_dot = jnp.sum(grad.astype(F32) * r["att"][:, columns], axis=0, keepdims=True)
            scores = jnp.dot(key_rows, query, preferred_element_type=F32)
            allowed = codes == r["qseg"][:, columns]
            if causal:
                places = index * block + lax.broadcasted_iota(jnp.int32, (1, block), 1)
                positions = ((places // rows) * parts + part) * rows + places % rows
                key_places = key_index * block + lax.broadcasted_iota(jnp.int32, (block, block), 0)
                allowed = allowed & (key_places <= positions)
            weights = jnp.where(allowed, jnp.exp2(scores * EXP2_SCALE - r["log"][:, columns]), 0.0)
            weight_grad = jnp.dot(value_rows, grad, preferred_element_type=F32)
            score_grad = (weights * (weight_grad - row_dot)).astype(BF16)
            s["dq_acc"][:, columns] += jnp.dot(keys, score_grad, preferred_element_type=F32)
            return (dk + dot(query, score_grad, 1, 1), dv + dot(grad, weights.astype(BF16), 1, 1))

        zeros = jnp.zeros((HEAD_DIM, block), F32)
        first_index = key_index // parts
        grads = fold(first_index, (zeros, zeros), True)
        dk, dv = lax.fori_loop(
            first_index + 1, mine_total // block, lambda i, g: fold(i, g, False), grads
        )
        r["qkv"][1, :, here] = (dk * SCALE).astype(BF16)
        r["qkv"][2, :, here] = dv.astype(BF16)
        return 0

    lax.fori_loop(0, total // block, key_block, 0)
    if parts == 1:
        r["qkv"][0] = (s["dq_acc"][...] * SCALE).astype(BF16)
        dq_copies = links.collect(r["qkv"].at[0], s["in_small"].at[1])
    else:
        r["qkv"][0] = jnp.zeros((HEAD_DIM, total), BF16)
        for number in range(count // parts):
            value = (s["dq_acc"][:, number * rows : (number + 1) * rows] * SCALE).astype(BF16)
            s["dq_low"][:, number * rows : (number + 1) * rows] = value
            r["qkv"][0, :, pl.ds((number * parts + part) * rows, rows)] = value
        dq_copies = links.collect(s["dq_low"], s["in_small"].at[1])
    unit_copy = links.to_other_core(r["qkv"], s["unit_other"])
    dkv_copies = []
    for offset in range(count):
        peer = me ^ offset
        source = r["qkv"].at[pl.ds(1, 2), :, pl.ds(peer * rows, rows)]
        place = s["dkv_recv"].at[part, :, pl.ds(head * HEAD_DIM, HEAD_DIM), pl.ds(pack * rows, rows)]
        dkv_copies.append(links.to(offset, source, place))
    unit_copy.wait()
    first_send, first_recv = links.take(count), links.take(count)
    number_to = count // 2

    def first_copy(index, number, source_device=None):
        target_core = core if index == 0 else 1 - core
        slot = me if source_device is None else source_device
        return pltpu.make_async_remote_copy(
            src_ref=s["first_low"].at[index, pl.ds(number * share, share), :],
            dst_ref=s["first_recv"].at[slot],
            send_sem=links.send_sem.at[first_send + index * number_to + number],
            recv_sem=links.recv_sem.at[first_recv + slot],
            device_id={"blk": core * number_to + number, "tp": target_core},
            device_id_type=MESH,
        )

    for index, ref in enumerate((r["qkv"], s["unit_other"])):
        value, most = None, s["h1"].shape[1]
        for start in range(0, total, most):
            if start + index > 0 and total > most:
                h1_copy = links.local(r["h1_pack"].at[:, pl.ds(start, most)], s["h1"])
            if start + index == 0 or total > most:
                h1_copy.wait()
            term = dot(s["h1"][...], ref[:, :, start : start + most].reshape(3 * HEAD_DIM, most), 1, 1)
            value = term if value is None else value + term
        s["first_low"][index] = value.astype(BF16)
        for number in range(number_to):
            if index == 1:
                first_copy(index, number).start()
                continue
            own = me == core * number_to + number

            @pl.when(jnp.logical_not(own))
            def _(number=number):
                first_copy(0, number).start()

            @pl.when(own)
            def _(number=number):
                pltpu.make_async_copy(
                    s["first_low"].at[0, pl.ds(number * share, share), :],
                    s["first_recv"].at[me],
                    links.recv_sem.at[first_recv + me],
                ).start()

    down.keep_jobs()
    middle.keep_jobs()

    ready("mem", "w_ck", "w_cv")
    wait_all(memory_copies)
    if parts > 1:
        for kind in range(2):
            value = s["mem_recv"][0, kind].astype(F32)
            for index in range(1, parts):
                value = value + s["mem_recv"][index, kind].astype(F32)
            s["mem_recv"][0, kind] = value.astype(BF16)
    relative(s["rel_mem"], r["mem"])
    weight_job(pages, 0, s["rel_mem"], s["mem_recv"].at[0, 0])
    weight_job(pages, 1, s["rel_mem"], s["mem_recv"].at[0, 1])
    for start in range(0, lay.mem_pad, LANES):
        here = slice(start, start + LANES)
        s["mem_send"][here, :] = (
            dot(s["mem_recv"][0, 0, :, here].T, r["w_ck"][...], 1, 1)
            + dot(s["mem_recv"][0, 1, :, here].T, r["w_cv"][...], 1, 1)
        ).astype(BF16)
    wait_all(du_copies)
    up.add_job(0, slice_width // 2, feed_job(s["rel_h3"], s["du_group"]))
    load("w_k")
    load("w_v")
    mem_copies = [
        links.to_other_core(s["mem_send"], o["memory_other"]),
        links.local(s["mem_send"], o["memory_own"]),
    ]

    ready("w_q", "w_k", "w_v", "x")
    wait_all(dq_copies)
    wait_all(dkv_copies)
    if parts > 1:
        for kind in range(2):
            value = s["dkv_recv"][0, kind].astype(F32)
            for index in range(1, parts):
                value = value + s["dkv_recv"][index, kind].astype(F32)
            s["dkv_recv"][0, kind] = value.astype(BF16)
    pieces = (s["in_small"].at[1], s["dkv_recv"].at[0, 0], s["dkv_recv"].at[0, 1])
    tp_copies = []
    for start in range(0, flat_rows, rows):
        here = slice(start, start + rows)
        s["tp_send"][here, :] = sum(
            dot(value[:, here].T, r[weight][...], 1, 1)
            for value, weight in zip(pieces, ("w_q", "w_k", "w_v"), strict=True)
        ).astype(BF16)
        tp_copies.append(
            links.to_other_core(s["tp_send"].at[pl.ds(start, rows)], s["tp_recv"].at[1, pl.ds(start, rows)])
        )
    middle.receive(1)
    wait_all(tp_copies)
    norm_back_rows(
        o["input"],
        both_cores(1),
        lambda here: r["x"][here, :].astype(F32),
        r["gain_one"],
        lambda here: s["grad_one"][here, :],
    )
    pages.keep_jobs()
    up.keep_jobs()
    down.receive(1)
    up.receive(1)
    for step in range(2, bits - 2):
        down.receive(step)
        up.receive(step)
    final_copies = []
    for offset in range(group):
        rows_to = pl.ds(lax.rem(me ^ offset, group) * share, share)
        for index, sums in enumerate((s["down_sums"], s["up_sums"])):
            place = s["feed_last"].at[index, lax.rem(me, group)]
            final_copies.append(links.to(offset, sums.at[:, rows_to, :], place))

    for step in range(2, bits + 1):
        pages.receive(step - 1, s["pages_result"] if step == bits else None)
        if step < bits:
            middle.receive(step, s["middle_result"] if step == bits - 1 else None)
    wait_all(final_copies)
    for number in range(group):
        for kind in range(2):
            start = number * slice_width + kind * slice_width // 2
            here = slice(start, start + slice_width // 2)
            o["down"][here, :] = s["feed_last"][0, number, kind].astype(F32).T
            o["up"][:, here] = s["feed_last"][1, number, kind].astype(F32)
    for kind in range(2):
        here = slice(kind * piece, (kind + 1) * piece)
        o["cross_out"][here, :] = s["middle_result"][kind, :, :piece].T
        o["cross_query"][:, here] = s["middle_result"][kind, :, piece : 2 * piece]
        o["out"][here, :] = s["middle_result"][kind, :, 2 * piece :].T
        o["cross_key"][:, here] = s["pages_result"][kind, :, :piece]
        o["cross_value"][:, here] = s["pages_result"][kind, :, piece:]
    for index in range(2):
        for number in range(number_to):
            if index == 1:
                first_copy(index, number).wait_send()
            else:

                @pl.when(me != core * number_to + number)
                def _(number=number):
                    first_copy(0, number).wait_send()

    for device in range(count):
        first_copy(0, 0, device).wait_recv()
    for index in range(lay.heads):
        value = None
        for side in range(2):
            for number in range(parts):
                term = s["first_recv"][side * half + index * parts + number].astype(F32)
                value = term if value is None else value + term
        for place, name in enumerate(("query", "key", "value")):
            o[name][:, index * HEAD_DIM : (index + 1) * HEAD_DIM] = value[
                :, place * HEAD_DIM : (place + 1) * HEAD_DIM
            ]

    wait_all(row_copies)
    lanes = lax.broadcasted_iota(jnp.int32, (share, LANES), 1)
    sums, gains = jnp.zeros((share, LANES), F32), jnp.ones((share, LANES), F32)
    pairs = (
        ("gain_one", (("w_q", "query"), ("w_k", "key"), ("w_v", "value"))),
        ("gain_two", (("w_cross_query", "cross_query"),)),
        ("gain_three", (("w_up", "up"),)),
    )
    for index, (gain, terms) in enumerate(pairs):
        value = sum(
            jnp.sum(s["rows_" + weight][...].astype(F32) * o[name][...], axis=1, keepdims=True)
            for weight, name in terms
        )
        s["gain_turned"][...] = jnp.broadcast_to(r[gain][...], (8, width)).T
        sums = jnp.where(lanes == index, value, sums)
        gains = jnp.where(lanes == index, s["gain_turned"][own_rows, :1], gains)
    s["gain_sums"][0] = sums
    links.to_other_core(s["gain_sums"].at[0], s["gain_sums"].at[1]).wait()
    o["gains"][...] = ((s["gain_sums"][0] + s["gain_sums"][1]) / gains).T[:8, :]
    wait_all(mem_copies)


def backward(lay, values, ff):
    parts, count, half, rows = lay.parts, lay.count, lay.half, lay.rows
    flat_rows, width = values["dc"].shape
    wide = lay.heads * HEAD_DIM
    total = count * rows
    mine_total = total // parts
    span = lay.pieces * lay.mem_pad
    bits = count.bit_length() - 1
    late = [
        "doc_unit", "kv_slots", "cross_unit", "cross_att", "w_out", "dm_group", "h3_group",
        "cross_mixed", "w_cross_query", "r1", "grad_two", "mixed", "qkv", "mem", "h2", "w_ck", "w_cv",
    ]
    if parts > 1:
        late.append("query")
    late = {name: name for name in late}
    late.update(w_q="w_cross_query", w_k="w_ck", w_v="w_cv", att="cross_att", x="h2")
    far = ["h1_pack", "gelu", "du", "w_up"]
    early = [name for name in values if name not in late and name not in far + ["segment_page"]]
    names = ["segment_page"] + early + list(late) + far
    vmem, anywhere = pl.BlockSpec(memory_space=pltpu.VMEM), pl.BlockSpec(memory_space=pl.ANY)

    def buffer(*shape, dtype=BF16):
        return pltpu.VMEM(shape, dtype)

    share = width // count
    scratch = {
        "send_sem": pltpu.SemaphoreType.DMA((9 * count + 128,)),
        "recv_sem": pltpu.SemaphoreType.DMA((9 * count + 128,)),
        "out_small": buffer(1, wide, flat_rows),
        "in_small": buffer(2, wide, flat_rows),
        "do_unit": buffer(HEAD_DIM, mine_total),
        "dq_acc": buffer(HEAD_DIM, mine_total, dtype=F32),
        "dq_low": buffer(HEAD_DIM, mine_total),
        "turn": buffer(width, flat_rows),
        "rel_dm": buffer(width, 4 * flat_rows),
        "rel_h3": buffer(width, 4 * flat_rows),
        "rel_dc": buffer(width, flat_rows),
        "rel_h2": buffer(width, flat_rows),
        "rel_da": buffer(width, flat_rows),
        "rel_mem": buffer(width, lay.mem_pad),
        "feed_last": buffer(2, 4, 2, share, ff // 8),
        "gelu_group": buffer(4, flat_rows, ff // 4),
        "du_group": buffer(4, flat_rows, ff // 4),
        "h1": buffer(wide, min(total, 2048)),
        "cross_key": buffer(span, HEAD_DIM),
        "cross_value": buffer(span, HEAD_DIM),
        "cross_acc": buffer(2, HEAD_DIM, span, dtype=F32),
        "dkv_low": buffer(2, NSEG, 2, HEAD_DIM, span),
        "dkv_twin": buffer(NSEG, 2, HEAD_DIM, span),
        "page_grad": buffer(half, 2, HEAD_DIM, lay.mem_pad),
        "mem_recv": buffer(parts, 2, wide, lay.mem_pad),
        "mem_send": buffer(lay.mem_pad, width),
        "tp_send": buffer(flat_rows, width),
        "tp_recv": buffer(2, flat_rows, width),
        "grad_one": buffer(flat_rows, width, dtype=F32),
        "da": buffer(flat_rows, width),
        "dkv_recv": buffer(parts, 2, wide, flat_rows),
        "unit_other": buffer(3, HEAD_DIM, total),
        "first_low": buffer(2, wide, 3 * HEAD_DIM),
        "first_recv": buffer(count, share, 3 * HEAD_DIM),
        "middle_result": buffer(2, share, 3 * wide // 2, dtype=F32),
        "pages_result": buffer(2, share, wide, dtype=F32),
        "gain_turned": buffer(width, 8, dtype=F32),
        "gain_sums": buffer(2, share, LANES, dtype=F32),
        "rows_w_up": buffer(share, ff),
    }
    for name in ("w_q", "w_k", "w_v", "w_cross_query"):
        scratch["rows_" + name] = buffer(share, wide)
    columns = {"down": ff // 8, "up": ff // 8, "middle": 3 * wide // 2, "pages": wide}
    for name, number in columns.items():
        scratch[name + "_sums"] = buffer(2, width // 2, number)
        steps = bits - 2 if name in ("down", "up") else bits
        for index, shape in enumerate(arrivals_shapes(steps, width, number)):
            scratch[f"{name}_{index}"] = shape
    homes = {}
    for name, home in late.items():
        homes.setdefault(home, values[name])
    for home, value in homes.items():
        scratch["in_" + home] = pltpu.VMEM(value.shape, value.dtype)

    side, across = (share, wide), (wide, share)
    shapes = {"cross_out": across, "out": across, "up": (share, ff), "down": (ff, share), "gains": (8, share)}
    outs = {name: jax.ShapeDtypeStruct(shapes.get(name, side), F32) for name in OUTS}
    outs["input"] = jax.ShapeDtypeStruct((flat_rows, width), F32)
    for name in ("memory_own", "memory_other"):
        outs[name] = jax.ShapeDtypeStruct((lay.mem_pad, width), BF16)
    results = pl.pallas_call(
        functools.partial(backward_body, lay, names, late, list(scratch)),
        out_shape=list(outs.values()),
        in_specs=[pl.BlockSpec(memory_space=pltpu.SMEM)]
        + [vmem] * len(early)
        + [anywhere] * (len(late) + len(far)),
        out_specs=[anywhere if name.startswith("memory") else vmem for name in OUTS],
        scratch_shapes=list(scratch.values()),
        compiler_params=pltpu.CompilerParams(
            collective_id=1, has_side_effects=True, vmem_limit_bytes=63 * 1024 * 1024 + 512 * 1024
        ),
    )(*[values[name] for name in names])
    return dict(zip(OUTS, results, strict=True))


def local(
    tokens,
    memory,
    segment_ids,
    token_valid,
    segment_page,
    gain_one,
    weight_query,
    weight_key,
    weight_value,
    weight_out,
    gain_two,
    cross_query,
    cross_key,
    cross_value,
    cross_out,
    gain_three,
    weight_up,
    weight_down,
    cotangent,
):
    packs, rows, width = tokens.shape
    wide, ff = weight_query.shape[1], weight_up.shape[1]
    lay = Layout(lax.axis_size("blk"), packs, wide // HEAD_DIM, rows, memory.shape[0])
    flat_rows = packs * rows
    x = tokens.reshape(flat_rows, width)
    kept = forward(
        lay,
        {
            "segment_page": segment_page,
            "x": x,
            "segment_ids": segment_ids,
            "token_valid": token_valid,
            "memory": memory,
            "gain_one": gain_one[None],
            "gain_two": gain_two[None],
            "gain_three": gain_three[None],
            "w_q": weight_query,
            "w_k": weight_key,
            "w_v": weight_value,
            "w_ck": cross_key,
            "w_cv": cross_value,
            "cot": cotangent.reshape(flat_rows, width),
            "w_out": weight_out,
            "w_cross_query": cross_query,
            "w_cross_out": cross_out,
            "w_up": weight_up,
            "w_down": weight_down,
        },
        ff,
    )
    out = kept.pop("out").reshape(packs, rows, width)
    grads = backward(
        lay,
        {
            **kept,
            "segment_page": segment_page,
            "x": x,
            "gain_one": gain_one[None],
            "gain_two": gain_two[None],
            "gain_three": gain_three[None],
            "w_cross_query": cross_query,
            "w_out": weight_out,
            "w_ck": cross_key,
            "w_cv": cross_value,
            "w_q": weight_query,
            "w_k": weight_key,
            "w_v": weight_value,
            "w_up": weight_up,
        },
        ff,
    )
    grad_memory = (grads["memory_own"].astype(F32) + grads["memory_other"].astype(F32))[: lay.mem_rows]
    return (
        out,
        grads["input"].reshape(packs, rows, width),
        grad_memory,
        grads["query"],
        grads["key"],
        grads["value"],
        grads["out"],
        grads["cross_query"],
        grads["cross_key"],
        grads["cross_value"],
        grads["cross_out"],
        grads["up"],
        grads["down"],
        grads["gains"][0],
        grads["gains"][1],
        grads["gains"][2],
    )


def solution(mesh):
    in_specs = (
        P(None, "blk", None),
        P("blk", None),
        P(None, "blk"),
        P(None, "blk"),
        P(),
        P(),
        P(None, "tp"),
        P(None, "tp"),
        P(None, "tp"),
        P("tp", None),
        P(),
        P(None, "tp"),
        P(None, "tp"),
        P(None, "tp"),
        P("tp", None),
        P(),
        P(None, "tp"),
        P("tp", None),
        P(None, "blk", None),
    )
    out_specs = (
        P(None, "blk", None),
        P(None, "blk", None),
        P("blk", None),
        P("blk", "tp"),
        P("blk", "tp"),
        P("blk", "tp"),
        P("tp", "blk"),
        P("blk", "tp"),
        P("blk", "tp"),
        P("blk", "tp"),
        P("tp", "blk"),
        P("blk", "tp"),
        P("tp", "blk"),
        P("blk"),
        P("blk"),
        P("blk"),
    )
    return jax.shard_map(local, mesh=mesh, in_specs=in_specs, out_specs=out_specs, check_vma=False)
```

```python
import functools

import jax
import jax.numpy as jnp
from jax import lax
from jax.experimental import pallas as pl
from jax.experimental.pallas import tpu as pltpu
from jax.sharding import PartitionSpec as P

MEM_LEN = 588
HEAD_DIM = 64
NSEG = 3
EPS = 1e-05
NEG = -1e30
EXP2_SCALE = HEAD_DIM**-0.5 * 1.4426950408889634
SCALE = HEAD_DIM**-0.5
LANES = 128
BF16 = jnp.bfloat16
F32 = jnp.float32
MESH = pl.DeviceIdType.MESH


def dot(left, right, contract_left, contract_right):
    return lax.dot_general(
        left, right, (((contract_left,), (contract_right,)), ((), ())), preferred_element_type=F32
    )


def wait_all(copies):
    for copy in copies:
        copy.wait()


class Layout:
    def __init__(self, count, packs, heads, rows, mem_rows):
        self.count, self.packs, self.heads, self.rows = count, packs, heads, rows
        self.half = count // packs
        self.parts = self.half // heads
        self.mem_rows = mem_rows
        self.mem_pad = -(-mem_rows // LANES) * LANES
        self.pieces = MEM_LEN // mem_rows
        self.pages_half = self.half // self.pieces

    def head(self, device):
        return lax.rem(device, self.half) // self.parts


def page_rows(span, piece, real):
    places = lax.broadcasted_iota(jnp.int32, (span, 1), 0)
    return lax.rem(places, piece) < real


def erf(value):
    x = jnp.clip(value, -3.832506856900711, 3.832506856900711)
    square = x * x
    top = jnp.float32(0.00022905065861350646)
    for coefficient in (0.0034082910107109506, 0.050955695062380861, 0.18520832239976145, 1.128379143519084):
        top = top * square + coefficient
    low = jnp.float32(-1.1791602954361697e-7)
    for coefficient in (
        0.000023547966471313185,
        0.0010179625278914885,
        0.014070470171167667,
        0.11098505178285362,
        0.49746925110067538,
        1.0,
    ):
        low = low * square + coefficient
    return x * top / low


def normed_rows(source, gain, low):
    step = 32

    def body(index, _):
        rows = pl.ds(pl.multiple_of(index * step, step), step)
        value = source(rows)
        centred = value - jnp.mean(value, axis=1, keepdims=True)
        inv_std = lax.rsqrt(jnp.mean(centred * centred, axis=1, keepdims=True) + EPS)
        low[rows, :] = (centred * inv_std * gain[...]).astype(BF16)
        return 0

    lax.fori_loop(0, low.shape[0] // step, body, 0)


def norm_back_rows(target, grad, source, gain, residual, low=None):
    step = 32

    def body(index, _):
        rows = pl.ds(pl.multiple_of(index * step, step), step)
        value = source(rows)
        centred = value - jnp.mean(value, axis=1, keepdims=True)
        inv_std = lax.rsqrt(jnp.mean(centred * centred, axis=1, keepdims=True) + EPS)
        z = centred * inv_std
        w = grad(rows) * gain[...]
        inner = w - jnp.mean(w, axis=1, keepdims=True) - z * jnp.mean(w * z, axis=1, keepdims=True)
        value = residual(rows) + inner * inv_std
        target[rows, :] = value
        if low is not None:
            low[rows, :] = value.astype(BF16)
        return 0

    lax.fori_loop(0, target.shape[0] // step, body, 0)


class Links:
    def __init__(self, lay, scratch):
        self.lay = lay
        self.me, self.core = lax.axis_index("blk"), lax.axis_index("tp")
        self.head, self.pack = lay.head(self.me), self.me // lay.half
        self.part = lax.rem(self.me, lay.parts)
        self.send_sem, self.recv_sem, self.used = scratch["send_sem"], scratch["recv_sem"], 0
        self.own_sem, self.own_used = scratch["own_sem"], 0
        self.barrier = pltpu.get_barrier_semaphore()

    def announce(self, everyone=False):
        for offset in range(self.lay.count):
            if offset > 0:
                self.signal(offset, self.core)
            if offset == 0 or everyone:
                self.signal(offset, 1 - self.core)

    def signal(self, offset, core):
        device = {"blk": self.me ^ offset, "tp": core}
        pl.semaphore_signal(self.barrier, inc=1, device_id=device, device_id_type=MESH)

    def all_here(self, everyone=False):
        pl.semaphore_wait(self.barrier, (2 if everyone else 1) * self.lay.count - (1 if everyone else 0))

    def take(self, number=1):
        index, self.used = self.used, self.used + number
        return index

    def described(self, index, source, target, device):
        return pltpu.make_async_remote_copy(
            src_ref=source,
            dst_ref=target,
            send_sem=self.send_sem.at[index],
            recv_sem=self.recv_sem.at[index],
            device_id=device,
            device_id_type=MESH,
        )

    def remote(self, source, target, device):
        copy = self.described(self.take(), source, target, device)
        copy.start()
        return copy

    def local(self, source, target):
        copy = pltpu.make_async_copy(source, target, self.own_sem.at[self.own_used])
        self.own_used += 1
        copy.start()
        return copy

    def to(self, offset, source, target):
        if offset == 0:
            return self.local(source, target)
        return self.remote(source, target, {"blk": self.me ^ offset})

    def to_other_core(self, source, target):
        return self.remote(source, target, {"tp": 1 - self.core})

    def spread(self, source, target, every=False):
        lay, step = self.lay, 1 if every else self.lay.parts
        started = []
        for offset in range(0, lay.count, step):
            peer = self.me ^ offset
            piece = source.at[
                pl.ds(lay.head(peer) * HEAD_DIM, HEAD_DIM), pl.ds((peer // lay.half) * lay.rows, lay.rows)
            ]
            started.append(self.to(offset, piece, target.at[:, pl.ds((self.me // step) * lay.rows, lay.rows)]))
        return started

    def unit_place(self, target):
        lay = self.lay
        return target.at[pl.ds(self.head * HEAD_DIM, HEAD_DIM), pl.ds(self.pack * lay.rows, lay.rows)]

    def collect(self, source, target):
        lay, started = self.lay, []
        for offset in range(0, lay.count, lay.parts):
            peer = self.me ^ offset
            piece = source.at[:, pl.ds((peer // lay.parts) * lay.rows, lay.rows)]
            started.append(self.to(offset, piece, self.unit_place(target)))
        return started

    def collect_later(self, source, target):
        lay = self.lay
        first = self.take(lay.count // lay.parts)

        def send(number):
            peer = number * lay.parts + self.part
            piece, place = source.at[:, pl.ds(number * lay.rows, lay.rows)], self.unit_place(target)

            @pl.when(peer != self.me)
            def _():
                index = first + (peer ^ self.me) // lay.parts
                self.described(index, piece, place, {"blk": peer}).start()

            @pl.when(peer == self.me)
            def _():
                pltpu.make_async_copy(piece, place, self.send_sem.at[first]).start()

        def wait():
            piece = source.at[:, pl.ds(0, lay.rows)]
            for offset in range(0, lay.count, lay.parts):
                peer = self.me ^ offset
                index = first + offset // lay.parts
                if offset == 0:
                    pltpu.make_async_copy(piece, self.unit_place(target), self.send_sem.at[index]).wait()
                else:
                    self.described(index, piece, self.unit_place(target), {"blk": peer}).wait()

        return send, wait


HALVES = ("keys_half", "values_half")


def forward_body(lay, names, late, out_names, scratch_names, *refs):
    r = dict(zip(names, refs, strict=False))
    o = dict(zip(out_names, refs[len(names) :], strict=False))
    s = dict(zip(scratch_names, refs[len(names) + len(out_names) :], strict=True))
    count, parts, half, rows = lay.count, lay.parts, lay.half, lay.rows
    links = Links(lay, s)
    me, core = links.me, links.core
    links.announce()
    flat_rows, width = r["x"].shape
    wide, ff = s["w_out"].shape[0], s["w_up"].shape[1]
    total = count * rows
    mine_total = total // parts
    loading = {name: links.local(r[name], s[name]) for name in late}
    leaving = []

    def page_of(side, slot):
        place = r["segment_page"][links.pack if side == 0 else 1 - links.pack, slot] - (
            links.pack * lay.pages_half
        )
        inside = (place >= 0) & (place < lay.pages_half)
        return jnp.clip(place, 0, lay.pages_half - 1), jnp.where(inside, 1.0, 0.0)

    codes = (r["segment_ids"][...] * 2 + r["token_valid"][...]).astype(F32)
    for pack in range(lay.packs):
        s["code_tok"][pack] = jnp.broadcast_to(codes[pack : pack + 1, :], (8, rows))

    def ready(*wanted):
        for name in wanted:
            loading[name].wait()

    def emit(*wanted):
        for name in wanted:
            leaving.append(links.local(s[name], o[name]))

    half_rows = pl.ds(pl.multiple_of(core * wide, wide), wide)
    other, group = me ^ half, 4
    normed_rows(lambda here: r["x"][here, :].astype(F32), r["gain_one"], s["h1"])
    for index, name in enumerate(("w_q", "w_k", "w_v")):
        ready(name)
        s["tok"][index] = dot(s["h1"][...], s[name][...], 1, 0).astype(BF16).T
    links.all_here()
    all_copies = []
    for index in range(3):
        target = s["query"] if index == 0 and parts > 1 else s["qkv"].at[index]
        all_copies += links.spread(s["tok"].at[index], target, index > 0)
    for offset in range(count):
        piece = s["code_tok"].at[(me ^ offset) // half]
        all_copies.append(links.to(offset, piece, s["codes"].at[:, pl.ds(me * rows, rows)]))

    s["mem"][lay.mem_rows // 16 * 16 :, :] = jnp.zeros_like(s["mem"][lay.mem_rows // 16 * 16 :, :])
    s["mem"][: lay.mem_rows, :] = r["memory"][...]
    emit("mem")
    ready("w_ck", "w_cv")
    memory_copies = []
    for kind, name in enumerate(("w_ck", "w_cv")):
        s["kv_tok"][kind] = dot(s["mem"][...], s[name][...], 1, 0).astype(BF16).T
        started = []
        for offset in range(half):
            piece = s["kv_tok"].at[kind, pl.ds(lay.head(me ^ offset) * HEAD_DIM, HEAD_DIM), :]
            started.append(links.to(offset, piece, s[HALVES[kind]].at[lax.rem(me, half)]))
        memory_copies.append(started)
    twin_copies = []

    def find_pages(kind):
        wait_all(memory_copies[kind])
        for side in range(2):
            for slot in range(NSEG):
                page, here = page_of(side, slot)
                for piece in range(lay.pieces):
                    value = s[HALVES[kind]][page * lay.pieces + piece].astype(F32) * here
                    columns = slice(piece * lay.mem_pad, (piece + 1) * lay.mem_pad)
                    s["kv_found"][kind, side, slot, :, columns] = value.astype(BF16)
        twin_copies.append(
            links.remote(s["kv_found"].at[kind, 1], s["kv_twin"].at[kind], {"blk": other})
        )

    s["h1_turned"][...] = s["h1"][:, half_rows].T

    def pack_chunk(owner, first=0, size=wide):
        return o["h1_pack"].at[pl.ds(first, size), pl.ds(pl.multiple_of(owner * rows, rows), rows)]

    def hand_over():
        return [
            links.remote(
                s["h1_turned"].at[:, pl.ds((1 - links.pack) * rows, rows)], pack_chunk(me), {"blk": other}
            ),
            links.local(s["h1_turned"].at[:, pl.ds(links.pack * rows, rows)], pack_chunk(me)),
        ]

    ways = half.bit_length() - 1
    shares = [16 * (wide // 16 // ways + (way < wide // 16 % ways)) for way in range(ways)]

    def double(step, owners):
        started = []
        for way in range(ways):
            first, order = sum(shares[:way]), [(way + turn) % ways for turn in range(step + 1)]
            held = [0]
            for bit in order[:-1]:
                held += [offset ^ (1 << bit) for offset in held]
            for owner in owners:
                for offset in held:
                    piece = pack_chunk(owner ^ offset, first, shares[way])
                    started.append(links.to(1 << order[-1], piece, piece))
        return started

    def to_group(source, target):
        started = [links.local(source, target.at[0])]
        for offset in range(1, group):
            started.append(links.to(offset, source.at[:, half_rows], target.at[offset, :, half_rows]))
        return started

    wait_all(all_copies)
    pack_copies = hand_over()

    codes = s["codes"][:1, :]
    segments = jnp.floor(codes * 0.5)
    s["code"][...] = jnp.where(codes - 2.0 * segments > 0.5, segments, -1.0)
    lengths = [
        jnp.sum((segments == float(slot)).astype(F32), axis=1, keepdims=True) for slot in range(NSEG)
    ]
    first_longest = ((lengths[0] >= lengths[1]) & (lengths[0] >= lengths[2])).astype(F32)
    second_longest = (lengths[1] >= lengths[2]).astype(F32) * (1.0 - first_longest)
    longest = 2.0 - 2.0 * first_longest - second_longest
    order = segments - longest
    order = jnp.where(order < 0.0, order + float(NSEG), order)
    if parts == 1:
        s["qseg"][...], s["qslot"][...] = segments, order
    else:
        s["rows"][0:1, :], s["rows"][1:2, :] = segments, order
        for piece in range(count // parts):
            there = pl.ds((piece * parts + links.part) * rows, rows)
            s["qseg"][:, piece * rows : (piece + 1) * rows] = s["rows"][0:1, there]
            s["qslot"][:, piece * rows : (piece + 1) * rows] = s["rows"][1:2, there]
    s["longest"][...] = jnp.broadcast_to(longest, s["longest"].shape)
    emit("qkv", "code", "qseg", "qslot", "longest")
    if parts > 1:
        emit("query")

    block = min(512 if parts == 1 else 256, mine_total)
    s["key"][...] = s["qkv"][1].T
    send_mixed, wait_mixed = links.collect_later(s["low"].at[0], s["mixed"])
    for index in reversed(range(mine_total // block)):
        columns = slice(index * block, (index + 1) * block)
        query = s["query"][:, columns] if parts > 1 else s["qkv"][0, :, columns]
        mine = s["qseg"][:, columns]
        places = index * block + lax.broadcasted_iota(jnp.int32, (1, block), 1)
        positions = ((places // rows) * parts + links.part) * rows + places % rows

        def fold(key_index, state, causal, query=query, mine=mine, positions=positions):
            largest, weight_sum, weighted = state
            start = pl.multiple_of(key_index * block, block)
            here = pl.ds(start, block)
            scores = jnp.dot(s["key"][here, :], query, preferred_element_type=F32)
            allowed = jnp.broadcast_to(s["code"][:, here], (8, block)).T[:, :1] == mine
            if causal:
                key_places = start + lax.broadcasted_iota(jnp.int32, (block, block), 0)
                allowed = allowed & (key_places <= positions)
            scores = jnp.where(allowed, scores, NEG)
            new = jnp.maximum(largest, jnp.max(scores, axis=0, keepdims=True))
            weights = jnp.exp2((scores - new) * EXP2_SCALE)
            keep = jnp.exp2((largest - new) * EXP2_SCALE)
            weight_sum = weight_sum * keep + jnp.sum(weights, axis=0, keepdims=True)
            update = jnp.dot(s["qkv"][2, :, here], weights.astype(BF16), preferred_element_type=F32)
            return (new, weight_sum, weighted * keep + update)

        state = (
            jnp.full((1, block), NEG, F32),
            jnp.zeros((1, block), F32),
            jnp.zeros((HEAD_DIM, block), F32),
        )
        state = lax.fori_loop(0, index * parts, lambda j, c, fold=fold: fold(j, c, False), state)
        for extra in range(parts):
            state = fold(index * parts + extra, state, True)
        largest, weight_sum, weighted = state
        result = weighted / weight_sum
        s["att"][:, columns] = result
        s["low"][0, :, columns] = result.astype(BF16)
        s["log"][:, columns] = largest * EXP2_SCALE + jnp.log2(weight_sum)
        for piece in range(index * block // rows, (index + 1) * block // rows):
            send_mixed(piece)
    emit("att", "log")

    def product_rows(left, right, sent, arrived):
        started = []
        for start in range(0, flat_rows, rows):
            here = slice(start, start + rows)
            sent[here, :] = dot(left[:, here].T, right[...], 1, 0).astype(BF16)
            started.append(links.to_other_core(sent.at[pl.ds(start, rows)], arrived.at[pl.ds(start, rows)]))
        return started

    def group_to_other_core(target):
        others = target.at[pl.ds(1, group - 1), :, half_rows]
        return links.to_other_core(others, others)

    def both(sent, arrived):
        return lambda here: sent[here, :].astype(F32) + arrived[here, :].astype(F32)

    def add_rows(target, *terms):
        step = 32

        def body(index, _):
            here = pl.ds(pl.multiple_of(index * step, step), step)
            target[here, :] = sum(term(here) for term in terms).astype(target.dtype)
            return 0

        lax.fori_loop(0, flat_rows // step, body, 0)

    for kind in range(2):
        find_pages(kind)
    ready("w_out")
    wait_mixed()
    wait_all(pack_copies)
    pack_copies = double(0, [me, other])
    emit("mixed")
    started = product_rows(s["mixed"], s["w_out"], s["sent"].at[0], s["arrived"].at[0])
    wait_all(started)
    add_rows(
        s["r1"], lambda here: r["x"][here, :].astype(F32), both(s["sent"].at[0], s["arrived"].at[0])
    )
    normed_rows(lambda here: s["r1"][here, :], r["gain_two"], s["h2"])
    ready("w_cross_query")
    s["tok"][0] = dot(s["h2"][...], s["w_cross_query"][...], 1, 0).astype(BF16).T
    query_copies = links.spread(s["tok"].at[0], s["cross_unit"])
    ready("cot")
    cot_copies = to_group(s["cot"], o["dm_group"])
    emit("r1", "h2")

    wait_all(twin_copies)
    is_first = (s["longest"][:1, :1] < 0.5).astype(F32)
    is_second = (s["longest"][:1, :1] < 1.5).astype(F32) - is_first
    is_third = 1.0 - is_first - is_second
    for kind in range(2):
        found = [
            s["kv_found"][kind, 0, slot].astype(F32)
            + s["kv_twin"][kind, slot].astype(F32) * (1.0 - page_of(0, slot)[1])
            for slot in range(NSEG)
        ]
        for slot in range(NSEG):
            value = (
                found[slot] * is_first
                + found[(slot + 1) % NSEG] * is_second
                + found[(slot + 2) % NSEG] * is_third
            )
            s["kv_slots"][slot, kind] = value.astype(BF16)
    emit("kv_slots")

    narrow = min(256, mine_total)
    present = page_rows(lay.pieces * lay.mem_pad, lay.mem_pad, lay.mem_rows)
    key_rows = [s["kv_slots"][slot, 0].T for slot in range(NSEG)]
    send_cross, wait_cross = links.collect_later(s["low"].at[1], s["cross_mixed"])
    wait_all(query_copies)
    emit("cross_unit")
    wait_all(pack_copies)
    pack_copies = double(1, [me, other])

    def attend(columns, slot):
        scores = jnp.dot(key_rows[slot], s["cross_unit"][:, columns], preferred_element_type=F32)
        scores = jnp.where(present, scores, NEG)
        largest = jnp.max(scores, axis=0, keepdims=True)
        weights = jnp.exp2((scores - largest) * EXP2_SCALE)
        weight_sum = jnp.sum(weights, axis=0, keepdims=True)
        result = jnp.dot(s["kv_slots"][slot, 1], weights.astype(BF16), preferred_element_type=F32)
        return result / weight_sum, largest * EXP2_SCALE + jnp.log2(weight_sum)

    for index in range(mine_total // narrow):
        columns = slice(index * narrow, (index + 1) * narrow)
        s["cross_att"][:, columns], s["cross_log"][:, columns] = attend(columns, 0)
        ends = [0] if index == 0 else []
        ends += [mine_total - LANES] if index == mine_total // narrow - 1 else []
        for start in ends:
            columns = slice(start, start + LANES)
            for slot in range(1, NSEG):
                result, logs = attend(columns, slot)
                here = s["qslot"][:, columns] == float(slot)
                s["cross_att"][:, columns] = jnp.where(here, result, s["cross_att"][:, columns])
                s["cross_log"][:, columns] = jnp.where(here, logs, s["cross_log"][:, columns])
        columns = slice(index * narrow, (index + 1) * narrow)
        s["low"][1, :, columns] = s["cross_att"][:, columns].astype(BF16)
        for piece in range(index * narrow // rows, (index + 1) * narrow // rows):
            send_cross(piece)
    emit("cross_att", "cross_log")
    ready("w_cross_out")
    wait_cross()
    for step in range(2, ways):
        wait_all(pack_copies)
        pack_copies = double(step, [me, other])
    emit("cross_mixed")
    started = product_rows(s["cross_mixed"], s["w_cross_out"], s["sent"].at[1], s["arrived"].at[1])
    wait_all(started)
    add_rows(s["r2"], lambda here: s["r1"][here, :], both(s["sent"].at[1], s["arrived"].at[1]))
    normed_rows(lambda here: s["r2"][here, :], r["gain_three"], s["h1"])
    h3_copies = to_group(s["h1"], o["h3_group"])

    ready("w_up", "w_down")
    slice_width = ff // group
    s["down_sum"][...] = jnp.zeros_like(s["down_sum"])
    s["up_sum"][...] = jnp.zeros_like(s["up_sum"])
    piece_rows = LANES
    for number in range(group):
        columns = slice(number * slice_width, (number + 1) * slice_width)
        for start in range(0, flat_rows, piece_rows):
            here = slice(start, start + piece_rows)
            u = dot(s["h1"][here, :], s["w_up"][:, columns], 1, 0)
            grad = dot(s["cot"][here, :], s["w_down"][columns, :], 1, 1)
            normal = 0.5 + 0.5 * erf(u * 0.7071067811865476)
            s["gelu"][here, columns] = (u * normal).astype(BF16)
            slope = normal + u * jnp.exp2(u * u * -0.7213475204444817) * 0.3989422804014327
            s["du"][here, columns] = (slope * grad).astype(BF16)
        s["down_sum"][...] += dot(s["gelu"][:, columns], s["w_down"][columns, :], 1, 0)
        s["up_sum"][...] += dot(s["du"][:, columns], s["w_up"][:, columns], 1, 1)
    emit("gelu", "du")
    s["sent"][2] = s["up_sum"][...].astype(BF16)
    up_copy = links.to_other_core(s["sent"].at[2], s["arrived"].at[2])
    s["sent"][3] = s["down_sum"][...].astype(BF16)
    down_copy = links.to_other_core(s["sent"].at[3], s["arrived"].at[3])
    up_copy.wait()
    norm_back_rows(
        s["grad_two"],
        both(s["sent"].at[2], s["arrived"].at[2]),
        lambda here: s["r2"][here, :],
        r["gain_three"],
        lambda here: s["cot"][here, :].astype(F32),
        s["dc"],
    )
    s["tok"][0] = dot(s["w_cross_out"][...], s["dc"][...], 1, 1).astype(BF16)
    doc_copies = links.spread(s["tok"].at[0], s["doc_unit"])
    emit("grad_two", "dc")
    wait_all(cot_copies)
    wait_all(h3_copies)
    group_copies = [group_to_other_core(o["dm_group"]), group_to_other_core(o["h3_group"])]
    down_copy.wait()
    add_rows(s["sent"].at[3], lambda here: s["r2"][here, :], both(s["sent"].at[3], s["arrived"].at[3]))
    leaving.append(links.local(s["sent"].at[3], o["out"]))
    wait_all(doc_copies)
    emit("doc_unit")
    wait_all(group_copies)
    wait_all(pack_copies)
    wait_all(leaving)
    assert links.used <= links.send_sem.shape[0] and links.own_used <= links.own_sem.shape[0]


def forward(lay, values, ff):
    parts, count, half, rows = lay.parts, lay.count, lay.half, lay.rows
    flat_rows, width = values["x"].shape
    wide, total = lay.heads * HEAD_DIM, lay.count * lay.rows
    mine_total = total // parts
    span = lay.pieces * lay.mem_pad
    early = ["x", "segment_ids", "token_valid", "memory", "gain_one", "gain_two", "gain_three"]
    late = [name for name in values if name not in early + ["segment_page"]]
    names = ["segment_page"] + early + late

    def shape(*dims, dtype=BF16):
        return jax.ShapeDtypeStruct(dims, dtype)

    kept = {
        "qkv": shape(3, HEAD_DIM, total),
        "code": shape(1, total, dtype=F32),
        "qseg": shape(1, mine_total, dtype=F32),
        "qslot": shape(1, mine_total, dtype=F32),
        "longest": shape(8, LANES, dtype=F32),
        "att": shape(HEAD_DIM, mine_total, dtype=F32),
        "log": shape(1, mine_total, dtype=F32),
        "mixed": shape(wide, flat_rows),
        "r1": shape(flat_rows, width, dtype=F32),
        "h2": shape(flat_rows, width),
        "cross_unit": shape(HEAD_DIM, mine_total),
        "kv_slots": shape(NSEG, 2, HEAD_DIM, span),
        "cross_att": shape(HEAD_DIM, mine_total, dtype=F32),
        "cross_log": shape(1, mine_total, dtype=F32),
        "cross_mixed": shape(wide, flat_rows),
        "grad_two": shape(flat_rows, width, dtype=F32),
        "dc": shape(flat_rows, width),
        "doc_unit": shape(HEAD_DIM, mine_total),
        "mem": shape(lay.mem_pad, width),
        "gelu": shape(flat_rows, ff),
        "du": shape(flat_rows, ff),
    }
    if parts > 1:
        kept["query"] = shape(HEAD_DIM, mine_total)
    gathered = {
        "dm_group": shape(4, flat_rows, width),
        "h3_group": shape(4, flat_rows, width),
        "out": shape(flat_rows, width),
        "h1_pack": shape(wide, total),
    }
    scratch = {
        "h1": shape(flat_rows, width),
        "tok": shape(3, wide, flat_rows),
        "codes": shape(8, total, dtype=F32),
        "code_tok": shape(lay.packs, 8, rows, dtype=F32),
        "kv_tok": shape(2, wide, lay.mem_pad),
        "keys_half": shape(half, HEAD_DIM, lay.mem_pad),
        "values_half": shape(half, HEAD_DIM, lay.mem_pad),
        "kv_found": shape(2, 2, NSEG, HEAD_DIM, span),
        "kv_twin": shape(2, NSEG, HEAD_DIM, span),
        "key": shape(total, HEAD_DIM),
        "low": shape(2, HEAD_DIM, mine_total),
        "h1_turned": shape(wide, flat_rows),
        "sent": shape(4, flat_rows, width),
        "arrived": shape(4, flat_rows, width),
        "r2": shape(flat_rows, width, dtype=F32),
        "down_sum": shape(flat_rows, width, dtype=F32),
        "up_sum": shape(flat_rows, width, dtype=F32),
    }
    if parts > 1:
        scratch["rows"] = shape(8, total, dtype=F32)
    scratch = {name: pltpu.VMEM(value.shape, value.dtype) for name, value in {**scratch, **kept}.items()}
    for name in late:
        scratch[name] = pltpu.VMEM(values[name].shape, values[name].dtype)
    semaphores = pltpu.SemaphoreType.DMA((10 * count + 35,))
    scratch = {"send_sem": semaphores, "recv_sem": semaphores, **scratch}
    scratch["own_sem"] = pltpu.SemaphoreType.DMA((48,))
    outs = {**kept, **gathered}
    anywhere = pl.BlockSpec(memory_space=pl.ANY)
    results = pl.pallas_call(
        functools.partial(forward_body, lay, names, late, list(outs), list(scratch)),
        out_shape=list(outs.values()),
        in_specs=[pl.BlockSpec(memory_space=pltpu.SMEM)]
        + [pl.BlockSpec(memory_space=pltpu.VMEM)] * len(early)
        + [anywhere] * len(late),
        out_specs=[anywhere] * len(outs),
        scratch_shapes=list(scratch.values()),
        compiler_params=pltpu.CompilerParams(
            collective_id=0, has_side_effects=True, vmem_limit_bytes=63 * 1024 * 1024
        ),
    )(*[values[name] for name in names])
    return dict(zip(outs, results, strict=True))


def reversed_bits(value, bits):
    return sum(((value >> b) & 1) << (bits - 1 - b) for b in range(bits))


class Halving:
    def __init__(self, links, bits, sums, arrivals, crossed=True):
        self.links, self.bits, self.crossed = links, bits, crossed
        self.sums, self.arrivals = sums, arrivals
        self.quarter = sums.shape[1] // 2
        self.jobs, self.pending = [], []

    def neighbour(self, kind, step):
        bit = self.bits[1 - step if self.crosses(kind) and step < 2 else step]
        return {"blk": self.links.me ^ (1 << bit)}

    def crosses(self, kind):
        return kind == 1 and self.crossed

    def add_job(self, column, width, make):
        here, started = pl.ds(column, width), []
        for kind in range(2):
            for half, quarter in enumerate((1, 3) if self.crosses(kind) else (2, 3)):
                rows = pl.ds(half * self.quarter, self.quarter)
                self.sums[kind, rows, here] = make(kind, quarter).astype(BF16)
            started.append(
                self.links.remote(
                    self.sums.at[kind, :, here],
                    self.arrivals[0].at[kind, :, here],
                    self.neighbour(kind, 0),
                )
            )
        self.jobs.append((here, make, started))

    def keep_jobs(self):
        for here, make, started in self.jobs:
            wait_all(started)
            for kind in range(2):
                for half, quarter in enumerate((0, 2) if self.crosses(kind) else (0, 1)):
                    rows = pl.ds(half * self.quarter, self.quarter)
                    arrived = self.arrivals[0][kind, rows, here].astype(F32)
                    self.sums[kind, rows, here] = (make(kind, quarter) + arrived).astype(BF16)
        self.send(1)

    def send(self, step):
        rows = self.sums.shape[1] >> step
        self.pending = [
            self.links.remote(
                self.sums.at[kind, pl.ds(rows, rows), :],
                self.arrivals[step].at[kind],
                self.neighbour(kind, step),
            )
            for kind in range(2)
        ]

    def receive(self, step, result=None):
        rows = self.sums.shape[1] >> step
        wait_all(self.pending)
        size = min(rows, 32)

        def add(index, _):
            here = pl.ds(pl.multiple_of(index * size, size), size)
            for kind in range(2):
                mine = self.sums[kind, here, :].astype(F32)
                total = mine + self.arrivals[step][kind, here, :].astype(F32)
                if result is None:
                    self.sums[kind, here, :] = total.astype(BF16)
                else:
                    result[kind, here, :] = total
            return 0

        lax.fori_loop(0, rows // size, add, 0)
        if step + 1 < len(self.bits):
            self.send(step + 1)


def arrivals_shapes(bits, width, columns):
    return [pltpu.VMEM((2, width >> (step + 1), columns), BF16) for step in range(bits)]


OUTS = (
    "input", "memory_own", "memory_other", "query", "key", "value", "out", "cross_query", "cross_key",
    "cross_value", "cross_out", "up", "down", "gains",
)


def backward_body(lay, names, late, scratch_names, *refs):
    r = dict(zip(names, refs, strict=False))
    o = dict(zip(OUTS, refs[len(names) :], strict=False))
    s = dict(zip(scratch_names, refs[len(names) + len(OUTS) :], strict=True))
    far = dict(r)
    count, parts, half, rows = lay.count, lay.parts, lay.half, lay.rows
    links = Links(lay, s)
    me, core, head, pack, part = links.me, links.core, links.head, links.pack, links.part
    bits = count.bit_length() - 1
    flat_rows, width = r["dc"].shape
    wide = r["w_out"].shape[0]
    total = r["qkv"].shape[2]
    mine_total = total // parts
    share = width // count
    block = min(512 if parts == 1 else 256, mine_total)
    links.announce(everyone=True)
    loading = {}

    def load(name):
        loading[name] = links.local(r[name], s["in_" + late[name]])

    for name, home in late.items():
        if name == home:
            load(name)
    own_rows = pl.ds(pl.multiple_of(me * share, share), share)
    row_copies = [
        links.local(far[name].at[own_rows, :], s["rows_" + name])
        for name in ("w_q", "w_k", "w_v", "w_cross_query", "w_up")
    ]
    h1_copy = links.local(r["h1_pack"].at[:, pl.ds(0, s["h1"].shape[1])], s["h1"])

    def ready(*wanted):
        for name in wanted:
            loading[name].wait()
            r[name] = s["in_" + late[name]]

    def relative(target, value, shift=0, column=0):
        number, most = count >> shift, s["turn"].shape[1]
        size_rows = width // number
        for start in range(0, value.shape[0], most):
            size = min(most, value.shape[0] - start)
            s["turn"][:, :size] = value[start : start + size, :].T
            for place in range(number):
                chunk = (me >> shift) ^ reversed_bits(place, bits - shift)
                target[pl.ds(place * size_rows, size_rows), column + start : column + start + size] = s[
                    "turn"
                ][pl.ds(pl.multiple_of(chunk * size_rows, size_rows), size_rows), :size]

    quarter = width // 4

    def quarter_of(ref, index):
        return ref[pl.ds(index * quarter, quarter), :]

    def batch(name, chosen, crossed=True):
        arrivals = [s[f"{name}_{i}"] for i in range(len(chosen))]
        return Halving(links, chosen, s[name + "_sums"], arrivals, crossed)

    piece = wide // 2

    def weight_job(target, place, left, right):
        def make(kind, index):
            return dot(quarter_of(left, index), right[kind * piece : (kind + 1) * piece, :], 1, 1)

        target.add_job(place * piece, piece, make)

    group = 4
    slice_width = s["gelu_group"].shape[2]
    links.all_here(everyone=True)

    def to_group(name):
        started = []
        for offset in range(group):
            number = lax.rem(me ^ offset, group)
            columns = pl.ds(pl.multiple_of(number * slice_width, slice_width), slice_width)
            started.append(links.to(offset, r[name].at[:, columns], s[name + "_group"].at[offset]))
        return started

    gelu_copies = to_group("gelu")

    ready("kv_slots", "cross_unit", "cross_att", "doc_unit")
    slots, span = r["kv_slots"].shape[0], r["kv_slots"].shape[3]
    s["cross_key"][...] = r["kv_slots"][0, 0].T
    s["cross_value"][...] = r["kv_slots"][0, 1].T
    s["cross_acc"][...] = jnp.zeros_like(s["cross_acc"])
    present = page_rows(span, lay.mem_pad, lay.mem_rows)

    def cross_block(here, slot, key_rows, value_rows):
        query, grad = r["cross_unit"][:, here], r["doc_unit"][:, here]
        row_dot = jnp.sum(grad.astype(F32) * r["cross_att"][:, here], axis=0, keepdims=True)
        scores = jnp.dot(key_rows, query, preferred_element_type=F32)
        allowed = present & (r["qslot"][:, here] == float(slot))
        weights = jnp.where(allowed, jnp.exp2(scores * EXP2_SCALE - r["cross_log"][:, here]), 0.0)
        weight_grad = jnp.dot(value_rows, grad, preferred_element_type=F32)
        score_grad = (weights * (weight_grad - row_dot)).astype(BF16)
        dq = jnp.dot(r["kv_slots"][slot, 0], score_grad, preferred_element_type=F32)
        return dq, dot(query, score_grad, 1, 1), dot(grad, weights.astype(BF16), 1, 1)

    narrow = min(256, mine_total)

    def main_slot(index, _):
        here = pl.ds(pl.multiple_of(index * narrow, narrow), narrow)
        dq, dk, dv = cross_block(here, 0, s["cross_key"][...], s["cross_value"][...])
        s["dq_acc"][:, here] = dq
        s["cross_acc"][0] += dk
        s["cross_acc"][1] += dv
        return 0

    lax.fori_loop(0, mine_total // narrow, main_slot, 0)
    s["dkv_low"][1, 0, 0] = (s["cross_acc"][0] * SCALE).astype(BF16)
    s["dkv_low"][1, 0, 1] = s["cross_acc"][1].astype(BF16)
    for slot in range(1, slots):
        key_rows, value_rows = r["kv_slots"][slot, 0].T, r["kv_slots"][slot, 1].T
        ends = []
        for start in (0, mine_total - LANES):
            here = pl.ds(start, LANES)
            ends.append(cross_block(here, slot, key_rows, value_rows))
            s["dq_acc"][:, here] += ends[-1][0]
        s["dkv_low"][1, slot, 0] = ((ends[0][1] + ends[1][1]) * SCALE).astype(BF16)
        s["dkv_low"][1, slot, 1] = (ends[0][2] + ends[1][2]).astype(BF16)
    load("att")
    s["dq_low"][...] = (s["dq_acc"][...] * SCALE).astype(BF16)
    dqc_copies = links.collect(s["dq_low"], s["in_small"].at[0])
    is_first = (r["longest"][:1, :1] < 0.5).astype(F32)
    is_second = (r["longest"][:1, :1] < 1.5).astype(F32) - is_first
    is_third = 1.0 - is_first - is_second
    for kind in range(2):
        found = [s["dkv_low"][1, slot, kind].astype(F32) for slot in range(slots)]
        for slot in range(slots):
            value = (
                found[slot] * is_first
                + found[(slot + 2) % slots] * is_second
                + found[(slot + 1) % slots] * is_third
            )
            s["dkv_low"][0, slot, kind] = value.astype(BF16)
    def to_twin(slot):
        return links.remote(s["dkv_low"].at[0, slot], s["dkv_twin"].at[slot], {"blk": me ^ half})

    twin_copies = [to_twin(slot) for slot in range(slots)]

    ready("dm_group")
    for offset in range(group):
        relative(s["rel_dm"], r["dm_group"].at[offset], 2, offset * flat_rows)

    def feed_job(left, right):
        def make(kind, index):
            here = slice(kind * slice_width // 2, (kind + 1) * slice_width // 2)
            return dot(
                quarter_of(left, index), right[:, :, here].reshape(group * flat_rows, slice_width // 2), 1, 0
            )

        return make

    down, up = [batch(name, range(2, bits), crossed=False) for name in ("down", "up")]
    wait_all(gelu_copies)
    down.add_job(0, slice_width // 2, feed_job(s["rel_dm"], s["gelu_group"]))
    du_copies = to_group("du")
    middle, pages = batch("middle", range(bits)), batch("pages", range(bits))
    ready("cross_mixed")
    relative(s["rel_dc"], r["dc"])
    weight_job(middle, 0, s["rel_dc"], r["cross_mixed"])
    ready("h3_group")
    for offset in range(group):
        relative(s["rel_h3"], r["h3_group"].at[offset], 2, offset * flat_rows)

    ready("w_cross_query")
    wait_all(dqc_copies)
    tp_copies = []
    for start in range(0, flat_rows, rows):
        here = slice(start, start + rows)
        s["tp_send"][here, :] = dot(s["in_small"][0, :, here].T, r["w_cross_query"][...], 1, 1).astype(BF16)
        tp_copies.append(
            links.to_other_core(s["tp_send"].at[pl.ds(start, rows)], s["tp_recv"].at[0, pl.ds(start, rows)])
        )
    ready("h2", "r1", "grad_two")
    relative(s["rel_h2"], r["h2"])
    load("x")
    weight_job(middle, 1, s["rel_h2"], s["in_small"].at[0])
    wait_all(tp_copies)

    def both_cores(index):
        def grad(here):
            return s["tp_send"][here, :].astype(F32) + s["tp_recv"][index, here, :].astype(F32)

        return grad

    norm_back_rows(
        s["grad_one"],
        both_cores(0),
        lambda here: r["r1"][here, :],
        r["gain_two"],
        lambda here: r["grad_two"][here, :],
        s["da"],
    )
    ready("w_out")
    s["out_small"][0] = dot(r["w_out"][...], s["da"][...], 1, 1).astype(BF16)
    do_copies = links.spread(s["out_small"].at[0], s["do_unit"])
    load("w_q")
    ready("mixed")
    relative(s["rel_da"], s["da"])
    weight_job(middle, 2, s["rel_da"], r["mixed"])
    def hot(side, slot, page):
        wanted = r["segment_page"][pack if side == 0 else 1 - pack, slot]
        return jnp.where(wanted == pack * lay.pages_half + page, 1.0, 0.0)

    wait_all(twin_copies)
    for page in range(lay.pages_half):
        for piece_index in range(lay.pieces):
            here = slice(piece_index * lay.mem_pad, (piece_index + 1) * lay.mem_pad)
            value = None
            for side, source in enumerate((s["dkv_low"].at[0], s["dkv_twin"])):
                for slot in range(slots):
                    term = hot(side, slot, page) * source[slot, :, :, here].astype(F32)
                    value = term if value is None else value + term
            s["page_grad"][page * lay.pieces + piece_index] = value.astype(BF16)
    memory_copies = []
    for offset in range(half):
        source = s["page_grad"].at[lax.rem(me ^ offset, half)]
        place = s["mem_recv"].at[part, :, pl.ds(head * HEAD_DIM, HEAD_DIM), :]
        memory_copies.append(links.to(offset, source, place))

    ready("qkv", "att")
    if parts > 1:
        ready("query")
    s["dq_acc"][...] = jnp.zeros_like(s["dq_acc"])
    wait_all(do_copies)

    def key_block(key_index, _):
        here = pl.ds(pl.multiple_of(key_index * block, block), block)
        keys, values = r["qkv"][1, :, here], r["qkv"][2, :, here]
        key_rows, value_rows = keys.T, values.T
        codes = jnp.broadcast_to(r["code"][:, here], (8, block)).T[:, :1]

        def fold(index, grads, causal):
            dk, dv = grads
            columns = pl.ds(pl.multiple_of(index * block, block), block)
            query = r["query"][:, columns] if parts > 1 else r["qkv"][0, :, columns]
            grad = s["do_unit"][:, columns]
            row_dot = jnp.sum(grad.astype(F32) * r["att"][:, columns], axis=0, keepdims=True)
            scores = jnp.dot(key_rows, query, preferred_element_type=F32)
            allowed = codes == r["qseg"][:, columns]
            if causal:
                places = index * block + lax.broadcasted_iota(jnp.int32, (1, block), 1)
                positions = ((places // rows) * parts + part) * rows + places % rows
                key_places = key_index * block + lax.broadcasted_iota(jnp.int32, (block, block), 0)
                allowed = allowed & (key_places <= positions)
            weights = jnp.where(allowed, jnp.exp2(scores * EXP2_SCALE - r["log"][:, columns]), 0.0)
            weight_grad = jnp.dot(value_rows, grad, preferred_element_type=F32)
            score_grad = (weights * (weight_grad - row_dot)).astype(BF16)
            s["dq_acc"][:, columns] += jnp.dot(keys, score_grad, preferred_element_type=F32)
            return (dk + dot(query, score_grad, 1, 1), dv + dot(grad, weights.astype(BF16), 1, 1))

        zeros = jnp.zeros((HEAD_DIM, block), F32)
        first_index = key_index // parts
        grads = fold(first_index, (zeros, zeros), True)
        dk, dv = lax.fori_loop(
            first_index + 1, mine_total // block, lambda i, g: fold(i, g, False), grads
        )
        r["qkv"][1, :, here] = (dk * SCALE).astype(BF16)
        r["qkv"][2, :, here] = dv.astype(BF16)
        return 0

    lax.fori_loop(0, total // block, key_block, 0)
    if parts == 1:
        r["qkv"][0] = (s["dq_acc"][...] * SCALE).astype(BF16)
        dq_copies = links.collect(r["qkv"].at[0], s["in_small"].at[1])
    else:
        r["qkv"][0] = jnp.zeros((HEAD_DIM, total), BF16)
        for number in range(count // parts):
            value = (s["dq_acc"][:, number * rows : (number + 1) * rows] * SCALE).astype(BF16)
            s["dq_low"][:, number * rows : (number + 1) * rows] = value
            r["qkv"][0, :, pl.ds((number * parts + part) * rows, rows)] = value
        dq_copies = links.collect(s["dq_low"], s["in_small"].at[1])
    unit_copy = links.to_other_core(r["qkv"], s["unit_other"])
    dkv_copies = []
    for offset in range(count):
        peer = me ^ offset
        source = r["qkv"].at[pl.ds(1, 2), :, pl.ds(peer * rows, rows)]
        place = s["dkv_recv"].at[part, :, pl.ds(head * HEAD_DIM, HEAD_DIM), pl.ds(pack * rows, rows)]
        dkv_copies.append(links.to(offset, source, place))
    unit_copy.wait()
    first_send, first_recv = links.take(count), links.take(count)
    number_to = count // 2

    def first_copy(index, number, source_device=None):
        target_core = core if index == 0 else 1 - core
        slot = me if source_device is None else source_device
        return pltpu.make_async_remote_copy(
            src_ref=s["first_low"].at[index, pl.ds(number * share, share), :],
            dst_ref=s["first_recv"].at[slot],
            send_sem=links.send_sem.at[first_send + index * number_to + number],
            recv_sem=links.recv_sem.at[first_recv + slot],
            device_id={"blk": core * number_to + number, "tp": target_core},
            device_id_type=MESH,
        )

    for index, ref in enumerate((r["qkv"], s["unit_other"])):
        value, most = None, s["h1"].shape[1]
        for start in range(0, total, most):
            if start + index > 0 and total > most:
                h1_copy = links.local(r["h1_pack"].at[:, pl.ds(start, most)], s["h1"])
            if start + index == 0 or total > most:
                h1_copy.wait()
            term = dot(s["h1"][...], ref[:, :, start : start + most].reshape(3 * HEAD_DIM, most), 1, 1)
            value = term if value is None else value + term
        s["first_low"][index] = value.astype(BF16)
        for number in range(number_to):
            if index == 1:
                first_copy(index, number).start()
                continue
            own = me == core * number_to + number

            @pl.when(jnp.logical_not(own))
            def _(number=number):
                first_copy(0, number).start()

            @pl.when(own)
            def _(number=number):
                pltpu.make_async_copy(
                    s["first_low"].at[0, pl.ds(number * share, share), :],
                    s["first_recv"].at[me],
                    links.recv_sem.at[first_recv + me],
                ).start()

    down.keep_jobs()
    middle.keep_jobs()

    ready("mem", "w_ck", "w_cv")
    wait_all(memory_copies)
    if parts > 1:
        for kind in range(2):
            value = s["mem_recv"][0, kind].astype(F32)
            for index in range(1, parts):
                value = value + s["mem_recv"][index, kind].astype(F32)
            s["mem_recv"][0, kind] = value.astype(BF16)
    relative(s["rel_mem"], r["mem"])
    weight_job(pages, 0, s["rel_mem"], s["mem_recv"].at[0, 0])
    weight_job(pages, 1, s["rel_mem"], s["mem_recv"].at[0, 1])
    for start in range(0, lay.mem_pad, LANES):
        here = slice(start, start + LANES)
        s["mem_send"][here, :] = (
            dot(s["mem_recv"][0, 0, :, here].T, r["w_ck"][...], 1, 1)
            + dot(s["mem_recv"][0, 1, :, here].T, r["w_cv"][...], 1, 1)
        ).astype(BF16)
    wait_all(du_copies)
    up.add_job(0, slice_width // 2, feed_job(s["rel_h3"], s["du_group"]))
    load("w_k")
    load("w_v")
    mem_copies = [
        links.to_other_core(s["mem_send"], o["memory_other"]),
        links.local(s["mem_send"], o["memory_own"]),
    ]

    ready("w_q", "w_k", "w_v", "x")
    wait_all(dq_copies)
    wait_all(dkv_copies)
    if parts > 1:
        for kind in range(2):
            value = s["dkv_recv"][0, kind].astype(F32)
            for index in range(1, parts):
                value = value + s["dkv_recv"][index, kind].astype(F32)
            s["dkv_recv"][0, kind] = value.astype(BF16)
    pieces = (s["in_small"].at[1], s["dkv_recv"].at[0, 0], s["dkv_recv"].at[0, 1])
    tp_copies = []
    for start in range(0, flat_rows, rows):
        here = slice(start, start + rows)
        s["tp_send"][here, :] = sum(
            dot(value[:, here].T, r[weight][...], 1, 1)
            for value, weight in zip(pieces, ("w_q", "w_k", "w_v"), strict=True)
        ).astype(BF16)
        tp_copies.append(
            links.to_other_core(s["tp_send"].at[pl.ds(start, rows)], s["tp_recv"].at[1, pl.ds(start, rows)])
        )
    middle.receive(1)
    wait_all(tp_copies)
    norm_back_rows(
        o["input"],
        both_cores(1),
        lambda here: r["x"][here, :].astype(F32),
        r["gain_one"],
        lambda here: s["grad_one"][here, :],
    )
    pages.keep_jobs()
    up.keep_jobs()
    down.receive(1)
    up.receive(1)
    for step in range(2, bits - 2):
        down.receive(step)
        up.receive(step)
    final_copies = []
    for offset in range(group):
        rows_to = pl.ds(lax.rem(me ^ offset, group) * share, share)
        for index, sums in enumerate((s["down_sums"], s["up_sums"])):
            place = s["feed_last"].at[index, lax.rem(me, group)]
            final_copies.append(links.to(offset, sums.at[:, rows_to, :], place))

    for step in range(2, bits + 1):
        pages.receive(step - 1, s["pages_result"] if step == bits else None)
        if step < bits:
            middle.receive(step, s["middle_result"] if step == bits - 1 else None)
    wait_all(final_copies)
    for number in range(group):
        for kind in range(2):
            start = number * slice_width + kind * slice_width // 2
            here = slice(start, start + slice_width // 2)
            o["down"][:, here] = s["feed_last"][0, number, kind].astype(F32)
            o["up"][:, here] = s["feed_last"][1, number, kind].astype(F32)
    for kind in range(2):
        here = slice(kind * piece, (kind + 1) * piece)
        o["cross_out"][:, here] = s["middle_result"][kind, :, :piece]
        o["cross_query"][:, here] = s["middle_result"][kind, :, piece : 2 * piece]
        o["out"][:, here] = s["middle_result"][kind, :, 2 * piece :]
        o["cross_key"][:, here] = s["pages_result"][kind, :, :piece]
        o["cross_value"][:, here] = s["pages_result"][kind, :, piece:]
    for index in range(2):
        for number in range(number_to):
            if index == 1:
                first_copy(index, number).wait_send()
            else:

                @pl.when(me != core * number_to + number)
                def _(number=number):
                    first_copy(0, number).wait_send()

    for device in range(count):
        first_copy(0, 0, device).wait_recv()
    for index in range(lay.heads):
        value = None
        for side in range(2):
            for number in range(parts):
                term = s["first_recv"][side * half + index * parts + number].astype(F32)
                value = term if value is None else value + term
        for place, name in enumerate(("query", "key", "value")):
            o[name][:, index * HEAD_DIM : (index + 1) * HEAD_DIM] = value[
                :, place * HEAD_DIM : (place + 1) * HEAD_DIM
            ]

    wait_all(row_copies)
    lanes = lax.broadcasted_iota(jnp.int32, (share, LANES), 1)
    sums, gains = jnp.zeros((share, LANES), F32), jnp.ones((share, LANES), F32)
    pairs = (
        ("gain_one", (("w_q", "query"), ("w_k", "key"), ("w_v", "value"))),
        ("gain_two", (("w_cross_query", "cross_query"),)),
        ("gain_three", (("w_up", "up"),)),
    )
    for index, (gain, terms) in enumerate(pairs):
        value = sum(
            jnp.sum(s["rows_" + weight][...].astype(F32) * o[name][...], axis=1, keepdims=True)
            for weight, name in terms
        )
        s["gain_turned"][...] = jnp.broadcast_to(r[gain][...], (8, width)).T
        sums = jnp.where(lanes == index, value, sums)
        gains = jnp.where(lanes == index, s["gain_turned"][own_rows, :1], gains)
    s["gain_sums"][0] = sums
    links.to_other_core(s["gain_sums"].at[0], s["gain_sums"].at[1]).wait()
    o["gains"][...] = ((s["gain_sums"][0] + s["gain_sums"][1]) / gains).T[:8, :]
    wait_all(mem_copies)
    assert links.used <= links.send_sem.shape[0] and links.own_used <= links.own_sem.shape[0]


def backward(lay, values, ff):
    parts, count, half, rows = lay.parts, lay.count, lay.half, lay.rows
    flat_rows, width = values["dc"].shape
    wide = lay.heads * HEAD_DIM
    total = count * rows
    mine_total = total // parts
    span = lay.pieces * lay.mem_pad
    bits = count.bit_length() - 1
    late = [
        "doc_unit", "kv_slots", "cross_unit", "cross_att", "w_out", "dm_group", "h3_group",
        "cross_mixed", "w_cross_query", "r1", "grad_two", "mixed", "qkv", "mem", "h2", "w_ck", "w_cv",
    ]
    if parts > 1:
        late.append("query")
    late = {name: name for name in late}
    late.update(w_q="w_cross_query", w_k="w_ck", w_v="w_cv", att="cross_att", x="h2")
    far = ["h1_pack", "gelu", "du", "w_up"]
    early = [name for name in values if name not in late and name not in far + ["segment_page"]]
    names = ["segment_page"] + early + list(late) + far
    vmem, anywhere = pl.BlockSpec(memory_space=pltpu.VMEM), pl.BlockSpec(memory_space=pl.ANY)

    def buffer(*shape, dtype=BF16):
        return pltpu.VMEM(shape, dtype)

    share = width // count
    scratch = {
        "send_sem": pltpu.SemaphoreType.DMA((4 * count + 87,)),
        "recv_sem": pltpu.SemaphoreType.DMA((4 * count + 87,)),
        "own_sem": pltpu.SemaphoreType.DMA((48,)),
        "out_small": buffer(1, wide, flat_rows),
        "in_small": buffer(2, wide, flat_rows),
        "do_unit": buffer(HEAD_DIM, mine_total),
        "dq_acc": buffer(HEAD_DIM, mine_total, dtype=F32),
        "dq_low": buffer(HEAD_DIM, mine_total),
        "turn": buffer(width, flat_rows),
        "rel_dm": buffer(width, 4 * flat_rows),
        "rel_h3": buffer(width, 4 * flat_rows),
        "rel_dc": buffer(width, flat_rows),
        "rel_h2": buffer(width, flat_rows),
        "rel_da": buffer(width, flat_rows),
        "rel_mem": buffer(width, lay.mem_pad),
        "feed_last": buffer(2, 4, 2, share, ff // 8),
        "gelu_group": buffer(4, flat_rows, ff // 4),
        "du_group": buffer(4, flat_rows, ff // 4),
        "h1": buffer(wide, min(total, 2048)),
        "cross_key": buffer(span, HEAD_DIM),
        "cross_value": buffer(span, HEAD_DIM),
        "cross_acc": buffer(2, HEAD_DIM, span, dtype=F32),
        "dkv_low": buffer(2, NSEG, 2, HEAD_DIM, span),
        "dkv_twin": buffer(NSEG, 2, HEAD_DIM, span),
        "page_grad": buffer(half, 2, HEAD_DIM, lay.mem_pad),
        "mem_recv": buffer(parts, 2, wide, lay.mem_pad),
        "mem_send": buffer(lay.mem_pad, width),
        "tp_send": buffer(flat_rows, width),
        "tp_recv": buffer(2, flat_rows, width),
        "grad_one": buffer(flat_rows, width, dtype=F32),
        "da": buffer(flat_rows, width),
        "dkv_recv": buffer(parts, 2, wide, flat_rows),
        "unit_other": buffer(3, HEAD_DIM, total),
        "first_low": buffer(2, wide, 3 * HEAD_DIM),
        "first_recv": buffer(count, share, 3 * HEAD_DIM),
        "middle_result": buffer(2, share, 3 * wide // 2, dtype=F32),
        "pages_result": buffer(2, share, wide, dtype=F32),
        "gain_turned": buffer(width, 8, dtype=F32),
        "gain_sums": buffer(2, share, LANES, dtype=F32),
        "rows_w_up": buffer(share, ff),
    }
    for name in ("w_q", "w_k", "w_v", "w_cross_query"):
        scratch["rows_" + name] = buffer(share, wide)
    columns = {"down": ff // 8, "up": ff // 8, "middle": 3 * wide // 2, "pages": wide}
    for name, number in columns.items():
        scratch[name + "_sums"] = buffer(2, width // 2, number)
        steps = bits - 2 if name in ("down", "up") else bits
        for index, shape in enumerate(arrivals_shapes(steps, width, number)):
            scratch[f"{name}_{index}"] = shape
    homes = {}
    for name, home in late.items():
        homes.setdefault(home, values[name])
    for home, value in homes.items():
        scratch["in_" + home] = pltpu.VMEM(value.shape, value.dtype)

    shapes = {"up": (share, ff), "down": (share, ff), "gains": (8, share)}
    outs = {name: jax.ShapeDtypeStruct(shapes.get(name, (share, wide)), F32) for name in OUTS}
    outs["input"] = jax.ShapeDtypeStruct((flat_rows, width), F32)
    for name in ("memory_own", "memory_other"):
        outs[name] = jax.ShapeDtypeStruct((lay.mem_pad, width), BF16)
    results = pl.pallas_call(
        functools.partial(backward_body, lay, names, late, list(scratch)),
        out_shape=list(outs.values()),
        in_specs=[pl.BlockSpec(memory_space=pltpu.SMEM)]
        + [vmem] * len(early)
        + [anywhere] * (len(late) + len(far)),
        out_specs=[anywhere if name.startswith("memory") else vmem for name in OUTS],
        scratch_shapes=list(scratch.values()),
        compiler_params=pltpu.CompilerParams(
            collective_id=1, has_side_effects=True, vmem_limit_bytes=63 * 1024 * 1024 + 512 * 1024
        ),
    )(*[values[name] for name in names])
    return dict(zip(OUTS, results, strict=True))


def local(
    tokens,
    memory,
    segment_ids,
    token_valid,
    segment_page,
    gain_one,
    weight_query,
    weight_key,
    weight_value,
    weight_out,
    gain_two,
    cross_query,
    cross_key,
    cross_value,
    cross_out,
    gain_three,
    weight_up,
    weight_down,
    cotangent,
):
    packs, rows, width = tokens.shape
    wide, ff = weight_query.shape[1], weight_up.shape[1]
    lay = Layout(lax.axis_size("blk"), packs, wide // HEAD_DIM, rows, memory.shape[0])
    flat_rows = packs * rows
    x = tokens.reshape(flat_rows, width)
    kept = forward(
        lay,
        {
            "segment_page": segment_page,
            "x": x,
            "segment_ids": segment_ids,
            "token_valid": token_valid,
            "memory": memory,
            "gain_one": gain_one[None],
            "gain_two": gain_two[None],
            "gain_three": gain_three[None],
            "w_q": weight_query,
            "w_k": weight_key,
            "w_v": weight_value,
            "w_ck": cross_key,
            "w_cv": cross_value,
            "cot": cotangent.reshape(flat_rows, width),
            "w_out": weight_out,
            "w_cross_query": cross_query,
            "w_cross_out": cross_out,
            "w_up": weight_up,
            "w_down": weight_down,
        },
        ff,
    )
    out = kept.pop("out").reshape(packs, rows, width)
    grads = backward(
        lay,
        {
            **kept,
            "segment_page": segment_page,
            "x": x,
            "gain_one": gain_one[None],
            "gain_two": gain_two[None],
            "gain_three": gain_three[None],
            "w_cross_query": cross_query,
            "w_out": weight_out,
            "w_ck": cross_key,
            "w_cv": cross_value,
            "w_q": weight_query,
            "w_k": weight_key,
            "w_v": weight_value,
            "w_up": weight_up,
        },
        ff,
    )
    grad_memory = (grads["memory_own"].astype(F32) + grads["memory_other"].astype(F32))[: lay.mem_rows]
    return (
        out,
        grads["input"].reshape(packs, rows, width),
        grad_memory,
        grads["query"],
        grads["key"],
        grads["value"],
        grads["out"].T,
        grads["cross_query"],
        grads["cross_key"],
        grads["cross_value"],
        grads["cross_out"].T,
        grads["up"],
        grads["down"].T,
        grads["gains"][0],
        grads["gains"][1],
        grads["gains"][2],
    )


def solution(mesh):
    in_specs = (
        P(None, "blk", None),
        P("blk", None),
        P(None, "blk"),
        P(None, "blk"),
        P(),
        P(),
        P(None, "tp"),
        P(None, "tp"),
        P(None, "tp"),
        P("tp", None),
        P(),
        P(None, "tp"),
        P(None, "tp"),
        P(None, "tp"),
        P("tp", None),
        P(),
        P(None, "tp"),
        P("tp", None),
        P(None, "blk", None),
    )
    out_specs = (
        P(None, "blk", None),
        P(None, "blk", None),
        P("blk", None),
        P("blk", "tp"),
        P("blk", "tp"),
        P("blk", "tp"),
        P("tp", "blk"),
        P("blk", "tp"),
        P("blk", "tp"),
        P("blk", "tp"),
        P("tp", "blk"),
        P("blk", "tp"),
        P("tp", "blk"),
        P("blk"),
        P("blk"),
        P("blk"),
    )
    return jax.shard_map(local, mesh=mesh, in_specs=in_specs, out_specs=out_specs, check_vma=False)
```

```python
import functools

import jax
import jax.numpy as jnp
from jax import lax
from jax.experimental import pallas as pl
from jax.experimental.pallas import tpu as pltpu
from jax.sharding import PartitionSpec as P

MEM_LEN = 588
HEAD_DIM = 64
NSEG = 3
EPS = 1e-05
NEG = -1e30
EXP2_SCALE = HEAD_DIM**-0.5 * 1.4426950408889634
SCALE = HEAD_DIM**-0.5
LANES = 128
BF16 = jnp.bfloat16
F32 = jnp.float32
MESH = pl.DeviceIdType.MESH


def dot(left, right, contract_left, contract_right):
    return lax.dot_general(
        left, right, (((contract_left,), (contract_right,)), ((), ())), preferred_element_type=F32
    )


def wait_all(copies):
    for copy in copies:
        copy.wait()


class Layout:
    def __init__(self, count, packs, heads, rows, mem_rows):
        self.count, self.packs, self.heads, self.rows = count, packs, heads, rows
        self.half = count // packs
        self.parts = self.half // heads
        self.mem_rows = mem_rows
        self.mem_pad = -(-mem_rows // LANES) * LANES
        self.pieces = MEM_LEN // mem_rows
        self.pages_half = self.half // self.pieces

    def head(self, device):
        return lax.rem(device, self.half) // self.parts


def page_rows(span, piece, real):
    places = lax.broadcasted_iota(jnp.int32, (span, 1), 0)
    return lax.rem(places, piece) < real


def erf(value):
    x = jnp.clip(value, -3.832506856900711, 3.832506856900711)
    square = x * x
    top = jnp.float32(0.00022905065861350646)
    for coefficient in (0.0034082910107109506, 0.050955695062380861, 0.18520832239976145, 1.128379143519084):
        top = top * square + coefficient
    low = jnp.float32(-1.1791602954361697e-7)
    for coefficient in (
        0.000023547966471313185,
        0.0010179625278914885,
        0.014070470171167667,
        0.11098505178285362,
        0.49746925110067538,
        1.0,
    ):
        low = low * square + coefficient
    return x * top / low


def normed_rows(source, gain, low):
    step = 32

    def body(index, _):
        rows = pl.ds(pl.multiple_of(index * step, step), step)
        value = source(rows)
        centred = value - jnp.mean(value, axis=1, keepdims=True)
        inv_std = lax.rsqrt(jnp.mean(centred * centred, axis=1, keepdims=True) + EPS)
        low[rows, :] = (centred * inv_std * gain[...]).astype(BF16)
        return 0

    lax.fori_loop(0, low.shape[0] // step, body, 0)


def norm_back_rows(target, grad, source, gain, residual, low=None):
    step = 32

    def body(index, _):
        rows = pl.ds(pl.multiple_of(index * step, step), step)
        value = source(rows)
        centred = value - jnp.mean(value, axis=1, keepdims=True)
        inv_std = lax.rsqrt(jnp.mean(centred * centred, axis=1, keepdims=True) + EPS)
        z = centred * inv_std
        w = grad(rows) * gain[...]
        inner = w - jnp.mean(w, axis=1, keepdims=True) - z * jnp.mean(w * z, axis=1, keepdims=True)
        value = residual(rows) + inner * inv_std
        target[rows, :] = value
        if low is not None:
            low[rows, :] = value.astype(BF16)
        return 0

    lax.fori_loop(0, target.shape[0] // step, body, 0)


class Exchange:
    def __init__(self, links, received, sent):
        self.links, self.index = links, links.take()
        self.received, self.sent = received, sent

    def start(self, offset, source, target):
        if offset == 0:
            self.keep(source, target)
        else:
            self.links.described(self.index, source, target, {"blk": self.links.me ^ offset}).start()

    def keep(self, source, target):
        pltpu.make_async_copy(source, target, self.links.recv_sem.at[self.index]).start()

    def wait(self):
        for sem, buffers in ((self.links.recv_sem, self.received), (self.links.send_sem, self.sent)):
            for buffer in buffers:
                pltpu.make_async_copy(buffer, buffer, sem.at[self.index]).wait()


class Links:
    def __init__(self, lay, scratch):
        self.lay = lay
        self.me, self.core = lax.axis_index("blk"), lax.axis_index("tp")
        self.head, self.pack = lay.head(self.me), self.me // lay.half
        self.part = lax.rem(self.me, lay.parts)
        self.send_sem, self.recv_sem, self.used = scratch["send_sem"], scratch["recv_sem"], 0
        self.own_sem, self.own_used = scratch["own_sem"], 0
        self.barrier = pltpu.get_barrier_semaphore()

    def page_of(self, pages, side, slot):
        place = pages[self.pack if side == 0 else 1 - self.pack, slot] - self.pack * self.lay.pages_half
        inside = (place >= 0) & (place < self.lay.pages_half)
        return jnp.clip(place, 0, self.lay.pages_half - 1), jnp.where(inside, 1.0, 0.0)

    def announce(self, everyone=False):
        for offset in range(self.lay.count):
            if offset > 0:
                self.signal(offset, self.core)
            if offset == 0 or everyone:
                self.signal(offset, 1 - self.core)

    def signal(self, offset, core):
        device = {"blk": self.me ^ offset, "tp": core}
        pl.semaphore_signal(self.barrier, inc=1, device_id=device, device_id_type=MESH)

    def all_here(self, everyone=False):
        pl.semaphore_wait(self.barrier, (2 if everyone else 1) * self.lay.count - (1 if everyone else 0))

    def take(self, number=1):
        index, self.used = self.used, self.used + number
        return index

    def described(self, index, source, target, device):
        return pltpu.make_async_remote_copy(
            src_ref=source,
            dst_ref=target,
            send_sem=self.send_sem.at[index],
            recv_sem=self.recv_sem.at[index],
            device_id=device,
            device_id_type=MESH,
        )

    def remote(self, source, target, device):
        copy = self.described(self.take(), source, target, device)
        copy.start()
        return copy

    def local(self, source, target):
        copy = pltpu.make_async_copy(source, target, self.own_sem.at[self.own_used])
        self.own_used += 1
        copy.start()
        return copy

    def to(self, offset, source, target):
        if offset == 0:
            return self.local(source, target)
        return self.remote(source, target, {"blk": self.me ^ offset})

    def to_other_core(self, source, target):
        return self.remote(source, target, {"tp": 1 - self.core})

    def spread(self, source, target, every=False):
        lay, step = self.lay, 1 if every else self.lay.parts
        most = lay.count // step * lay.rows
        exchange = Exchange(self, [target], [target.at[:, pl.ds(0, most - lay.rows)]])
        for offset in range(0, lay.count, step):
            peer = self.me ^ offset
            piece = source.at[
                pl.ds(lay.head(peer) * HEAD_DIM, HEAD_DIM), pl.ds((peer // lay.half) * lay.rows, lay.rows)
            ]
            exchange.start(offset, piece, target.at[:, pl.ds((self.me // step) * lay.rows, lay.rows)])
        return exchange

    def unit_place(self, target):
        lay = self.lay
        return target.at[pl.ds(self.head * HEAD_DIM, HEAD_DIM), pl.ds(self.pack * lay.rows, lay.rows)]

    def collect(self, source, target):
        lay, exchange = self.lay, self.to_tokens(target)
        for offset in range(0, lay.count, lay.parts):
            peer = self.me ^ offset
            piece = source.at[:, pl.ds((peer // lay.parts) * lay.rows, lay.rows)]
            exchange.start(offset, piece, self.unit_place(target))
        return exchange

    def to_tokens(self, target):
        return Exchange(self, [target], [target.at[pl.ds(0, (2 * self.lay.heads - 1) * HEAD_DIM // 2), :]])

    def collect_later(self, source, target):
        lay, exchange = self.lay, self.to_tokens(target)

        def send(number):
            peer = number * lay.parts + self.part
            piece, place = source.at[:, pl.ds(number * lay.rows, lay.rows)], self.unit_place(target)

            @pl.when(peer != self.me)
            def _():
                self.described(exchange.index, piece, place, {"blk": peer}).start()

            @pl.when(peer == self.me)
            def _():
                exchange.keep(piece, place)

        return send, exchange.wait


HALVES = ("keys_half", "values_half")


def by_length(longest):
    first = (longest[:1, :1] < 0.5).astype(F32)
    second = (longest[:1, :1] < 1.5).astype(F32) - first
    places = (first, second, 1.0 - first - second)
    return lambda rank, slot: places[(slot - rank) % NSEG]


def forward_body(lay, names, late, out_names, scratch_names, *refs):
    r = dict(zip(names, refs, strict=False))
    o = dict(zip(out_names, refs[len(names) :], strict=False))
    s = dict(zip(scratch_names, refs[len(names) + len(out_names) :], strict=True))
    count, parts, half, rows = lay.count, lay.parts, lay.half, lay.rows
    links = Links(lay, s)
    me, core = links.me, links.core
    links.announce()
    flat_rows, width = r["x"].shape
    wide, ff = s["w_out"].shape[0], s["w_up"].shape[1]
    total = count * rows
    mine_total = total // parts
    loading = {name: links.local(r[name], s[name]) for name in late}
    leaving = []

    codes = (r["segment_ids"][...] * 2 + r["token_valid"][...]).astype(F32)
    for pack in range(lay.packs):
        s["code_tok"][pack] = jnp.broadcast_to(codes[pack : pack + 1, :], (8, rows))

    def ready(*wanted):
        for name in wanted:
            loading[name].wait()

    def emit(*wanted):
        for name in wanted:
            leaving.append(links.local(s[name], o[name]))

    half_rows = pl.ds(pl.multiple_of(core * wide, wide), wide)
    other, group = me ^ half, 4
    normed_rows(lambda here: r["x"][here, :].astype(F32), r["gain_one"], s["h1"])
    for index, name in enumerate(("w_q", "w_k", "w_v")):
        ready(name)
        s["tok"][index] = dot(s["h1"][...], s[name][...], 1, 0).astype(BF16).T
    links.all_here()
    all_copies = []
    for index in range(3):
        target = s["query"] if index == 0 and parts > 1 else s["qkv"].at[index]
        all_copies.append(links.spread(s["tok"].at[index], target, index > 0))
    all_copies.append(Exchange(links, [s["codes"]], [s["codes"].at[:, pl.ds(0, total - rows)]]))
    for offset in range(count):
        piece = s["code_tok"].at[(me ^ offset) // half]
        all_copies[-1].start(offset, piece, s["codes"].at[:, pl.ds(me * rows, rows)])

    s["mem"][lay.mem_rows // 16 * 16 :, :] = jnp.zeros_like(s["mem"][lay.mem_rows // 16 * 16 :, :])
    s["mem"][: lay.mem_rows, :] = r["memory"][...]
    emit("mem")
    ready("w_ck", "w_cv")
    memory_copies = []
    for kind, name in enumerate(("w_ck", "w_cv")):
        s["kv_tok"][kind] = dot(s["mem"][...], s[name][...], 1, 0).astype(BF16).T
        target = s[HALVES[kind]]
        memory_copies.append(Exchange(links, [target], [target.at[pl.ds(0, half - 1)]]))
        for offset in range(half):
            piece = s["kv_tok"].at[kind, pl.ds(lay.head(me ^ offset) * HEAD_DIM, HEAD_DIM), :]
            memory_copies[-1].start(offset, piece, target.at[lax.rem(me, half)])
    twin_copies = []

    def find_pages(kind):
        memory_copies[kind].wait()
        for side in range(2):
            order = by_length(s["longest"][side])
            found = [links.page_of(r["segment_page"], side, slot) for slot in range(NSEG)]
            for piece in range(lay.pieces):
                columns = slice(piece * lay.mem_pad, (piece + 1) * lay.mem_pad)
                values = [
                    s[HALVES[kind]][page * lay.pieces + piece].astype(F32) * here for page, here in found
                ]
                for rank in range(NSEG):
                    value = sum(order(rank, slot) * values[slot] for slot in range(NSEG)).astype(BF16)
                    if rank > 0:
                        s["kv_small"][side, rank - 1, kind, :, columns] = value
                    else:
                        s["main_found"][kind, side, :, columns] = value
        twin_copies.append(
            links.remote(s["main_found"].at[kind, 1], s["main_twin"].at[kind], {"blk": other})
        )

    s["h1_turned"][...] = s["h1"][:, half_rows].T

    def pack_chunk(owner, first=0, size=wide):
        return o["h1_pack"].at[pl.ds(first, size), pl.ds(pl.multiple_of(owner * rows, rows), rows)]

    def hand_over():
        return [
            links.remote(
                s["h1_turned"].at[:, pl.ds((1 - links.pack) * rows, rows)], pack_chunk(me), {"blk": other}
            ),
            links.local(s["h1_turned"].at[:, pl.ds(links.pack * rows, rows)], pack_chunk(me)),
        ]

    ways = half.bit_length() - 1
    shares = [16 * (wide // 16 // ways + (way < wide // 16 % ways)) for way in range(ways)]

    def double(step, owners):
        moved = o["h1_pack"].at[:, pl.ds(0, len(owners) * rows << step)]
        exchange = Exchange(links, [moved], [moved])
        for way in range(ways):
            first, order = sum(shares[:way]), [(way + turn) % ways for turn in range(step + 1)]
            held = [0]
            for bit in order[:-1]:
                held += [offset ^ (1 << bit) for offset in held]
            for owner in owners:
                for offset in held:
                    piece = pack_chunk(owner ^ offset, first, shares[way])
                    exchange.start(1 << order[-1], piece, piece)
        return [exchange]

    def to_group(source, target):
        moved = target.at[pl.ds(1, group - 1), :, half_rows]
        exchange = Exchange(links, [moved], [moved])
        for offset in range(1, group):
            exchange.start(offset, source.at[:, half_rows], target.at[offset, :, half_rows])
        return [exchange, links.local(source, target.at[0])]

    wait_all(all_copies)
    pack_copies = hand_over()

    codes = s["codes"][:1, :]
    segments = jnp.floor(codes * 0.5)
    s["code"][...] = jnp.where(codes - 2.0 * segments > 0.5, segments, -1.0)
    lengths = [
        jnp.sum((segments == float(slot)).astype(F32), axis=1, keepdims=True) for slot in range(NSEG)
    ]
    first_longest = ((lengths[0] >= lengths[1]) & (lengths[0] >= lengths[2])).astype(F32)
    second_longest = (lengths[1] >= lengths[2]).astype(F32) * (1.0 - first_longest)
    longest = 2.0 - 2.0 * first_longest - second_longest
    order = segments - longest
    order = jnp.where(order < 0.0, order + float(NSEG), order)
    if parts == 1:
        s["qseg"][...], s["qslot"][...] = segments, order
    else:
        s["rows"][0:1, :], s["rows"][1:2, :] = segments, order
        for piece in range(count // parts):
            there = pl.ds((piece * parts + links.part) * rows, rows)
            s["qseg"][:, piece * rows : (piece + 1) * rows] = s["rows"][0:1, there]
            s["qslot"][:, piece * rows : (piece + 1) * rows] = s["rows"][1:2, there]
    s["longest"][0] = jnp.broadcast_to(longest, s["longest"].shape[1:])
    ends = [slice(0, LANES), slice(mine_total - LANES, mine_total)]
    for index, here in enumerate(ends):
        s["ends_slot"][0, :, index * LANES : (index + 1) * LANES] = jnp.broadcast_to(
            s["qslot"][:, here], (8, LANES)
        )
    early_copies = [
        links.remote(s[name].at[0], s[name].at[1], {"blk": other}) for name in ("longest", "ends_slot")
    ]
    emit("qkv", "code", "qseg", "qslot")
    if parts > 1:
        emit("query")

    block = min(512 if parts == 1 else 256, mine_total)
    s["key"][...] = s["qkv"][1].T
    send_mixed, wait_mixed = links.collect_later(s["low"].at[0], s["mixed"])
    for index in reversed(range(mine_total // block)):
        columns = slice(index * block, (index + 1) * block)
        query = s["query"][:, columns] if parts > 1 else s["qkv"][0, :, columns]
        mine = s["qseg"][:, columns]
        places = index * block + lax.broadcasted_iota(jnp.int32, (1, block), 1)
        positions = ((places // rows) * parts + links.part) * rows + places % rows

        def fold(key_index, state, causal, query=query, mine=mine, positions=positions):
            largest, weight_sum, weighted = state
            start = pl.multiple_of(key_index * block, block)
            here = pl.ds(start, block)
            scores = jnp.dot(s["key"][here, :], query, preferred_element_type=F32)
            allowed = jnp.broadcast_to(s["code"][:, here], (8, block)).T[:, :1] == mine
            if causal:
                key_places = start + lax.broadcasted_iota(jnp.int32, (block, block), 0)
                allowed = allowed & (key_places <= positions)
            scores = jnp.where(allowed, scores, NEG)
            new = jnp.maximum(largest, jnp.max(scores, axis=0, keepdims=True))
            weights = jnp.exp2((scores - new) * EXP2_SCALE)
            keep = jnp.exp2((largest - new) * EXP2_SCALE)
            weight_sum = weight_sum * keep + jnp.sum(weights, axis=0, keepdims=True)
            update = jnp.dot(s["qkv"][2, :, here], weights.astype(BF16), preferred_element_type=F32)
            return (new, weight_sum, weighted * keep + update)

        state = (
            jnp.full((1, block), NEG, F32),
            jnp.zeros((1, block), F32),
            jnp.zeros((HEAD_DIM, block), F32),
        )
        state = lax.fori_loop(0, index * parts, lambda j, c, fold=fold: fold(j, c, False), state)
        for extra in range(parts):
            state = fold(index * parts + extra, state, True)
        largest, weight_sum, weighted = state
        result = weighted / weight_sum
        s["att"][:, columns] = result
        s["low"][0, :, columns] = result.astype(BF16)
        s["log"][:, columns] = largest * EXP2_SCALE + jnp.log2(weight_sum)
        for piece in range(index * block // rows, (index + 1) * block // rows):
            send_mixed(piece)
    emit("att", "log")

    def product_rows(left, right, sent, arrived):
        started = []
        for start in range(0, flat_rows, rows):
            here = slice(start, start + rows)
            sent[here, :] = dot(left[:, here].T, right[...], 1, 0).astype(BF16)
            started.append(links.to_other_core(sent.at[pl.ds(start, rows)], arrived.at[pl.ds(start, rows)]))
        return started

    def group_to_other_core(target):
        others = target.at[pl.ds(1, group - 1), :, half_rows]
        return links.to_other_core(others, others)

    def both(sent, arrived):
        return lambda here: sent[here, :].astype(F32) + arrived[here, :].astype(F32)

    def add_rows(target, *terms):
        step = 32

        def body(index, _):
            here = pl.ds(pl.multiple_of(index * step, step), step)
            target[here, :] = sum(term(here) for term in terms).astype(target.dtype)
            return 0

        lax.fori_loop(0, flat_rows // step, body, 0)

    wait_all(early_copies)
    for kind in range(2):
        find_pages(kind)
    for side in range(2):
        order = by_length(s["longest"][side])
        for rank in range(1, NSEG):
            here = sum(
                order(rank, slot) * links.page_of(r["segment_page"], side, slot)[1] for slot in range(NSEG)
            )
            row = 2 * side + rank - 1
            s["ends_mask"][row : row + 1, :] = (s["ends_slot"][side, :1, :] == float(rank)).astype(F32) * here
    emit("longest", "kv_small", "ends_mask")
    ready("w_out")
    wait_mixed()
    wait_all(pack_copies)
    pack_copies = double(0, [me, other])
    emit("mixed")
    started = product_rows(s["mixed"], s["w_out"], s["sent"].at[0], s["arrived"].at[0])
    wait_all(started)
    add_rows(
        s["r1"], lambda here: r["x"][here, :].astype(F32), both(s["sent"].at[0], s["arrived"].at[0])
    )
    normed_rows(lambda here: s["r1"][here, :], r["gain_two"], s["h2"])
    ready("w_cross_query")
    s["tok"][0] = dot(s["h2"][...], s["w_cross_query"][...], 1, 0).astype(BF16).T
    query_copies = links.spread(s["tok"].at[0], s["cross_unit"])
    ready("cot")
    cot_copies = to_group(s["cot"], o["dm_group"])
    emit("r1", "h2")

    narrow = min(256, mine_total)
    present = page_rows(lay.pieces * lay.mem_pad, lay.mem_pad, lay.mem_rows)
    send_cross, wait_cross = links.collect_later(s["low"].at[1], s["cross_mixed"])
    wait_all(twin_copies)
    for kind in range(2):
        value = s["main_found"][kind, 0].astype(F32) + s["main_twin"][kind].astype(F32)
        s["kv_main"][kind] = value.astype(BF16)
    emit("kv_main")
    query_copies.wait()
    ends_copies = [
        links.remote(s["cross_unit"].at[:, pl.ds(here.start, LANES)], s["ends_query"].at[index], {"blk": other})
        for index, here in enumerate(ends)
    ]
    emit("cross_unit")
    wait_all(pack_copies)
    pack_copies = double(1, [me, other])

    def attend(query, keys, values):
        scores = jnp.dot(keys, query, preferred_element_type=F32)
        scores = jnp.where(present, scores, NEG)
        largest = jnp.max(scores, axis=0, keepdims=True)
        weights = jnp.exp2((scores - largest) * EXP2_SCALE)
        weight_sum = jnp.sum(weights, axis=0, keepdims=True)
        result = jnp.dot(values, weights.astype(BF16), preferred_element_type=F32)
        return result / weight_sum, largest * EXP2_SCALE + jnp.log2(weight_sum)

    key_rows = s["kv_main"][0].T
    pieces = mine_total // rows
    for index in range(mine_total // narrow):
        columns = slice(index * narrow, (index + 1) * narrow)
        result, logs = attend(s["cross_unit"][:, columns], key_rows, s["kv_main"][1])
        s["cross_att"][:, columns], s["cross_log"][:, columns] = result, logs
        s["low"][1, :, columns] = result.astype(BF16)
        for piece in range(index * narrow // rows, (index + 1) * narrow // rows):
            if 0 < piece < pieces - 1:
                send_cross(piece)

    def attend_ends(side, query_of):
        results = [(jnp.zeros((HEAD_DIM, LANES), F32), jnp.zeros((1, LANES), F32)) for _ in ends]
        for rank in range(1, NSEG):
            keys = s["kv_small"][side, rank - 1, 0].T
            for index in range(2):
                result, logs = attend(query_of(index), keys, s["kv_small"][side, rank - 1, 1])
                row = 2 * side + rank - 1
                here = s["ends_mask"][row : row + 1, index * LANES : (index + 1) * LANES] > 0.5
                results[index] = (
                    jnp.where(here, result, results[index][0]),
                    jnp.where(here, logs, results[index][1]),
                )
        return results

    wait_all(ends_copies)
    for index, (result, logs) in enumerate(attend_ends(1, lambda index: s["ends_query"][index])):
        s["ends_att"][0, index] = result.astype(BF16)
        s["ends_log"][0, :, index * LANES : (index + 1) * LANES] = jnp.broadcast_to(logs, (8, LANES))
    ends_copies = [
        links.remote(s[name].at[0], s[name].at[1], {"blk": other}) for name in ("ends_att", "ends_log")
    ]
    own_ends = attend_ends(0, lambda index: s["cross_unit"][:, ends[index]])
    wait_all(ends_copies)
    for index, (here, (result, logs)) in enumerate(zip(ends, own_ends, strict=True)):
        small = s["qslot"][:, here] > 0.5
        result = result + s["ends_att"][1, index].astype(F32)
        logs = logs + s["ends_log"][1, :1, index * LANES : (index + 1) * LANES]
        result = jnp.where(small, result, s["cross_att"][:, here])
        s["cross_att"][:, here] = result
        s["cross_log"][:, here] = jnp.where(small, logs, s["cross_log"][:, here])
        s["low"][1, :, here] = result.astype(BF16)
        send_cross(here.start // rows)
    emit("ends_query")
    emit("cross_att", "cross_log")
    ready("w_cross_out")
    wait_cross()
    for step in range(2, ways):
        wait_all(pack_copies)
        pack_copies = double(step, [me, other])
    emit("cross_mixed")
    started = product_rows(s["cross_mixed"], s["w_cross_out"], s["sent"].at[1], s["arrived"].at[1])
    wait_all(started)
    add_rows(s["r2"], lambda here: s["r1"][here, :], both(s["sent"].at[1], s["arrived"].at[1]))
    normed_rows(lambda here: s["r2"][here, :], r["gain_three"], s["h1"])
    h3_copies = to_group(s["h1"], o["h3_group"])

    ready("w_up", "w_down")
    slice_width = ff // group
    s["down_sum"][...] = jnp.zeros_like(s["down_sum"])
    s["up_sum"][...] = jnp.zeros_like(s["up_sum"])
    piece_rows = LANES
    for number in range(group):
        columns = slice(number * slice_width, (number + 1) * slice_width)
        for start in range(0, flat_rows, piece_rows):
            here = slice(start, start + piece_rows)
            u = dot(s["h1"][here, :], s["w_up"][:, columns], 1, 0)
            grad = dot(s["cot"][here, :], s["w_down"][columns, :], 1, 1)
            normal = 0.5 + 0.5 * erf(u * 0.7071067811865476)
            s["gelu"][here, columns] = (u * normal).astype(BF16)
            slope = normal + u * jnp.exp2(u * u * -0.7213475204444817) * 0.3989422804014327
            s["du"][here, columns] = (slope * grad).astype(BF16)
        s["down_sum"][...] += dot(s["gelu"][:, columns], s["w_down"][columns, :], 1, 0)
        s["up_sum"][...] += dot(s["du"][:, columns], s["w_up"][:, columns], 1, 1)
    emit("gelu", "du")
    s["sent"][2] = s["up_sum"][...].astype(BF16)
    up_copy = links.to_other_core(s["sent"].at[2], s["arrived"].at[2])
    s["sent"][3] = s["down_sum"][...].astype(BF16)
    down_copy = links.to_other_core(s["sent"].at[3], s["arrived"].at[3])
    up_copy.wait()
    norm_back_rows(
        s["grad_two"],
        both(s["sent"].at[2], s["arrived"].at[2]),
        lambda here: s["r2"][here, :],
        r["gain_three"],
        lambda here: s["cot"][here, :].astype(F32),
        s["dc"],
    )
    s["tok"][0] = dot(s["w_cross_out"][...], s["dc"][...], 1, 1).astype(BF16)
    doc_copies = links.spread(s["tok"].at[0], s["doc_unit"])
    emit("grad_two", "dc")
    wait_all(cot_copies)
    wait_all(h3_copies)
    group_copies = [group_to_other_core(o["dm_group"]), group_to_other_core(o["h3_group"])]
    down_copy.wait()
    add_rows(s["sent"].at[3], lambda here: s["r2"][here, :], both(s["sent"].at[3], s["arrived"].at[3]))
    leaving.append(links.local(s["sent"].at[3], o["out"]))
    doc_copies.wait()
    emit("doc_unit")
    wait_all(group_copies)
    wait_all(pack_copies)
    wait_all(leaving)
    assert links.used <= links.send_sem.shape[0] and links.own_used <= links.own_sem.shape[0]


def forward(lay, values, ff):
    parts, count, half, rows = lay.parts, lay.count, lay.half, lay.rows
    flat_rows, width = values["x"].shape
    wide, total = lay.heads * HEAD_DIM, lay.count * lay.rows
    mine_total = total // parts
    span = lay.pieces * lay.mem_pad
    early = ["x", "segment_ids", "token_valid", "memory", "gain_one", "gain_two", "gain_three"]
    late = [name for name in values if name not in early + ["segment_page"]]
    names = ["segment_page"] + early + late

    def shape(*dims, dtype=BF16):
        return jax.ShapeDtypeStruct(dims, dtype)

    kept = {
        "qkv": shape(3, HEAD_DIM, total),
        "code": shape(1, total, dtype=F32),
        "qseg": shape(1, mine_total, dtype=F32),
        "qslot": shape(1, mine_total, dtype=F32),
        "longest": shape(2, 8, LANES, dtype=F32),
        "att": shape(HEAD_DIM, mine_total, dtype=F32),
        "log": shape(1, mine_total, dtype=F32),
        "mixed": shape(wide, flat_rows),
        "r1": shape(flat_rows, width, dtype=F32),
        "h2": shape(flat_rows, width),
        "cross_unit": shape(HEAD_DIM, mine_total),
        "kv_main": shape(2, HEAD_DIM, span),
        "kv_small": shape(2, NSEG - 1, 2, HEAD_DIM, span),
        "ends_query": shape(2, HEAD_DIM, LANES),
        "ends_mask": shape(8, 2 * LANES, dtype=F32),
        "cross_att": shape(HEAD_DIM, mine_total, dtype=F32),
        "cross_log": shape(1, mine_total, dtype=F32),
        "cross_mixed": shape(wide, flat_rows),
        "grad_two": shape(flat_rows, width, dtype=F32),
        "dc": shape(flat_rows, width),
        "doc_unit": shape(HEAD_DIM, mine_total),
        "mem": shape(lay.mem_pad, width),
        "gelu": shape(flat_rows, ff),
        "du": shape(flat_rows, ff),
    }
    if parts > 1:
        kept["query"] = shape(HEAD_DIM, mine_total)
    gathered = {
        "dm_group": shape(4, flat_rows, width),
        "h3_group": shape(4, flat_rows, width),
        "out": shape(flat_rows, width),
        "h1_pack": shape(wide, total),
    }
    scratch = {
        "h1": shape(flat_rows, width),
        "tok": shape(3, wide, flat_rows),
        "codes": shape(8, total, dtype=F32),
        "code_tok": shape(lay.packs, 8, rows, dtype=F32),
        "kv_tok": shape(2, wide, lay.mem_pad),
        "keys_half": shape(half, HEAD_DIM, lay.mem_pad),
        "values_half": shape(half, HEAD_DIM, lay.mem_pad),
        "main_found": shape(2, 2, HEAD_DIM, span),
        "main_twin": shape(2, HEAD_DIM, span),
        "ends_slot": shape(2, 8, 2 * LANES, dtype=F32),
        "ends_att": shape(2, 2, HEAD_DIM, LANES),
        "ends_log": shape(2, 8, 2 * LANES, dtype=F32),
        "key": shape(total, HEAD_DIM),
        "low": shape(2, HEAD_DIM, mine_total),
        "h1_turned": shape(wide, flat_rows),
        "sent": shape(4, flat_rows, width),
        "arrived": shape(4, flat_rows, width),
        "r2": shape(flat_rows, width, dtype=F32),
        "down_sum": shape(flat_rows, width, dtype=F32),
        "up_sum": shape(flat_rows, width, dtype=F32),
    }
    if parts > 1:
        scratch["rows"] = shape(8, total, dtype=F32)
    scratch = {name: pltpu.VMEM(value.shape, value.dtype) for name, value in {**scratch, **kept}.items()}
    for name in late:
        scratch[name] = pltpu.VMEM(values[name].shape, values[name].dtype)
    semaphores = pltpu.SemaphoreType.DMA((34,))
    scratch = {"send_sem": semaphores, "recv_sem": semaphores, **scratch}
    scratch["own_sem"] = pltpu.SemaphoreType.DMA((40,))
    outs = {**kept, **gathered}
    anywhere = pl.BlockSpec(memory_space=pl.ANY)
    results = pl.pallas_call(
        functools.partial(forward_body, lay, names, late, list(outs), list(scratch)),
        out_shape=list(outs.values()),
        in_specs=[pl.BlockSpec(memory_space=pltpu.SMEM)]
        + [pl.BlockSpec(memory_space=pltpu.VMEM)] * len(early)
        + [anywhere] * len(late),
        out_specs=[anywhere] * len(outs),
        scratch_shapes=list(scratch.values()),
        compiler_params=pltpu.CompilerParams(
            collective_id=0, has_side_effects=True, vmem_limit_bytes=63 * 1024 * 1024
        ),
    )(*[values[name] for name in names])
    return dict(zip(outs, results, strict=True))


def reversed_bits(value, bits):
    return sum(((value >> b) & 1) << (bits - 1 - b) for b in range(bits))


class Halving:
    def __init__(self, links, bits, sums, arrivals, crossed=True):
        self.links, self.bits, self.crossed = links, bits, crossed
        self.sums, self.arrivals = sums, arrivals
        self.quarter = sums.shape[1] // 2
        self.jobs, self.pending = [], []

    def neighbour(self, kind, step):
        bit = self.bits[1 - step if self.crosses(kind) and step < 2 else step]
        return {"blk": self.links.me ^ (1 << bit)}

    def crosses(self, kind):
        return kind == 1 and self.crossed

    def add_job(self, column, width, make):
        here, started = pl.ds(column, width), []
        for kind in range(2):
            for half, quarter in enumerate((1, 3) if self.crosses(kind) else (2, 3)):
                rows = pl.ds(half * self.quarter, self.quarter)
                self.sums[kind, rows, here] = make(kind, quarter).astype(BF16)
            started.append(
                self.links.remote(
                    self.sums.at[kind, :, here],
                    self.arrivals[0].at[kind, :, here],
                    self.neighbour(kind, 0),
                )
            )
        self.jobs.append((here, make, started))

    def keep_jobs(self):
        for here, make, started in self.jobs:
            wait_all(started)
            for kind in range(2):
                for half, quarter in enumerate((0, 2) if self.crosses(kind) else (0, 1)):
                    rows = pl.ds(half * self.quarter, self.quarter)
                    arrived = self.arrivals[0][kind, rows, here].astype(F32)
                    self.sums[kind, rows, here] = (make(kind, quarter) + arrived).astype(BF16)
        self.send(1)

    def send(self, step):
        rows = self.sums.shape[1] >> step
        self.pending = [
            self.links.remote(
                self.sums.at[kind, pl.ds(rows, rows), :],
                self.arrivals[step].at[kind],
                self.neighbour(kind, step),
            )
            for kind in range(2)
        ]

    def receive(self, step, result=None):
        rows = self.sums.shape[1] >> step
        wait_all(self.pending)
        size = min(rows, 32)

        def add(index, _):
            here = pl.ds(pl.multiple_of(index * size, size), size)
            for kind in range(2):
                mine = self.sums[kind, here, :].astype(F32)
                total = mine + self.arrivals[step][kind, here, :].astype(F32)
                if result is None:
                    self.sums[kind, here, :] = total.astype(BF16)
                else:
                    result[kind, here, :] = total
            return 0

        lax.fori_loop(0, rows // size, add, 0)
        if step + 1 < len(self.bits):
            self.send(step + 1)


def arrivals_shapes(bits, width, columns):
    return [pltpu.VMEM((2, width >> (step + 1), columns), BF16) for step in range(bits)]


OUTS = (
    "input", "memory_own", "memory_other", "query", "key", "value", "out", "cross_query", "cross_key",
    "cross_value", "cross_out", "up", "down", "gains",
)


def backward_body(lay, names, late, scratch_names, *refs):
    r = dict(zip(names, refs, strict=False))
    o = dict(zip(OUTS, refs[len(names) :], strict=False))
    s = dict(zip(scratch_names, refs[len(names) + len(OUTS) :], strict=True))
    far = dict(r)
    count, parts, half, rows = lay.count, lay.parts, lay.half, lay.rows
    links = Links(lay, s)
    me, core, head, pack, part = links.me, links.core, links.head, links.pack, links.part
    bits = count.bit_length() - 1
    flat_rows, width = r["dc"].shape
    wide = r["w_out"].shape[0]
    total = r["qkv"].shape[2]
    mine_total = total // parts
    share = width // count
    block = min(512 if parts == 1 else 256, mine_total)
    links.announce(everyone=True)
    loading = {}

    def load(name):
        loading[name] = links.local(r[name], s["in_" + late[name]])

    for name, home in late.items():
        if name == home:
            load(name)
    own_rows = pl.ds(pl.multiple_of(me * share, share), share)
    row_copies = [
        links.local(far[name].at[own_rows, :], s["rows_" + name])
        for name in ("w_q", "w_k", "w_v", "w_cross_query", "w_up")
    ]
    h1_copy = links.local(r["h1_pack"].at[:, pl.ds(0, s["h1"].shape[1])], s["h1"])

    def ready(*wanted):
        for name in wanted:
            loading[name].wait()
            r[name] = s["in_" + late[name]]

    def relative(target, value, shift=0, column=0):
        number, most = count >> shift, s["turn"].shape[1]
        size_rows = width // number
        for start in range(0, value.shape[0], most):
            size = min(most, value.shape[0] - start)
            s["turn"][:, :size] = value[start : start + size, :].T
            for place in range(number):
                chunk = (me >> shift) ^ reversed_bits(place, bits - shift)
                target[pl.ds(place * size_rows, size_rows), column + start : column + start + size] = s[
                    "turn"
                ][pl.ds(pl.multiple_of(chunk * size_rows, size_rows), size_rows), :size]

    quarter = width // 4

    def quarter_of(ref, index):
        return ref[pl.ds(index * quarter, quarter), :]

    def from_units(target, sent_rows):
        sent = [target.at[index] for index in range(1, parts)] + [target.at[0, :, pl.ds(0, sent_rows), :]]
        return Exchange(links, [target], sent)

    def batch(name, chosen, crossed=True):
        arrivals = [s[f"{name}_{i}"] for i in range(len(chosen))]
        return Halving(links, chosen, s[name + "_sums"], arrivals, crossed)

    piece = wide // 2

    def weight_job(target, place, left, right):
        def make(kind, index):
            return dot(quarter_of(left, index), right[kind * piece : (kind + 1) * piece, :], 1, 1)

        target.add_job(place * piece, piece, make)

    group = 4
    slice_width = s["gelu_group"].shape[2]
    links.all_here(everyone=True)

    def to_group(name):
        target = s[name + "_group"]
        exchange = Exchange(links, [target], [target.at[pl.ds(0, group - 1)]])
        for offset in range(group):
            number = lax.rem(me ^ offset, group)
            columns = pl.ds(pl.multiple_of(number * slice_width, slice_width), slice_width)
            exchange.start(offset, r[name].at[:, columns], target.at[offset])
        return exchange

    gelu_copies, du_copies = to_group("gelu"), to_group("du")

    ready("doc_unit", "kv_main", "cross_unit", "cross_att", "kv_small")
    span = r["kv_main"].shape[2]
    other = me ^ half
    ends = [slice(0, LANES), slice(mine_total - LANES, mine_total)]
    for index, here in enumerate(ends):
        columns = slice(index * LANES, (index + 1) * LANES)
        grad = r["doc_unit"][:, here].astype(F32)
        s["ends_rows"][0, 0:1, columns] = r["cross_log"][:, here]
        s["ends_rows"][0, 1:2, columns] = jnp.sum(grad * r["cross_att"][:, here], axis=0, keepdims=True)
    ends_copies = [links.remote(s["ends_rows"].at[0], s["ends_rows"].at[1], {"blk": other})]
    for index, here in enumerate(ends):
        piece_of = r["doc_unit"].at[:, pl.ds(here.start, LANES)]
        ends_copies.append(links.remote(piece_of, s["ends_doc"].at[index], {"blk": other}))
    s["cross_key"][...] = r["kv_main"][0].T
    s["cross_value"][...] = r["kv_main"][1].T
    s["cross_acc"][...] = jnp.zeros_like(s["cross_acc"])
    present = page_rows(span, lay.mem_pad, lay.mem_rows)

    def cross_block(query, grad, logs, row_dot, allowed, keys, key_rows, value_rows):
        scores = jnp.dot(key_rows, query, preferred_element_type=F32)
        weights = jnp.where(present & allowed, jnp.exp2(scores * EXP2_SCALE - logs), 0.0)
        weight_grad = jnp.dot(value_rows, grad, preferred_element_type=F32)
        score_grad = (weights * (weight_grad - row_dot)).astype(BF16)
        dq = jnp.dot(keys, score_grad, preferred_element_type=F32)
        return dq, dot(query, score_grad, 1, 1), dot(grad, weights.astype(BF16), 1, 1)

    narrow = min(256, mine_total)

    def main_slot(index, _):
        here = pl.ds(pl.multiple_of(index * narrow, narrow), narrow)
        grad = r["doc_unit"][:, here]
        row_dot = jnp.sum(grad.astype(F32) * r["cross_att"][:, here], axis=0, keepdims=True)
        dq, dk, dv = cross_block(
            r["cross_unit"][:, here],
            grad,
            r["cross_log"][:, here],
            row_dot,
            r["qslot"][:, here] < 0.5,
            r["kv_main"][0],
            s["cross_key"][...],
            s["cross_value"][...],
        )
        s["dq_acc"][:, here] = dq
        s["cross_acc"][0] += dk
        s["cross_acc"][1] += dv
        return 0

    lax.fori_loop(0, mine_total // narrow, main_slot, 0)
    s["main_low"][0] = (s["cross_acc"][0] * SCALE).astype(BF16)
    s["main_low"][1] = s["cross_acc"][1].astype(BF16)
    send_dqc, wait_dqc = links.collect_later(s["dq_low"], s["in_small"].at[0])
    s["dq_low"][...] = (s["dq_acc"][...] * SCALE).astype(BF16)
    last_piece = mine_total // rows - 1
    def small_slots(side, queries, grads):
        dq_ends = [jnp.zeros((HEAD_DIM, LANES), F32) for _ in ends]
        for rank in range(1, NSEG):
            keys, values = r["kv_small"][side, rank - 1, 0], r["kv_small"][side, rank - 1, 1]
            key_rows, value_rows = keys.T, values.T
            row, sums = 2 * side + rank - 1, None
            for index in range(2):
                columns = slice(index * LANES, (index + 1) * LANES)
                dq, dk, dv = cross_block(
                    queries(index),
                    grads(index),
                    s["ends_rows"][side, 0:1, columns],
                    s["ends_rows"][side, 1:2, columns],
                    r["ends_mask"][row : row + 1, columns] > 0.5,
                    keys,
                    key_rows,
                    value_rows,
                )
                dq_ends[index] = dq_ends[index] + dq
                sums = (dk, dv) if sums is None else (sums[0] + dk, sums[1] + dv)
            s["small_grad"][side, rank - 1, 0] = (sums[0] * SCALE).astype(BF16)
            s["small_grad"][side, rank - 1, 1] = sums[1].astype(BF16)
        return dq_ends

    wait_all(ends_copies)
    other_dq = small_slots(1, lambda index: r["ends_query"][index], lambda index: s["ends_doc"][index])
    for index in range(2):
        s["ends_dq"][0, index] = other_dq[index].astype(BF16)
    ends_copy = links.remote(s["ends_dq"].at[0], s["ends_dq"].at[1], {"blk": other})
    for number in range(1, last_piece):
        send_dqc(number)
    own_dq = small_slots(
        0, lambda index: r["cross_unit"][:, ends[index]], lambda index: r["doc_unit"][:, ends[index]]
    )
    ends_copy.wait()
    for index, here in enumerate(ends):
        value = s["dq_acc"][:, here] + own_dq[index] + s["ends_dq"][1, index].astype(F32)
        s["dq_low"][:, here] = (value * SCALE).astype(BF16)
    send_dqc(0)
    send_dqc(last_piece)
    load("att")
    twin_copies = [links.remote(s["main_low"], s["main_twin"], {"blk": other})]

    ready("dm_group")
    for offset in range(group):
        relative(s["rel_dm"], r["dm_group"].at[offset], 2, offset * flat_rows)

    def feed_job(left, right):
        def make(kind, index):
            here = slice(kind * slice_width // 2, (kind + 1) * slice_width // 2)
            return dot(
                quarter_of(left, index), right[:, :, here].reshape(group * flat_rows, slice_width // 2), 1, 0
            )

        return make

    down, up = [batch(name, range(2, bits), crossed=False) for name in ("down", "up")]
    gelu_copies.wait()
    down.add_job(0, slice_width // 2, feed_job(s["rel_dm"], s["gelu_group"]))
    middle, pages = batch("middle", range(bits)), batch("pages", range(bits))
    ready("cross_mixed")
    relative(s["rel_dc"], r["dc"])
    weight_job(middle, 0, s["rel_dc"], r["cross_mixed"])
    ready("h3_group")
    for offset in range(group):
        relative(s["rel_h3"], r["h3_group"].at[offset], 2, offset * flat_rows)

    ready("w_cross_query")
    wait_dqc()
    tp_copies = []
    for start in range(0, flat_rows, rows):
        here = slice(start, start + rows)
        s["tp_send"][here, :] = dot(s["in_small"][0, :, here].T, r["w_cross_query"][...], 1, 1).astype(BF16)
        tp_copies.append(
            links.to_other_core(s["tp_send"].at[pl.ds(start, rows)], s["tp_recv"].at[0, pl.ds(start, rows)])
        )
    ready("h2", "r1", "grad_two")
    relative(s["rel_h2"], r["h2"])
    load("x")
    weight_job(middle, 1, s["rel_h2"], s["in_small"].at[0])
    wait_all(tp_copies)

    def both_cores(index):
        def grad(here):
            return s["tp_send"][here, :].astype(F32) + s["tp_recv"][index, here, :].astype(F32)

        return grad

    norm_back_rows(
        s["grad_one"],
        both_cores(0),
        lambda here: r["r1"][here, :],
        r["gain_two"],
        lambda here: r["grad_two"][here, :],
        s["da"],
    )
    ready("w_out")
    s["out_small"][0] = dot(r["w_out"][...], s["da"][...], 1, 1).astype(BF16)
    do_copies = links.spread(s["out_small"].at[0], s["do_unit"])
    load("w_q")
    ready("mixed")
    relative(s["rel_da"], s["da"])
    orders = [by_length(r["longest"][side]) for side in range(2)]

    def hot(side, rank, page):
        value = None
        for slot in range(NSEG):
            wanted = r["segment_page"][pack if side == 0 else 1 - pack, slot]
            term = orders[side](rank, slot) * jnp.where(wanted == pack * lay.pages_half + page, 1.0, 0.0)
            value = term if value is None else value + term
        return value

    wait_all(twin_copies)
    terms = [(0, 0, s["main_low"]), (1, 0, s["main_twin"])]
    terms += [(side, rank, s["small_grad"].at[side, rank - 1]) for side in range(2) for rank in range(1, NSEG)]

    def add_page(page, _):
        weights = [hot(side, rank, page) for side, rank, _ in terms]
        for piece_index in range(lay.pieces):
            here = slice(piece_index * lay.mem_pad, (piece_index + 1) * lay.mem_pad)
            for kind in range(2):
                value = None
                for weight, (_, _, source) in zip(weights, terms, strict=True):
                    term = weight * source[kind, :, here].astype(F32)
                    value = term if value is None else value + term
                s["page_grad"][page * lay.pieces + piece_index, kind] = value.astype(BF16)
        return 0

    lax.fori_loop(0, lay.pages_half, add_page, 0)

    ready("qkv", "att")
    if parts > 1:
        ready("query")
    s["dq_acc"][...] = jnp.zeros_like(s["dq_acc"])
    do_copies.wait()
    memory_copies = from_units(s["mem_recv"], (lay.heads - 1) * HEAD_DIM)
    for offset in range(half):
        source = s["page_grad"].at[lax.rem(me ^ offset, half)]
        place = s["mem_recv"].at[part, :, pl.ds(head * HEAD_DIM, HEAD_DIM), :]
        memory_copies.start(offset, source, place)
    weight_job(middle, 2, s["rel_da"], r["mixed"])

    def key_block(key_index, _):
        here = pl.ds(pl.multiple_of(key_index * block, block), block)
        keys, values = r["qkv"][1, :, here], r["qkv"][2, :, here]
        key_rows, value_rows = keys.T, values.T
        codes = jnp.broadcast_to(r["code"][:, here], (8, block)).T[:, :1]

        def fold(index, grads, causal):
            dk, dv = grads
            columns = pl.ds(pl.multiple_of(index * block, block), block)
            query = r["query"][:, columns] if parts > 1 else r["qkv"][0, :, columns]
            grad = s["do_unit"][:, columns]
            row_dot = jnp.sum(grad.astype(F32) * r["att"][:, columns], axis=0, keepdims=True)
            scores = jnp.dot(key_rows, query, preferred_element_type=F32)
            allowed = codes == r["qseg"][:, columns]
            if causal:
                places = index * block + lax.broadcasted_iota(jnp.int32, (1, block), 1)
                positions = ((places // rows) * parts + part) * rows + places % rows
                key_places = key_index * block + lax.broadcasted_iota(jnp.int32, (block, block), 0)
                allowed = allowed & (key_places <= positions)
            weights = jnp.where(allowed, jnp.exp2(scores * EXP2_SCALE - r["log"][:, columns]), 0.0)
            weight_grad = jnp.dot(value_rows, grad, preferred_element_type=F32)
            score_grad = (weights * (weight_grad - row_dot)).astype(BF16)
            s["dq_acc"][:, columns] += jnp.dot(keys, score_grad, preferred_element_type=F32)
            return (dk + dot(query, score_grad, 1, 1), dv + dot(grad, weights.astype(BF16), 1, 1))

        zeros = jnp.zeros((HEAD_DIM, block), F32)
        first_index = key_index // parts
        grads = fold(first_index, (zeros, zeros), True)
        dk, dv = lax.fori_loop(
            first_index + 1, mine_total // block, lambda i, g: fold(i, g, False), grads
        )
        r["qkv"][1, :, here] = (dk * SCALE).astype(BF16)
        r["qkv"][2, :, here] = dv.astype(BF16)
        return 0

    lax.fori_loop(0, total // block, key_block, 0)
    if parts == 1:
        r["qkv"][0] = (s["dq_acc"][...] * SCALE).astype(BF16)
        dq_copies = links.collect(r["qkv"].at[0], s["in_small"].at[1])
    else:
        r["qkv"][0] = jnp.zeros((HEAD_DIM, total), BF16)
        for number in range(count // parts):
            value = (s["dq_acc"][:, number * rows : (number + 1) * rows] * SCALE).astype(BF16)
            s["dq_low"][:, number * rows : (number + 1) * rows] = value
            r["qkv"][0, :, pl.ds((number * parts + part) * rows, rows)] = value
        dq_copies = links.collect(s["dq_low"], s["in_small"].at[1])
    unit_copy = links.to_other_core(r["qkv"], s["unit_other"])
    dkv_copies = from_units(s["dkv_recv"], (2 * lay.heads - 1) * HEAD_DIM // 2)
    for offset in range(count):
        peer = me ^ offset
        source = r["qkv"].at[pl.ds(1, 2), :, pl.ds(peer * rows, rows)]
        place = s["dkv_recv"].at[part, :, pl.ds(head * HEAD_DIM, HEAD_DIM), pl.ds(pack * rows, rows)]
        dkv_copies.start(offset, source, place)
    unit_copy.wait()
    number_to = count // 2
    first_exchange = Exchange(links, [s["first_recv"]], [s["first_low"].at[1]])

    def first_copy(index, number):
        device = {"blk": core * number_to + number, "tp": core if index == 0 else 1 - core}
        source = s["first_low"].at[index, pl.ds(number * share, share), :]
        return links.described(first_exchange.index, source, s["first_recv"].at[me], device)

    for index, ref in enumerate((r["qkv"], s["unit_other"])):
        value, most = None, s["h1"].shape[1]
        for start in range(0, total, most):
            if start + index > 0 and total > most:
                h1_copy = links.local(r["h1_pack"].at[:, pl.ds(start, most)], s["h1"])
            if start + index == 0 or total > most:
                h1_copy.wait()
            term = dot(s["h1"][...], ref[:, :, start : start + most].reshape(3 * HEAD_DIM, most), 1, 1)
            value = term if value is None else value + term
        s["first_low"][index] = value.astype(BF16)
        for number in range(number_to):
            if index == 1:
                first_copy(index, number).start()
                continue
            own = me == core * number_to + number

            @pl.when(jnp.logical_not(own))
            def _(number=number):
                first_copy(0, number).start()

            @pl.when(own)
            def _(number=number):
                first_exchange.keep(
                    s["first_low"].at[0, pl.ds(number * share, share), :], s["first_recv"].at[me]
                )

    down.keep_jobs()

    ready("mem", "w_ck", "w_cv")
    memory_copies.wait()
    if parts > 1:
        for kind in range(2):
            value = s["mem_recv"][0, kind].astype(F32)
            for index in range(1, parts):
                value = value + s["mem_recv"][index, kind].astype(F32)
            s["mem_recv"][0, kind] = value.astype(BF16)
    relative(s["rel_mem"], r["mem"])
    weight_job(pages, 0, s["rel_mem"], s["mem_recv"].at[0, 0])
    weight_job(pages, 1, s["rel_mem"], s["mem_recv"].at[0, 1])
    for start in range(0, lay.mem_pad, LANES):
        here = slice(start, start + LANES)
        s["mem_send"][here, :] = (
            dot(s["mem_recv"][0, 0, :, here].T, r["w_ck"][...], 1, 1)
            + dot(s["mem_recv"][0, 1, :, here].T, r["w_cv"][...], 1, 1)
        ).astype(BF16)
    du_copies.wait()
    up.add_job(0, slice_width // 2, feed_job(s["rel_h3"], s["du_group"]))
    load("w_k")
    load("w_v")
    mem_copies = [
        links.to_other_core(s["mem_send"], o["memory_other"]),
        links.local(s["mem_send"], o["memory_own"]),
    ]

    ready("w_q", "w_k", "w_v", "x")
    dq_copies.wait()
    dkv_copies.wait()
    if parts > 1:
        for kind in range(2):
            value = s["dkv_recv"][0, kind].astype(F32)
            for index in range(1, parts):
                value = value + s["dkv_recv"][index, kind].astype(F32)
            s["dkv_recv"][0, kind] = value.astype(BF16)
    pieces = (s["in_small"].at[1], s["dkv_recv"].at[0, 0], s["dkv_recv"].at[0, 1])
    tp_copies = []
    for start in range(0, flat_rows, rows):
        here = slice(start, start + rows)
        s["tp_send"][here, :] = sum(
            dot(value[:, here].T, r[weight][...], 1, 1)
            for value, weight in zip(pieces, ("w_q", "w_k", "w_v"), strict=True)
        ).astype(BF16)
        tp_copies.append(
            links.to_other_core(s["tp_send"].at[pl.ds(start, rows)], s["tp_recv"].at[1, pl.ds(start, rows)])
        )
    middle.keep_jobs()
    wait_all(tp_copies)
    norm_back_rows(
        o["input"],
        both_cores(1),
        lambda here: r["x"][here, :].astype(F32),
        r["gain_one"],
        lambda here: s["grad_one"][here, :],
    )
    pages.keep_jobs()
    up.keep_jobs()
    down.receive(1)
    middle.receive(1)
    up.receive(1)
    for step in range(2, bits - 2):
        down.receive(step)
        up.receive(step)
    final_copies = []
    for offset in range(group):
        rows_to = pl.ds(lax.rem(me ^ offset, group) * share, share)
        for index, sums in enumerate((s["down_sums"], s["up_sums"])):
            place = s["feed_last"].at[index, lax.rem(me, group)]
            final_copies.append(links.to(offset, sums.at[:, rows_to, :], place))

    for step in range(2, bits + 1):
        pages.receive(step - 1, s["pages_result"] if step == bits else None)
        if step < bits:
            middle.receive(step, s["middle_result"] if step == bits - 1 else None)
    wait_all(final_copies)
    for number in range(group):
        for kind in range(2):
            start = number * slice_width + kind * slice_width // 2
            here = slice(start, start + slice_width // 2)
            o["down"][:, here] = s["feed_last"][0, number, kind].astype(F32)
            o["up"][:, here] = s["feed_last"][1, number, kind].astype(F32)
    for kind in range(2):
        here = slice(kind * piece, (kind + 1) * piece)
        o["cross_out"][:, here] = s["middle_result"][kind, :, :piece]
        o["cross_query"][:, here] = s["middle_result"][kind, :, piece : 2 * piece]
        o["out"][:, here] = s["middle_result"][kind, :, 2 * piece :]
        o["cross_key"][:, here] = s["pages_result"][kind, :, :piece]
        o["cross_value"][:, here] = s["pages_result"][kind, :, piece:]
    first_exchange.wait()
    keeps = me // number_to == core

    def wait_rest(size):
        rest = s["first_low"].at[0, pl.ds(0, size), :]
        pltpu.make_async_copy(rest, rest, links.send_sem.at[first_exchange.index]).wait()

    pl.when(keeps)(lambda: wait_rest(wide - share))
    pl.when(jnp.logical_not(keeps))(lambda: wait_rest(wide))
    for index in range(lay.heads):
        value = None
        for side in range(2):
            for number in range(parts):
                term = s["first_recv"][side * half + index * parts + number].astype(F32)
                value = term if value is None else value + term
        for place, name in enumerate(("query", "key", "value")):
            o[name][:, index * HEAD_DIM : (index + 1) * HEAD_DIM] = value[
                :, place * HEAD_DIM : (place + 1) * HEAD_DIM
            ]

    wait_all(row_copies)
    lanes = lax.broadcasted_iota(jnp.int32, (share, LANES), 1)
    sums, gains = jnp.zeros((share, LANES), F32), jnp.ones((share, LANES), F32)
    pairs = (
        ("gain_one", (("w_q", "query"), ("w_k", "key"), ("w_v", "value"))),
        ("gain_two", (("w_cross_query", "cross_query"),)),
        ("gain_three", (("w_up", "up"),)),
    )
    for index, (gain, terms) in enumerate(pairs):
        value = sum(
            jnp.sum(s["rows_" + weight][...].astype(F32) * o[name][...], axis=1, keepdims=True)
            for weight, name in terms
        )
        s["gain_turned"][...] = jnp.broadcast_to(r[gain][...], (8, width)).T
        sums = jnp.where(lanes == index, value, sums)
        gains = jnp.where(lanes == index, s["gain_turned"][own_rows, :1], gains)
    s["gain_sums"][0] = sums
    links.to_other_core(s["gain_sums"].at[0], s["gain_sums"].at[1]).wait()
    o["gains"][...] = ((s["gain_sums"][0] + s["gain_sums"][1]) / gains).T[:8, :]
    wait_all(mem_copies)
    assert links.used <= links.send_sem.shape[0] and links.own_used <= links.own_sem.shape[0]


def backward(lay, values, ff):
    parts, count, half, rows = lay.parts, lay.count, lay.half, lay.rows
    flat_rows, width = values["dc"].shape
    wide = lay.heads * HEAD_DIM
    total = count * rows
    mine_total = total // parts
    span = lay.pieces * lay.mem_pad
    bits = count.bit_length() - 1
    late = [
        "doc_unit", "kv_main", "kv_small", "cross_unit", "cross_att", "w_out", "dm_group", "h3_group",
        "cross_mixed", "w_cross_query", "r1", "grad_two", "mixed", "qkv", "mem", "h2", "w_ck", "w_cv",
    ]
    if parts > 1:
        late.append("query")
    late = {name: name for name in late}
    late.update(w_q="w_cross_query", w_k="w_ck", w_v="w_cv", att="cross_att", x="h2")
    far = ["h1_pack", "gelu", "du", "w_up"]
    early = [name for name in values if name not in late and name not in far + ["segment_page"]]
    names = ["segment_page"] + early + list(late) + far
    vmem, anywhere = pl.BlockSpec(memory_space=pltpu.VMEM), pl.BlockSpec(memory_space=pl.ANY)

    def buffer(*shape, dtype=BF16):
        return pltpu.VMEM(shape, dtype)

    share = width // count
    scratch = {
        "send_sem": pltpu.SemaphoreType.DMA((8 * bits + 24,)),
        "recv_sem": pltpu.SemaphoreType.DMA((8 * bits + 24,)),
        "own_sem": pltpu.SemaphoreType.DMA((40,)),
        "out_small": buffer(1, wide, flat_rows),
        "in_small": buffer(2, wide, flat_rows),
        "do_unit": buffer(HEAD_DIM, mine_total),
        "dq_acc": buffer(HEAD_DIM, mine_total, dtype=F32),
        "dq_low": buffer(HEAD_DIM, mine_total),
        "turn": buffer(width, flat_rows),
        "rel_dm": buffer(width, 4 * flat_rows),
        "rel_h3": buffer(width, 4 * flat_rows),
        "rel_dc": buffer(width, flat_rows),
        "rel_h2": buffer(width, flat_rows),
        "rel_da": buffer(width, flat_rows),
        "rel_mem": buffer(width, lay.mem_pad),
        "feed_last": buffer(2, 4, 2, share, ff // 8),
        "gelu_group": buffer(4, flat_rows, ff // 4),
        "du_group": buffer(4, flat_rows, ff // 4),
        "h1": buffer(wide, min(total, 2048)),
        "cross_key": buffer(span, HEAD_DIM),
        "cross_value": buffer(span, HEAD_DIM),
        "cross_acc": buffer(2, HEAD_DIM, span, dtype=F32),
        "main_low": buffer(2, HEAD_DIM, span),
        "main_twin": buffer(2, HEAD_DIM, span),
        "small_grad": buffer(2, NSEG - 1, 2, HEAD_DIM, span),
        "ends_rows": buffer(2, 8, 2 * LANES, dtype=F32),
        "ends_doc": buffer(2, HEAD_DIM, LANES),
        "ends_dq": buffer(2, 2, HEAD_DIM, LANES),
        "page_grad": buffer(half, 2, HEAD_DIM, lay.mem_pad),
        "mem_recv": buffer(parts, 2, wide, lay.mem_pad),
        "mem_send": buffer(lay.mem_pad, width),
        "tp_send": buffer(flat_rows, width),
        "tp_recv": buffer(2, flat_rows, width),
        "grad_one": buffer(flat_rows, width, dtype=F32),
        "da": buffer(flat_rows, width),
        "dkv_recv": buffer(parts, 2, wide, flat_rows),
        "unit_other": buffer(3, HEAD_DIM, total),
        "first_low": buffer(2, wide, 3 * HEAD_DIM),
        "first_recv": buffer(count, share, 3 * HEAD_DIM),
        "middle_result": buffer(2, share, 3 * wide // 2, dtype=F32),
        "pages_result": buffer(2, share, wide, dtype=F32),
        "gain_turned": buffer(width, 8, dtype=F32),
        "gain_sums": buffer(2, share, LANES, dtype=F32),
        "rows_w_up": buffer(share, ff),
    }
    for name in ("w_q", "w_k", "w_v", "w_cross_query"):
        scratch["rows_" + name] = buffer(share, wide)
    columns = {"down": ff // 8, "up": ff // 8, "middle": 3 * wide // 2, "pages": wide}
    for name, number in columns.items():
        scratch[name + "_sums"] = buffer(2, width // 2, number)
        steps = bits - 2 if name in ("down", "up") else bits
        for index, shape in enumerate(arrivals_shapes(steps, width, number)):
            scratch[f"{name}_{index}"] = shape
    homes = {}
    for name, home in late.items():
        homes.setdefault(home, values[name])
    for home, value in homes.items():
        scratch["in_" + home] = pltpu.VMEM(value.shape, value.dtype)

    shapes = {"up": (share, ff), "down": (share, ff), "gains": (8, share)}
    outs = {name: jax.ShapeDtypeStruct(shapes.get(name, (share, wide)), F32) for name in OUTS}
    outs["input"] = jax.ShapeDtypeStruct((flat_rows, width), F32)
    for name in ("memory_own", "memory_other"):
        outs[name] = jax.ShapeDtypeStruct((lay.mem_pad, width), BF16)
    results = pl.pallas_call(
        functools.partial(backward_body, lay, names, late, list(scratch)),
        out_shape=list(outs.values()),
        in_specs=[pl.BlockSpec(memory_space=pltpu.SMEM)]
        + [vmem] * len(early)
        + [anywhere] * (len(late) + len(far)),
        out_specs=[anywhere if name.startswith("memory") else vmem for name in OUTS],
        scratch_shapes=list(scratch.values()),
        compiler_params=pltpu.CompilerParams(
            collective_id=1, has_side_effects=True, vmem_limit_bytes=63 * 1024 * 1024 + 512 * 1024
        ),
    )(*[values[name] for name in names])
    return dict(zip(OUTS, results, strict=True))


def local(
    tokens,
    memory,
    segment_ids,
    token_valid,
    segment_page,
    gain_one,
    weight_query,
    weight_key,
    weight_value,
    weight_out,
    gain_two,
    cross_query,
    cross_key,
    cross_value,
    cross_out,
    gain_three,
    weight_up,
    weight_down,
    cotangent,
):
    packs, rows, width = tokens.shape
    wide, ff = weight_query.shape[1], weight_up.shape[1]
    lay = Layout(lax.axis_size("blk"), packs, wide // HEAD_DIM, rows, memory.shape[0])
    flat_rows = packs * rows
    x = tokens.reshape(flat_rows, width)
    kept = forward(
        lay,
        {
            "segment_page": segment_page,
            "x": x,
            "segment_ids": segment_ids,
            "token_valid": token_valid,
            "memory": memory,
            "gain_one": gain_one[None],
            "gain_two": gain_two[None],
            "gain_three": gain_three[None],
            "w_q": weight_query,
            "w_k": weight_key,
            "w_v": weight_value,
            "w_ck": cross_key,
            "w_cv": cross_value,
            "cot": cotangent.reshape(flat_rows, width),
            "w_out": weight_out,
            "w_cross_query": cross_query,
            "w_cross_out": cross_out,
            "w_up": weight_up,
            "w_down": weight_down,
        },
        ff,
    )
    out = kept.pop("out").reshape(packs, rows, width)
    grads = backward(
        lay,
        {
            **kept,
            "segment_page": segment_page,
            "x": x,
            "gain_one": gain_one[None],
            "gain_two": gain_two[None],
            "gain_three": gain_three[None],
            "w_cross_query": cross_query,
            "w_out": weight_out,
            "w_ck": cross_key,
            "w_cv": cross_value,
            "w_q": weight_query,
            "w_k": weight_key,
            "w_v": weight_value,
            "w_up": weight_up,
        },
        ff,
    )
    grad_memory = (grads["memory_own"].astype(F32) + grads["memory_other"].astype(F32))[: lay.mem_rows]
    return (
        out,
        grads["input"].reshape(packs, rows, width),
        grad_memory,
        grads["query"],
        grads["key"],
        grads["value"],
        grads["out"].T,
        grads["cross_query"],
        grads["cross_key"],
        grads["cross_value"],
        grads["cross_out"].T,
        grads["up"],
        grads["down"].T,
        grads["gains"][0],
        grads["gains"][1],
        grads["gains"][2],
    )


def solution(mesh):
    in_specs = (
        P(None, "blk", None),
        P("blk", None),
        P(None, "blk"),
        P(None, "blk"),
        P(),
        P(),
        P(None, "tp"),
        P(None, "tp"),
        P(None, "tp"),
        P("tp", None),
        P(),
        P(None, "tp"),
        P(None, "tp"),
        P(None, "tp"),
        P("tp", None),
        P(),
        P(None, "tp"),
        P("tp", None),
        P(None, "blk", None),
    )
    out_specs = (
        P(None, "blk", None),
        P(None, "blk", None),
        P("blk", None),
        P("blk", "tp"),
        P("blk", "tp"),
        P("blk", "tp"),
        P("tp", "blk"),
        P("blk", "tp"),
        P("blk", "tp"),
        P("blk", "tp"),
        P("tp", "blk"),
        P("blk", "tp"),
        P("tp", "blk"),
        P("blk"),
        P("blk"),
        P("blk"),
    )
    return jax.shard_map(local, mesh=mesh, in_specs=in_specs, out_specs=out_specs, check_vma=False)
```

```python
import functools

import jax
import jax.numpy as jnp
from jax import lax
from jax.experimental import pallas as pl
from jax.experimental.pallas import tpu as pltpu
from jax.sharding import PartitionSpec as P

MEM_LEN = 588
HEAD_DIM = 64
NSEG = 3
EPS = 1e-05
NEG = -1e30
EXP2_SCALE = HEAD_DIM**-0.5 * 1.4426950408889634
SCALE = HEAD_DIM**-0.5
LANES = 128
BF16 = jnp.bfloat16
F32 = jnp.float32
MESH = pl.DeviceIdType.MESH


def dot(left, right, contract_left, contract_right):
    return lax.dot_general(
        left, right, (((contract_left,), (contract_right,)), ((), ())), preferred_element_type=F32
    )


def wait_all(copies):
    for copy in copies:
        copy.wait()


class Layout:
    def __init__(self, count, packs, heads, rows, mem_rows):
        self.count, self.packs, self.heads, self.rows = count, packs, heads, rows
        self.half = count // packs
        self.parts = self.half // heads
        self.mem_rows = mem_rows
        self.mem_pad = -(-mem_rows // LANES) * LANES
        self.pieces = MEM_LEN // mem_rows
        self.pages_half = self.half // self.pieces

    def head(self, device):
        return lax.rem(device, self.half) // self.parts


def page_rows(span, piece, real):
    places = lax.broadcasted_iota(jnp.int32, (span, 1), 0)
    return lax.rem(places, piece) < real


def erf(value):
    x = jnp.clip(value, -3.832506856900711, 3.832506856900711)
    square = x * x
    top = jnp.float32(0.00022905065861350646)
    for coefficient in (0.0034082910107109506, 0.050955695062380861, 0.18520832239976145, 1.128379143519084):
        top = top * square + coefficient
    low = jnp.float32(-1.1791602954361697e-7)
    for coefficient in (
        0.000023547966471313185,
        0.0010179625278914885,
        0.014070470171167667,
        0.11098505178285362,
        0.49746925110067538,
        1.0,
    ):
        low = low * square + coefficient
    return x * top / low


def normed_rows(source, gain, low):
    step = 32

    def body(index, _):
        rows = pl.ds(pl.multiple_of(index * step, step), step)
        value = source(rows)
        centred = value - jnp.mean(value, axis=1, keepdims=True)
        inv_std = lax.rsqrt(jnp.mean(centred * centred, axis=1, keepdims=True) + EPS)
        low[rows, :] = (centred * inv_std * gain[...]).astype(BF16)
        return 0

    lax.fori_loop(0, low.shape[0] // step, body, 0)


def norm_back_rows(target, grad, source, gain, residual, low=None):
    step = 32

    def body(index, _):
        rows = pl.ds(pl.multiple_of(index * step, step), step)
        value = source(rows)
        centred = value - jnp.mean(value, axis=1, keepdims=True)
        inv_std = lax.rsqrt(jnp.mean(centred * centred, axis=1, keepdims=True) + EPS)
        z = centred * inv_std
        w = grad(rows) * gain[...]
        inner = w - jnp.mean(w, axis=1, keepdims=True) - z * jnp.mean(w * z, axis=1, keepdims=True)
        value = residual(rows) + inner * inv_std
        target[rows, :] = value
        if low is not None:
            low[rows, :] = value.astype(BF16)
        return 0

    lax.fori_loop(0, target.shape[0] // step, body, 0)


class Exchange:
    def __init__(self, links, received, sent):
        self.links, self.index = links, links.take()
        self.received, self.sent = received, sent

    def start(self, offset, source, target):
        if offset == 0:
            self.keep(source, target)
        else:
            self.links.described(self.index, source, target, {"blk": self.links.me ^ offset}).start()

    def keep(self, source, target):
        pltpu.make_async_copy(source, target, self.links.recv_sem.at[self.index]).start()

    def wait(self):
        for sem, buffers in ((self.links.recv_sem, self.received), (self.links.send_sem, self.sent)):
            for buffer in buffers:
                pltpu.make_async_copy(buffer, buffer, sem.at[self.index]).wait()


class Links:
    def __init__(self, lay, scratch):
        self.lay = lay
        self.me, self.core = lax.axis_index("blk"), lax.axis_index("tp")
        self.head, self.pack = lay.head(self.me), self.me // lay.half
        self.part = lax.rem(self.me, lay.parts)
        self.send_sem, self.recv_sem, self.used = scratch["send_sem"], scratch["recv_sem"], 0
        self.own_sem, self.own_used = scratch["own_sem"], 0
        self.barrier = pltpu.get_barrier_semaphore()

    def page_of(self, pages, side, slot):
        place = pages[self.pack if side == 0 else 1 - self.pack, slot] - self.pack * self.lay.pages_half
        inside = (place >= 0) & (place < self.lay.pages_half)
        return jnp.clip(place, 0, self.lay.pages_half - 1), jnp.where(inside, 1.0, 0.0)

    def announce(self, everyone=False):
        for offset in range(self.lay.count):
            if offset > 0:
                self.signal(offset, self.core)
            if offset == 0 or everyone:
                self.signal(offset, 1 - self.core)

    def signal(self, offset, core):
        device = {"blk": self.me ^ offset, "tp": core}
        pl.semaphore_signal(self.barrier, inc=1, device_id=device, device_id_type=MESH)

    def all_here(self, everyone=False):
        pl.semaphore_wait(self.barrier, (2 if everyone else 1) * self.lay.count - (1 if everyone else 0))

    def take(self, number=1):
        index, self.used = self.used, self.used + number
        return index

    def described(self, index, source, target, device):
        return pltpu.make_async_remote_copy(
            src_ref=source,
            dst_ref=target,
            send_sem=self.send_sem.at[index],
            recv_sem=self.recv_sem.at[index],
            device_id=device,
            device_id_type=MESH,
        )

    def remote(self, source, target, device):
        copy = self.described(self.take(), source, target, device)
        copy.start()
        return copy

    def local(self, source, target):
        copy = pltpu.make_async_copy(source, target, self.own_sem.at[self.own_used])
        self.own_used += 1
        copy.start()
        return copy

    def to(self, offset, source, target):
        if offset == 0:
            return self.local(source, target)
        return self.remote(source, target, {"blk": self.me ^ offset})

    def to_other_core(self, source, target):
        return self.remote(source, target, {"tp": 1 - self.core})

    def spread(self, source, target, every=False):
        lay, step = self.lay, 1 if every else self.lay.parts
        most = lay.count // step * lay.rows
        exchange = Exchange(self, [target], [target.at[:, pl.ds(0, most - lay.rows)]])
        for offset in range(0, lay.count, step):
            peer = self.me ^ offset
            piece = source.at[
                pl.ds(lay.head(peer) * HEAD_DIM, HEAD_DIM), pl.ds((peer // lay.half) * lay.rows, lay.rows)
            ]
            exchange.start(offset, piece, target.at[:, pl.ds((self.me // step) * lay.rows, lay.rows)])
        return exchange

    def unit_place(self, target):
        lay = self.lay
        return target.at[pl.ds(self.head * HEAD_DIM, HEAD_DIM), pl.ds(self.pack * lay.rows, lay.rows)]

    def collect(self, source, target):
        lay, exchange = self.lay, self.to_tokens(target)
        for offset in range(0, lay.count, lay.parts):
            peer = self.me ^ offset
            piece = source.at[:, pl.ds((peer // lay.parts) * lay.rows, lay.rows)]
            exchange.start(offset, piece, self.unit_place(target))
        return exchange

    def to_tokens(self, target):
        return Exchange(self, [target], [target.at[pl.ds(0, (2 * self.lay.heads - 1) * HEAD_DIM // 2), :]])

    def collect_later(self, source, target):
        lay, exchange = self.lay, self.to_tokens(target)

        def send(number):
            peer = number * lay.parts + self.part
            piece, place = source.at[:, pl.ds(number * lay.rows, lay.rows)], self.unit_place(target)

            @pl.when(peer != self.me)
            def _():
                self.described(exchange.index, piece, place, {"blk": peer}).start()

            @pl.when(peer == self.me)
            def _():
                exchange.keep(piece, place)

        return send, exchange.wait


HALVES = ("keys_half", "values_half")


def by_length(longest):
    first = (longest[:1, :1] < 0.5).astype(F32)
    second = (longest[:1, :1] < 1.5).astype(F32) - first
    places = (first, second, 1.0 - first - second)
    return lambda rank, slot: places[(slot - rank) % NSEG]


def forward_body(lay, names, late, out_names, scratch_names, *refs):
    r = dict(zip(names, refs, strict=False))
    o = dict(zip(out_names, refs[len(names) :], strict=False))
    s = dict(zip(scratch_names, refs[len(names) + len(out_names) :], strict=True))
    count, parts, half, rows = lay.count, lay.parts, lay.half, lay.rows
    links = Links(lay, s)
    me, core = links.me, links.core
    links.announce()
    flat_rows, width = r["x"].shape
    wide, ff = s["w_out"].shape[0], s["w_up"].shape[1]
    total = count * rows
    mine_total = total // parts
    loading = {name: links.local(r[name], s[name]) for name in late}
    leaving = []

    codes = (r["segment_ids"][...] * 2 + r["token_valid"][...]).astype(F32)
    for pack in range(lay.packs):
        s["code_tok"][pack] = jnp.broadcast_to(codes[pack : pack + 1, :], (8, rows))

    def ready(*wanted):
        for name in wanted:
            loading[name].wait()

    def emit(*wanted):
        for name in wanted:
            leaving.append(links.local(s[name], o[name]))

    half_rows = pl.ds(pl.multiple_of(core * wide, wide), wide)
    other, group = me ^ half, 4
    normed_rows(lambda here: r["x"][here, :].astype(F32), r["gain_one"], s["h1"])
    for index, name in enumerate(("w_q", "w_k", "w_v")):
        ready(name)
        s["tok"][index] = dot(s["h1"][...], s[name][...], 1, 0).astype(BF16).T
    links.all_here()
    all_copies = []
    for index in range(3):
        target = s["query"] if index == 0 and parts > 1 else s["qkv"].at[index]
        all_copies.append(links.spread(s["tok"].at[index], target, index > 0))
    all_copies.append(Exchange(links, [s["codes"]], [s["codes"].at[:, pl.ds(0, total - rows)]]))
    for offset in range(count):
        piece = s["code_tok"].at[(me ^ offset) // half]
        all_copies[-1].start(offset, piece, s["codes"].at[:, pl.ds(me * rows, rows)])

    s["mem"][lay.mem_rows // 16 * 16 :, :] = jnp.zeros_like(s["mem"][lay.mem_rows // 16 * 16 :, :])
    s["mem"][: lay.mem_rows, :] = r["memory"][...]
    emit("mem")
    ready("w_ck", "w_cv")
    memory_copies = []
    for kind, name in enumerate(("w_ck", "w_cv")):
        s["kv_tok"][kind] = dot(s["mem"][...], s[name][...], 1, 0).astype(BF16).T
        target = s[HALVES[kind]]
        memory_copies.append(Exchange(links, [target], [target.at[pl.ds(0, half - 1)]]))
        for offset in range(half):
            piece = s["kv_tok"].at[kind, pl.ds(lay.head(me ^ offset) * HEAD_DIM, HEAD_DIM), :]
            memory_copies[-1].start(offset, piece, target.at[lax.rem(me, half)])
    twin_copies = []

    def find_pages(kind):
        memory_copies[kind].wait()
        for side in range(2):
            order = by_length(s["longest"][side])
            found = [links.page_of(r["segment_page"], side, slot) for slot in range(NSEG)]
            for piece in range(lay.pieces):
                columns = slice(piece * lay.mem_pad, (piece + 1) * lay.mem_pad)
                values = [
                    s[HALVES[kind]][page * lay.pieces + piece].astype(F32) * here for page, here in found
                ]
                for rank in range(NSEG):
                    value = sum(order(rank, slot) * values[slot] for slot in range(NSEG)).astype(BF16)
                    if rank > 0:
                        s["kv_small"][side, rank - 1, kind, :, columns] = value
                    else:
                        s["main_found"][kind, side, :, columns] = value
        twin_copies.append(
            links.remote(s["main_found"].at[kind, 1], s["main_twin"].at[kind], {"blk": other})
        )

    s["h1_turned"][...] = s["h1"][:, half_rows].T

    def pack_chunk(owner, first=0, size=wide):
        return o["h1_pack"].at[pl.ds(first, size), pl.ds(pl.multiple_of(owner * rows, rows), rows)]

    def hand_over():
        return [
            links.remote(
                s["h1_turned"].at[:, pl.ds((1 - links.pack) * rows, rows)], pack_chunk(me), {"blk": other}
            ),
            links.local(s["h1_turned"].at[:, pl.ds(links.pack * rows, rows)], pack_chunk(me)),
        ]

    ways = half.bit_length() - 1
    shares = [16 * (wide // 16 // ways + (way < wide // 16 % ways)) for way in range(ways)]

    def double(step, owners):
        moved = o["h1_pack"].at[:, pl.ds(0, len(owners) * rows << step)]
        exchange = Exchange(links, [moved], [moved])
        for way in range(ways):
            first, order = sum(shares[:way]), [(way + turn) % ways for turn in range(step + 1)]
            held = [0]
            for bit in order[:-1]:
                held += [offset ^ (1 << bit) for offset in held]
            for owner in owners:
                for offset in held:
                    piece = pack_chunk(owner ^ offset, first, shares[way])
                    exchange.start(1 << order[-1], piece, piece)
        return [exchange]

    def to_group(source, target):
        moved = target.at[pl.ds(1, group - 1), :, half_rows]
        exchange = Exchange(links, [moved], [moved])
        for offset in range(1, group):
            exchange.start(offset, source.at[:, half_rows], target.at[offset, :, half_rows])
        return [exchange, links.local(source, target.at[0])]

    wait_all(all_copies)
    pack_copies = hand_over()

    codes = s["codes"][:1, :]
    segments = jnp.floor(codes * 0.5)
    s["code"][...] = jnp.where(codes - 2.0 * segments > 0.5, segments, -1.0)
    lengths = [
        jnp.sum((segments == float(slot)).astype(F32), axis=1, keepdims=True) for slot in range(NSEG)
    ]
    first_longest = ((lengths[0] >= lengths[1]) & (lengths[0] >= lengths[2])).astype(F32)
    second_longest = (lengths[1] >= lengths[2]).astype(F32) * (1.0 - first_longest)
    longest = 2.0 - 2.0 * first_longest - second_longest
    order = segments - longest
    order = jnp.where(order < 0.0, order + float(NSEG), order)
    if parts == 1:
        s["qseg"][...], s["qslot"][...] = segments, order
    else:
        s["rows"][0:1, :], s["rows"][1:2, :] = segments, order
        for piece in range(count // parts):
            there = pl.ds((piece * parts + links.part) * rows, rows)
            s["qseg"][:, piece * rows : (piece + 1) * rows] = s["rows"][0:1, there]
            s["qslot"][:, piece * rows : (piece + 1) * rows] = s["rows"][1:2, there]
    s["longest"][0] = jnp.broadcast_to(longest, s["longest"].shape[1:])
    ends = [slice(0, LANES), slice(mine_total - LANES, mine_total)]
    for index, here in enumerate(ends):
        s["ends_slot"][0, :, index * LANES : (index + 1) * LANES] = jnp.broadcast_to(
            s["qslot"][:, here], (8, LANES)
        )
    early_copies = [
        links.remote(s[name].at[0], s[name].at[1], {"blk": other}) for name in ("longest", "ends_slot")
    ]
    emit("qkv", "code", "qseg", "qslot")
    if parts > 1:
        emit("query")

    block = min(512 if parts == 1 else 256, mine_total)
    s["key"][...] = s["qkv"][1].T
    send_mixed, wait_mixed = links.collect_later(s["low"].at[0], s["mixed"])
    for index in reversed(range(mine_total // block)):
        columns = slice(index * block, (index + 1) * block)
        query = s["query"][:, columns] if parts > 1 else s["qkv"][0, :, columns]
        mine = s["qseg"][:, columns]
        places = index * block + lax.broadcasted_iota(jnp.int32, (1, block), 1)
        positions = ((places // rows) * parts + links.part) * rows + places % rows

        def fold(key_index, state, causal, query=query, mine=mine, positions=positions):
            largest, weight_sum, weighted = state
            start = pl.multiple_of(key_index * block, block)
            here = pl.ds(start, block)
            scores = jnp.dot(s["key"][here, :], query, preferred_element_type=F32)
            allowed = jnp.broadcast_to(s["code"][:, here], (8, block)).T[:, :1] == mine
            if causal:
                key_places = start + lax.broadcasted_iota(jnp.int32, (block, block), 0)
                allowed = allowed & (key_places <= positions)
            scores = jnp.where(allowed, scores, NEG)
            new = jnp.maximum(largest, jnp.max(scores, axis=0, keepdims=True))
            weights = jnp.exp2((scores - new) * EXP2_SCALE)
            keep = jnp.exp2((largest - new) * EXP2_SCALE)
            weight_sum = weight_sum * keep + jnp.sum(weights, axis=0, keepdims=True)
            update = jnp.dot(s["qkv"][2, :, here], weights.astype(BF16), preferred_element_type=F32)
            return (new, weight_sum, weighted * keep + update)

        state = (
            jnp.full((1, block), NEG, F32),
            jnp.zeros((1, block), F32),
            jnp.zeros((HEAD_DIM, block), F32),
        )
        state = lax.fori_loop(0, index * parts, lambda j, c, fold=fold: fold(j, c, False), state)
        for extra in range(parts):
            state = fold(index * parts + extra, state, True)
        largest, weight_sum, weighted = state
        result = weighted / weight_sum
        s["att"][:, columns] = result
        s["low"][0, :, columns] = result.astype(BF16)
        s["log"][:, columns] = largest * EXP2_SCALE + jnp.log2(weight_sum)
        for piece in range(index * block // rows, (index + 1) * block // rows):
            send_mixed(piece)
    emit("att", "log")

    def product_rows(left, right, sent, arrived):
        started = []
        for start in range(0, flat_rows, rows):
            here = slice(start, start + rows)
            sent[here, :] = dot(left[:, here].T, right[...], 1, 0).astype(BF16)
            started.append(links.to_other_core(sent.at[pl.ds(start, rows)], arrived.at[pl.ds(start, rows)]))
        return started

    def group_to_other_core(target):
        others = target.at[pl.ds(1, group - 1), :, half_rows]
        return links.to_other_core(others, others)

    def both(sent, arrived):
        return lambda here: sent[here, :].astype(F32) + arrived[here, :].astype(F32)

    def add_rows(target, *terms):
        step = 32

        def body(index, _):
            here = pl.ds(pl.multiple_of(index * step, step), step)
            target[here, :] = sum(term(here) for term in terms).astype(target.dtype)
            return 0

        lax.fori_loop(0, flat_rows // step, body, 0)

    wait_all(early_copies)
    for kind in range(2):
        find_pages(kind)
    for side in range(2):
        order = by_length(s["longest"][side])
        for rank in range(1, NSEG):
            here = sum(
                order(rank, slot) * links.page_of(r["segment_page"], side, slot)[1] for slot in range(NSEG)
            )
            row = 2 * side + rank - 1
            s["ends_mask"][row : row + 1, :] = (s["ends_slot"][side, :1, :] == float(rank)).astype(F32) * here
    emit("longest", "kv_small", "ends_mask")
    ready("w_out")
    wait_mixed()
    wait_all(pack_copies)
    pack_copies = double(0, [me, other])
    emit("mixed")
    started = product_rows(s["mixed"], s["w_out"], s["sent"].at[0], s["arrived"].at[0])
    wait_all(started)
    add_rows(
        s["r1"], lambda here: r["x"][here, :].astype(F32), both(s["sent"].at[0], s["arrived"].at[0])
    )
    normed_rows(lambda here: s["r1"][here, :], r["gain_two"], s["h2"])
    ready("w_cross_query")
    s["tok"][0] = dot(s["h2"][...], s["w_cross_query"][...], 1, 0).astype(BF16).T
    query_copies = links.spread(s["tok"].at[0], s["cross_unit"])
    ready("cot")
    cot_copies = to_group(s["cot"], o["dm_group"])
    emit("r1", "h2")

    narrow = min(256, mine_total)
    present = page_rows(lay.pieces * lay.mem_pad, lay.mem_pad, lay.mem_rows)
    send_cross, wait_cross = links.collect_later(s["low"].at[1], s["cross_mixed"])
    wait_all(twin_copies)
    for kind in range(2):
        value = s["main_found"][kind, 0].astype(F32) + s["main_twin"][kind].astype(F32)
        s["kv_main"][kind] = value.astype(BF16)
    emit("kv_main")
    query_copies.wait()
    ends_copies = [
        links.remote(s["cross_unit"].at[:, pl.ds(here.start, LANES)], s["ends_query"].at[index], {"blk": other})
        for index, here in enumerate(ends)
    ]
    emit("cross_unit")
    wait_all(pack_copies)
    pack_copies = double(1, [me, other])

    def attend(query, keys, values):
        scores = jnp.dot(keys, query, preferred_element_type=F32)
        scores = jnp.where(present, scores, NEG)
        largest = jnp.max(scores, axis=0, keepdims=True)
        weights = jnp.exp2((scores - largest) * EXP2_SCALE)
        weight_sum = jnp.sum(weights, axis=0, keepdims=True)
        result = jnp.dot(values, weights.astype(BF16), preferred_element_type=F32)
        return result / weight_sum, largest * EXP2_SCALE + jnp.log2(weight_sum)

    key_rows = s["kv_main"][0].T
    pieces = mine_total // rows
    for index in range(mine_total // narrow):
        columns = slice(index * narrow, (index + 1) * narrow)
        result, logs = attend(s["cross_unit"][:, columns], key_rows, s["kv_main"][1])
        s["cross_att"][:, columns], s["cross_log"][:, columns] = result, logs
        s["low"][1, :, columns] = result.astype(BF16)
        for piece in range(index * narrow // rows, (index + 1) * narrow // rows):
            if 0 < piece < pieces - 1:
                send_cross(piece)

    def attend_ends(side, query_of):
        results = [(jnp.zeros((HEAD_DIM, LANES), F32), jnp.zeros((1, LANES), F32)) for _ in ends]
        for rank in range(1, NSEG):
            keys = s["kv_small"][side, rank - 1, 0].T
            for index in range(2):
                result, logs = attend(query_of(index), keys, s["kv_small"][side, rank - 1, 1])
                row = 2 * side + rank - 1
                here = s["ends_mask"][row : row + 1, index * LANES : (index + 1) * LANES] > 0.5
                results[index] = (
                    jnp.where(here, result, results[index][0]),
                    jnp.where(here, logs, results[index][1]),
                )
        return results

    wait_all(ends_copies)
    for index, (result, logs) in enumerate(attend_ends(1, lambda index: s["ends_query"][index])):
        s["ends_att"][0, index] = result.astype(BF16)
        s["ends_log"][0, :, index * LANES : (index + 1) * LANES] = jnp.broadcast_to(logs, (8, LANES))
    ends_copies = [
        links.remote(s[name].at[0], s[name].at[1], {"blk": other}) for name in ("ends_att", "ends_log")
    ]
    own_ends = attend_ends(0, lambda index: s["cross_unit"][:, ends[index]])
    wait_all(ends_copies)
    for index, (here, (result, logs)) in enumerate(zip(ends, own_ends, strict=True)):
        small = s["qslot"][:, here] > 0.5
        result = result + s["ends_att"][1, index].astype(F32)
        logs = logs + s["ends_log"][1, :1, index * LANES : (index + 1) * LANES]
        result = jnp.where(small, result, s["cross_att"][:, here])
        s["cross_att"][:, here] = result
        s["cross_log"][:, here] = jnp.where(small, logs, s["cross_log"][:, here])
        s["low"][1, :, here] = result.astype(BF16)
        send_cross(here.start // rows)
    emit("ends_query")
    emit("cross_att", "cross_log")
    ready("w_cross_out")
    wait_cross()
    for step in range(2, ways):
        wait_all(pack_copies)
        pack_copies = double(step, [me, other])
    emit("cross_mixed")
    started = product_rows(s["cross_mixed"], s["w_cross_out"], s["sent"].at[1], s["arrived"].at[1])
    wait_all(started)
    add_rows(s["r2"], lambda here: s["r1"][here, :], both(s["sent"].at[1], s["arrived"].at[1]))
    normed_rows(lambda here: s["r2"][here, :], r["gain_three"], s["h1"])
    h3_copies = to_group(s["h1"], o["h3_group"])

    ready("w_up", "w_down")
    slice_width = ff // group
    s["down_sum"][...] = jnp.zeros_like(s["down_sum"])
    s["up_sum"][...] = jnp.zeros_like(s["up_sum"])
    piece_rows = LANES
    for number in range(group):
        columns = slice(number * slice_width, (number + 1) * slice_width)
        for start in range(0, flat_rows, piece_rows):
            here = slice(start, start + piece_rows)
            u = dot(s["h1"][here, :], s["w_up"][:, columns], 1, 0)
            grad = dot(s["cot"][here, :], s["w_down"][columns, :], 1, 1)
            normal = 0.5 + 0.5 * erf(u * 0.7071067811865476)
            s["gelu"][here, columns] = (u * normal).astype(BF16)
            slope = normal + u * jnp.exp2(u * u * -0.7213475204444817) * 0.3989422804014327
            s["du"][here, columns] = (slope * grad).astype(BF16)
        s["down_sum"][...] += dot(s["gelu"][:, columns], s["w_down"][columns, :], 1, 0)
        s["up_sum"][...] += dot(s["du"][:, columns], s["w_up"][:, columns], 1, 1)
    emit("gelu", "du")
    s["sent"][2] = s["up_sum"][...].astype(BF16)
    up_copy = links.to_other_core(s["sent"].at[2], s["arrived"].at[2])
    s["sent"][3] = s["down_sum"][...].astype(BF16)
    down_copy = links.to_other_core(s["sent"].at[3], s["arrived"].at[3])
    up_copy.wait()
    norm_back_rows(
        s["grad_two"],
        both(s["sent"].at[2], s["arrived"].at[2]),
        lambda here: s["r2"][here, :],
        r["gain_three"],
        lambda here: s["cot"][here, :].astype(F32),
        s["dc"],
    )
    s["tok"][0] = dot(s["w_cross_out"][...], s["dc"][...], 1, 1).astype(BF16)
    doc_copies = links.spread(s["tok"].at[0], s["doc_unit"])
    emit("grad_two", "dc")
    wait_all(cot_copies)
    wait_all(h3_copies)
    group_copies = [group_to_other_core(o["dm_group"]), group_to_other_core(o["h3_group"])]
    down_copy.wait()
    add_rows(s["sent"].at[3], lambda here: s["r2"][here, :], both(s["sent"].at[3], s["arrived"].at[3]))
    leaving.append(links.local(s["sent"].at[3], o["out"]))
    doc_copies.wait()
    emit("doc_unit")
    wait_all(group_copies)
    wait_all(pack_copies)
    wait_all(leaving)
    assert links.used <= links.send_sem.shape[0] and links.own_used <= links.own_sem.shape[0]


def forward(lay, values, ff):
    parts, count, half, rows = lay.parts, lay.count, lay.half, lay.rows
    flat_rows, width = values["x"].shape
    wide, total = lay.heads * HEAD_DIM, lay.count * lay.rows
    mine_total = total // parts
    span = lay.pieces * lay.mem_pad
    early = ["x", "segment_ids", "token_valid", "memory", "gain_one", "gain_two", "gain_three"]
    late = [name for name in values if name not in early + ["segment_page"]]
    names = ["segment_page"] + early + late

    def shape(*dims, dtype=BF16):
        return jax.ShapeDtypeStruct(dims, dtype)

    kept = {
        "qkv": shape(3, HEAD_DIM, total),
        "code": shape(1, total, dtype=F32),
        "qseg": shape(1, mine_total, dtype=F32),
        "qslot": shape(1, mine_total, dtype=F32),
        "longest": shape(2, 8, LANES, dtype=F32),
        "att": shape(HEAD_DIM, mine_total, dtype=F32),
        "log": shape(1, mine_total, dtype=F32),
        "mixed": shape(wide, flat_rows),
        "r1": shape(flat_rows, width, dtype=F32),
        "h2": shape(flat_rows, width),
        "cross_unit": shape(HEAD_DIM, mine_total),
        "kv_main": shape(2, HEAD_DIM, span),
        "kv_small": shape(2, NSEG - 1, 2, HEAD_DIM, span),
        "ends_query": shape(2, HEAD_DIM, LANES),
        "ends_mask": shape(8, 2 * LANES, dtype=F32),
        "cross_att": shape(HEAD_DIM, mine_total, dtype=F32),
        "cross_log": shape(1, mine_total, dtype=F32),
        "cross_mixed": shape(wide, flat_rows),
        "grad_two": shape(flat_rows, width, dtype=F32),
        "dc": shape(flat_rows, width),
        "doc_unit": shape(HEAD_DIM, mine_total),
        "mem": shape(lay.mem_pad, width),
        "gelu": shape(flat_rows, ff),
        "du": shape(flat_rows, ff),
    }
    if parts > 1:
        kept["query"] = shape(HEAD_DIM, mine_total)
    gathered = {
        "dm_group": shape(4, flat_rows, width),
        "h3_group": shape(4, flat_rows, width),
        "out": shape(flat_rows, width),
        "h1_pack": shape(wide, total),
    }
    scratch = {
        "h1": shape(flat_rows, width),
        "tok": shape(3, wide, flat_rows),
        "codes": shape(8, total, dtype=F32),
        "code_tok": shape(lay.packs, 8, rows, dtype=F32),
        "kv_tok": shape(2, wide, lay.mem_pad),
        "keys_half": shape(half, HEAD_DIM, lay.mem_pad),
        "values_half": shape(half, HEAD_DIM, lay.mem_pad),
        "main_found": shape(2, 2, HEAD_DIM, span),
        "main_twin": shape(2, HEAD_DIM, span),
        "ends_slot": shape(2, 8, 2 * LANES, dtype=F32),
        "ends_att": shape(2, 2, HEAD_DIM, LANES),
        "ends_log": shape(2, 8, 2 * LANES, dtype=F32),
        "key": shape(total, HEAD_DIM),
        "low": shape(2, HEAD_DIM, mine_total),
        "h1_turned": shape(wide, flat_rows),
        "sent": shape(4, flat_rows, width),
        "arrived": shape(4, flat_rows, width),
        "r2": shape(flat_rows, width, dtype=F32),
        "down_sum": shape(flat_rows, width, dtype=F32),
        "up_sum": shape(flat_rows, width, dtype=F32),
    }
    if parts > 1:
        scratch["rows"] = shape(8, total, dtype=F32)
    scratch = {name: pltpu.VMEM(value.shape, value.dtype) for name, value in {**scratch, **kept}.items()}
    for name in late:
        scratch[name] = pltpu.VMEM(values[name].shape, values[name].dtype)
    semaphores = pltpu.SemaphoreType.DMA((34,))
    scratch = {"send_sem": semaphores, "recv_sem": semaphores, **scratch}
    scratch["own_sem"] = pltpu.SemaphoreType.DMA((40,))
    outs = {**kept, **gathered}
    anywhere = pl.BlockSpec(memory_space=pl.ANY)
    results = pl.pallas_call(
        functools.partial(forward_body, lay, names, late, list(outs), list(scratch)),
        out_shape=list(outs.values()),
        in_specs=[pl.BlockSpec(memory_space=pltpu.SMEM)]
        + [pl.BlockSpec(memory_space=pltpu.VMEM)] * len(early)
        + [anywhere] * len(late),
        out_specs=[anywhere] * len(outs),
        scratch_shapes=list(scratch.values()),
        compiler_params=pltpu.CompilerParams(
            collective_id=0, has_side_effects=True, vmem_limit_bytes=63 * 1024 * 1024
        ),
    )(*[values[name] for name in names])
    return dict(zip(outs, results, strict=True))


def reversed_bits(value, bits):
    return sum(((value >> b) & 1) << (bits - 1 - b) for b in range(bits))


class Halving:
    def __init__(self, links, bits, sums, arrivals, crossed=True):
        self.links, self.bits, self.crossed = links, bits, crossed
        self.sums, self.arrivals = sums, arrivals
        self.quarter = sums.shape[1] // 2
        self.jobs, self.pending = [], []

    def neighbour(self, kind, step):
        bit = self.bits[1 - step if self.crosses(kind) and step < 2 else step]
        return {"blk": self.links.me ^ (1 << bit)}

    def crosses(self, kind):
        return kind == 1 and self.crossed

    def add_job(self, column, width, make):
        here, started = pl.ds(column, width), []
        for kind in range(2):
            for half, quarter in enumerate((1, 3) if self.crosses(kind) else (2, 3)):
                rows = pl.ds(half * self.quarter, self.quarter)
                self.sums[kind, rows, here] = make(kind, quarter).astype(BF16)
            started.append(
                self.links.remote(
                    self.sums.at[kind, :, here],
                    self.arrivals[0].at[kind, :, here],
                    self.neighbour(kind, 0),
                )
            )
        self.jobs.append((here, make, started))

    def keep_jobs(self):
        for here, make, started in self.jobs:
            wait_all(started)
            for kind in range(2):
                for half, quarter in enumerate((0, 2) if self.crosses(kind) else (0, 1)):
                    rows = pl.ds(half * self.quarter, self.quarter)
                    arrived = self.arrivals[0][kind, rows, here].astype(F32)
                    self.sums[kind, rows, here] = (make(kind, quarter) + arrived).astype(BF16)
        self.send(1)

    def send(self, step):
        rows = self.sums.shape[1] >> step
        self.pending = [
            self.links.remote(
                self.sums.at[kind, pl.ds(rows, rows), :],
                self.arrivals[step].at[kind],
                self.neighbour(kind, step),
            )
            for kind in range(2)
        ]

    def receive(self, step, result=None):
        rows = self.sums.shape[1] >> step
        wait_all(self.pending)
        size = min(rows, 32)

        def add(index, _):
            here = pl.ds(pl.multiple_of(index * size, size), size)
            for kind in range(2):
                mine = self.sums[kind, here, :].astype(F32)
                total = mine + self.arrivals[step][kind, here, :].astype(F32)
                if result is None:
                    self.sums[kind, here, :] = total.astype(BF16)
                else:
                    result[kind, here, :] = total
            return 0

        lax.fori_loop(0, rows // size, add, 0)
        if step + 1 < len(self.bits):
            self.send(step + 1)


def arrivals_shapes(bits, width, columns):
    return [pltpu.VMEM((2, width >> (step + 1), columns), BF16) for step in range(bits)]


OUTS = (
    "input", "memory_own", "memory_other", "query", "key", "value", "out", "cross_query", "cross_key",
    "cross_value", "cross_out", "up", "down", "gain_one", "gain_two", "gain_three",
)


def backward_body(lay, names, late, scratch_names, *refs):
    r = dict(zip(names, refs, strict=False))
    o = dict(zip(OUTS, refs[len(names) :], strict=False))
    s = dict(zip(scratch_names, refs[len(names) + len(OUTS) :], strict=True))
    far = dict(r)
    count, parts, half, rows = lay.count, lay.parts, lay.half, lay.rows
    links = Links(lay, s)
    me, core, head, pack, part = links.me, links.core, links.head, links.pack, links.part
    bits = count.bit_length() - 1
    flat_rows, width = r["dc"].shape
    wide = r["w_out"].shape[0]
    total = r["qkv"].shape[2]
    mine_total = total // parts
    share = width // count
    block = min(512 if parts == 1 else 256, mine_total)
    links.announce(everyone=True)
    loading = {}

    def load(name):
        loading[name] = links.local(r[name], s["in_" + late[name]])

    for name, home in late.items():
        if name == home:
            load(name)
    own_rows = pl.ds(pl.multiple_of(me * share, share), share)
    row_copies = [
        links.local(far[name].at[own_rows, :], s["rows_" + name])
        for name in ("w_q", "w_k", "w_v", "w_cross_query", "w_up")
    ]
    h1_copy = links.local(r["h1_pack"].at[:, pl.ds(0, s["h1"].shape[1])], s["h1"])

    def ready(*wanted):
        for name in wanted:
            loading[name].wait()
            r[name] = s["in_" + late[name]]

    def relative(target, value, shift=0, column=0):
        number, most = count >> shift, s["turn"].shape[1]
        size_rows = width // number
        for start in range(0, value.shape[0], most):
            size = min(most, value.shape[0] - start)
            s["turn"][:, :size] = value[start : start + size, :].T
            for place in range(number):
                chunk = (me >> shift) ^ reversed_bits(place, bits - shift)
                target[pl.ds(place * size_rows, size_rows), column + start : column + start + size] = s[
                    "turn"
                ][pl.ds(pl.multiple_of(chunk * size_rows, size_rows), size_rows), :size]

    quarter = width // 4

    def quarter_of(ref, index):
        return ref[pl.ds(index * quarter, quarter), :]

    def from_units(target, sent_rows):
        sent = [target.at[index] for index in range(1, parts)] + [target.at[0, :, pl.ds(0, sent_rows), :]]
        return Exchange(links, [target], sent)

    def batch(name, chosen, crossed=True):
        arrivals = [s[f"{name}_{i}"] for i in range(len(chosen))]
        return Halving(links, chosen, s[name + "_sums"], arrivals, crossed)

    piece = wide // 2

    def weight_job(target, place, left, right):
        def make(kind, index):
            return dot(quarter_of(left, index), right[kind * piece : (kind + 1) * piece, :], 1, 1)

        target.add_job(place * piece, piece, make)

    group = 4
    slice_width = s["gelu_group"].shape[2]
    links.all_here(everyone=True)

    def to_group(name):
        target = s[name + "_group"]
        exchange = Exchange(links, [target], [target.at[pl.ds(0, group - 1)]])
        for offset in range(group):
            number = lax.rem(me ^ offset, group)
            columns = pl.ds(pl.multiple_of(number * slice_width, slice_width), slice_width)
            exchange.start(offset, r[name].at[:, columns], target.at[offset])
        return exchange

    gelu_copies, du_copies = to_group("gelu"), to_group("du")

    ready("doc_unit", "kv_main", "cross_unit", "cross_att", "kv_small")
    span = r["kv_main"].shape[2]
    other = me ^ half
    ends = [slice(0, LANES), slice(mine_total - LANES, mine_total)]
    for index, here in enumerate(ends):
        columns = slice(index * LANES, (index + 1) * LANES)
        grad = r["doc_unit"][:, here].astype(F32)
        s["ends_rows"][0, 0:1, columns] = r["cross_log"][:, here]
        s["ends_rows"][0, 1:2, columns] = jnp.sum(grad * r["cross_att"][:, here], axis=0, keepdims=True)
    ends_copies = [links.remote(s["ends_rows"].at[0], s["ends_rows"].at[1], {"blk": other})]
    for index, here in enumerate(ends):
        piece_of = r["doc_unit"].at[:, pl.ds(here.start, LANES)]
        ends_copies.append(links.remote(piece_of, s["ends_doc"].at[index], {"blk": other}))
    s["cross_key"][...] = r["kv_main"][0].T
    s["cross_value"][...] = r["kv_main"][1].T
    s["cross_acc"][...] = jnp.zeros_like(s["cross_acc"])
    present = page_rows(span, lay.mem_pad, lay.mem_rows)

    def cross_block(query, grad, logs, row_dot, allowed, keys, key_rows, value_rows):
        scores = jnp.dot(key_rows, query, preferred_element_type=F32)
        weights = jnp.where(present & allowed, jnp.exp2(scores * EXP2_SCALE - logs), 0.0)
        weight_grad = jnp.dot(value_rows, grad, preferred_element_type=F32)
        score_grad = (weights * (weight_grad - row_dot)).astype(BF16)
        dq = jnp.dot(keys, score_grad, preferred_element_type=F32)
        return dq, dot(query, score_grad, 1, 1), dot(grad, weights.astype(BF16), 1, 1)

    narrow = min(256, mine_total)

    def main_slot(index, _):
        here = pl.ds(pl.multiple_of(index * narrow, narrow), narrow)
        grad = r["doc_unit"][:, here]
        row_dot = jnp.sum(grad.astype(F32) * r["cross_att"][:, here], axis=0, keepdims=True)
        dq, dk, dv = cross_block(
            r["cross_unit"][:, here],
            grad,
            r["cross_log"][:, here],
            row_dot,
            r["qslot"][:, here] < 0.5,
            r["kv_main"][0],
            s["cross_key"][...],
            s["cross_value"][...],
        )
        s["dq_acc"][:, here] = dq
        s["cross_acc"][0] += dk
        s["cross_acc"][1] += dv
        return 0

    lax.fori_loop(0, mine_total // narrow, main_slot, 0)
    s["main_low"][0] = (s["cross_acc"][0] * SCALE).astype(BF16)
    s["main_low"][1] = s["cross_acc"][1].astype(BF16)
    send_dqc, wait_dqc = links.collect_later(s["dq_low"], s["in_small"].at[0])
    s["dq_low"][...] = (s["dq_acc"][...] * SCALE).astype(BF16)
    last_piece = mine_total // rows - 1
    def small_slots(side, queries, grads):
        dq_ends = [jnp.zeros((HEAD_DIM, LANES), F32) for _ in ends]
        for rank in range(1, NSEG):
            keys, values = r["kv_small"][side, rank - 1, 0], r["kv_small"][side, rank - 1, 1]
            key_rows, value_rows = keys.T, values.T
            row, sums = 2 * side + rank - 1, None
            for index in range(2):
                columns = slice(index * LANES, (index + 1) * LANES)
                dq, dk, dv = cross_block(
                    queries(index),
                    grads(index),
                    s["ends_rows"][side, 0:1, columns],
                    s["ends_rows"][side, 1:2, columns],
                    r["ends_mask"][row : row + 1, columns] > 0.5,
                    keys,
                    key_rows,
                    value_rows,
                )
                dq_ends[index] = dq_ends[index] + dq
                sums = (dk, dv) if sums is None else (sums[0] + dk, sums[1] + dv)
            s["small_grad"][side, rank - 1, 0] = (sums[0] * SCALE).astype(BF16)
            s["small_grad"][side, rank - 1, 1] = sums[1].astype(BF16)
        return dq_ends

    wait_all(ends_copies)
    other_dq = small_slots(1, lambda index: r["ends_query"][index], lambda index: s["ends_doc"][index])
    for index in range(2):
        s["ends_dq"][0, index] = other_dq[index].astype(BF16)
    ends_copy = links.remote(s["ends_dq"].at[0], s["ends_dq"].at[1], {"blk": other})
    for number in range(1, last_piece):
        send_dqc(number)
    own_dq = small_slots(
        0, lambda index: r["cross_unit"][:, ends[index]], lambda index: r["doc_unit"][:, ends[index]]
    )
    ends_copy.wait()
    for index, here in enumerate(ends):
        value = s["dq_acc"][:, here] + own_dq[index] + s["ends_dq"][1, index].astype(F32)
        s["dq_low"][:, here] = (value * SCALE).astype(BF16)
    send_dqc(0)
    send_dqc(last_piece)
    load("att")
    twin_copies = [links.remote(s["main_low"], s["main_twin"], {"blk": other})]

    ready("dm_group")
    for offset in range(group):
        relative(s["rel_dm"], r["dm_group"].at[offset], 2, offset * flat_rows)

    def feed_job(left, right):
        def make(kind, index):
            here = slice(kind * slice_width // 2, (kind + 1) * slice_width // 2)
            return dot(
                quarter_of(left, index), right[:, :, here].reshape(group * flat_rows, slice_width // 2), 1, 0
            )

        return make

    down, up = [batch(name, range(2, bits), crossed=False) for name in ("down", "up")]
    gelu_copies.wait()
    down.add_job(0, slice_width // 2, feed_job(s["rel_dm"], s["gelu_group"]))
    middle, pages = batch("middle", range(bits)), batch("pages", range(bits))
    ready("cross_mixed")
    relative(s["rel_dc"], r["dc"])
    weight_job(middle, 0, s["rel_dc"], r["cross_mixed"])
    ready("h3_group")
    for offset in range(group):
        relative(s["rel_h3"], r["h3_group"].at[offset], 2, offset * flat_rows)

    ready("w_cross_query")
    wait_dqc()
    tp_copies = []
    for start in range(0, flat_rows, rows):
        here = slice(start, start + rows)
        s["tp_send"][here, :] = dot(s["in_small"][0, :, here].T, r["w_cross_query"][...], 1, 1).astype(BF16)
        tp_copies.append(
            links.to_other_core(s["tp_send"].at[pl.ds(start, rows)], s["tp_recv"].at[0, pl.ds(start, rows)])
        )
    ready("h2", "r1", "grad_two")
    relative(s["rel_h2"], r["h2"])
    load("x")
    weight_job(middle, 1, s["rel_h2"], s["in_small"].at[0])
    wait_all(tp_copies)

    def both_cores(index):
        def grad(here):
            return s["tp_send"][here, :].astype(F32) + s["tp_recv"][index, here, :].astype(F32)

        return grad

    norm_back_rows(
        s["grad_one"],
        both_cores(0),
        lambda here: r["r1"][here, :],
        r["gain_two"],
        lambda here: r["grad_two"][here, :],
        s["da"],
    )
    ready("w_out")
    s["out_small"][0] = dot(r["w_out"][...], s["da"][...], 1, 1).astype(BF16)
    do_copies = links.spread(s["out_small"].at[0], s["do_unit"])
    load("w_q")
    ready("mixed")
    relative(s["rel_da"], s["da"])
    orders = [by_length(r["longest"][side]) for side in range(2)]

    def hot(side, rank, page):
        value = None
        for slot in range(NSEG):
            wanted = r["segment_page"][pack if side == 0 else 1 - pack, slot]
            term = orders[side](rank, slot) * jnp.where(wanted == pack * lay.pages_half + page, 1.0, 0.0)
            value = term if value is None else value + term
        return value

    wait_all(twin_copies)
    terms = [(0, 0, s["main_low"]), (1, 0, s["main_twin"])]
    terms += [(side, rank, s["small_grad"].at[side, rank - 1]) for side in range(2) for rank in range(1, NSEG)]

    def add_page(page, _):
        weights = [hot(side, rank, page) for side, rank, _ in terms]
        for piece_index in range(lay.pieces):
            here = slice(piece_index * lay.mem_pad, (piece_index + 1) * lay.mem_pad)
            for kind in range(2):
                value = None
                for weight, (_, _, source) in zip(weights, terms, strict=True):
                    term = weight * source[kind, :, here].astype(F32)
                    value = term if value is None else value + term
                s["page_grad"][page * lay.pieces + piece_index, kind] = value.astype(BF16)
        return 0

    lax.fori_loop(0, lay.pages_half, add_page, 0)

    ready("qkv", "att")
    if parts > 1:
        ready("query")
    s["dq_acc"][...] = jnp.zeros_like(s["dq_acc"])
    do_copies.wait()
    memory_copies = from_units(s["mem_recv"], (lay.heads - 1) * HEAD_DIM)
    for offset in range(half):
        source = s["page_grad"].at[lax.rem(me ^ offset, half)]
        place = s["mem_recv"].at[part, :, pl.ds(head * HEAD_DIM, HEAD_DIM), :]
        memory_copies.start(offset, source, place)
    weight_job(middle, 2, s["rel_da"], r["mixed"])

    def key_block(key_index, _):
        here = pl.ds(pl.multiple_of(key_index * block, block), block)
        keys, values = r["qkv"][1, :, here], r["qkv"][2, :, here]
        key_rows, value_rows = keys.T, values.T
        codes = jnp.broadcast_to(r["code"][:, here], (8, block)).T[:, :1]

        def fold(index, grads, causal):
            dk, dv = grads
            columns = pl.ds(pl.multiple_of(index * block, block), block)
            query = r["query"][:, columns] if parts > 1 else r["qkv"][0, :, columns]
            grad = s["do_unit"][:, columns]
            row_dot = jnp.sum(grad.astype(F32) * r["att"][:, columns], axis=0, keepdims=True)
            scores = jnp.dot(key_rows, query, preferred_element_type=F32)
            allowed = codes == r["qseg"][:, columns]
            if causal:
                places = index * block + lax.broadcasted_iota(jnp.int32, (1, block), 1)
                positions = ((places // rows) * parts + part) * rows + places % rows
                key_places = key_index * block + lax.broadcasted_iota(jnp.int32, (block, block), 0)
                allowed = allowed & (key_places <= positions)
            weights = jnp.where(allowed, jnp.exp2(scores * EXP2_SCALE - r["log"][:, columns]), 0.0)
            weight_grad = jnp.dot(value_rows, grad, preferred_element_type=F32)
            score_grad = (weights * (weight_grad - row_dot)).astype(BF16)
            s["dq_acc"][:, columns] += jnp.dot(keys, score_grad, preferred_element_type=F32)
            return (dk + dot(query, score_grad, 1, 1), dv + dot(grad, weights.astype(BF16), 1, 1))

        zeros = jnp.zeros((HEAD_DIM, block), F32)
        first_index = key_index // parts
        grads = fold(first_index, (zeros, zeros), True)
        dk, dv = lax.fori_loop(
            first_index + 1, mine_total // block, lambda i, g: fold(i, g, False), grads
        )
        r["qkv"][1, :, here] = (dk * SCALE).astype(BF16)
        r["qkv"][2, :, here] = dv.astype(BF16)
        return 0

    lax.fori_loop(0, total // block, key_block, 0)
    if parts == 1:
        r["qkv"][0] = (s["dq_acc"][...] * SCALE).astype(BF16)
        dq_copies = links.collect(r["qkv"].at[0], s["in_small"].at[1])
    else:
        r["qkv"][0] = jnp.zeros((HEAD_DIM, total), BF16)
        for number in range(count // parts):
            value = (s["dq_acc"][:, number * rows : (number + 1) * rows] * SCALE).astype(BF16)
            s["dq_low"][:, number * rows : (number + 1) * rows] = value
            r["qkv"][0, :, pl.ds((number * parts + part) * rows, rows)] = value
        dq_copies = links.collect(s["dq_low"], s["in_small"].at[1])
    unit_copy = links.to_other_core(r["qkv"], s["unit_other"])
    dkv_copies = from_units(s["dkv_recv"], (2 * lay.heads - 1) * HEAD_DIM // 2)
    for offset in range(count):
        peer = me ^ offset
        source = r["qkv"].at[pl.ds(1, 2), :, pl.ds(peer * rows, rows)]
        place = s["dkv_recv"].at[part, :, pl.ds(head * HEAD_DIM, HEAD_DIM), pl.ds(pack * rows, rows)]
        dkv_copies.start(offset, source, place)
    unit_copy.wait()
    number_to = count // 2
    first_exchange = Exchange(links, [s["first_recv"]], [s["first_low"].at[1]])

    def first_copy(index, number):
        device = {"blk": core * number_to + number, "tp": core if index == 0 else 1 - core}
        source = s["first_low"].at[index, pl.ds(number * share, share), :]
        return links.described(first_exchange.index, source, s["first_recv"].at[me], device)

    for index, ref in enumerate((r["qkv"], s["unit_other"])):
        value, most = None, s["h1"].shape[1]
        for start in range(0, total, most):
            if start + index > 0 and total > most:
                h1_copy = links.local(r["h1_pack"].at[:, pl.ds(start, most)], s["h1"])
            if start + index == 0 or total > most:
                h1_copy.wait()
            term = dot(s["h1"][...], ref[:, :, start : start + most].reshape(3 * HEAD_DIM, most), 1, 1)
            value = term if value is None else value + term
        s["first_low"][index] = value.astype(BF16)
        for number in range(number_to):
            if index == 1:
                first_copy(index, number).start()
                continue
            own = me == core * number_to + number

            @pl.when(jnp.logical_not(own))
            def _(number=number):
                first_copy(0, number).start()

            @pl.when(own)
            def _(number=number):
                first_exchange.keep(
                    s["first_low"].at[0, pl.ds(number * share, share), :], s["first_recv"].at[me]
                )

    down.keep_jobs()

    ready("mem", "w_ck", "w_cv")
    memory_copies.wait()
    if parts > 1:
        for kind in range(2):
            value = s["mem_recv"][0, kind].astype(F32)
            for index in range(1, parts):
                value = value + s["mem_recv"][index, kind].astype(F32)
            s["mem_recv"][0, kind] = value.astype(BF16)
    relative(s["rel_mem"], r["mem"])
    weight_job(pages, 0, s["rel_mem"], s["mem_recv"].at[0, 0])
    weight_job(pages, 1, s["rel_mem"], s["mem_recv"].at[0, 1])
    du_copies.wait()
    up.add_job(0, slice_width // 2, feed_job(s["rel_h3"], s["du_group"]))
    for start in range(0, lay.mem_pad, LANES):
        here = slice(start, start + LANES)
        s["mem_send"][here, :] = (
            dot(s["mem_recv"][0, 0, :, here].T, r["w_ck"][...], 1, 1)
            + dot(s["mem_recv"][0, 1, :, here].T, r["w_cv"][...], 1, 1)
        ).astype(BF16)
    load("w_k")
    load("w_v")
    mem_copies = [
        links.to_other_core(s["mem_send"], o["memory_other"]),
        links.local(s["mem_send"], o["memory_own"]),
    ]

    ready("w_q", "w_k", "w_v", "x")
    dq_copies.wait()
    dkv_copies.wait()
    if parts > 1:
        for kind in range(2):
            value = s["dkv_recv"][0, kind].astype(F32)
            for index in range(1, parts):
                value = value + s["dkv_recv"][index, kind].astype(F32)
            s["dkv_recv"][0, kind] = value.astype(BF16)
    pieces = (s["in_small"].at[1], s["dkv_recv"].at[0, 0], s["dkv_recv"].at[0, 1])
    tp_copies = []
    for start in range(0, flat_rows, rows):
        here = slice(start, start + rows)
        s["tp_send"][here, :] = sum(
            dot(value[:, here].T, r[weight][...], 1, 1)
            for value, weight in zip(pieces, ("w_q", "w_k", "w_v"), strict=True)
        ).astype(BF16)
        tp_copies.append(
            links.to_other_core(s["tp_send"].at[pl.ds(start, rows)], s["tp_recv"].at[1, pl.ds(start, rows)])
        )
    middle.keep_jobs()
    wait_all(tp_copies)
    norm_back_rows(
        o["input"],
        both_cores(1),
        lambda here: r["x"][here, :].astype(F32),
        r["gain_one"],
        lambda here: s["grad_one"][here, :],
    )
    pages.keep_jobs()
    up.keep_jobs()

    final_copies = []

    def finish_feed():
        for offset in range(group):
            rows_to = pl.ds(lax.rem(me ^ offset, group) * share, share)
            for index, sums in enumerate((s["down_sums"], s["up_sums"])):
                place = s["feed_last"].at[index, lax.rem(me, group)]
                final_copies.append(links.to(offset, sums.at[:, rows_to, :], place))

    for step in range(1, bits):
        last = step == bits - 1
        middle.receive(step, s["middle_result"] if last else None)
        if 2 <= step <= bits - 2:
            up.receive(step - 1)
        if step == bits - 2:
            finish_feed()
        pages.receive(step, s["pages_result"] if last else None)
        if step <= bits - 3:
            down.receive(step)
    wait_all(final_copies)
    for number in range(group):
        for kind in range(2):
            start = number * slice_width + kind * slice_width // 2
            here = slice(start, start + slice_width // 2)
            o["down"][:, here] = s["feed_last"][0, number, kind].astype(F32)
            o["up"][:, here] = s["feed_last"][1, number, kind].astype(F32)
    for kind in range(2):
        here = slice(kind * piece, (kind + 1) * piece)
        o["cross_out"][:, here] = s["middle_result"][kind, :, :piece]
        o["cross_query"][:, here] = s["middle_result"][kind, :, piece : 2 * piece]
        o["out"][:, here] = s["middle_result"][kind, :, 2 * piece :]
        o["cross_key"][:, here] = s["pages_result"][kind, :, :piece]
        o["cross_value"][:, here] = s["pages_result"][kind, :, piece:]
    first_exchange.wait()
    keeps = me // number_to == core

    def wait_rest(size):
        rest = s["first_low"].at[0, pl.ds(0, size), :]
        pltpu.make_async_copy(rest, rest, links.send_sem.at[first_exchange.index]).wait()

    pl.when(keeps)(lambda: wait_rest(wide - share))
    pl.when(jnp.logical_not(keeps))(lambda: wait_rest(wide))
    for index in range(lay.heads):
        value = None
        for side in range(2):
            for number in range(parts):
                term = s["first_recv"][side * half + index * parts + number].astype(F32)
                value = term if value is None else value + term
        for place, name in enumerate(("query", "key", "value")):
            o[name][:, index * HEAD_DIM : (index + 1) * HEAD_DIM] = value[
                :, place * HEAD_DIM : (place + 1) * HEAD_DIM
            ]

    wait_all(row_copies)
    lanes = lax.broadcasted_iota(jnp.int32, (share, LANES), 1)
    sums, gains = jnp.zeros((share, LANES), F32), jnp.ones((share, LANES), F32)
    pairs = (
        ("gain_one", (("w_q", "query"), ("w_k", "key"), ("w_v", "value"))),
        ("gain_two", (("w_cross_query", "cross_query"),)),
        ("gain_three", (("w_up", "up"),)),
    )
    for index, (gain, terms) in enumerate(pairs):
        value = sum(
            jnp.sum(s["rows_" + weight][...].astype(F32) * o[name][...], axis=1, keepdims=True)
            for weight, name in terms
        )
        s["gain_turned"][...] = jnp.broadcast_to(r[gain][...], (8, width)).T
        sums = jnp.where(lanes == index, value, sums)
        gains = jnp.where(lanes == index, s["gain_turned"][own_rows, :1], gains)
    s["gain_sums"][0] = sums
    links.to_other_core(s["gain_sums"].at[0], s["gain_sums"].at[1]).wait()
    turned = ((s["gain_sums"][0] + s["gain_sums"][1]) / gains).T
    for index, (gain, _) in enumerate(pairs):
        o[gain][...] = turned[index : index + 1, :]
    wait_all(mem_copies)
    assert links.used <= links.send_sem.shape[0] and links.own_used <= links.own_sem.shape[0]


def backward(lay, values, ff):
    parts, count, half, rows = lay.parts, lay.count, lay.half, lay.rows
    flat_rows, width = values["dc"].shape
    wide = lay.heads * HEAD_DIM
    total = count * rows
    mine_total = total // parts
    span = lay.pieces * lay.mem_pad
    bits = count.bit_length() - 1
    late = [
        "doc_unit", "kv_main", "kv_small", "cross_unit", "cross_att", "w_out", "dm_group", "h3_group",
        "cross_mixed", "w_cross_query", "r1", "grad_two", "mixed", "qkv", "mem", "h2", "w_ck", "w_cv",
    ]
    if parts > 1:
        late.append("query")
    late = {name: name for name in late}
    late.update(w_q="w_cross_query", w_k="w_ck", w_v="w_cv", att="cross_att", x="h2")
    far = ["h1_pack", "gelu", "du", "w_up"]
    early = [name for name in values if name not in late and name not in far + ["segment_page"]]
    names = ["segment_page"] + early + list(late) + far
    vmem, anywhere = pl.BlockSpec(memory_space=pltpu.VMEM), pl.BlockSpec(memory_space=pl.ANY)

    def buffer(*shape, dtype=BF16):
        return pltpu.VMEM(shape, dtype)

    share = width // count
    scratch = {
        "send_sem": pltpu.SemaphoreType.DMA((8 * bits + 24,)),
        "recv_sem": pltpu.SemaphoreType.DMA((8 * bits + 24,)),
        "own_sem": pltpu.SemaphoreType.DMA((40,)),
        "out_small": buffer(1, wide, flat_rows),
        "in_small": buffer(2, wide, flat_rows),
        "do_unit": buffer(HEAD_DIM, mine_total),
        "dq_acc": buffer(HEAD_DIM, mine_total, dtype=F32),
        "dq_low": buffer(HEAD_DIM, mine_total),
        "turn": buffer(width, flat_rows),
        "rel_dm": buffer(width, 4 * flat_rows),
        "rel_h3": buffer(width, 4 * flat_rows),
        "rel_dc": buffer(width, flat_rows),
        "rel_h2": buffer(width, flat_rows),
        "rel_da": buffer(width, flat_rows),
        "rel_mem": buffer(width, lay.mem_pad),
        "feed_last": buffer(2, 4, 2, share, ff // 8),
        "gelu_group": buffer(4, flat_rows, ff // 4),
        "du_group": buffer(4, flat_rows, ff // 4),
        "h1": buffer(wide, min(total, 2048)),
        "cross_key": buffer(span, HEAD_DIM),
        "cross_value": buffer(span, HEAD_DIM),
        "cross_acc": buffer(2, HEAD_DIM, span, dtype=F32),
        "main_low": buffer(2, HEAD_DIM, span),
        "main_twin": buffer(2, HEAD_DIM, span),
        "small_grad": buffer(2, NSEG - 1, 2, HEAD_DIM, span),
        "ends_rows": buffer(2, 8, 2 * LANES, dtype=F32),
        "ends_doc": buffer(2, HEAD_DIM, LANES),
        "ends_dq": buffer(2, 2, HEAD_DIM, LANES),
        "page_grad": buffer(half, 2, HEAD_DIM, lay.mem_pad),
        "mem_recv": buffer(parts, 2, wide, lay.mem_pad),
        "mem_send": buffer(lay.mem_pad, width),
        "tp_send": buffer(flat_rows, width),
        "tp_recv": buffer(2, flat_rows, width),
        "grad_one": buffer(flat_rows, width, dtype=F32),
        "da": buffer(flat_rows, width),
        "dkv_recv": buffer(parts, 2, wide, flat_rows),
        "unit_other": buffer(3, HEAD_DIM, total),
        "first_low": buffer(2, wide, 3 * HEAD_DIM),
        "first_recv": buffer(count, share, 3 * HEAD_DIM),
        "middle_result": buffer(2, share, 3 * wide // 2, dtype=F32),
        "pages_result": buffer(2, share, wide, dtype=F32),
        "gain_turned": buffer(width, 8, dtype=F32),
        "gain_sums": buffer(2, share, LANES, dtype=F32),
        "rows_w_up": buffer(share, ff),
    }
    for name in ("w_q", "w_k", "w_v", "w_cross_query"):
        scratch["rows_" + name] = buffer(share, wide)
    columns = {"down": ff // 8, "up": ff // 8, "middle": 3 * wide // 2, "pages": wide}
    for name, number in columns.items():
        scratch[name + "_sums"] = buffer(2, width // 2, number)
        steps = bits - 2 if name in ("down", "up") else bits
        for index, shape in enumerate(arrivals_shapes(steps, width, number)):
            scratch[f"{name}_{index}"] = shape
    homes = {}
    for name, home in late.items():
        homes.setdefault(home, values[name])
    for home, value in homes.items():
        scratch["in_" + home] = pltpu.VMEM(value.shape, value.dtype)

    shapes = {"up": (share, ff), "down": (share, ff)}
    shapes.update({name: (1, share) for name in ("gain_one", "gain_two", "gain_three")})
    outs = {name: jax.ShapeDtypeStruct(shapes.get(name, (share, wide)), F32) for name in OUTS}
    outs["input"] = jax.ShapeDtypeStruct((flat_rows, width), F32)
    for name in ("memory_own", "memory_other"):
        outs[name] = jax.ShapeDtypeStruct((lay.mem_pad, width), BF16)
    results = pl.pallas_call(
        functools.partial(backward_body, lay, names, late, list(scratch)),
        out_shape=list(outs.values()),
        in_specs=[pl.BlockSpec(memory_space=pltpu.SMEM)]
        + [vmem] * len(early)
        + [anywhere] * (len(late) + len(far)),
        out_specs=[anywhere if name.startswith("memory") else vmem for name in OUTS],
        scratch_shapes=list(scratch.values()),
        compiler_params=pltpu.CompilerParams(
            collective_id=1, has_side_effects=True, vmem_limit_bytes=63 * 1024 * 1024 + 512 * 1024
        ),
    )(*[values[name] for name in names])
    return dict(zip(OUTS, results, strict=True))


def local(
    tokens,
    memory,
    segment_ids,
    token_valid,
    segment_page,
    gain_one,
    weight_query,
    weight_key,
    weight_value,
    weight_out,
    gain_two,
    cross_query,
    cross_key,
    cross_value,
    cross_out,
    gain_three,
    weight_up,
    weight_down,
    cotangent,
):
    packs, rows, width = tokens.shape
    wide, ff = weight_query.shape[1], weight_up.shape[1]
    lay = Layout(lax.axis_size("blk"), packs, wide // HEAD_DIM, rows, memory.shape[0])
    flat_rows = packs * rows
    x = tokens.reshape(flat_rows, width)
    kept = forward(
        lay,
        {
            "segment_page": segment_page,
            "x": x,
            "segment_ids": segment_ids,
            "token_valid": token_valid,
            "memory": memory,
            "gain_one": gain_one[None],
            "gain_two": gain_two[None],
            "gain_three": gain_three[None],
            "w_q": weight_query,
            "w_k": weight_key,
            "w_v": weight_value,
            "w_ck": cross_key,
            "w_cv": cross_value,
            "cot": cotangent.reshape(flat_rows, width),
            "w_out": weight_out,
            "w_cross_query": cross_query,
            "w_cross_out": cross_out,
            "w_up": weight_up,
            "w_down": weight_down,
        },
        ff,
    )
    out = kept.pop("out").reshape(packs, rows, width)
    grads = backward(
        lay,
        {
            **kept,
            "segment_page": segment_page,
            "x": x,
            "gain_one": gain_one[None],
            "gain_two": gain_two[None],
            "gain_three": gain_three[None],
            "w_cross_query": cross_query,
            "w_out": weight_out,
            "w_ck": cross_key,
            "w_cv": cross_value,
            "w_q": weight_query,
            "w_k": weight_key,
            "w_v": weight_value,
            "w_up": weight_up,
        },
        ff,
    )
    grad_memory = (grads["memory_own"].astype(F32) + grads["memory_other"].astype(F32))[: lay.mem_rows]
    return (
        out,
        grads["input"].reshape(packs, rows, width),
        grad_memory,
        grads["query"],
        grads["key"],
        grads["value"],
        grads["out"].T,
        grads["cross_query"],
        grads["cross_key"],
        grads["cross_value"],
        grads["cross_out"].T,
        grads["up"],
        grads["down"].T,
        grads["gain_one"].reshape(width // lay.count),
        grads["gain_two"].reshape(width // lay.count),
        grads["gain_three"].reshape(width // lay.count),
    )


def solution(mesh):
    in_specs = (
        P(None, "blk", None),
        P("blk", None),
        P(None, "blk"),
        P(None, "blk"),
        P(),
        P(),
        P(None, "tp"),
        P(None, "tp"),
        P(None, "tp"),
        P("tp", None),
        P(),
        P(None, "tp"),
        P(None, "tp"),
        P(None, "tp"),
        P("tp", None),
        P(),
        P(None, "tp"),
        P("tp", None),
        P(None, "blk", None),
    )
    out_specs = (
        P(None, "blk", None),
        P(None, "blk", None),
        P("blk", None),
        P("blk", "tp"),
        P("blk", "tp"),
        P("blk", "tp"),
        P("tp", "blk"),
        P("blk", "tp"),
        P("blk", "tp"),
        P("blk", "tp"),
        P("tp", "blk"),
        P("blk", "tp"),
        P("tp", "blk"),
        P("blk"),
        P("blk"),
        P("blk"),
    )
    return jax.shard_map(local, mesh=mesh, in_specs=in_specs, out_specs=out_specs, check_vma=False)
```

```python
import functools

import jax
import jax.numpy as jnp
from jax import lax
from jax.experimental import pallas as pl
from jax.experimental.pallas import tpu as pltpu
from jax.sharding import PartitionSpec as P

MEM_LEN = 588
HEAD_DIM = 64
NSEG = 3
EPS = 1e-05
NEG = -1e30
EXP2_SCALE = HEAD_DIM**-0.5 * 1.4426950408889634
SCALE = HEAD_DIM**-0.5
LANES = 128
BF16 = jnp.bfloat16
F32 = jnp.float32
MESH = pl.DeviceIdType.MESH


def dot(left, right, contract_left, contract_right):
    return lax.dot_general(
        left, right, (((contract_left,), (contract_right,)), ((), ())), preferred_element_type=F32
    )


def wait_all(copies):
    for copy in copies:
        copy.wait()


class Layout:
    def __init__(self, count, packs, heads, rows, mem_rows):
        self.count, self.packs, self.heads, self.rows = count, packs, heads, rows
        self.half = count // packs
        self.parts = self.half // heads
        self.mem_rows = mem_rows
        self.mem_pad = -(-mem_rows // LANES) * LANES
        self.pieces = MEM_LEN // mem_rows
        self.pages_half = self.half // self.pieces

    def head(self, device):
        return lax.rem(device, self.half) // self.parts


def page_rows(span, piece, real):
    places = lax.broadcasted_iota(jnp.int32, (span, 1), 0)
    return lax.rem(places, piece) < real


def erf(value):
    x = jnp.clip(value, -3.832506856900711, 3.832506856900711)
    square = x * x
    top = jnp.float32(0.00022905065861350646)
    for coefficient in (0.0034082910107109506, 0.050955695062380861, 0.18520832239976145, 1.128379143519084):
        top = top * square + coefficient
    low = jnp.float32(-1.1791602954361697e-7)
    for coefficient in (
        0.000023547966471313185,
        0.0010179625278914885,
        0.014070470171167667,
        0.11098505178285362,
        0.49746925110067538,
        1.0,
    ):
        low = low * square + coefficient
    return x * top / low


def normed_rows(source, gain, low):
    step = 32

    def body(index, _):
        rows = pl.ds(pl.multiple_of(index * step, step), step)
        value = source(rows)
        centred = value - jnp.mean(value, axis=1, keepdims=True)
        inv_std = lax.rsqrt(jnp.mean(centred * centred, axis=1, keepdims=True) + EPS)
        low[rows, :] = (centred * inv_std * gain[...]).astype(BF16)
        return 0

    lax.fori_loop(0, low.shape[0] // step, body, 0)


def norm_back_rows(target, grad, source, gain, residual, low=None):
    step = 32

    def body(index, _):
        rows = pl.ds(pl.multiple_of(index * step, step), step)
        value = source(rows)
        centred = value - jnp.mean(value, axis=1, keepdims=True)
        inv_std = lax.rsqrt(jnp.mean(centred * centred, axis=1, keepdims=True) + EPS)
        z = centred * inv_std
        w = grad(rows) * gain[...]
        inner = w - jnp.mean(w, axis=1, keepdims=True) - z * jnp.mean(w * z, axis=1, keepdims=True)
        value = residual(rows) + inner * inv_std
        target[rows, :] = value
        if low is not None:
            low[rows, :] = value.astype(BF16)
        return 0

    lax.fori_loop(0, target.shape[0] // step, body, 0)


class Exchange:
    def __init__(self, links, received, sent):
        self.links, self.index = links, links.take()
        self.received, self.sent = received, sent

    def start(self, offset, source, target):
        if offset == 0:
            self.keep(source, target)
        else:
            self.links.described(self.index, source, target, {"blk": self.links.me ^ offset}).start()

    def keep(self, source, target):
        pltpu.make_async_copy(source, target, self.links.recv_sem.at[self.index]).start()

    def wait(self):
        for sem, buffers in ((self.links.recv_sem, self.received), (self.links.send_sem, self.sent)):
            for buffer in buffers:
                pltpu.make_async_copy(buffer, buffer, sem.at[self.index]).wait()


class Links:
    def __init__(self, lay, scratch):
        self.lay = lay
        self.me, self.core = lax.axis_index("blk"), lax.axis_index("tp")
        self.head, self.pack = lay.head(self.me), self.me // lay.half
        self.part = lax.rem(self.me, lay.parts)
        self.send_sem, self.recv_sem, self.used = scratch["send_sem"], scratch["recv_sem"], 0
        self.own_sem, self.own_used = scratch["own_sem"], 0
        self.barrier = pltpu.get_barrier_semaphore()

    def page_of(self, pages, side, slot):
        place = pages[self.pack if side == 0 else 1 - self.pack, slot] - self.pack * self.lay.pages_half
        inside = (place >= 0) & (place < self.lay.pages_half)
        return jnp.clip(place, 0, self.lay.pages_half - 1), jnp.where(inside, 1.0, 0.0)

    def announce(self, everyone=False):
        for offset in range(self.lay.count):
            if offset > 0:
                self.signal(offset, self.core)
            if offset == 0 or everyone:
                self.signal(offset, 1 - self.core)

    def signal(self, offset, core):
        device = {"blk": self.me ^ offset, "tp": core}
        pl.semaphore_signal(self.barrier, inc=1, device_id=device, device_id_type=MESH)

    def all_here(self, everyone=False):
        pl.semaphore_wait(self.barrier, (2 if everyone else 1) * self.lay.count - (1 if everyone else 0))

    def take(self, number=1):
        index, self.used = self.used, self.used + number
        return index

    def described(self, index, source, target, device):
        return pltpu.make_async_remote_copy(
            src_ref=source,
            dst_ref=target,
            send_sem=self.send_sem.at[index],
            recv_sem=self.recv_sem.at[index],
            device_id=device,
            device_id_type=MESH,
        )

    def remote(self, source, target, device):
        copy = self.described(self.take(), source, target, device)
        copy.start()
        return copy

    def local(self, source, target):
        copy = pltpu.make_async_copy(source, target, self.own_sem.at[self.own_used])
        self.own_used += 1
        copy.start()
        return copy

    def to(self, offset, source, target):
        if offset == 0:
            return self.local(source, target)
        return self.remote(source, target, {"blk": self.me ^ offset})

    def to_other_core(self, source, target):
        return self.remote(source, target, {"tp": 1 - self.core})

    def spread(self, source, target, every=False):
        lay, step = self.lay, 1 if every else self.lay.parts
        most = lay.count // step * lay.rows
        exchange = Exchange(self, [target], [target.at[:, pl.ds(0, most - lay.rows)]])
        for offset in range(0, lay.count, step):
            peer = self.me ^ offset
            piece = source.at[
                pl.ds(lay.head(peer) * HEAD_DIM, HEAD_DIM), pl.ds((peer // lay.half) * lay.rows, lay.rows)
            ]
            exchange.start(offset, piece, target.at[:, pl.ds((self.me // step) * lay.rows, lay.rows)])
        return exchange

    def unit_place(self, target):
        lay = self.lay
        return target.at[pl.ds(self.head * HEAD_DIM, HEAD_DIM), pl.ds(self.pack * lay.rows, lay.rows)]

    def collect(self, source, target):
        lay, exchange = self.lay, self.to_tokens(target)
        for offset in range(0, lay.count, lay.parts):
            peer = self.me ^ offset
            piece = source.at[:, pl.ds((peer // lay.parts) * lay.rows, lay.rows)]
            exchange.start(offset, piece, self.unit_place(target))
        return exchange

    def to_tokens(self, target):
        return Exchange(self, [target], [target.at[pl.ds(0, (2 * self.lay.heads - 1) * HEAD_DIM // 2), :]])

    def collect_later(self, source, target):
        lay, exchange = self.lay, self.to_tokens(target)

        def send(number):
            peer = number * lay.parts + self.part
            piece, place = source.at[:, pl.ds(number * lay.rows, lay.rows)], self.unit_place(target)

            @pl.when(peer != self.me)
            def _():
                self.described(exchange.index, piece, place, {"blk": peer}).start()

            @pl.when(peer == self.me)
            def _():
                exchange.keep(piece, place)

        return send, exchange.wait


HALVES = ("keys_half", "values_half")


def by_length(longest):
    first = (longest[:1, :1] < 0.5).astype(F32)
    second = (longest[:1, :1] < 1.5).astype(F32) - first
    places = (first, second, 1.0 - first - second)
    return lambda rank, slot: places[(slot - rank) % NSEG]


def forward_body(lay, names, late, out_names, scratch_names, *refs):
    r = dict(zip(names, refs, strict=False))
    o = dict(zip(out_names, refs[len(names) :], strict=False))
    s = dict(zip(scratch_names, refs[len(names) + len(out_names) :], strict=True))
    count, parts, half, rows = lay.count, lay.parts, lay.half, lay.rows
    links = Links(lay, s)
    me, core = links.me, links.core
    links.announce()
    flat_rows, width = r["x"].shape
    wide, ff = s["w_out"].shape[0], s["w_up"].shape[1]
    total = count * rows
    mine_total = total // parts
    loading = {name: links.local(r[name], s[name]) for name in late}
    leaving = []

    codes = (r["segment_ids"][...] * 2 + r["token_valid"][...]).astype(F32)
    for pack in range(lay.packs):
        s["code_tok"][pack] = jnp.broadcast_to(codes[pack : pack + 1, :], (8, rows))

    def ready(*wanted):
        for name in wanted:
            loading[name].wait()

    def emit(*wanted):
        for name in wanted:
            leaving.append(links.local(s[name], o[name]))

    half_rows = pl.ds(pl.multiple_of(core * wide, wide), wide)
    other, group = me ^ half, 4
    normed_rows(lambda here: r["x"][here, :].astype(F32), r["gain_one"], s["h1"])
    for index, name in enumerate(("w_q", "w_k", "w_v")):
        ready(name)
        s["tok"][index] = dot(s["h1"][...], s[name][...], 1, 0).astype(BF16).T
    links.all_here()
    all_copies = []
    for index in range(3):
        target = s["query"] if index == 0 and parts > 1 else s["qkv"].at[index]
        all_copies.append(links.spread(s["tok"].at[index], target, index > 0))
    all_copies.append(Exchange(links, [s["codes"]], [s["codes"].at[:, pl.ds(0, total - rows)]]))
    for offset in range(count):
        piece = s["code_tok"].at[(me ^ offset) // half]
        all_copies[-1].start(offset, piece, s["codes"].at[:, pl.ds(me * rows, rows)])

    s["mem"][lay.mem_rows // 16 * 16 :, :] = jnp.zeros_like(s["mem"][lay.mem_rows // 16 * 16 :, :])
    s["mem"][: lay.mem_rows, :] = r["memory"][...]
    emit("mem")
    ready("w_ck", "w_cv")
    memory_copies = []
    for kind, name in enumerate(("w_ck", "w_cv")):
        s["kv_tok"][kind] = dot(s["mem"][...], s[name][...], 1, 0).astype(BF16).T
        target = s[HALVES[kind]]
        memory_copies.append(Exchange(links, [target], [target.at[pl.ds(0, half - 1)]]))
        for offset in range(half):
            piece = s["kv_tok"].at[kind, pl.ds(lay.head(me ^ offset) * HEAD_DIM, HEAD_DIM), :]
            memory_copies[-1].start(offset, piece, target.at[lax.rem(me, half)])
    twin_copies = []

    def find_pages(kind):
        memory_copies[kind].wait()
        for side in range(2):
            order = by_length(s["longest"][side])
            found = [links.page_of(r["segment_page"], side, slot) for slot in range(NSEG)]
            for piece in range(lay.pieces):
                columns = slice(piece * lay.mem_pad, (piece + 1) * lay.mem_pad)
                values = [
                    s[HALVES[kind]][page * lay.pieces + piece].astype(F32) * here for page, here in found
                ]
                for rank in range(NSEG):
                    value = sum(order(rank, slot) * values[slot] for slot in range(NSEG)).astype(BF16)
                    if rank > 0:
                        s["kv_small"][side, rank - 1, kind, :, columns] = value
                    else:
                        s["main_found"][kind, side, :, columns] = value
        twin_copies.append(
            links.remote(s["main_found"].at[kind, 1], s["main_twin"].at[kind], {"blk": other})
        )

    s["h1_turned"][...] = s["h1"][:, half_rows].T

    def pack_chunk(owner, first=0, size=wide):
        return o["h1_pack"].at[pl.ds(first, size), pl.ds(pl.multiple_of(owner * rows, rows), rows)]

    def hand_over():
        return [
            links.remote(
                s["h1_turned"].at[:, pl.ds((1 - links.pack) * rows, rows)], pack_chunk(me), {"blk": other}
            ),
            links.local(s["h1_turned"].at[:, pl.ds(links.pack * rows, rows)], pack_chunk(me)),
        ]

    ways = half.bit_length() - 1
    shares = [16 * (wide // 16 // ways + (way < wide // 16 % ways)) for way in range(ways)]

    def double(step, owners):
        moved = o["h1_pack"].at[:, pl.ds(0, len(owners) * rows << step)]
        exchange = Exchange(links, [moved], [moved])
        for way in range(ways):
            first, order = sum(shares[:way]), [(way + turn) % ways for turn in range(step + 1)]
            held = [0]
            for bit in order[:-1]:
                held += [offset ^ (1 << bit) for offset in held]
            for owner in owners:
                for offset in held:
                    piece = pack_chunk(owner ^ offset, first, shares[way])
                    exchange.start(1 << order[-1], piece, piece)
        return [exchange]

    def to_group(source, target):
        moved = target.at[pl.ds(1, group - 1), :, half_rows]
        exchange = Exchange(links, [moved], [moved])
        for offset in range(1, group):
            exchange.start(offset, source.at[:, half_rows], target.at[offset, :, half_rows])
        return [exchange, links.local(source, target.at[0])]

    wait_all(all_copies)
    pack_copies = hand_over()

    codes = s["codes"][:1, :]
    segments = jnp.floor(codes * 0.5)
    s["code"][...] = jnp.where(codes - 2.0 * segments > 0.5, segments, -1.0)
    lengths = [
        jnp.sum((segments == float(slot)).astype(F32), axis=1, keepdims=True) for slot in range(NSEG)
    ]
    first_longest = ((lengths[0] >= lengths[1]) & (lengths[0] >= lengths[2])).astype(F32)
    second_longest = (lengths[1] >= lengths[2]).astype(F32) * (1.0 - first_longest)
    longest = 2.0 - 2.0 * first_longest - second_longest
    order = segments - longest
    order = jnp.where(order < 0.0, order + float(NSEG), order)
    if parts == 1:
        s["qseg"][...], s["qslot"][...] = segments, order
    else:
        s["rows"][0:1, :], s["rows"][1:2, :] = segments, order
        for piece in range(count // parts):
            there = pl.ds((piece * parts + links.part) * rows, rows)
            s["qseg"][:, piece * rows : (piece + 1) * rows] = s["rows"][0:1, there]
            s["qslot"][:, piece * rows : (piece + 1) * rows] = s["rows"][1:2, there]
    s["longest"][0] = jnp.broadcast_to(longest, s["longest"].shape[1:])
    ends = [slice(0, LANES), slice(mine_total - LANES, mine_total)]
    for index, here in enumerate(ends):
        s["ends_slot"][0, :, index * LANES : (index + 1) * LANES] = jnp.broadcast_to(
            s["qslot"][:, here], (8, LANES)
        )
    early_copies = [
        links.remote(s[name].at[0], s[name].at[1], {"blk": other}) for name in ("longest", "ends_slot")
    ]
    emit("qkv", "code", "qseg", "qslot")
    if parts > 1:
        emit("query")

    block = min(512 if parts == 1 else 256, mine_total)
    s["key"][...] = s["qkv"][1].T
    send_mixed, wait_mixed = links.collect_later(s["low"].at[0], s["mixed"])
    for index in reversed(range(mine_total // block)):
        columns = slice(index * block, (index + 1) * block)
        query = s["query"][:, columns] if parts > 1 else s["qkv"][0, :, columns]
        mine = s["qseg"][:, columns]
        places = index * block + lax.broadcasted_iota(jnp.int32, (1, block), 1)
        positions = ((places // rows) * parts + links.part) * rows + places % rows

        def fold(key_index, state, causal, query=query, mine=mine, positions=positions):
            largest, weight_sum, weighted = state
            start = pl.multiple_of(key_index * block, block)
            here = pl.ds(start, block)
            scores = jnp.dot(s["key"][here, :], query, preferred_element_type=F32)
            allowed = jnp.broadcast_to(s["code"][:, here], (8, block)).T[:, :1] == mine
            if causal:
                key_places = start + lax.broadcasted_iota(jnp.int32, (block, block), 0)
                allowed = allowed & (key_places <= positions)
            scores = jnp.where(allowed, scores, NEG)
            new = jnp.maximum(largest, jnp.max(scores, axis=0, keepdims=True))
            weights = jnp.exp2((scores - new) * EXP2_SCALE)
            keep = jnp.exp2((largest - new) * EXP2_SCALE)
            weight_sum = weight_sum * keep + jnp.sum(weights, axis=0, keepdims=True)
            update = jnp.dot(s["qkv"][2, :, here], weights.astype(BF16), preferred_element_type=F32)
            return (new, weight_sum, weighted * keep + update)

        state = (
            jnp.full((1, block), NEG, F32),
            jnp.zeros((1, block), F32),
            jnp.zeros((HEAD_DIM, block), F32),
        )
        state = lax.fori_loop(0, index * parts, lambda j, c, fold=fold: fold(j, c, False), state)
        for extra in range(parts):
            state = fold(index * parts + extra, state, True)
        largest, weight_sum, weighted = state
        result = weighted / weight_sum
        s["att"][:, columns] = result
        s["low"][0, :, columns] = result.astype(BF16)
        s["log"][:, columns] = largest * EXP2_SCALE + jnp.log2(weight_sum)
        for piece in range(index * block // rows, (index + 1) * block // rows):
            send_mixed(piece)
    emit("att", "log")

    def product_rows(left, right, sent, arrived):
        started = []
        for start in range(0, flat_rows, rows):
            here = slice(start, start + rows)
            sent[here, :] = dot(left[:, here].T, right[...], 1, 0).astype(BF16)
            started.append(links.to_other_core(sent.at[pl.ds(start, rows)], arrived.at[pl.ds(start, rows)]))
        return started

    def group_to_other_core(target):
        others = target.at[pl.ds(1, group - 1), :, half_rows]
        return links.to_other_core(others, others)

    def both(sent, arrived):
        return lambda here: sent[here, :].astype(F32) + arrived[here, :].astype(F32)

    def add_rows(target, *terms):
        step = 32

        def body(index, _):
            here = pl.ds(pl.multiple_of(index * step, step), step)
            target[here, :] = sum(term(here) for term in terms).astype(target.dtype)
            return 0

        lax.fori_loop(0, flat_rows // step, body, 0)

    wait_all(early_copies)
    for kind in range(2):
        find_pages(kind)
    for side in range(2):
        order = by_length(s["longest"][side])
        for rank in range(1, NSEG):
            here = sum(
                order(rank, slot) * links.page_of(r["segment_page"], side, slot)[1] for slot in range(NSEG)
            )
            row = 2 * side + rank - 1
            s["ends_mask"][row : row + 1, :] = (s["ends_slot"][side, :1, :] == float(rank)).astype(F32) * here
    emit("longest", "kv_small", "ends_mask")
    ready("w_out")
    wait_mixed()
    wait_all(pack_copies)
    pack_copies = double(0, [me, other])
    emit("mixed")
    started = product_rows(s["mixed"], s["w_out"], s["sent"].at[0], s["arrived"].at[0])
    wait_all(started)
    add_rows(
        s["r1"], lambda here: r["x"][here, :].astype(F32), both(s["sent"].at[0], s["arrived"].at[0])
    )
    normed_rows(lambda here: s["r1"][here, :], r["gain_two"], s["h2"])
    ready("w_cross_query")
    s["tok"][0] = dot(s["h2"][...], s["w_cross_query"][...], 1, 0).astype(BF16).T
    query_copies = links.spread(s["tok"].at[0], s["cross_unit"])
    ready("cot")
    cot_copies = to_group(s["cot"], o["dm_group"])
    emit("r1", "h2")

    narrow = min(256, mine_total)
    present = page_rows(lay.pieces * lay.mem_pad, lay.mem_pad, lay.mem_rows)
    send_cross, wait_cross = links.collect_later(s["low"].at[1], s["cross_mixed"])
    wait_all(twin_copies)
    for kind in range(2):
        value = s["main_found"][kind, 0].astype(F32) + s["main_twin"][kind].astype(F32)
        s["kv_main"][kind] = value.astype(BF16)
    emit("kv_main")
    query_copies.wait()
    ends_copies = [
        links.remote(s["cross_unit"].at[:, pl.ds(here.start, LANES)], s["ends_query"].at[index], {"blk": other})
        for index, here in enumerate(ends)
    ]
    emit("cross_unit")
    wait_all(pack_copies)
    pack_copies = double(1, [me, other])

    def attend(query, keys, values):
        scores = jnp.dot(keys, query, preferred_element_type=F32)
        scores = jnp.where(present, scores, NEG)
        largest = jnp.max(scores, axis=0, keepdims=True)
        weights = jnp.exp2((scores - largest) * EXP2_SCALE)
        weight_sum = jnp.sum(weights, axis=0, keepdims=True)
        result = jnp.dot(values, weights.astype(BF16), preferred_element_type=F32)
        return result / weight_sum, largest * EXP2_SCALE + jnp.log2(weight_sum)

    key_rows = s["kv_main"][0].T
    pieces = mine_total // rows
    for index in range(mine_total // narrow):
        columns = slice(index * narrow, (index + 1) * narrow)
        result, logs = attend(s["cross_unit"][:, columns], key_rows, s["kv_main"][1])
        s["cross_att"][:, columns], s["cross_log"][:, columns] = result, logs
        s["low"][1, :, columns] = result.astype(BF16)
        for piece in range(index * narrow // rows, (index + 1) * narrow // rows):
            if 0 < piece < pieces - 1:
                send_cross(piece)

    def attend_ends(side, query_of):
        results = [(jnp.zeros((HEAD_DIM, LANES), F32), jnp.zeros((1, LANES), F32)) for _ in ends]
        for rank in range(1, NSEG):
            keys = s["kv_small"][side, rank - 1, 0].T
            for index in range(2):
                result, logs = attend(query_of(index), keys, s["kv_small"][side, rank - 1, 1])
                row = 2 * side + rank - 1
                here = s["ends_mask"][row : row + 1, index * LANES : (index + 1) * LANES] > 0.5
                results[index] = (
                    jnp.where(here, result, results[index][0]),
                    jnp.where(here, logs, results[index][1]),
                )
        return results

    wait_all(ends_copies)
    for index, (result, logs) in enumerate(attend_ends(1, lambda index: s["ends_query"][index])):
        s["ends_att"][0, index] = result.astype(BF16)
        s["ends_log"][0, :, index * LANES : (index + 1) * LANES] = jnp.broadcast_to(logs, (8, LANES))
    ends_copies = [
        links.remote(s[name].at[0], s[name].at[1], {"blk": other}) for name in ("ends_att", "ends_log")
    ]
    own_ends = attend_ends(0, lambda index: s["cross_unit"][:, ends[index]])
    wait_all(ends_copies)
    for index, (here, (result, logs)) in enumerate(zip(ends, own_ends, strict=True)):
        small = s["qslot"][:, here] > 0.5
        result = result + s["ends_att"][1, index].astype(F32)
        logs = logs + s["ends_log"][1, :1, index * LANES : (index + 1) * LANES]
        result = jnp.where(small, result, s["cross_att"][:, here])
        s["cross_att"][:, here] = result
        s["cross_log"][:, here] = jnp.where(small, logs, s["cross_log"][:, here])
        s["low"][1, :, here] = result.astype(BF16)
        send_cross(here.start // rows)
    emit("ends_query")
    emit("cross_att", "cross_log")
    ready("w_cross_out")
    wait_cross()
    for step in range(2, ways):
        wait_all(pack_copies)
        pack_copies = double(step, [me, other])
    emit("cross_mixed")
    started = product_rows(s["cross_mixed"], s["w_cross_out"], s["sent"].at[1], s["arrived"].at[1])
    wait_all(started)
    add_rows(s["r2"], lambda here: s["r1"][here, :], both(s["sent"].at[1], s["arrived"].at[1]))
    normed_rows(lambda here: s["r2"][here, :], r["gain_three"], s["h1"])
    h3_copies = to_group(s["h1"], o["h3_group"])

    ready("w_up", "w_down")
    slice_width = ff // group
    s["down_sum"][...] = jnp.zeros_like(s["down_sum"])
    s["up_sum"][...] = jnp.zeros_like(s["up_sum"])
    piece_rows = LANES
    for number in range(group):
        columns = slice(number * slice_width, (number + 1) * slice_width)
        for start in range(0, flat_rows, piece_rows):
            here = slice(start, start + piece_rows)
            u = dot(s["h1"][here, :], s["w_up"][:, columns], 1, 0)
            grad = dot(s["cot"][here, :], s["w_down"][columns, :], 1, 1)
            normal = 0.5 + 0.5 * erf(u * 0.7071067811865476)
            s["gelu"][here, columns] = (u * normal).astype(BF16)
            slope = normal + u * jnp.exp2(u * u * -0.7213475204444817) * 0.3989422804014327
            s["du"][here, columns] = (slope * grad).astype(BF16)
        s["down_sum"][...] += dot(s["gelu"][:, columns], s["w_down"][columns, :], 1, 0)
        s["up_sum"][...] += dot(s["du"][:, columns], s["w_up"][:, columns], 1, 1)
    emit("gelu", "du")
    s["sent"][2] = s["up_sum"][...].astype(BF16)
    up_copy = links.to_other_core(s["sent"].at[2], s["arrived"].at[2])
    s["sent"][3] = s["down_sum"][...].astype(BF16)
    down_copy = links.to_other_core(s["sent"].at[3], s["arrived"].at[3])
    up_copy.wait()
    norm_back_rows(
        s["grad_two"],
        both(s["sent"].at[2], s["arrived"].at[2]),
        lambda here: s["r2"][here, :],
        r["gain_three"],
        lambda here: s["cot"][here, :].astype(F32),
        s["dc"],
    )
    s["tok"][0] = dot(s["w_cross_out"][...], s["dc"][...], 1, 1).astype(BF16)
    doc_copies = links.spread(s["tok"].at[0], s["doc_unit"])
    emit("grad_two", "dc")
    wait_all(cot_copies)
    wait_all(h3_copies)
    group_copies = [group_to_other_core(o["dm_group"]), group_to_other_core(o["h3_group"])]
    down_copy.wait()
    add_rows(s["sent"].at[3], lambda here: s["r2"][here, :], both(s["sent"].at[3], s["arrived"].at[3]))
    leaving.append(links.local(s["sent"].at[3], o["out"]))
    doc_copies.wait()
    emit("doc_unit")
    wait_all(group_copies)
    wait_all(pack_copies)
    wait_all(leaving)
    assert links.used <= links.send_sem.shape[0] and links.own_used <= links.own_sem.shape[0]


def forward(lay, values, ff):
    parts, count, half, rows = lay.parts, lay.count, lay.half, lay.rows
    flat_rows, width = values["x"].shape
    wide, total = lay.heads * HEAD_DIM, lay.count * lay.rows
    mine_total = total // parts
    span = lay.pieces * lay.mem_pad
    early = ["x", "segment_ids", "token_valid", "memory", "gain_one", "gain_two", "gain_three"]
    late = [name for name in values if name not in early + ["segment_page"]]
    names = ["segment_page"] + early + late

    def shape(*dims, dtype=BF16):
        return jax.ShapeDtypeStruct(dims, dtype)

    kept = {
        "qkv": shape(3, HEAD_DIM, total),
        "code": shape(1, total, dtype=F32),
        "qseg": shape(1, mine_total, dtype=F32),
        "qslot": shape(1, mine_total, dtype=F32),
        "longest": shape(2, 8, LANES, dtype=F32),
        "att": shape(HEAD_DIM, mine_total, dtype=F32),
        "log": shape(1, mine_total, dtype=F32),
        "mixed": shape(wide, flat_rows),
        "r1": shape(flat_rows, width, dtype=F32),
        "h2": shape(flat_rows, width),
        "cross_unit": shape(HEAD_DIM, mine_total),
        "kv_main": shape(2, HEAD_DIM, span),
        "kv_small": shape(2, NSEG - 1, 2, HEAD_DIM, span),
        "ends_query": shape(2, HEAD_DIM, LANES),
        "ends_mask": shape(8, 2 * LANES, dtype=F32),
        "cross_att": shape(HEAD_DIM, mine_total, dtype=F32),
        "cross_log": shape(1, mine_total, dtype=F32),
        "cross_mixed": shape(wide, flat_rows),
        "grad_two": shape(flat_rows, width, dtype=F32),
        "dc": shape(flat_rows, width),
        "doc_unit": shape(HEAD_DIM, mine_total),
        "mem": shape(lay.mem_pad, width),
        "gelu": shape(flat_rows, ff),
        "du": shape(flat_rows, ff),
    }
    if parts > 1:
        kept["query"] = shape(HEAD_DIM, mine_total)
    gathered = {
        "dm_group": shape(4, flat_rows, width),
        "h3_group": shape(4, flat_rows, width),
        "out": shape(flat_rows, width),
        "h1_pack": shape(wide, total),
    }
    scratch = {
        "h1": shape(flat_rows, width),
        "tok": shape(3, wide, flat_rows),
        "codes": shape(8, total, dtype=F32),
        "code_tok": shape(lay.packs, 8, rows, dtype=F32),
        "kv_tok": shape(2, wide, lay.mem_pad),
        "keys_half": shape(half, HEAD_DIM, lay.mem_pad),
        "values_half": shape(half, HEAD_DIM, lay.mem_pad),
        "main_found": shape(2, 2, HEAD_DIM, span),
        "main_twin": shape(2, HEAD_DIM, span),
        "ends_slot": shape(2, 8, 2 * LANES, dtype=F32),
        "ends_att": shape(2, 2, HEAD_DIM, LANES),
        "ends_log": shape(2, 8, 2 * LANES, dtype=F32),
        "key": shape(total, HEAD_DIM),
        "low": shape(2, HEAD_DIM, mine_total),
        "h1_turned": shape(wide, flat_rows),
        "sent": shape(4, flat_rows, width),
        "arrived": shape(4, flat_rows, width),
        "r2": shape(flat_rows, width, dtype=F32),
        "down_sum": shape(flat_rows, width, dtype=F32),
        "up_sum": shape(flat_rows, width, dtype=F32),
    }
    if parts > 1:
        scratch["rows"] = shape(8, total, dtype=F32)
    scratch = {name: pltpu.VMEM(value.shape, value.dtype) for name, value in {**scratch, **kept}.items()}
    for name in late:
        scratch[name] = pltpu.VMEM(values[name].shape, values[name].dtype)
    semaphores = pltpu.SemaphoreType.DMA((34,))
    scratch = {"send_sem": semaphores, "recv_sem": semaphores, **scratch}
    scratch["own_sem"] = pltpu.SemaphoreType.DMA((40,))
    outs = {**kept, **gathered}
    anywhere = pl.BlockSpec(memory_space=pl.ANY)
    results = pl.pallas_call(
        functools.partial(forward_body, lay, names, late, list(outs), list(scratch)),
        out_shape=list(outs.values()),
        in_specs=[pl.BlockSpec(memory_space=pltpu.SMEM)]
        + [pl.BlockSpec(memory_space=pltpu.VMEM)] * len(early)
        + [anywhere] * len(late),
        out_specs=[anywhere] * len(outs),
        scratch_shapes=list(scratch.values()),
        compiler_params=pltpu.CompilerParams(
            collective_id=0, has_side_effects=True, vmem_limit_bytes=63 * 1024 * 1024
        ),
    )(*[values[name] for name in names])
    return dict(zip(outs, results, strict=True))


def reversed_bits(value, bits):
    return sum(((value >> b) & 1) << (bits - 1 - b) for b in range(bits))


class Halving:
    def __init__(self, links, bits, sums, arrivals, crossed=True):
        self.links, self.bits, self.crossed = links, bits, crossed
        self.sums, self.arrivals = sums, arrivals
        self.quarter = sums.shape[1] // 2
        self.jobs, self.pending = [], []

    def neighbour(self, kind, step):
        bit = self.bits[1 - step if self.crosses(kind) and step < 2 else step]
        return {"blk": self.links.me ^ (1 << bit)}

    def crosses(self, kind):
        return kind == 1 and self.crossed

    def add_job(self, column, width, make):
        here, started = pl.ds(column, width), []
        for kind in range(2):
            for half, quarter in enumerate((1, 3) if self.crosses(kind) else (2, 3)):
                rows = pl.ds(half * self.quarter, self.quarter)
                self.sums[kind, rows, here] = make(kind, quarter).astype(BF16)
            started.append(
                self.links.remote(
                    self.sums.at[kind, :, here],
                    self.arrivals[0].at[kind, :, here],
                    self.neighbour(kind, 0),
                )
            )
        self.jobs.append((here, make, started))

    def keep_jobs(self):
        for here, make, started in self.jobs:
            wait_all(started)
            for kind in range(2):
                for half, quarter in enumerate((0, 2) if self.crosses(kind) else (0, 1)):
                    rows = pl.ds(half * self.quarter, self.quarter)
                    arrived = self.arrivals[0][kind, rows, here].astype(F32)
                    self.sums[kind, rows, here] = (make(kind, quarter) + arrived).astype(BF16)
        self.send(1)

    def send(self, step):
        rows = self.sums.shape[1] >> step
        self.pending = [
            self.links.remote(
                self.sums.at[kind, pl.ds(rows, rows), :],
                self.arrivals[step].at[kind],
                self.neighbour(kind, step),
            )
            for kind in range(2)
        ]

    def receive(self, step, result=None):
        rows = self.sums.shape[1] >> step
        wait_all(self.pending)
        size = min(rows, 32)

        def add(index, _):
            here = pl.ds(pl.multiple_of(index * size, size), size)
            for kind in range(2):
                mine = self.sums[kind, here, :].astype(F32)
                total = mine + self.arrivals[step][kind, here, :].astype(F32)
                if result is None:
                    self.sums[kind, here, :] = total.astype(BF16)
                else:
                    result[kind, here, :] = total
            return 0

        lax.fori_loop(0, rows // size, add, 0)
        if step + 1 < len(self.bits):
            self.send(step + 1)


def arrivals_shapes(bits, width, columns):
    return [pltpu.VMEM((2, width >> (step + 1), columns), BF16) for step in range(bits)]


OUTS = (
    "input", "memory_own", "memory_other", "query", "key", "value", "out", "cross_query", "cross_key",
    "cross_value", "cross_out", "up", "down", "gain_one", "gain_two", "gain_three",
)


def backward_body(lay, names, late, scratch_names, *refs):
    r = dict(zip(names, refs, strict=False))
    o = dict(zip(OUTS, refs[len(names) :], strict=False))
    s = dict(zip(scratch_names, refs[len(names) + len(OUTS) :], strict=True))
    far = dict(r)
    count, parts, half, rows = lay.count, lay.parts, lay.half, lay.rows
    links = Links(lay, s)
    me, core, head, pack, part = links.me, links.core, links.head, links.pack, links.part
    bits = count.bit_length() - 1
    flat_rows, width = r["dc"].shape
    wide = r["w_out"].shape[0]
    total = r["qkv"].shape[2]
    mine_total = total // parts
    share = width // count
    block = min(512 if parts == 1 else 256, mine_total)
    links.announce(everyone=True)
    loading = {}

    def load(name):
        loading[name] = links.local(r[name], s["in_" + late[name]])

    for name, home in late.items():
        if name == home:
            load(name)
    own_rows = pl.ds(pl.multiple_of(me * share, share), share)
    row_copies = [
        links.local(far[name].at[own_rows, :], s["rows_" + name])
        for name in ("w_q", "w_k", "w_v", "w_cross_query", "w_up")
    ]
    h1_copy = links.local(r["h1_pack"].at[:, pl.ds(0, s["h1"].shape[1])], s["h1"])

    def ready(*wanted):
        for name in wanted:
            loading[name].wait()
            r[name] = s["in_" + late[name]]

    def relative(target, value, shift=0, column=0):
        number, most = count >> shift, s["turn"].shape[1]
        size_rows = width // number
        for start in range(0, value.shape[0], most):
            size = min(most, value.shape[0] - start)
            s["turn"][:, :size] = value[start : start + size, :].T
            for place in range(number):
                chunk = (me >> shift) ^ reversed_bits(place, bits - shift)
                target[pl.ds(place * size_rows, size_rows), column + start : column + start + size] = s[
                    "turn"
                ][pl.ds(pl.multiple_of(chunk * size_rows, size_rows), size_rows), :size]

    quarter = width // 4

    def quarter_of(ref, index):
        return ref[pl.ds(index * quarter, quarter), :]

    def from_units(target, sent_rows):
        sent = [target.at[index] for index in range(1, parts)] + [target.at[0, :, pl.ds(0, sent_rows), :]]
        return Exchange(links, [target], sent)

    def batch(name, chosen, crossed=True):
        arrivals = [s[f"{name}_{i}"] for i in range(len(chosen))]
        return Halving(links, chosen, s[name + "_sums"], arrivals, crossed)

    piece = wide // 2

    def weight_job(target, place, left, right):
        def make(kind, index):
            return dot(quarter_of(left, index), right[kind * piece : (kind + 1) * piece, :], 1, 1)

        target.add_job(place * piece, piece, make)

    group = 4
    slice_width = s["gelu_group"].shape[2]
    links.all_here(everyone=True)

    def to_group(name):
        target = s[name + "_group"]
        exchange = Exchange(links, [target], [target.at[pl.ds(0, group - 1)]])
        for offset in range(group):
            number = lax.rem(me ^ offset, group)
            columns = pl.ds(pl.multiple_of(number * slice_width, slice_width), slice_width)
            exchange.start(offset, r[name].at[:, columns], target.at[offset])
        return exchange

    gelu_copies, du_copies = to_group("gelu"), to_group("du")

    ready("doc_unit", "kv_main", "cross_unit", "cross_att", "kv_small")
    span = r["kv_main"].shape[2]
    other = me ^ half
    ends = [slice(0, LANES), slice(mine_total - LANES, mine_total)]
    for index, here in enumerate(ends):
        columns = slice(index * LANES, (index + 1) * LANES)
        grad = r["doc_unit"][:, here].astype(F32)
        s["ends_rows"][0, 0:1, columns] = r["cross_log"][:, here]
        s["ends_rows"][0, 1:2, columns] = jnp.sum(grad * r["cross_att"][:, here], axis=0, keepdims=True)
    ends_copies = [links.remote(s["ends_rows"].at[0], s["ends_rows"].at[1], {"blk": other})]
    for index, here in enumerate(ends):
        piece_of = r["doc_unit"].at[:, pl.ds(here.start, LANES)]
        ends_copies.append(links.remote(piece_of, s["ends_doc"].at[index], {"blk": other}))
    s["cross_key"][...] = r["kv_main"][0].T
    s["cross_value"][...] = r["kv_main"][1].T
    s["cross_acc"][...] = jnp.zeros_like(s["cross_acc"])
    present = page_rows(span, lay.mem_pad, lay.mem_rows)

    def cross_block(query, grad, logs, row_dot, allowed, keys, key_rows, value_rows):
        scores = jnp.dot(key_rows, query, preferred_element_type=F32)
        weights = jnp.where(present & allowed, jnp.exp2(scores * EXP2_SCALE - logs), 0.0)
        weight_grad = jnp.dot(value_rows, grad, preferred_element_type=F32)
        score_grad = (weights * (weight_grad - row_dot)).astype(BF16)
        dq = jnp.dot(keys, score_grad, preferred_element_type=F32)
        return dq, dot(query, score_grad, 1, 1), dot(grad, weights.astype(BF16), 1, 1)

    narrow = min(256, mine_total)

    def main_slot(index, _):
        here = pl.ds(pl.multiple_of(index * narrow, narrow), narrow)
        grad = r["doc_unit"][:, here]
        row_dot = jnp.sum(grad.astype(F32) * r["cross_att"][:, here], axis=0, keepdims=True)
        dq, dk, dv = cross_block(
            r["cross_unit"][:, here],
            grad,
            r["cross_log"][:, here],
            row_dot,
            r["qslot"][:, here] < 0.5,
            r["kv_main"][0],
            s["cross_key"][...],
            s["cross_value"][...],
        )
        s["dq_acc"][:, here] = dq
        s["cross_acc"][0] += dk
        s["cross_acc"][1] += dv
        return 0

    lax.fori_loop(0, mine_total // narrow, main_slot, 0)
    s["main_low"][0] = (s["cross_acc"][0] * SCALE).astype(BF16)
    s["main_low"][1] = s["cross_acc"][1].astype(BF16)
    send_dqc, wait_dqc = links.collect_later(s["dq_low"], s["in_small"].at[0])
    s["dq_low"][...] = (s["dq_acc"][...] * SCALE).astype(BF16)
    last_piece = mine_total // rows - 1
    def small_slots(side, queries, grads):
        dq_ends = [jnp.zeros((HEAD_DIM, LANES), F32) for _ in ends]
        for rank in range(1, NSEG):
            keys, values = r["kv_small"][side, rank - 1, 0], r["kv_small"][side, rank - 1, 1]
            key_rows, value_rows = keys.T, values.T
            row, sums = 2 * side + rank - 1, None
            for index in range(2):
                columns = slice(index * LANES, (index + 1) * LANES)
                dq, dk, dv = cross_block(
                    queries(index),
                    grads(index),
                    s["ends_rows"][side, 0:1, columns],
                    s["ends_rows"][side, 1:2, columns],
                    r["ends_mask"][row : row + 1, columns] > 0.5,
                    keys,
                    key_rows,
                    value_rows,
                )
                dq_ends[index] = dq_ends[index] + dq
                sums = (dk, dv) if sums is None else (sums[0] + dk, sums[1] + dv)
            s["small_grad"][side, rank - 1, 0] = (sums[0] * SCALE).astype(BF16)
            s["small_grad"][side, rank - 1, 1] = sums[1].astype(BF16)
        return dq_ends

    wait_all(ends_copies)
    other_dq = small_slots(1, lambda index: r["ends_query"][index], lambda index: s["ends_doc"][index])
    for index in range(2):
        s["ends_dq"][0, index] = other_dq[index].astype(BF16)
    ends_copy = links.remote(s["ends_dq"].at[0], s["ends_dq"].at[1], {"blk": other})
    for number in range(1, last_piece):
        send_dqc(number)
    own_dq = small_slots(
        0, lambda index: r["cross_unit"][:, ends[index]], lambda index: r["doc_unit"][:, ends[index]]
    )
    ends_copy.wait()
    for index, here in enumerate(ends):
        value = s["dq_acc"][:, here] + own_dq[index] + s["ends_dq"][1, index].astype(F32)
        s["dq_low"][:, here] = (value * SCALE).astype(BF16)
    send_dqc(0)
    send_dqc(last_piece)
    load("att")
    twin_copies = [links.remote(s["main_low"], s["main_twin"], {"blk": other})]

    ready("dm_group")
    for offset in range(group):
        relative(s["rel_dm"], r["dm_group"].at[offset], 2, offset * flat_rows)

    def feed_job(left, right):
        def make(kind, index):
            here = slice(kind * slice_width // 2, (kind + 1) * slice_width // 2)
            return dot(
                quarter_of(left, index), right[:, :, here].reshape(group * flat_rows, slice_width // 2), 1, 0
            )

        return make

    down, up = [batch(name, range(2, bits), crossed=False) for name in ("down", "up")]
    gelu_copies.wait()
    down.add_job(0, slice_width // 2, feed_job(s["rel_dm"], s["gelu_group"]))
    middle, pages = batch("middle", range(bits)), batch("pages", range(bits))
    ready("cross_mixed")
    relative(s["rel_dc"], r["dc"])
    weight_job(middle, 0, s["rel_dc"], r["cross_mixed"])
    ready("h3_group")
    for offset in range(group):
        relative(s["rel_h3"], r["h3_group"].at[offset], 2, offset * flat_rows)

    ready("w_cross_query")
    wait_dqc()
    tp_copies = []
    for start in range(0, flat_rows, rows):
        here = slice(start, start + rows)
        s["tp_send"][here, :] = dot(s["in_small"][0, :, here].T, r["w_cross_query"][...], 1, 1).astype(BF16)
        tp_copies.append(
            links.to_other_core(s["tp_send"].at[pl.ds(start, rows)], s["tp_recv"].at[0, pl.ds(start, rows)])
        )
    ready("h2", "r1", "grad_two")
    relative(s["rel_h2"], r["h2"])
    load("x")
    weight_job(middle, 1, s["rel_h2"], s["in_small"].at[0])
    wait_all(tp_copies)

    def both_cores(index):
        def grad(here):
            return s["tp_send"][here, :].astype(F32) + s["tp_recv"][index, here, :].astype(F32)

        return grad

    norm_back_rows(
        s["grad_one"],
        both_cores(0),
        lambda here: r["r1"][here, :],
        r["gain_two"],
        lambda here: r["grad_two"][here, :],
        s["da"],
    )
    ready("w_out")
    s["out_small"][0] = dot(r["w_out"][...], s["da"][...], 1, 1).astype(BF16)
    do_copies = links.spread(s["out_small"].at[0], s["do_unit"])
    load("w_q")
    ready("mixed")
    relative(s["rel_da"], s["da"])
    orders = [by_length(r["longest"][side]) for side in range(2)]

    def hot(side, rank, page):
        value = None
        for slot in range(NSEG):
            wanted = r["segment_page"][pack if side == 0 else 1 - pack, slot]
            term = orders[side](rank, slot) * jnp.where(wanted == pack * lay.pages_half + page, 1.0, 0.0)
            value = term if value is None else value + term
        return value

    wait_all(twin_copies)
    terms = [(0, 0, s["main_low"]), (1, 0, s["main_twin"])]
    terms += [(side, rank, s["small_grad"].at[side, rank - 1]) for side in range(2) for rank in range(1, NSEG)]

    def add_page(page, _):
        weights = [hot(side, rank, page) for side, rank, _ in terms]
        for piece_index in range(lay.pieces):
            here = slice(piece_index * lay.mem_pad, (piece_index + 1) * lay.mem_pad)
            for kind in range(2):
                value = None
                for weight, (_, _, source) in zip(weights, terms, strict=True):
                    term = weight * source[kind, :, here].astype(F32)
                    value = term if value is None else value + term
                s["page_grad"][page * lay.pieces + piece_index, kind] = value.astype(BF16)
        return 0

    lax.fori_loop(0, lay.pages_half, add_page, 0)

    ready("qkv", "att")
    if parts > 1:
        ready("query")
    s["dq_acc"][...] = jnp.zeros_like(s["dq_acc"])
    do_copies.wait()
    memory_copies = from_units(s["mem_recv"], (lay.heads - 1) * HEAD_DIM)
    for offset in range(half):
        source = s["page_grad"].at[lax.rem(me ^ offset, half)]
        place = s["mem_recv"].at[part, :, pl.ds(head * HEAD_DIM, HEAD_DIM), :]
        memory_copies.start(offset, source, place)
    weight_job(middle, 2, s["rel_da"], r["mixed"])

    def key_block(key_index, _):
        here = pl.ds(pl.multiple_of(key_index * block, block), block)
        keys, values = r["qkv"][1, :, here], r["qkv"][2, :, here]
        key_rows, value_rows = keys.T, values.T
        codes = jnp.broadcast_to(r["code"][:, here], (8, block)).T[:, :1]

        def fold(index, grads, causal):
            dk, dv = grads
            columns = pl.ds(pl.multiple_of(index * block, block), block)
            query = r["query"][:, columns] if parts > 1 else r["qkv"][0, :, columns]
            grad = s["do_unit"][:, columns]
            row_dot = jnp.sum(grad.astype(F32) * r["att"][:, columns], axis=0, keepdims=True)
            scores = jnp.dot(key_rows, query, preferred_element_type=F32)
            allowed = codes == r["qseg"][:, columns]
            if causal:
                places = index * block + lax.broadcasted_iota(jnp.int32, (1, block), 1)
                positions = ((places // rows) * parts + part) * rows + places % rows
                key_places = key_index * block + lax.broadcasted_iota(jnp.int32, (block, block), 0)
                allowed = allowed & (key_places <= positions)
            weights = jnp.where(allowed, jnp.exp2(scores * EXP2_SCALE - r["log"][:, columns]), 0.0)
            weight_grad = jnp.dot(value_rows, grad, preferred_element_type=F32)
            score_grad = (weights * (weight_grad - row_dot)).astype(BF16)
            s["dq_acc"][:, columns] += jnp.dot(keys, score_grad, preferred_element_type=F32)
            return (dk + dot(query, score_grad, 1, 1), dv + dot(grad, weights.astype(BF16), 1, 1))

        zeros = jnp.zeros((HEAD_DIM, block), F32)
        first_index = key_index // parts
        grads = fold(first_index, (zeros, zeros), True)
        dk, dv = lax.fori_loop(
            first_index + 1, mine_total // block, lambda i, g: fold(i, g, False), grads
        )
        r["qkv"][1, :, here] = (dk * SCALE).astype(BF16)
        r["qkv"][2, :, here] = dv.astype(BF16)
        return 0

    lax.fori_loop(0, total // block, key_block, 0)
    if parts == 1:
        r["qkv"][0] = (s["dq_acc"][...] * SCALE).astype(BF16)
        dq_copies = links.collect(r["qkv"].at[0], s["in_small"].at[1])
    else:
        r["qkv"][0] = jnp.zeros((HEAD_DIM, total), BF16)
        for number in range(count // parts):
            value = (s["dq_acc"][:, number * rows : (number + 1) * rows] * SCALE).astype(BF16)
            s["dq_low"][:, number * rows : (number + 1) * rows] = value
            r["qkv"][0, :, pl.ds((number * parts + part) * rows, rows)] = value
        dq_copies = links.collect(s["dq_low"], s["in_small"].at[1])
    unit_copy = links.to_other_core(r["qkv"], s["unit_other"])
    dkv_copies = from_units(s["dkv_recv"], (2 * lay.heads - 1) * HEAD_DIM // 2)
    for offset in range(count):
        peer = me ^ offset
        source = r["qkv"].at[pl.ds(1, 2), :, pl.ds(peer * rows, rows)]
        place = s["dkv_recv"].at[part, :, pl.ds(head * HEAD_DIM, HEAD_DIM), pl.ds(pack * rows, rows)]
        dkv_copies.start(offset, source, place)
    unit_copy.wait()
    number_to = count // 2
    first_exchange = Exchange(links, [s["first_recv"]], [s["first_low"].at[1]])

    def first_copy(index, number):
        device = {"blk": core * number_to + number, "tp": core if index == 0 else 1 - core}
        source = s["first_low"].at[index, pl.ds(number * share, share), :]
        return links.described(first_exchange.index, source, s["first_recv"].at[me], device)

    for index, ref in enumerate((r["qkv"], s["unit_other"])):
        value, most = None, s["h1"].shape[1]
        for start in range(0, total, most):
            if start + index > 0 and total > most:
                h1_copy = links.local(r["h1_pack"].at[:, pl.ds(start, most)], s["h1"])
            if start + index == 0 or total > most:
                h1_copy.wait()
            term = dot(s["h1"][...], ref[:, :, start : start + most].reshape(3 * HEAD_DIM, most), 1, 1)
            value = term if value is None else value + term
        s["first_low"][index] = value.astype(BF16)
        for number in range(number_to):
            if index == 1:
                first_copy(index, number).start()
                continue
            own = me == core * number_to + number

            @pl.when(jnp.logical_not(own))
            def _(number=number):
                first_copy(0, number).start()

            @pl.when(own)
            def _(number=number):
                first_exchange.keep(
                    s["first_low"].at[0, pl.ds(number * share, share), :], s["first_recv"].at[me]
                )

    down.keep_jobs()
    for index, name in enumerate(("w_k", "w_v")):
        home = s["rel_dm"].at[:, pl.ds(index * wide, wide)]
        loading[name], r[name] = links.local(r[name], home), home

    ready("mem", "w_ck", "w_cv")
    memory_copies.wait()
    if parts > 1:
        for kind in range(2):
            value = s["mem_recv"][0, kind].astype(F32)
            for index in range(1, parts):
                value = value + s["mem_recv"][index, kind].astype(F32)
            s["mem_recv"][0, kind] = value.astype(BF16)
    relative(s["rel_mem"], r["mem"])
    weight_job(pages, 0, s["rel_mem"], s["mem_recv"].at[0, 0])
    weight_job(pages, 1, s["rel_mem"], s["mem_recv"].at[0, 1])
    du_copies.wait()
    up.add_job(0, slice_width // 2, feed_job(s["rel_h3"], s["du_group"]))

    ready("w_q", "x")
    loading["w_k"].wait()
    loading["w_v"].wait()
    dq_copies.wait()
    dkv_copies.wait()
    if parts > 1:
        for kind in range(2):
            value = s["dkv_recv"][0, kind].astype(F32)
            for index in range(1, parts):
                value = value + s["dkv_recv"][index, kind].astype(F32)
            s["dkv_recv"][0, kind] = value.astype(BF16)
    pieces = (s["in_small"].at[1], s["dkv_recv"].at[0, 0], s["dkv_recv"].at[0, 1])
    tp_copies = []
    for start in range(0, flat_rows, rows):
        here = slice(start, start + rows)
        s["tp_send"][here, :] = sum(
            dot(value[:, here].T, r[weight][...], 1, 1)
            for value, weight in zip(pieces, ("w_q", "w_k", "w_v"), strict=True)
        ).astype(BF16)
        tp_copies.append(
            links.to_other_core(s["tp_send"].at[pl.ds(start, rows)], s["tp_recv"].at[1, pl.ds(start, rows)])
        )
    middle.keep_jobs()
    wait_all(tp_copies)
    norm_back_rows(
        o["input"],
        both_cores(1),
        lambda here: r["x"][here, :].astype(F32),
        r["gain_one"],
        lambda here: s["grad_one"][here, :],
    )
    for start in range(0, lay.mem_pad, LANES):
        here = slice(start, start + LANES)
        s["mem_send"][here, :] = (
            dot(s["mem_recv"][0, 0, :, here].T, r["w_ck"][...], 1, 1)
            + dot(s["mem_recv"][0, 1, :, here].T, r["w_cv"][...], 1, 1)
        ).astype(BF16)
    mem_copies = [
        links.to_other_core(s["mem_send"], o["memory_other"]),
        links.local(s["mem_send"], o["memory_own"]),
    ]
    pages.keep_jobs()
    up.keep_jobs()

    final_copies = []

    def finish_feed():
        for offset in range(group):
            rows_to = pl.ds(lax.rem(me ^ offset, group) * share, share)
            for index, sums in enumerate((s["down_sums"], s["up_sums"])):
                place = s["feed_last"].at[index, lax.rem(me, group)]
                final_copies.append(links.to(offset, sums.at[:, rows_to, :], place))

    for step in range(1, bits):
        last = step == bits - 1
        middle.receive(step, s["middle_result"] if last else None)
        if 2 <= step <= bits - 2:
            up.receive(step - 1)
        if step == bits - 2:
            finish_feed()
        pages.receive(step, s["pages_result"] if last else None)
        if step <= bits - 3:
            down.receive(step)
    wait_all(final_copies)
    for number in range(group):
        for kind in range(2):
            start = number * slice_width + kind * slice_width // 2
            here = slice(start, start + slice_width // 2)
            o["down"][:, here] = s["feed_last"][0, number, kind].astype(F32)
            o["up"][:, here] = s["feed_last"][1, number, kind].astype(F32)
    for kind in range(2):
        here = slice(kind * piece, (kind + 1) * piece)
        o["cross_out"][:, here] = s["middle_result"][kind, :, :piece]
        o["cross_query"][:, here] = s["middle_result"][kind, :, piece : 2 * piece]
        o["out"][:, here] = s["middle_result"][kind, :, 2 * piece :]
        o["cross_key"][:, here] = s["pages_result"][kind, :, :piece]
        o["cross_value"][:, here] = s["pages_result"][kind, :, piece:]
    first_exchange.wait()
    keeps = me // number_to == core

    def wait_rest(size):
        rest = s["first_low"].at[0, pl.ds(0, size), :]
        pltpu.make_async_copy(rest, rest, links.send_sem.at[first_exchange.index]).wait()

    pl.when(keeps)(lambda: wait_rest(wide - share))
    pl.when(jnp.logical_not(keeps))(lambda: wait_rest(wide))
    for index in range(lay.heads):
        value = None
        for side in range(2):
            for number in range(parts):
                term = s["first_recv"][side * half + index * parts + number].astype(F32)
                value = term if value is None else value + term
        for place, name in enumerate(("query", "key", "value")):
            o[name][:, index * HEAD_DIM : (index + 1) * HEAD_DIM] = value[
                :, place * HEAD_DIM : (place + 1) * HEAD_DIM
            ]

    wait_all(row_copies)
    lanes = lax.broadcasted_iota(jnp.int32, (share, LANES), 1)
    sums, gains = jnp.zeros((share, LANES), F32), jnp.ones((share, LANES), F32)
    pairs = (
        ("gain_one", (("w_q", "query"), ("w_k", "key"), ("w_v", "value"))),
        ("gain_two", (("w_cross_query", "cross_query"),)),
        ("gain_three", (("w_up", "up"),)),
    )
    for index, (gain, terms) in enumerate(pairs):
        value = sum(
            jnp.sum(s["rows_" + weight][...].astype(F32) * o[name][...], axis=1, keepdims=True)
            for weight, name in terms
        )
        s["gain_turned"][...] = jnp.broadcast_to(r[gain][...], (8, width)).T
        sums = jnp.where(lanes == index, value, sums)
        gains = jnp.where(lanes == index, s["gain_turned"][own_rows, :1], gains)
    s["gain_sums"][0] = sums
    links.to_other_core(s["gain_sums"].at[0], s["gain_sums"].at[1]).wait()
    turned = ((s["gain_sums"][0] + s["gain_sums"][1]) / gains).T
    for index, (gain, _) in enumerate(pairs):
        o[gain][...] = turned[index : index + 1, :]
    wait_all(mem_copies)
    assert links.used <= links.send_sem.shape[0] and links.own_used <= links.own_sem.shape[0]


def backward(lay, values, ff):
    parts, count, half, rows = lay.parts, lay.count, lay.half, lay.rows
    flat_rows, width = values["dc"].shape
    wide = lay.heads * HEAD_DIM
    total = count * rows
    mine_total = total // parts
    span = lay.pieces * lay.mem_pad
    bits = count.bit_length() - 1
    late = [
        "doc_unit", "kv_main", "kv_small", "cross_unit", "cross_att", "w_out", "dm_group", "h3_group",
        "cross_mixed", "w_cross_query", "r1", "grad_two", "mixed", "qkv", "mem", "h2", "w_ck", "w_cv",
    ]
    if parts > 1:
        late.append("query")
    late = {name: name for name in late}
    late.update(w_q="w_cross_query", att="cross_att", x="h2")
    far = ["h1_pack", "gelu", "du", "w_up", "w_k", "w_v"]
    early = [name for name in values if name not in late and name not in far + ["segment_page"]]
    names = ["segment_page"] + early + list(late) + far
    vmem, anywhere = pl.BlockSpec(memory_space=pltpu.VMEM), pl.BlockSpec(memory_space=pl.ANY)

    def buffer(*shape, dtype=BF16):
        return pltpu.VMEM(shape, dtype)

    share = width // count
    scratch = {
        "send_sem": pltpu.SemaphoreType.DMA((8 * bits + 24,)),
        "recv_sem": pltpu.SemaphoreType.DMA((8 * bits + 24,)),
        "own_sem": pltpu.SemaphoreType.DMA((40,)),
        "out_small": buffer(1, wide, flat_rows),
        "in_small": buffer(2, wide, flat_rows),
        "do_unit": buffer(HEAD_DIM, mine_total),
        "dq_acc": buffer(HEAD_DIM, mine_total, dtype=F32),
        "dq_low": buffer(HEAD_DIM, mine_total),
        "turn": buffer(width, flat_rows),
        "rel_dm": buffer(width, 4 * flat_rows),
        "rel_h3": buffer(width, 4 * flat_rows),
        "rel_dc": buffer(width, flat_rows),
        "rel_h2": buffer(width, flat_rows),
        "rel_da": buffer(width, flat_rows),
        "rel_mem": buffer(width, lay.mem_pad),
        "feed_last": buffer(2, 4, 2, share, ff // 8),
        "gelu_group": buffer(4, flat_rows, ff // 4),
        "du_group": buffer(4, flat_rows, ff // 4),
        "h1": buffer(wide, min(total, 2048)),
        "cross_key": buffer(span, HEAD_DIM),
        "cross_value": buffer(span, HEAD_DIM),
        "cross_acc": buffer(2, HEAD_DIM, span, dtype=F32),
        "main_low": buffer(2, HEAD_DIM, span),
        "main_twin": buffer(2, HEAD_DIM, span),
        "small_grad": buffer(2, NSEG - 1, 2, HEAD_DIM, span),
        "ends_rows": buffer(2, 8, 2 * LANES, dtype=F32),
        "ends_doc": buffer(2, HEAD_DIM, LANES),
        "ends_dq": buffer(2, 2, HEAD_DIM, LANES),
        "page_grad": buffer(half, 2, HEAD_DIM, lay.mem_pad),
        "mem_recv": buffer(parts, 2, wide, lay.mem_pad),
        "mem_send": buffer(lay.mem_pad, width),
        "tp_send": buffer(flat_rows, width),
        "tp_recv": buffer(2, flat_rows, width),
        "grad_one": buffer(flat_rows, width, dtype=F32),
        "da": buffer(flat_rows, width),
        "dkv_recv": buffer(parts, 2, wide, flat_rows),
        "unit_other": buffer(3, HEAD_DIM, total),
        "first_low": buffer(2, wide, 3 * HEAD_DIM),
        "first_recv": buffer(count, share, 3 * HEAD_DIM),
        "middle_result": buffer(2, share, 3 * wide // 2, dtype=F32),
        "pages_result": buffer(2, share, wide, dtype=F32),
        "gain_turned": buffer(width, 8, dtype=F32),
        "gain_sums": buffer(2, share, LANES, dtype=F32),
        "rows_w_up": buffer(share, ff),
    }
    for name in ("w_q", "w_k", "w_v", "w_cross_query"):
        scratch["rows_" + name] = buffer(share, wide)
    columns = {"down": ff // 8, "up": ff // 8, "middle": 3 * wide // 2, "pages": wide}
    for name, number in columns.items():
        scratch[name + "_sums"] = buffer(2, width // 2, number)
        steps = bits - 2 if name in ("down", "up") else bits
        for index, shape in enumerate(arrivals_shapes(steps, width, number)):
            scratch[f"{name}_{index}"] = shape
    homes = {}
    for name, home in late.items():
        homes.setdefault(home, values[name])
    for home, value in homes.items():
        scratch["in_" + home] = pltpu.VMEM(value.shape, value.dtype)

    shapes = {"up": (share, ff), "down": (share, ff)}
    shapes.update({name: (1, share) for name in ("gain_one", "gain_two", "gain_three")})
    outs = {name: jax.ShapeDtypeStruct(shapes.get(name, (share, wide)), F32) for name in OUTS}
    outs["input"] = jax.ShapeDtypeStruct((flat_rows, width), F32)
    for name in ("memory_own", "memory_other"):
        outs[name] = jax.ShapeDtypeStruct((lay.mem_pad, width), BF16)
    results = pl.pallas_call(
        functools.partial(backward_body, lay, names, late, list(scratch)),
        out_shape=list(outs.values()),
        in_specs=[pl.BlockSpec(memory_space=pltpu.SMEM)]
        + [vmem] * len(early)
        + [anywhere] * (len(late) + len(far)),
        out_specs=[anywhere if name.startswith("memory") else vmem for name in OUTS],
        scratch_shapes=list(scratch.values()),
        compiler_params=pltpu.CompilerParams(
            collective_id=1, has_side_effects=True, vmem_limit_bytes=63 * 1024 * 1024 + 512 * 1024
        ),
    )(*[values[name] for name in names])
    return dict(zip(OUTS, results, strict=True))


def local(
    tokens,
    memory,
    segment_ids,
    token_valid,
    segment_page,
    gain_one,
    weight_query,
    weight_key,
    weight_value,
    weight_out,
    gain_two,
    cross_query,
    cross_key,
    cross_value,
    cross_out,
    gain_three,
    weight_up,
    weight_down,
    cotangent,
):
    packs, rows, width = tokens.shape
    wide, ff = weight_query.shape[1], weight_up.shape[1]
    lay = Layout(lax.axis_size("blk"), packs, wide // HEAD_DIM, rows, memory.shape[0])
    flat_rows = packs * rows
    x = tokens.reshape(flat_rows, width)
    kept = forward(
        lay,
        {
            "segment_page": segment_page,
            "x": x,
            "segment_ids": segment_ids,
            "token_valid": token_valid,
            "memory": memory,
            "gain_one": gain_one[None],
            "gain_two": gain_two[None],
            "gain_three": gain_three[None],
            "w_q": weight_query,
            "w_k": weight_key,
            "w_v": weight_value,
            "w_ck": cross_key,
            "w_cv": cross_value,
            "cot": cotangent.reshape(flat_rows, width),
            "w_out": weight_out,
            "w_cross_query": cross_query,
            "w_cross_out": cross_out,
            "w_up": weight_up,
            "w_down": weight_down,
        },
        ff,
    )
    out = kept.pop("out").reshape(packs, rows, width)
    grads = backward(
        lay,
        {
            **kept,
            "segment_page": segment_page,
            "x": x,
            "gain_one": gain_one[None],
            "gain_two": gain_two[None],
            "gain_three": gain_three[None],
            "w_cross_query": cross_query,
            "w_out": weight_out,
            "w_ck": cross_key,
            "w_cv": cross_value,
            "w_q": weight_query,
            "w_k": weight_key,
            "w_v": weight_value,
            "w_up": weight_up,
        },
        ff,
    )
    grad_memory = (grads["memory_own"].astype(F32) + grads["memory_other"].astype(F32))[: lay.mem_rows]
    return (
        out,
        grads["input"].reshape(packs, rows, width),
        grad_memory,
        grads["query"],
        grads["key"],
        grads["value"],
        grads["out"].T,
        grads["cross_query"],
        grads["cross_key"],
        grads["cross_value"],
        grads["cross_out"].T,
        grads["up"],
        grads["down"].T,
        grads["gain_one"].reshape(width // lay.count),
        grads["gain_two"].reshape(width // lay.count),
        grads["gain_three"].reshape(width // lay.count),
    )


def solution(mesh):
    in_specs = (
        P(None, "blk", None),
        P("blk", None),
        P(None, "blk"),
        P(None, "blk"),
        P(),
        P(),
        P(None, "tp"),
        P(None, "tp"),
        P(None, "tp"),
        P("tp", None),
        P(),
        P(None, "tp"),
        P(None, "tp"),
        P(None, "tp"),
        P("tp", None),
        P(),
        P(None, "tp"),
        P("tp", None),
        P(None, "blk", None),
    )
    out_specs = (
        P(None, "blk", None),
        P(None, "blk", None),
        P("blk", None),
        P("blk", "tp"),
        P("blk", "tp"),
        P("blk", "tp"),
        P("tp", "blk"),
        P("blk", "tp"),
        P("blk", "tp"),
        P("blk", "tp"),
        P("tp", "blk"),
        P("blk", "tp"),
        P("tp", "blk"),
        P("blk"),
        P("blk"),
        P("blk"),
    )
    return jax.shard_map(local, mesh=mesh, in_specs=in_specs, out_specs=out_specs, check_vma=False)
```
